32 devices in a mesh: batch: 2 (over y), seq: 16 (over z, x, core).
Axes of the slice: x: 2, y: 2, z: 4, core: 2. Of those that a mesh axis runs over, the one named last changes fastest.
Arguments:
- tokens_in: bfloat16 [4, 4096, 768], P('batch', 'seq'), may hold values from -6 to 6
- earlier_outs: bfloat16 [9, 4, 4096, 768], P(None, 'batch', 'seq'), may hold values from -6 to 6
- out_cotangent: bfloat16 [4, 4096, 768], P('batch', 'seq'), may hold values from -6 to 6
- seq_lengths: int32 [4], P('batch'), may hold values from 1 to 4096, as said below
- qkv_weight: float32 [768, 2304], P(('batch', 'seq')), may hold values from -0.21875 to 0.21875
- out_weight: float32 [768, 768], P(('batch', 'seq')), may hold values from -1.75 to 1.75
- up_weight: float32 [768, 3072], P(('batch', 'seq')), may hold values from -0.21875 to 0.21875
- down_weight: float32 [3072, 768], P(('batch', 'seq')), may hold values from -0.109375 to 0.109375
- qkv_first: float32 [768, 2304], P(('batch', 'seq')), may hold values from -60 to 60
- qkv_second: float32 [768, 2304], P(('batch', 'seq')), may hold values from 1 to 10000
- out_first: float32 [768, 768], P(('batch', 'seq')), may hold values from -60 to 60
- out_second: float32 [768, 768], P(('batch', 'seq')), may hold values from 1 to 10000
- up_first: float32 [768, 3072], P(('batch', 'seq')), may hold values from -60 to 60
- up_second: float32 [768, 3072], P(('batch', 'seq')), may hold values from 1 to 10000
- down_first: float32 [3072, 768], P(('batch', 'seq')), may hold values from -60 to 60
- down_second: float32 [3072, 768], P(('batch', 'seq')), may hold values from 1 to 10000
- small_params: float32 [9995], replicated, may hold values from -1.5 to 1.5
- small_first: float32 [9995], replicated, may hold values from -60 to 60
- small_second: float32 [9995], replicated, may hold values from 1 to 10000
Outputs:
- mixed: bfloat16 [4, 4096, 768], P('batch', 'seq')
- input_grad: float32 [4, 4096, 768], P('batch', 'seq')
- qkv_grad: float32 [768, 2304], P(('batch', 'seq'))
- out_grad: float32 [768, 768], P(('batch', 'seq'))
- up_grad: float32 [768, 3072], P(('batch', 'seq'))
- down_grad: float32 [3072, 768], P(('batch', 'seq'))
- small_grad: float32 [9995], replicated
- qkv_step: float32 [768, 2304], P(('batch', 'seq'))
- out_step: float32 [768, 768], P(('batch', 'seq'))
- up_step: float32 [768, 3072], P(('batch', 'seq'))
- down_step: float32 [3072, 768], P(('batch', 'seq'))
- small_step: float32 [9995], replicated
- qkv_first_new: float32 [768, 2304], P(('batch', 'seq'))
- out_first_new: float32 [768, 768], P(('batch', 'seq'))
- up_first_new: float32 [768, 3072], P(('batch', 'seq'))
- down_first_new: float32 [3072, 768], P(('batch', 'seq'))
- small_first_new: float32 [9995], replicated
The draws below stay inside these ranges and needn't reach their ends.
Inputs may be any that keep to these rules, and one draw needn't show every extreme that they name: `seq_lengths`: in every group of 2 consecutive slots (the sequences of one batch index) one slot has length 4096.
All inputs are finite; a program needn't handle non-finite values.
Results may differ from the reference program's by a relative error of at most 0.015.
Values may be sent and summed in bfloat16 or wider, within the bound.
A program may use at most 128 MiB of HBM per device.

```python
import math
import jax
import jax.numpy as jnp
from jax import lax

D = 768
FF = 3072
HEAD = 64
LEN = 4096
SEQ_G = 2
PRIOR = 9
NDWA = 11
SEQS = 4
SMALL = 9995


def draw_seq_lengths(key, part):
    key = jax.random.fold_in(key, 5)
    pick_key, length_key = jax.random.split(key)
    slot = jnp.arange(SEQS)
    group = slot // SEQ_G
    group_count = SEQS // SEQ_G
    reach = 1 + (LEN - 1) * (group + 1) // group_count
    raw = jax.random.randint(length_key, (SEQS,), 0, LEN)
    ragged = 1 + raw % reach
    chosen = jax.random.randint(pick_key, (group_count,), 0, SEQ_G)
    whole = slot % SEQ_G == chosen[group]
    return jnp.where(whole, LEN, ragged).astype(jnp.int32)


def draw_small_params(key, part):
    key = jax.random.fold_in(key, 7)
    gain_key, bias_key, mix_key = jax.random.split(key, 3)
    bias_count = 7 * D + FF
    gains = jnp.clip(1.0 + 0.1 * jax.random.normal(gain_key, (2 * D,), jnp.float32), 0.5, 1.5)
    biases = jnp.clip(0.3 * jax.random.normal(bias_key, (bias_count,), jnp.float32), -1.5, 1.5)
    mixing = jax.random.uniform(mix_key, (NDWA,), jnp.float32, 0.2, 1.0)
    return jnp.concatenate([gains, biases, mixing])


def level_of(stream_key, dims, shards, least, largest):
    factor_of = 1.0
    for position, shards_of in shards:
        draws = jax.random.uniform(jax.random.fold_in(jax.random.fold_in(stream_key, 6), position), (shards_of,), jnp.float32, least / len(shards), largest / len(shards))
        factor_of = factor_of * jnp.repeat(jnp.exp(draws), dims[position] // shards_of).reshape((-1,) + (1,) * (len(dims) - 1 - position))
    return factor_of


def normal_values(own_key, extent, width, most, shards=(), kind=jnp.bfloat16):
    values = width * jax.random.normal(own_key, extent, jnp.float32)
    if shards:
        values = values * level_of(own_key, extent, shards, -0.22, 0.18)
    return jnp.clip(values, -most, most).astype(kind)


def setup_inputs(seed: int = 0) -> dict:
    streams_of = jax.random.split(jax.random.key(seed), 20)
    return {
        "tokens_in": normal_values(streams_of[0], (SEQS, LEN, D), 1.0, 6.0, ((0, 2), (1, 16))),
        "earlier_outs": normal_values(streams_of[1], (PRIOR, SEQS, LEN, D), 1.0, 6.0, ((1, 2), (2, 16))),
        "out_cotangent": normal_values(streams_of[2], (SEQS, LEN, D), 1.0, 6.0, ((0, 2), (1, 16))),
        "seq_lengths": draw_seq_lengths(jax.random.fold_in(streams_of[19], 71), 0),
        "qkv_weight": normal_values(streams_of[4], (D, 3 * D), D ** -0.5, 0.21875, ((0, 32),), jnp.float32),
        "out_weight": normal_values(streams_of[5], (D, D), (D // 64) ** -0.5, 1.75, ((0, 32),), jnp.float32),
        "up_weight": normal_values(streams_of[6], (D, FF), D ** -0.5, 0.21875, ((0, 32),), jnp.float32),
        "down_weight": normal_values(streams_of[7], (FF, D), FF ** -0.5, 0.109375, ((0, 32),), jnp.float32),
        "qkv_first": normal_values(streams_of[8], (D, 3 * D), 10.0, 60.0, ((0, 32),), jnp.float32),
        "qkv_second": jnp.clip(jnp.exp(math.log(10000.0) - 9.2103404 * jax.random.uniform(streams_of[9], (D, 3 * D), jnp.float32) ** level_of(streams_of[9], (D, 3 * D), ((0, 32),), -0.2, 0.2)), 1.0, 10000.0),
        "out_first": normal_values(streams_of[10], (D, D), 10.0, 60.0, ((0, 32),), jnp.float32),
        "out_second": jnp.clip(jnp.exp(math.log(10000.0) - 9.2103404 * jax.random.uniform(streams_of[11], (D, D), jnp.float32) ** level_of(streams_of[11], (D, D), ((0, 32),), -0.2, 0.2)), 1.0, 10000.0),
        "up_first": normal_values(streams_of[12], (D, FF), 10.0, 60.0, ((0, 32),), jnp.float32),
        "up_second": jnp.clip(jnp.exp(math.log(10000.0) - 9.2103404 * jax.random.uniform(streams_of[13], (D, FF), jnp.float32) ** level_of(streams_of[13], (D, FF), ((0, 32),), -0.2, 0.2)), 1.0, 10000.0),
        "down_first": normal_values(streams_of[14], (FF, D), 10.0, 60.0, ((0, 32),), jnp.float32),
        "down_second": jnp.clip(jnp.exp(math.log(10000.0) - 9.2103404 * jax.random.uniform(streams_of[15], (FF, D), jnp.float32) ** level_of(streams_of[15], (FF, D), ((0, 32),), -0.2, 0.2)), 1.0, 10000.0),
        "small_params": draw_small_params(jax.random.fold_in(streams_of[19], 71), 0),
        "small_first": normal_values(streams_of[17], (SMALL,), 10.0, 60.0, (), jnp.float32),
        "small_second": jnp.clip(jnp.exp(jax.random.uniform(streams_of[18], (SMALL,), jnp.float32, math.log(1.0), math.log(10000.0))), 1.0, 10000.0),
    }


highest = lax.Precision.HIGHEST
beta_one = 0.9
beta_two = 0.999
adam_eps = 1e-08
learn_rate = 0.01
decay_rate = 0.1
adam_step = 10

@jax.custom_vjp
def low(v):
    return lax.optimization_barrier(v.astype(jnp.bfloat16)).astype(jnp.float32)

@jax.custom_vjp
def low_back(v):
    return v

def low_keep(v):
    return (low(v), None)

def low_pass(kept, grad):
    return (grad,)

def back_keep(v):
    return (v, None)

def back_low(kept, grad):
    return (low(grad),)
low.defvjp(low_keep, low_pass)
low_back.defvjp(back_keep, back_low)

def matmul(left, right):
    return jnp.dot(left, right, precision=highest)

def layer_norm(values, gain, shift):
    center = values - lax.optimization_barrier(jnp.mean(values, -1, keepdims=True))
    spread = lax.optimization_barrier(jnp.mean(center * center, -1, keepdims=True))
    return center * lax.rsqrt(spread + 1e-05) * gain + shift

def gelu_tanh(values):
    inner = 0.7978845608028654 * (values + 0.044715 * values * values * values)
    return 0.5 * values * (1.0 + jnp.tanh(inner))

def angles(positions):
    freq = 10000.0 ** (-jnp.arange(HEAD // 2, dtype=jnp.float32) * 2.0 / HEAD)
    turned = positions.astype(jnp.float32)[:, None] * freq[None, :]
    return (jnp.cos(turned), jnp.sin(turned))

def rotate(tensor, cosine, sine):
    first = tensor[..., :HEAD // 2]
    second = tensor[..., HEAD // 2:]
    cosine = cosine[:, None, :]
    sine = sine[:, None, :]
    return jnp.concatenate([first * cosine - second * sine, first * sine + second * cosine], -1)

def split_small(vector):
    gain_one = vector[0:D]
    gain_two = vector[D:2 * D]
    shift_one = vector[2 * D:3 * D]
    shift_two = vector[3 * D:4 * D]
    bias_qkv = vector[4 * D:7 * D]
    bias_out = vector[7 * D:8 * D]
    bias_up = vector[8 * D:8 * D + FF]
    bias_down = vector[8 * D + FF:9 * D + FF]
    mixing = vector[9 * D + FF:]
    return (gain_one, gain_two, shift_one, shift_two, bias_qkv, bias_out, bias_up, bias_down, mixing)

def sequence_forward(small, qkv_mat, out_mat, up_mat, down_mat, tokens, prior, length):
    gain_one, gain_two, shift_one, shift_two, bias_qkv, bias_out, bias_up, bias_down, mixing = split_small(small)
    heads = D // HEAD
    normed = low(layer_norm(tokens, gain_one, shift_one))
    joined = low_back(matmul(normed, qkv_mat) + bias_qkv)
    cosine, sine = angles(jnp.arange(LEN))
    query = low(rotate(joined[:, :D].reshape(LEN, heads, HEAD), cosine, sine))
    keys = low(rotate(joined[:, D:2 * D].reshape(LEN, heads, HEAD), cosine, sine))
    values = low(joined[:, 2 * D:].reshape(LEN, heads, HEAD))
    block = min(512, LEN)
    key_pos = jnp.arange(LEN).astype(jnp.int32)

    def attend(inputs):
        rows, start = inputs
        scores = low_back(jnp.einsum('qhd,khd->hqk', rows, keys, precision=highest) * 0.125)
        query_pos = start + jnp.arange(block).astype(jnp.int32)
        allowed = (key_pos[None, :] <= query_pos[:, None]) & (key_pos[None, :] < length)
        scores = jnp.where(allowed[None], scores, -jnp.inf)
        top = lax.optimization_barrier(jnp.max(scores, -1, keepdims=True))
        log_total = top + jnp.log(lax.optimization_barrier(jnp.sum(jnp.exp(scores - top), -1, keepdims=True)))
        shares = low(jnp.exp(scores - log_total))
        return jnp.einsum('hqk,khd->qhd', shares, values, precision=highest)
    starts = (jnp.arange(LEN // block) * block).astype(jnp.int32)
    pieces = lax.map(jax.checkpoint(attend), (query.reshape(LEN // block, block, heads, HEAD), starts))
    attended = low_back(low(pieces.reshape(LEN, D)))
    branch = low_back(matmul(attended, out_mat) + bias_out)
    middle = tokens + branch
    normed_two = low(layer_norm(middle, gain_two, shift_two))
    hidden = low_back(matmul(normed_two, up_mat) + bias_up)
    active = low(gelu_tanh(hidden))
    result = low_back(matmul(active, down_mat) + bias_down)
    layer_out = middle + result
    earlier_sum = jnp.einsum('p,pld->ld', mixing[2:], prior, precision=highest)
    return mixing[0] * layer_out + mixing[1] * tokens + earlier_sum

def adam(param, grad, first, second, decay):
    first_new = beta_one * first + (1.0 - beta_one) * grad
    second_new = beta_two * second + (1.0 - beta_two) * grad * grad
    fix_one = 1.0 - beta_one ** adam_step
    fix_two = 1.0 - beta_two ** adam_step
    update = first_new / fix_one / (jnp.sqrt(second_new / fix_two) + adam_eps)
    return (-learn_rate * (update + decay * param), first_new)

def reference(tokens_in, earlier_outs, out_cotangent, seq_lengths, qkv_weight, out_weight, up_weight, down_weight, qkv_first, qkv_second, out_first, out_second, up_first, up_second, down_first, down_second, small_params, small_first, small_second):
    tokens = tokens_in.astype(jnp.float32)
    earlier = jnp.moveaxis(earlier_outs.astype(jnp.float32), 0, 1)

    def model(small, qkv_mat, out_mat, up_mat, down_mat, rows_all):
        qkv_low = low(qkv_mat)
        out_low = low(out_mat)
        up_low = low(up_mat)
        down_low = low(down_mat)

        def one(inputs):
            rows, prior, length = inputs
            return sequence_forward(small, qkv_low, out_low, up_low, down_low, rows, prior, length)
        return lax.map(jax.checkpoint(one), (rows_all, earlier, seq_lengths))
    mixture, pullback = jax.vjp(model, small_params, qkv_weight, out_weight, up_weight, down_weight, tokens)
    count = jnp.sum(seq_lengths).astype(jnp.float32)
    slots = SEQS * LEN
    live = (jnp.arange(LEN).astype(jnp.int32)[None, :] < seq_lengths[:, None]).astype(jnp.float32)
    scale = live * (slots / count)
    cotangent = out_cotangent.astype(jnp.float32) * scale[:, :, None]
    small_grad, qkv_grad, out_grad, up_grad, down_grad, input_grad = pullback(cotangent)
    qkv_step, qkv_first_new = adam(qkv_weight, qkv_grad, qkv_first, qkv_second, decay_rate)
    out_step, out_first_new = adam(out_weight, out_grad, out_first, out_second, decay_rate)
    up_step, up_first_new = adam(up_weight, up_grad, up_first, up_second, decay_rate)
    down_step, down_first_new = adam(down_weight, down_grad, down_first, down_second, decay_rate)
    small_step, small_first_new = adam(small_params, small_grad, small_first, small_second, 0.0)
    return (mixture.astype(jnp.bfloat16), input_grad, qkv_grad, out_grad, up_grad, down_grad, small_grad, qkv_step, out_step, up_step, down_step, small_step, qkv_first_new, out_first_new, up_first_new, down_first_new, small_first_new)
```

```python
import functools
import math

import jax
import jax.numpy as jnp
from jax import lax
from jax.experimental import pallas as pl
from jax.experimental.pallas import tpu as pltpu
from jax.sharding import PartitionSpec as P

D = 768
FF = 3072
HEAD = 64
bf16 = jnp.bfloat16
f32 = jnp.float32
NEG = -1e30


def mm(a, b):
    return lax.dot_general(a, b, (((1,), (0,)), ((), ())), preferred_element_type=f32)


def half_rows(block_t, half):
    z = jnp.zeros((HEAD, block_t.shape[1]), block_t.dtype)
    if half == 0:
        return jnp.concatenate([block_t[:HEAD], z], 0)
    return jnp.concatenate([z, block_t[HEAD:]], 0)


def flash_fwd_kernel(groups, per, span, inner, lens, q, k, v, o, ot, lse, vt, qt, m_s, l_s):
    outer, rows, width = q.shape
    units = groups * per
    total = k.shape[0]
    j = lax.rem(lax.axis_index("seq"), inner)
    blk = 512

    def turn_v(i, _):
        at = pl.ds(pl.multiple_of(i * blk, blk), blk)
        for t in range(width // 128):
            lanes = slice(128 * t, 128 * t + 128)
            vt[lanes, at] = v[at, lanes].T
        return 0

    lax.fori_loop(0, total // blk, turn_v, 0)

    def one(z, _):
        first = (z * inner + j) * rows
        for t in range(width // 128):
            lanes = slice(128 * t, 128 * t + 128)
            turned = (q[z, :, lanes] * 0.125).astype(bf16).T
            for half in range(2):
                qt[2 * t + half] = half_rows(turned, half)
        for g in range(groups):
            length = lens[g]
            ot[z, g * per * HEAD : (g + 1) * per * HEAD, :] = jnp.zeros((per * HEAD, rows), f32)
            m_s[...] = jnp.full(m_s.shape, NEG, f32)
            l_s[...] = jnp.zeros(l_s.shape, f32)

            def step(c, masked):
                at = pl.ds(pl.multiple_of(c * span, span), span)
                if masked:
                    key = c * span + lax.broadcasted_iota(jnp.int32, (span, rows), 0)
                    query = first + lax.broadcasted_iota(jnp.int32, (span, rows), 1)
                    allowed = (key <= query) & (key < length)
                scores, tops, news, shares, sums = [], [], [], [], []
                for h in range(per):
                    u = g * per + h
                    s = mm(k[at, 128 * (u // 2) : 128 * (u // 2) + 128], qt[u])
                    scores.append(jnp.where(allowed, s, NEG) if masked else s)
                for h in range(per):
                    tops.append(m_s[h : h + 1])
                    news.append(jnp.maximum(tops[h], jnp.max(scores[h], 0, keepdims=True)))
                for h in range(per):
                    p = jnp.exp(scores[h] - news[h])
                    sums.append(jnp.sum(p, 0, keepdims=True))
                    shares.append(p.astype(bf16))
                for h in range(per):
                    u = g * per + h
                    alpha = jnp.exp(tops[h] - news[h])
                    l_s[h : h + 1] = l_s[h : h + 1] * alpha + sums[h]
                    m_s[h : h + 1] = news[h]
                    span_u = slice(HEAD * u, HEAD * u + HEAD)
                    ot[z, span_u, :] = ot[z, span_u, :] * alpha + mm(vt[span_u, at], shares[h])

            whole = jnp.minimum(first, length) // span
            count = (jnp.minimum(first + rows, length) + span - 1) // span

            def full_step(c, _):
                step(c, False)
                return 0

            def edge_step(c, _):
                step(c, True)
                return 0

            lax.fori_loop(0, whole, full_step, 0)
            lax.fori_loop(whole, count, edge_step, 0)
            for h in range(per):
                u = g * per + h
                span_u = slice(HEAD * u, HEAD * u + HEAD)
                total_exp = l_s[h : h + 1]
                ot[z, span_u, :] = ot[z, span_u, :] / total_exp
                lse[z, u : u + 1, :] = m_s[h : h + 1] + jnp.log(total_exp)
        for t in range(width // 128):
            lanes = slice(128 * t, 128 * t + 128)
            o[z, :, lanes] = ot[z, lanes, :].T.astype(bf16)
        return 0

    lax.fori_loop(0, outer, one, 0)


def flash_fwd(lens, q, k, v, groups, per, inner, span=1024):
    outer, rows, width = q.shape
    units = groups * per
    total = k.shape[0]
    vm = pl.BlockSpec(memory_space=pltpu.VMEM)
    return pl.pallas_call(
        functools.partial(flash_fwd_kernel, groups, per, span, inner),
        out_shape=(
            jax.ShapeDtypeStruct((outer, rows, width), bf16),
            jax.ShapeDtypeStruct((outer, width, rows), f32),
            jax.ShapeDtypeStruct((outer, 8, rows), f32),
        ),
        in_specs=[pl.BlockSpec(memory_space=pltpu.SMEM), vm, vm, vm],
        out_specs=(vm, vm, vm),
        scratch_shapes=[
            pltpu.VMEM((width, total), bf16),
            pltpu.VMEM((units, 128, rows), bf16),
            pltpu.VMEM((8, rows), f32),
            pltpu.VMEM((8, rows), f32),
        ],
        compiler_params=pltpu.CompilerParams(vmem_limit_bytes=56 << 20),
        name="attend",
    )(lens, q, k, v)


def flash_bwd_kernel(groups, per, span, inner, lens, q, k, v, do, ot, lse, cos, sin, dq, dk, dv, kt, qt, dot_t, qz, dz, rd, dqt, dks, dvs):
    outer, rows, width = q.shape
    units = groups * per
    total = k.shape[0]
    j = lax.rem(lax.axis_index("seq"), inner)
    blk = 512

    def prepare(i, _):
        at = pl.ds(pl.multiple_of(i * blk, blk), blk)
        for t in range(width // 128):
            lanes = slice(128 * t, 128 * t + 128)
            kt[lanes, at] = k[at, lanes].T
        dks[at, :] = jnp.zeros((blk, width), f32)
        dvs[at, :] = jnp.zeros((blk, width), f32)
        return 0

    lax.fori_loop(0, total // blk, prepare, 0)

    def one(z, _):
        first = (z * inner + j) * rows
        low = lax.broadcasted_iota(jnp.int32, (rows, 128), 1) < HEAD
        for t in range(width // 128):
            lanes = slice(128 * t, 128 * t + 128)
            small = (q[z, :, lanes] * 0.125).astype(bf16)
            grad = do[z, :, lanes]
            turned = small.T
            grad_t = grad.T
            prod = grad_t.astype(f32) * ot[z, lanes, :]
            for half in range(2):
                u = 2 * t + half
                qt[u] = half_rows(turned, half)
                dot_t[u] = half_rows(grad_t, half)
                keep = low if half == 0 else ~low
                qz[u] = jnp.where(keep, small, jnp.zeros_like(small))
                dz[u] = jnp.where(keep, grad, jnp.zeros_like(grad))
                rd[u : u + 1, :] = jnp.sum(prod[HEAD * half : HEAD * half + HEAD], 0, keepdims=True)
        dqt[...] = jnp.zeros(dqt.shape, f32)
        for g in range(groups):
            length = lens[g]

            def step(c, masked):
                at = pl.ds(pl.multiple_of(c * span, span), span)
                if masked:
                    key = c * span + lax.broadcasted_iota(jnp.int32, (span, rows), 0)
                    query = first + lax.broadcasted_iota(jnp.int32, (span, rows), 1)
                    allowed = (key <= query) & (key < length)
                for h in range(per):
                    u = g * per + h
                    lanes = slice(128 * (u // 2), 128 * (u // 2) + 128)
                    span_u = slice(HEAD * u, HEAD * u + HEAD)
                    s = mm(k[at, lanes], qt[u])
                    p = jnp.exp(s - lse[z, u : u + 1, :])
                    if masked:
                        p = jnp.where(allowed, p, 0.0)
                    dp = mm(v[at, lanes], dot_t[u])
                    ds = (p * (dp - rd[u : u + 1, :])).astype(bf16)
                    dvs[at, lanes] += mm(p.astype(bf16), dz[u])
                    dks[at, lanes] += mm(ds, qz[u])
                    dqt[span_u, :] += mm(kt[span_u, at], ds)

            live = first < length
            whole = jnp.where(live, jnp.minimum(first, length) // span, 0)
            count = jnp.where(live, (jnp.minimum(first + rows, length) + span - 1) // span, 0)

            def full_step(c, _):
                step(c, False)
                return 0

            def edge_step(c, _):
                step(c, True)
                return 0

            lax.fori_loop(0, whole, full_step, 0)
            lax.fori_loop(whole, count, edge_step, 0)
        cosine = cos[z]
        sine = sin[z]
        for t in range(width // 128):
            parts = []
            for half in range(2):
                u = 2 * t + half
                a = dqt[HEAD * u : HEAD * u + 32, :] * 0.125
                b = dqt[HEAD * u + 32 : HEAD * u + 64, :] * 0.125
                parts.append(a * cosine + b * sine)
                parts.append(b * cosine - a * sine)
            dq[z, :, 128 * t : 128 * t + 128] = jnp.concatenate(parts, 0).T.astype(bf16)
        return 0

    lax.fori_loop(0, outer, one, 0)

    def finish(i, _):
        at = pl.ds(pl.multiple_of(i * blk, blk), blk)
        dk[at, :] = dks[at, :].astype(bf16)
        dv[at, :] = dvs[at, :].astype(bf16)
        return 0

    lax.fori_loop(0, total // blk, finish, 0)


def flash_bwd(lens, q, k, v, do, ot, lse, cos, sin, groups, per, inner, span=1024):
    outer, rows, width = q.shape
    units = groups * per
    total = k.shape[0]
    vm = pl.BlockSpec(memory_space=pltpu.VMEM)
    return pl.pallas_call(
        functools.partial(flash_bwd_kernel, groups, per, span, inner),
        out_shape=(
            jax.ShapeDtypeStruct((outer, rows, width), bf16),
            jax.ShapeDtypeStruct((total, width), bf16),
            jax.ShapeDtypeStruct((total, width), bf16),
        ),
        in_specs=[pl.BlockSpec(memory_space=pltpu.SMEM)] + [vm] * 8,
        out_specs=(vm, vm, vm),
        scratch_shapes=[
            pltpu.VMEM((width, total), bf16),
            pltpu.VMEM((units, 128, rows), bf16),
            pltpu.VMEM((units, 128, rows), bf16),
            pltpu.VMEM((units, rows, 128), bf16),
            pltpu.VMEM((units, rows, 128), bf16),
            pltpu.VMEM((8, rows), f32),
            pltpu.VMEM((width, rows), f32),
            pltpu.VMEM((total, width), f32),
            pltpu.VMEM((total, width), f32),
        ],
        compiler_params=pltpu.CompilerParams(vmem_limit_bytes=56 << 20),
        name="attend_back",
    )(lens, q, k, v, do, ot, lse, cos, sin)


MESH = pl.DeviceIdType.MESH


def place(inner):
    batch = lax.axis_index("batch")
    rank = lax.axis_index("seq")
    return batch, lax.div(rank, inner), lax.div(lax.rem(rank, inner), 2), lax.rem(rank, 2)


def greet(peers):
    barrier = pltpu.get_barrier_semaphore()
    for peer in peers:
        pl.semaphore_signal(barrier, inc=1, device_id=peer, device_id_type=MESH)
    pl.semaphore_wait(barrier, len(peers))


def push(src, dst, send, recv, peer):
    copy = pltpu.make_async_remote_copy(
        src_ref=src, dst_ref=dst, send_sem=send, recv_sem=recv, device_id=peer, device_id_type=MESH
    )
    copy.start()
    return copy


def swap_kernel(inner, x, out, send, recv, local):
    outer = x.shape[0]
    batch, o, a, c = place(inner)
    ring = [lax.rem(o + t, outer) for t in range(1, outer)]
    peers = [(batch, p * inner + a * 2 + c) for p in ring]
    greet(peers)
    own = pltpu.make_async_copy(x.at[o], out.at[o], local)
    own.start()
    copies = []
    for t in range(outer - 1):
        copies.append(push(x.at[ring[t]], out.at[o], send.at[t], recv.at[t], peers[t]))
    own.wait()
    for copy in copies:
        copy.wait()


def swap_outer(x, inner, ident):
    outer = x.shape[0]
    anywhere = pl.BlockSpec(memory_space=pl.ANY)
    return pl.pallas_call(
        functools.partial(swap_kernel, inner),
        out_shape=jax.ShapeDtypeStruct(x.shape, x.dtype),
        in_specs=[anywhere],
        out_specs=anywhere,
        scratch_shapes=[
            pltpu.SemaphoreType.DMA((outer - 1,)),
            pltpu.SemaphoreType.DMA((outer - 1,)),
            pltpu.SemaphoreType.DMA,
        ],
        compiler_params=pltpu.CompilerParams(collective_id=ident, has_side_effects=True),
        name="swap_heads",
    )(x)


def spread_kernel(inner, q, k, v, q_all, k_all, v_all, qs, qr, zs, zr, xs, xr, cs, cr, local):
    outer = q.shape[0]
    across = inner // 2
    batch, o, a, c = place(inner)
    j = a * 2 + c
    ring = [lax.rem(o + t, outer) for t in range(outer)]
    z_peers = [(batch, p * inner + j) for p in ring]
    beside = [lax.rem(a + t, across) for t in range(across)]
    x_peers = [(batch, o * inner + p * 2 + c) for p in beside]
    twin = (batch, o * inner + a * 2 + (1 - c))
    greet(z_peers[1:] + x_peers[1:] + [twin])
    own = [
        pltpu.make_async_copy(q.at[o], q_all.at[o], local.at[0]),
        pltpu.make_async_copy(k.at[o], k_all.at[o, j], local.at[1]),
        pltpu.make_async_copy(v.at[o], v_all.at[o, j], local.at[2]),
    ]
    for copy in own:
        copy.start()
    waits = []
    arriving = []
    for i, (source, dest) in enumerate(((k, k_all), (v, v_all))):
        for t in range(1, outer):
            copy = push(source.at[ring[t]], dest.at[o, j], zs.at[i, t], zr.at[i, t], z_peers[t])
            arriving.append((i, t, copy))
    for t in range(1, outer):
        waits.append(push(q.at[ring[t]], q_all.at[o], qs.at[t], qr.at[t], z_peers[t]))
    for i in (0, 1):
        own[1 + i].wait()
    order = [(0, 0, None), (1, 0, None)] + arriving
    late = []
    for i, t, copy in order:
        dest = (k_all, v_all)[i]
        if copy is not None:
            copy.wait()
        z = lax.rem(o + outer - t, outer)
        for d in range(1, across):
            late.append((i, t, d, push(dest.at[z, j], dest.at[z, j], xs.at[i, t, d], xr.at[i, t, d], x_peers[d])))
        waits.append(push(dest.at[z, j], dest.at[z, j], cs.at[i, t, 0], cr.at[i, t, 0], twin))
        while len(late) > across - 1 or (late and copy is order[-1][2] and i == order[-1][0]):
            li, lt, ld, waited = late.pop(0)
            waited.wait()
            lz = lax.rem(o + outer - lt, outer)
            came = lax.rem(a + across - ld, across) * 2 + c
            piece = (k_all, v_all)[li].at[lz, came]
            waits.append(push(piece, piece, cs.at[li, lt, ld], cr.at[li, lt, ld], twin))
    own[0].wait()
    for copy in waits:
        copy.wait()


def spread_heads(q, k, v, inner, ident):
    outer, rows, width = q.shape
    across = inner // 2
    anywhere = pl.BlockSpec(memory_space=pl.ANY)
    dma = pltpu.SemaphoreType.DMA
    full = jax.ShapeDtypeStruct((outer, inner, rows, width), q.dtype)
    return pl.pallas_call(
        functools.partial(spread_kernel, inner),
        out_shape=(jax.ShapeDtypeStruct(q.shape, q.dtype), full, full),
        in_specs=[anywhere] * 3,
        out_specs=(anywhere,) * 3,
        scratch_shapes=[
            dma((outer,)),
            dma((outer,)),
            dma((2, outer)),
            dma((2, outer)),
            dma((2, outer, across)),
            dma((2, outer, across)),
            dma((2, outer, across)),
            dma((2, outer, across)),
            dma((3,)),
        ],
        compiler_params=pltpu.CompilerParams(collective_id=ident, has_side_effects=True),
        name="spread_heads",
    )(q, k, v)


def fold_kernel(inner, dq, dk, dv, dq_all, dk_all, dv_all, cbuf, xbuf, done, qs, qr, zs, zr, xs, xr, cs, cr, local):
    outer = dq.shape[0]
    across = inner // 2
    batch, o, a, c = place(inner)
    j = a * 2 + c
    twin_c = 1 - c
    ring = [lax.rem(o + t, outer) for t in range(outer)]
    z_peers = [(batch, p * inner + j) for p in ring]
    beside = [lax.rem(a + t, across) for t in range(across)]
    x_peers = [(batch, o * inner + p * 2 + c) for p in beside]
    twin = (batch, o * inner + a * 2 + twin_c)
    greet(z_peers[1:] + x_peers[1:] + [twin])
    waits = []
    own = pltpu.make_async_copy(dq.at[o], dq_all.at[o], local.at[0])
    own.start()
    given = (dk, dv)
    results = (dk_all, dv_all)
    order = [t % outer for t in range(1, outer + 1)]
    to_twin = {}
    for t in order:
        for i in (0, 1):
            for d in range(across):
                at = (ring[t], beside[d])
                to_twin[i, t, d] = push(
                    given[i].at[at[0], at[1] * 2 + twin_c],
                    cbuf.at[i, at[0], at[1]],
                    cs.at[i, t, d],
                    cr.at[i, t, d],
                    twin,
                )
    for t in range(1, outer):
        waits.append(push(dq.at[ring[t]], dq_all.at[o], qs.at[t], qr.at[t], z_peers[t]))
    across_copies = {}
    for t in order:
        for i in (0, 1):
            for d in list(range(1, across)) + [0]:
                to_twin[i, t, d].wait()
                z, b = ring[t], beside[d]
                cbuf[i, z, b] = (cbuf[i, z, b].astype(f32) + given[i][z, b * 2 + c].astype(f32)).astype(bf16)
                if d:
                    across_copies[i, t, d] = push(
                        cbuf.at[i, z, b], xbuf.at[i, z, d], xs.at[i, t, d], xr.at[i, t, d], x_peers[d]
                    )
    final = []
    for t in order:
        for i in (0, 1):
            z = ring[t]
            total = cbuf[i, z, a].astype(f32)
            for d in range(1, across):
                across_copies[i, t, d].wait()
                total = total + xbuf[i, z, d].astype(f32)
            done[i, z] = total.astype(bf16)
            if t:
                waits.append(push(done.at[i, z], results[i].at[o], zs.at[i, t], zr.at[i, t], z_peers[t]))
            else:
                copy = pltpu.make_async_copy(done.at[i, z], results[i].at[o], local.at[1 + i])
                copy.start()
                final.append(copy)
    own.wait()
    for copy in final + waits:
        copy.wait()


def fold_heads(dq, dk, dv, inner, ident):
    outer, rows, width = dq.shape
    across = inner // 2
    vm = pl.BlockSpec(memory_space=pltpu.VMEM)
    anywhere = pl.BlockSpec(memory_space=pl.ANY)
    dma = pltpu.SemaphoreType.DMA
    piece = jax.ShapeDtypeStruct(dq.shape, dq.dtype)
    return pl.pallas_call(
        functools.partial(fold_kernel, inner),
        out_shape=(piece, piece, piece),
        in_specs=[anywhere, vm, vm],
        out_specs=(anywhere,) * 3,
        scratch_shapes=[
            pltpu.VMEM((2, outer, across, rows, width), bf16),
            pltpu.VMEM((2, outer, across, rows, width), bf16),
            pltpu.VMEM((2, outer, rows, width), bf16),
            dma((outer,)),
            dma((outer,)),
            dma((2, outer)),
            dma((2, outer)),
            dma((2, outer, across)),
            dma((2, outer, across)),
            dma((2, outer, across)),
            dma((2, outer, across)),
            dma((3,)),
        ],
        compiler_params=pltpu.CompilerParams(
            collective_id=ident, has_side_effects=True, vmem_limit_bytes=56 << 20
        ),
        name="fold_heads",
    )(dq, dk, dv)


beta_one = 0.9
beta_two = 0.999
adam_eps = 1e-08
learn_rate = 0.01
decay_rate = 0.1
adam_step = 10


def layer_norm(values, gain, shift):
    center = values - jnp.mean(values, -1, keepdims=True)
    spread = jnp.mean(center * center, -1, keepdims=True)
    return center * lax.rsqrt(spread + 1e-05) * gain + shift


def gelu_tanh(values):
    inner = 0.7978845608028654 * (values + 0.044715 * values * values * values)
    return 0.5 * values * (1.0 + jnp.tanh(inner))


def angles(positions):
    freq = 10000.0 ** (-jnp.arange(HEAD // 2, dtype=jnp.float32) * 2.0 / HEAD)
    turned = positions.astype(jnp.float32)[:, None] * freq[None, :]
    return (jnp.cos(turned), jnp.sin(turned))


def rotate(tensor, cosine, sine, direction):
    first = tensor[..., : HEAD // 2]
    second = tensor[..., HEAD // 2 :]
    cosine = cosine[None, :, None, :]
    sine = direction * sine[None, :, None, :]
    return jnp.concatenate([first * cosine - second * sine, first * sine + second * cosine], -1)


def split_small(vector):
    gain_one = vector[0:D]
    gain_two = vector[D : 2 * D]
    shift_one = vector[2 * D : 3 * D]
    shift_two = vector[3 * D : 4 * D]
    bias_qkv = vector[4 * D : 7 * D]
    bias_out = vector[7 * D : 8 * D]
    bias_up = vector[8 * D : 8 * D + FF]
    bias_down = vector[8 * D + FF : 9 * D + FF]
    mixing = vector[9 * D + FF :]
    return (
        gain_one,
        gain_two,
        shift_one,
        shift_two,
        bias_qkv,
        bias_out,
        bias_up,
        bias_down,
        mixing,
    )


def adam(param, grad, first, second, decay):
    first_new = beta_one * first + (1.0 - beta_one) * grad
    second_new = beta_two * second + (1.0 - beta_two) * grad * grad
    fix_one = 1.0 - beta_one**adam_step
    fix_two = 1.0 - beta_two**adam_step
    update = first_new / fix_one / (jnp.sqrt(second_new / fix_two) + adam_eps)
    return (-learn_rate * (update + decay * param), first_new)


def scattered(term):
    return lax.psum_scatter(
        term.astype(bf16), ("batch", "seq"), scatter_dimension=0, tiled=True
    ).astype(f32)


def body(
    tokens_in,
    earlier_outs,
    out_cotangent,
    seq_lengths,
    qkv_weight,
    out_weight,
    up_weight,
    down_weight,
    qkv_first,
    qkv_second,
    out_first,
    out_second,
    up_first,
    up_second,
    down_first,
    down_second,
    small_params,
    small_first,
    small_second,
):
    groups = tokens_in.shape[0]
    rows = tokens_in.shape[1]
    count_rows = groups * rows
    heads = D // HEAD
    seq_count = lax.axis_size("seq")
    seq_rank = lax.axis_index("seq")
    first_row = seq_rank * rows
    query_pos = first_row + jnp.arange(rows, dtype=jnp.int32)
    last_row = first_row + rows - 1
    total = lax.psum(jnp.sum(seq_lengths), "batch")
    slots = groups * lax.axis_size("batch") * rows * seq_count
    live = (query_pos[None, :] < seq_lengths[:, None]).astype(jnp.float32)
    scale = live * (slots / total.astype(jnp.float32))
    shards = (
        qkv_weight.astype(jnp.bfloat16),
        out_weight.astype(jnp.bfloat16),
        up_weight.astype(jnp.bfloat16),
        down_weight.astype(jnp.bfloat16),
    )
    mat_qkv, mat_out, mat_up, mat_down = (
        lax.all_gather(shards[0], ("batch", "seq"), axis=0, tiled=True),
        lax.all_gather(shards[1], ("batch", "seq"), axis=0, tiled=True),
        lax.all_gather(shards[2], ("batch", "seq"), axis=0, tiled=True),
        lax.all_gather(shards[3], ("batch", "seq"), axis=0, tiled=True),
    )
    gain_one, gain_two, shift_one, shift_two, bias_qkv, bias_out, bias_up, bias_down, mixing = (
        split_small(small_params)
    )
    tokens = tokens_in.reshape(count_rows, D).astype(jnp.float32)
    normed_one, pull_one = jax.vjp(layer_norm, tokens, gain_one, shift_one)
    normed_one_low = normed_one.astype(jnp.bfloat16)
    joined = jnp.dot(normed_one_low, mat_qkv, preferred_element_type=jnp.float32) + bias_qkv
    cosine, sine = angles(query_pos)
    query_low = rotate(joined[:, :D].reshape(groups, rows, heads, HEAD), cosine, sine, 1.0).astype(
        jnp.bfloat16
    )
    key_low = (
        rotate(joined[:, D : 2 * D].reshape(groups, rows, heads, HEAD), cosine, sine, 1.0)
        .astype(jnp.bfloat16)
        .reshape(groups, rows, D)
    )
    value_low = joined[:, 2 * D :].astype(jnp.bfloat16).reshape(groups, rows, D)

    outer = math.gcd(seq_count, heads)
    inner = seq_count // outer
    per = heads // outer

    def to_heads(value):
        return value.reshape(groups, rows, outer, per * HEAD).transpose(2, 1, 0, 3).reshape(outer, rows, groups * per * HEAD)

    def from_heads(value):
        return value.reshape(outer, rows, groups, per * HEAD).transpose(2, 1, 0, 3).reshape(count_rows, D)

    q_mine, k_mine, v_mine = spread_heads(to_heads(query_low), to_heads(key_low), to_heads(value_low), inner, 1)
    k_mine = k_mine.reshape(seq_count * rows, groups * per * HEAD)
    v_mine = v_mine.reshape(seq_count * rows, groups * per * HEAD)
    span = math.gcd(seq_count * rows, 1024)
    o_mine, o_turned, log_total = flash_fwd(seq_lengths, q_mine, k_mine, v_mine, groups, per, inner, span)
    attended_low = from_heads(swap_outer(o_mine, inner, 2))
    branch = jnp.dot(attended_low, mat_out, preferred_element_type=jnp.float32) + bias_out
    middle = tokens + branch
    normed_two, pull_two = jax.vjp(layer_norm, middle, gain_two, shift_two)
    normed_two_low = normed_two.astype(jnp.bfloat16)
    hidden = jnp.dot(normed_two_low, mat_up, preferred_element_type=jnp.float32) + bias_up
    active, pull_gelu = jax.vjp(gelu_tanh, hidden)
    active_low = active.astype(jnp.bfloat16)
    layer_out = (
        middle + jnp.dot(active_low, mat_down, preferred_element_type=jnp.float32) + bias_down
    )
    earlier_count = earlier_outs.shape[0]
    earlier_rows = earlier_outs.reshape(earlier_count, count_rows, D)
    mixture = mixing[0] * layer_out + mixing[1] * tokens
    for earlier_index in range(earlier_count):
        mixture = mixture + mixing[2 + earlier_index] * earlier_rows[earlier_index].astype(
            jnp.float32
        )
    mixed = mixture.astype(jnp.bfloat16).reshape(groups, rows, D)
    grad_rows = (out_cotangent.astype(jnp.float32) * scale[..., None]).reshape(count_rows, D)
    mixing_terms = [jnp.sum(grad_rows * layer_out), jnp.sum(grad_rows * tokens)]
    for earlier_index in range(earlier_count):
        mixing_terms.append(jnp.sum(grad_rows * earlier_rows[earlier_index].astype(jnp.float32)))
    mixing_grad = jnp.stack(mixing_terms)
    result_grad = mixing[0] * grad_rows
    result_low = result_grad.astype(jnp.bfloat16)
    down_term = jnp.einsum("nf,nd->fd", active_low, result_low, preferred_element_type=jnp.float32)
    bias_down_grad = jnp.sum(result_low.astype(jnp.float32), 0)
    active_grad = jnp.einsum("nd,fd->nf", result_low, mat_down, preferred_element_type=jnp.float32)
    hidden_low = pull_gelu(active_grad)[0].astype(jnp.bfloat16)
    up_term = jnp.einsum(
        "nd,nf->df", normed_two_low, hidden_low, preferred_element_type=jnp.float32
    )
    bias_up_grad = jnp.sum(hidden_low.astype(jnp.float32), 0)
    normed_two_grad = jnp.einsum(
        "nf,df->nd", hidden_low, mat_up, preferred_element_type=jnp.float32
    )
    middle_part, gain_two_grad, shift_two_grad = pull_two(normed_two_grad)
    middle_grad = result_grad + middle_part
    branch_low = middle_grad.astype(jnp.bfloat16)
    out_term = jnp.einsum("nd,ne->de", attended_low, branch_low, preferred_element_type=jnp.float32)
    bias_out_grad = jnp.sum(branch_low.astype(jnp.float32), 0)
    attended_grad = jnp.einsum(
        "ne,de->nd", branch_low, mat_out, preferred_element_type=jnp.float32
    ).astype(jnp.bfloat16)
    grad_mine = swap_outer(to_heads(attended_grad), inner, 3)
    block_pos = (jnp.arange(outer) * inner + seq_rank % inner)[:, None] * rows + jnp.arange(rows)[None, :]
    freq = 10000.0 ** (-jnp.arange(HEAD // 2, dtype=jnp.float32) * 2.0 / HEAD)
    turned = block_pos.astype(jnp.float32)[:, None, :] * freq[None, :, None]
    dq_mine, dk_mine, dv_mine = flash_bwd(
        seq_lengths, q_mine, k_mine, v_mine, grad_mine, o_turned, log_total, jnp.cos(turned), jnp.sin(turned), groups, per, inner, math.gcd(seq_count * rows, 512)
    )
    pieces = (outer, inner, rows, groups * per * HEAD)
    dq_home, dk_home, dv_home = fold_heads(dq_mine, dk_mine.reshape(pieces), dv_mine.reshape(pieces), inner, 4)
    key_grad = from_heads(dk_home).astype(jnp.float32)
    query_back = from_heads(dq_home)
    key_back = rotate(key_grad.reshape(groups, rows, heads, HEAD), cosine, sine, -1.0).reshape(
        count_rows, D
    )
    joined_low = jnp.concatenate(
        [query_back, key_back.astype(jnp.bfloat16), from_heads(dv_home)], -1
    )
    qkv_term = jnp.einsum(
        "nd,nf->df", normed_one_low, joined_low, preferred_element_type=jnp.float32
    )
    bias_qkv_grad = jnp.sum(joined_low.astype(jnp.float32), 0)
    normed_one_grad = jnp.einsum(
        "nf,df->nd", joined_low, mat_qkv, preferred_element_type=jnp.float32
    )
    input_part, gain_one_grad, shift_one_grad = pull_one(normed_one_grad)
    input_grad = (mixing[1] * grad_rows + middle_grad + input_part).reshape(groups, rows, D)
    terms = (qkv_term, out_term, up_term, down_term)
    qkv_grad, out_grad, up_grad, down_grad = (
        scattered(terms[0]),
        scattered(terms[1]),
        scattered(terms[2]),
        scattered(terms[3]),
    )
    small_local = jnp.concatenate(
        [
            gain_one_grad,
            gain_two_grad,
            shift_one_grad,
            shift_two_grad,
            bias_qkv_grad,
            bias_out_grad,
            bias_up_grad,
            bias_down_grad,
            mixing_grad,
        ]
    )
    small_grad = lax.psum(small_local, ("batch", "seq"))
    qkv_step, qkv_first_new = adam(qkv_weight, qkv_grad, qkv_first, qkv_second, decay_rate)
    out_step, out_first_new = adam(out_weight, out_grad, out_first, out_second, decay_rate)
    up_step, up_first_new = adam(up_weight, up_grad, up_first, up_second, decay_rate)
    down_step, down_first_new = adam(down_weight, down_grad, down_first, down_second, decay_rate)
    small_step, small_first_new = adam(small_params, small_grad, small_first, small_second, 0.0)
    return (
        mixed,
        input_grad,
        qkv_grad,
        out_grad,
        up_grad,
        down_grad,
        small_grad,
        qkv_step,
        out_step,
        up_step,
        down_step,
        small_step,
        qkv_first_new,
        out_first_new,
        up_first_new,
        down_first_new,
        small_first_new,
    )


def solution(mesh):
    placed = (
        P("batch", "seq", None),
        P(None, "batch", "seq", None),
        P("batch", "seq", None),
        P("batch"),
        P(("batch", "seq"), None),
        P(("batch", "seq"), None),
        P(("batch", "seq"), None),
        P(("batch", "seq"), None),
        P(("batch", "seq"), None),
        P(("batch", "seq"), None),
        P(("batch", "seq"), None),
        P(("batch", "seq"), None),
        P(("batch", "seq"), None),
        P(("batch", "seq"), None),
        P(("batch", "seq"), None),
        P(("batch", "seq"), None),
        P(),
        P(),
        P(),
    )
    return jax.shard_map(
        body,
        mesh=mesh,
        in_specs=placed,
        out_specs=(
            P("batch", "seq", None),
            P("batch", "seq", None),
            P(("batch", "seq"), None),
            P(("batch", "seq"), None),
            P(("batch", "seq"), None),
            P(("batch", "seq"), None),
            P(),
            P(("batch", "seq"), None),
            P(("batch", "seq"), None),
            P(("batch", "seq"), None),
            P(("batch", "seq"), None),
            P(),
            P(("batch", "seq"), None),
            P(("batch", "seq"), None),
            P(("batch", "seq"), None),
            P(("batch", "seq"), None),
            P(),
        ),
        check_vma=False,
    )
```

```python
import functools
import math

import jax
import jax.numpy as jnp
from jax import lax
from jax.experimental import pallas as pl
from jax.experimental.pallas import tpu as pltpu
from jax.sharding import PartitionSpec as P

D = 768
FF = 3072
HEAD = 64
bf16 = jnp.bfloat16
f32 = jnp.float32
NEG = -1e30


def mm(a, b):
    return lax.dot_general(a, b, (((1,), (0,)), ((), ())), preferred_element_type=f32)


def half_rows(block_t, half):
    z = jnp.zeros((HEAD, block_t.shape[1]), block_t.dtype)
    if half == 0:
        return jnp.concatenate([block_t[:HEAD], z], 0)
    return jnp.concatenate([z, block_t[HEAD:]], 0)


def flash_fwd_kernel(groups, per, span, inner, lens, q, k, v, o, ot, lse, vt, qt, m_s, l_s):
    outer, rows, width = q.shape
    units = groups * per
    total = k.shape[0]
    j = lax.rem(lax.axis_index("seq"), inner)
    blk = 512

    def turn_v(i, _):
        at = pl.ds(pl.multiple_of(i * blk, blk), blk)
        for t in range(width // 128):
            lanes = slice(128 * t, 128 * t + 128)
            vt[lanes, at] = v[at, lanes].T
        return 0

    lax.fori_loop(0, total // blk, turn_v, 0)

    def one(z, _):
        first = (z * inner + j) * rows
        for t in range(width // 128):
            lanes = slice(128 * t, 128 * t + 128)
            turned = (q[z, :, lanes] * 0.125).astype(bf16).T
            for half in range(2):
                qt[2 * t + half] = half_rows(turned, half)
        for g in range(groups):
            length = lens[g]
            ot[z, g * per * HEAD : (g + 1) * per * HEAD, :] = jnp.zeros((per * HEAD, rows), f32)
            m_s[...] = jnp.full(m_s.shape, NEG, f32)
            l_s[...] = jnp.zeros(l_s.shape, f32)

            def step(c, masked):
                at = pl.ds(pl.multiple_of(c * span, span), span)
                if masked:
                    key = c * span + lax.broadcasted_iota(jnp.int32, (span, rows), 0)
                    query = first + lax.broadcasted_iota(jnp.int32, (span, rows), 1)
                    allowed = (key <= query) & (key < length)
                scores, tops, news, shares, sums = [], [], [], [], []
                for h in range(per):
                    u = g * per + h
                    s = mm(k[at, 128 * (u // 2) : 128 * (u // 2) + 128], qt[u])
                    scores.append(jnp.where(allowed, s, NEG) if masked else s)
                for h in range(per):
                    tops.append(m_s[h : h + 1])
                    news.append(jnp.maximum(tops[h], jnp.max(scores[h], 0, keepdims=True)))
                for h in range(per):
                    p = jnp.exp(scores[h] - news[h])
                    sums.append(jnp.sum(p, 0, keepdims=True))
                    shares.append(p.astype(bf16))
                for h in range(per):
                    u = g * per + h
                    alpha = jnp.exp(tops[h] - news[h])
                    l_s[h : h + 1] = l_s[h : h + 1] * alpha + sums[h]
                    m_s[h : h + 1] = news[h]
                    span_u = slice(HEAD * u, HEAD * u + HEAD)
                    ot[z, span_u, :] = ot[z, span_u, :] * alpha + mm(vt[span_u, at], shares[h])

            whole = jnp.minimum(first, length) // span
            count = (jnp.minimum(first + rows, length) + span - 1) // span

            def full_step(c, _):
                step(c, False)
                return 0

            def edge_step(c, _):
                step(c, True)
                return 0

            lax.fori_loop(0, whole, full_step, 0)
            lax.fori_loop(whole, count, edge_step, 0)
            for h in range(per):
                u = g * per + h
                span_u = slice(HEAD * u, HEAD * u + HEAD)
                total_exp = l_s[h : h + 1]
                ot[z, span_u, :] = ot[z, span_u, :] / total_exp
                lse[z, u : u + 1, :] = m_s[h : h + 1] + jnp.log(total_exp)
        for t in range(width // 128):
            lanes = slice(128 * t, 128 * t + 128)
            o[z, :, lanes] = ot[z, lanes, :].T.astype(bf16)
        return 0

    lax.fori_loop(0, outer, one, 0)


def flash_fwd(lens, q, k, v, groups, per, inner, span=1024):
    outer, rows, width = q.shape
    units = groups * per
    total = k.shape[0]
    vm = pl.BlockSpec(memory_space=pltpu.VMEM)
    return pl.pallas_call(
        functools.partial(flash_fwd_kernel, groups, per, span, inner),
        out_shape=(
            jax.ShapeDtypeStruct((outer, rows, width), bf16),
            jax.ShapeDtypeStruct((outer, width, rows), f32),
            jax.ShapeDtypeStruct((outer, 8, rows), f32),
        ),
        in_specs=[pl.BlockSpec(memory_space=pltpu.SMEM), vm, vm, vm],
        out_specs=(vm, vm, vm),
        scratch_shapes=[
            pltpu.VMEM((width, total), bf16),
            pltpu.VMEM((units, 128, rows), bf16),
            pltpu.VMEM((8, rows), f32),
            pltpu.VMEM((8, rows), f32),
        ],
        compiler_params=pltpu.CompilerParams(vmem_limit_bytes=56 << 20),
        name="attend",
    )(lens, q, k, v)


def flash_bwd_kernel(groups, per, span, inner, lens, q, k, v, do, ot, lse, cos, sin, dq, dk, dv, kt, qt, dot_t, qz, dz, rd, dqt, dks, dvs):
    outer, rows, width = q.shape
    units = groups * per
    total = k.shape[0]
    j = lax.rem(lax.axis_index("seq"), inner)
    blk = 512

    def prepare(i, _):
        at = pl.ds(pl.multiple_of(i * blk, blk), blk)
        for t in range(width // 128):
            lanes = slice(128 * t, 128 * t + 128)
            kt[lanes, at] = k[at, lanes].T
        dks[at, :] = jnp.zeros((blk, width), f32)
        dvs[at, :] = jnp.zeros((blk, width), f32)
        return 0

    lax.fori_loop(0, total // blk, prepare, 0)

    def one(z, _):
        first = (z * inner + j) * rows
        low = lax.broadcasted_iota(jnp.int32, (rows, 128), 1) < HEAD
        for t in range(width // 128):
            lanes = slice(128 * t, 128 * t + 128)
            small = (q[z, :, lanes] * 0.125).astype(bf16)
            grad = do[z, :, lanes]
            turned = small.T
            grad_t = grad.T
            prod = grad_t.astype(f32) * ot[z, lanes, :]
            for half in range(2):
                u = 2 * t + half
                qt[u] = half_rows(turned, half)
                dot_t[u] = half_rows(grad_t, half)
                keep = low if half == 0 else ~low
                qz[u] = jnp.where(keep, small, jnp.zeros_like(small))
                dz[u] = jnp.where(keep, grad, jnp.zeros_like(grad))
                rd[u : u + 1, :] = jnp.sum(prod[HEAD * half : HEAD * half + HEAD], 0, keepdims=True)
        dqt[...] = jnp.zeros(dqt.shape, f32)
        for g in range(groups):
            length = lens[g]

            def step(c, masked):
                at = pl.ds(pl.multiple_of(c * span, span), span)
                if masked:
                    key = c * span + lax.broadcasted_iota(jnp.int32, (span, rows), 0)
                    query = first + lax.broadcasted_iota(jnp.int32, (span, rows), 1)
                    allowed = (key <= query) & (key < length)
                for h in range(per):
                    u = g * per + h
                    lanes = slice(128 * (u // 2), 128 * (u // 2) + 128)
                    span_u = slice(HEAD * u, HEAD * u + HEAD)
                    s = mm(k[at, lanes], qt[u])
                    p = jnp.exp(s - lse[z, u : u + 1, :])
                    if masked:
                        p = jnp.where(allowed, p, 0.0)
                    dp = mm(v[at, lanes], dot_t[u])
                    ds = (p * (dp - rd[u : u + 1, :])).astype(bf16)
                    dvs[at, lanes] += mm(p.astype(bf16), dz[u])
                    dks[at, lanes] += mm(ds, qz[u])
                    dqt[span_u, :] += mm(kt[span_u, at], ds)

            live = first < length
            whole = jnp.where(live, jnp.minimum(first, length) // span, 0)
            count = jnp.where(live, (jnp.minimum(first + rows, length) + span - 1) // span, 0)

            def full_step(c, _):
                step(c, False)
                return 0

            def edge_step(c, _):
                step(c, True)
                return 0

            lax.fori_loop(0, whole, full_step, 0)
            lax.fori_loop(whole, count, edge_step, 0)
        cosine = cos[z]
        sine = sin[z]
        for t in range(width // 128):
            parts = []
            for half in range(2):
                u = 2 * t + half
                a = dqt[HEAD * u : HEAD * u + 32, :] * 0.125
                b = dqt[HEAD * u + 32 : HEAD * u + 64, :] * 0.125
                parts.append(a * cosine + b * sine)
                parts.append(b * cosine - a * sine)
            dq[z, :, 128 * t : 128 * t + 128] = jnp.concatenate(parts, 0).T.astype(bf16)
        return 0

    lax.fori_loop(0, outer, one, 0)

    def finish(i, _):
        at = pl.ds(pl.multiple_of(i * blk, blk), blk)
        dk[at, :] = dks[at, :].astype(bf16)
        dv[at, :] = dvs[at, :].astype(bf16)
        return 0

    lax.fori_loop(0, total // blk, finish, 0)


def flash_bwd(lens, q, k, v, do, ot, lse, cos, sin, groups, per, inner, span=1024):
    outer, rows, width = q.shape
    units = groups * per
    total = k.shape[0]
    vm = pl.BlockSpec(memory_space=pltpu.VMEM)
    return pl.pallas_call(
        functools.partial(flash_bwd_kernel, groups, per, span, inner),
        out_shape=(
            jax.ShapeDtypeStruct((outer, rows, width), bf16),
            jax.ShapeDtypeStruct((total, width), bf16),
            jax.ShapeDtypeStruct((total, width), bf16),
        ),
        in_specs=[pl.BlockSpec(memory_space=pltpu.SMEM)] + [vm] * 8,
        out_specs=(vm, vm, vm),
        scratch_shapes=[
            pltpu.VMEM((width, total), bf16),
            pltpu.VMEM((units, 128, rows), bf16),
            pltpu.VMEM((units, 128, rows), bf16),
            pltpu.VMEM((units, rows, 128), bf16),
            pltpu.VMEM((units, rows, 128), bf16),
            pltpu.VMEM((8, rows), f32),
            pltpu.VMEM((width, rows), f32),
            pltpu.VMEM((total, width), f32),
            pltpu.VMEM((total, width), f32),
        ],
        compiler_params=pltpu.CompilerParams(vmem_limit_bytes=56 << 20),
        name="attend_back",
    )(lens, q, k, v, do, ot, lse, cos, sin)


MESH = pl.DeviceIdType.MESH
ANYWHERE = pl.BlockSpec(memory_space=pl.ANY)
IN_VMEM = pl.BlockSpec(memory_space=pltpu.VMEM)
DMA = pltpu.SemaphoreType.DMA
ROOM = 56 << 20


class Place:
    def __init__(self, batches, outer, inner):
        self.batch = lax.axis_index("batch")
        rank = lax.axis_index("seq")
        self.o = lax.div(rank, inner)
        self.j = lax.rem(rank, inner)
        self.a = lax.div(self.j, 2)
        self.c = lax.rem(rank, 2)
        across = inner // 2
        self.zs = [lax.rem(self.o + t, outer) for t in range(outer)]
        self.xs = [lax.rem(self.a + t, across) for t in range(across)]
        self.ys = [lax.rem(self.batch + t, batches) for t in range(batches)]
        self.z_peers = [(self.batch, z * inner + self.j) for z in self.zs]
        self.x_peers = [(self.batch, self.o * inner + x * 2 + self.c) for x in self.xs]
        self.y_peers = [(y, rank) for y in self.ys]
        self.twin = (self.batch, self.o * inner + self.a * 2 + (1 - self.c))


def greet(peers):
    barrier = pltpu.get_barrier_semaphore()
    for peer in peers:
        pl.semaphore_signal(barrier, inc=1, device_id=peer, device_id_type=MESH)
    pl.semaphore_wait(barrier, len(peers))


def push(src, dst, send, recv, peer):
    copy = pltpu.make_async_remote_copy(
        src_ref=src, dst_ref=dst, send_sem=send, recv_sem=recv, device_id=peer, device_id_type=MESH
    )
    copy.start()
    return copy


def carry(src, dst, sem):
    copy = pltpu.make_async_copy(src, dst, sem)
    copy.start()
    return copy


def remote_params(ident, vmem=None):
    return pltpu.CompilerParams(collective_id=ident, has_side_effects=True, vmem_limit_bytes=vmem)


def swap_kernel(batches, inner, x, out, send, recv, local):
    outer = x.shape[0]
    here = Place(batches, outer, inner)
    greet(here.z_peers[1:])
    own = carry(x.at[here.o], out.at[here.o], local)
    copies = []
    for t in range(1, outer):
        copies.append(push(x.at[here.zs[t]], out.at[here.o], send.at[t], recv.at[t], here.z_peers[t]))
    own.wait()
    for copy in copies:
        copy.wait()


def swap_outer(x, batches, inner, ident):
    outer = x.shape[0]
    return pl.pallas_call(
        functools.partial(swap_kernel, batches, inner),
        out_shape=jax.ShapeDtypeStruct(x.shape, x.dtype),
        in_specs=[ANYWHERE],
        out_specs=ANYWHERE,
        scratch_shapes=[DMA((outer,)), DMA((outer,)), DMA],
        compiler_params=remote_params(ident),
        name="swap_heads",
    )(x)


def first_kernel(batches, outer, inner, near, rest, count, near_all, rest_line, counts, zs, zr, xs, xr, ys, yr, cs, cr, rs, rr, ns, nr, local):
    across = inner // 2
    here = Place(batches, outer, inner)
    o, a, b, c = here.o, here.a, here.batch, here.c
    greet(here.z_peers[1:] + here.x_peers[1:] + here.y_peers[1:] + [here.twin])
    half = near.shape[0] // 2
    parts = [pl.ds(0, half), pl.ds(half, half)]
    waits = []

    def slot(y, z, x, p):
        return near_all.at[y, z, x, c, parts[p]]

    copies = {}
    for t in range(1, outer):
        for p in (0, 1):
            copies[t, p] = push(near.at[parts[p]], slot(b, o, a, p), zs.at[t, p], zr.at[t, p], here.z_peers[t])
    own = carry(near, near_all.at[b, o, a, c], local.at[0])
    own_rest = carry(rest, rest_line.at[o], local.at[1])
    own_count = carry(count, counts.at[b], local.at[2])
    for d in range(1, batches):
        waits.append(push(count, counts.at[b], ns.at[d], nr.at[d], here.y_peers[d]))
    arrivals = {}

    def onward(source, y, z, x, p, t, dx, dy):
        to = slot(y, z, x, p)
        if dx == 0 and (dy == 0 or p == 1):
            for d in range(1, across):
                key = (p, t, d, dy)
                arrivals["x", key] = push(source, to, xs.at[key], xr.at[key], here.x_peers[d])
        if dy == 0 and (dx == 0 or p == 0):
            for d in range(1, batches):
                key = (p, t, dx, d)
                arrivals["y", key] = push(source, to, ys.at[key], yr.at[key], here.y_peers[d])
        key = (p, t, dx, dy)
        waits.append(push(source, to, cs.at[key], cr.at[key], here.twin))

    for p in (0, 1):
        onward(near.at[parts[p]], b, o, a, p, 0, 0, 0)
    for t in range(1, outer):
        waits.append(push(rest, rest_line.at[o], rs.at[t], rr.at[t], here.z_peers[t]))
    for t in range(1, outer):
        z = lax.rem(o + outer - t, outer)
        for p in (0, 1):
            copies[t, p].wait()
            onward(slot(b, z, a, p), b, z, a, p, t, 0, 0)
    for t in range(outer):
        z = lax.rem(o + outer - t, outer)
        for d in range(1, across):
            arrivals["x", (0, t, d, 0)].wait()
            x = lax.rem(a + across - d, across)
            onward(slot(b, z, x, 0), b, z, x, 0, t, d, 0)
        for d in range(1, batches):
            arrivals["y", (1, t, 0, d)].wait()
            y = lax.rem(b + batches - d, batches)
            onward(slot(y, z, a, 1), y, z, a, 1, t, 0, d)
    for t in range(outer):
        z = lax.rem(o + outer - t, outer)
        for dx in range(across):
            x = lax.rem(a + across - dx, across)
            for dy in range(1, batches):
                y = lax.rem(b + batches - dy, batches)
                arrivals["y", (0, t, dx, dy)].wait()
                onward(slot(y, z, x, 0), y, z, x, 0, t, dx, dy)
        for dy in range(batches):
            y = lax.rem(b + batches - dy, batches)
            for dx in range(1, across):
                x = lax.rem(a + across - dx, across)
                arrivals["x", (1, t, dx, dy)].wait()
                onward(slot(y, z, x, 1), y, z, x, 1, t, dx, dy)
    own.wait()
    own_rest.wait()
    own_count.wait()
    for copy in waits:
        copy.wait()


def gather_first(near, rest, count, batches, outer, inner, ident):
    across = inner // 2
    return pl.pallas_call(
        functools.partial(first_kernel, batches, outer, inner),
        out_shape=(
            jax.ShapeDtypeStruct((batches, outer, across, 2) + near.shape, near.dtype),
            jax.ShapeDtypeStruct((outer,) + rest.shape, rest.dtype),
            jax.ShapeDtypeStruct((batches,) + count.shape, count.dtype),
        ),
        in_specs=[ANYWHERE] * 3,
        out_specs=(ANYWHERE,) * 3,
        scratch_shapes=[DMA((outer, 2))] * 2 + [DMA((2, outer, across, batches))] * 6 + [DMA((outer,))] * 2 + [DMA((batches,))] * 2 + [DMA((3,))],
        compiler_params=remote_params(ident),
        name="gather_first",
    )(near, rest, count)


def spread_kernel(batches, inner, with_rest, q, k, v, *refs):
    outer = q.shape[0]
    across = inner // 2
    if with_rest:
        line, q_all, k_all, v_all, rest_all, qs, qr, zs, zr, xs, xr, cs, cr, local, ax, axr, ay, ayr, ac, acr, alocal = refs
    else:
        q_all, k_all, v_all, qs, qr, zs, zr, xs, xr, cs, cr, local = refs
    here = Place(batches, outer, inner)
    o, a, b, c, j = here.o, here.a, here.batch, here.c, here.j
    greet(here.z_peers[1:] + here.x_peers[1:] + [here.twin] + (here.y_peers[1:] if with_rest else []))
    own = [carry(q.at[o], q_all.at[o], local.at[0]), carry(k.at[o], k_all.at[o, j], local.at[1]), carry(v.at[o], v_all.at[o, j], local.at[2])]
    waits = []
    arriving = []
    late = []
    rest_late = []
    for i, (source, dest) in enumerate(((k, k_all), (v, v_all))):
        for t in range(1, outer):
            copy = push(source.at[here.zs[t]], dest.at[o, j], zs.at[i, t], zr.at[i, t], here.z_peers[t])
            arriving.append((i, t, copy))
    for t in range(1, outer):
        waits.append(push(q.at[here.zs[t]], q_all.at[o], qs.at[t], qr.at[t], here.z_peers[t]))
    if with_rest:
        waits.append(carry(line, rest_all.at[b, :, a, c], alocal))
        for z in range(outer):
            for d in range(1, across):
                rest_late.append((z, d, push(line.at[z], rest_all.at[b, z, a, c], ax.at[z, d], axr.at[z, d], here.x_peers[d])))
        for z in range(outer):
            for d in range(1, batches):
                waits.append((z, 0, d, push(line.at[z], rest_all.at[b, z, a, c], ay.at[z, 0, d], ayr.at[z, 0, d], here.y_peers[d])))
            waits.append(push(line.at[z], rest_all.at[b, z, a, c], ac.at[z, 0, 0], acr.at[z, 0, 0], here.twin))

    def rest_step():
        z, d, copy = rest_late.pop(0)
        copy.wait()
        x = lax.rem(a + across - d, across)
        piece = rest_all.at[b, z, x, c]
        for e in range(1, batches):
            waits.append((z, d, e, push(piece, piece, ay.at[z, d, e], ayr.at[z, d, e], here.y_peers[e])))
        waits.append(push(piece, piece, ac.at[z, d, 0], acr.at[z, d, 0], here.twin))

    own[1].wait()
    own[2].wait()
    order = [(0, 0, None), (1, 0, None)] + arriving
    for n, (i, t, copy) in enumerate(order):
        dest = (k_all, v_all)[i]
        if copy is not None:
            copy.wait()
        z = lax.rem(o + outer - t, outer)
        piece = dest.at[z, j]
        for d in range(1, across):
            late.append((i, t, d, push(piece, piece, xs.at[i, t, d], xr.at[i, t, d], here.x_peers[d])))
        waits.append(push(piece, piece, cs.at[i, t, 0], cr.at[i, t, 0], here.twin))
        while len(late) > (across - 1 if n < len(order) - 1 else 0):
            li, lt, ld, waited = late.pop(0)
            waited.wait()
            lz = lax.rem(o + outer - lt, outer)
            came = lax.rem(a + across - ld, across) * 2 + c
            moved = (k_all, v_all)[li].at[lz, came]
            waits.append(push(moved, moved, cs.at[li, lt, ld], cr.at[li, lt, ld], here.twin))
        if rest_late and n >= 1:
            rest_step()
    while rest_late:
        rest_step()
    final = []
    for entry in waits:
        if isinstance(entry, tuple):
            z, d, e, copy = entry
            copy.wait()
            x = lax.rem(a + across - d, across)
            y = lax.rem(b + batches - e, batches)
            piece = rest_all.at[y, z, x, c]
            final.append(push(piece, piece, ac.at[z, d, e], acr.at[z, d, e], here.twin))
        else:
            final.append(entry)
    own[0].wait()
    for copy in final:
        copy.wait()


def spread_heads(q, k, v, line, batches, inner, ident):
    outer, rows, width = q.shape
    across = inner // 2
    full = jax.ShapeDtypeStruct((outer, inner, rows, width), q.dtype)
    with_rest = line is not None
    shapes = (jax.ShapeDtypeStruct(q.shape, q.dtype), full, full)
    scratch = [DMA((outer,))] * 2 + [DMA((2, outer))] * 2 + [DMA((2, outer, across))] * 4 + [DMA((3,))]
    args = (q, k, v)
    if with_rest:
        args += (line,)
        shapes += (jax.ShapeDtypeStruct((batches, outer, across, 2) + line.shape[1:], line.dtype),)
        scratch += [DMA((outer, across))] * 2 + [DMA((outer, across, batches))] * 4 + [DMA]
    return pl.pallas_call(
        functools.partial(spread_kernel, batches, inner, with_rest),
        out_shape=shapes,
        in_specs=[ANYWHERE] * len(args),
        out_specs=(ANYWHERE,) * len(shapes),
        scratch_shapes=scratch,
        compiler_params=remote_params(ident),
        name="spread_heads",
    )(*args)


def summed(into, index, more, other):
    into[index] = (into[index].astype(f32) + more[other].astype(f32)).astype(bf16)


def fold_kernel(batches, inner, with_rest, dq, dk, dv, *refs):
    outer = dq.shape[0]
    across = inner // 2
    if with_rest:
        terms, dq_all, dk_all, dv_all, rest_out, cbuf, xbuf, done, qs, qr, zs, zr, xs, xr, cs, cr, local, rc, ry, rx, rcs, rcr, rys, ryr, rxs, rxr = refs
    else:
        dq_all, dk_all, dv_all, cbuf, xbuf, done, qs, qr, zs, zr, xs, xr, cs, cr, local = refs
    here = Place(batches, outer, inner)
    o, a, b, c = here.o, here.a, here.batch, here.c
    greet(here.z_peers[1:] + here.x_peers[1:] + [here.twin] + (here.y_peers[1:] if with_rest else []))
    waits = []
    own = carry(dq.at[o], dq_all.at[o], local.at[0])
    given = (dk, dv)
    results = (dk_all, dv_all)
    order = [t % outer for t in range(1, outer + 1)]
    xorder = list(range(1, across)) + [0]
    yorder = list(range(1, batches)) + [0]
    to_twin = {}

    def give_block(t):
        for i in (0, 1):
            for d in xorder:
                z, x = here.zs[t], here.xs[d]
                to_twin[i, t, d] = push(given[i].at[z, x * 2 + 1 - c], cbuf.at[i, z, x], cs.at[i, t, d], cr.at[i, t, d], here.twin)

    rest_twin = {}

    def give_rest(dy, dx):
        y, x = here.ys[dy], here.xs[dx]
        rest_twin[dy, dx] = push(terms.at[y, :, x, 1 - c], rc.at[y, :, x], rcs.at[dy, dx], rcr.at[dy, dx], here.twin)

    give_block(order[0])
    if with_rest:
        for dy in yorder:
            for dx in xorder:
                give_rest(dy, dx)
    for t in order[1:]:
        give_block(t)
    for t in range(1, outer):
        waits.append(push(dq.at[here.zs[t]], dq_all.at[o], qs.at[t], qr.at[t], here.z_peers[t]))
    over = {}

    def fold_block(t):
        for i in (0, 1):
            for d in xorder:
                to_twin[i, t, d].wait()
                z, x = here.zs[t], here.xs[d]
                summed(cbuf, (i, z, x), given[i], (z, x * 2 + c))
                if d:
                    over[i, t, d] = push(cbuf.at[i, z, x], xbuf.at[i, z, d], xs.at[i, t, d], xr.at[i, t, d], here.x_peers[d])

    def finish_block(t):
        for i in (0, 1):
            z = here.zs[t]
            total = cbuf[i, z, a].astype(f32)
            for d in range(1, across):
                over[i, t, d].wait()
                total = total + xbuf[i, z, d].astype(f32)
            done[i, z] = total.astype(bf16)
            if t:
                waits.append(push(done.at[i, z], results[i].at[o], zs.at[i, t], zr.at[i, t], here.z_peers[t]))
            else:
                waits.append(carry(done.at[i, z], results[i].at[o], local.at[1 + i]))

    rest_over = {}

    def add_rest(y, x):
        def one(z, _):
            summed(rc, (y, z, x), terms, (y, z, x, c))
            return 0

        lax.fori_loop(0, outer, one, 0)

    def rest_core(dy, dx):
        rest_twin[dy, dx].wait()
        y, x = here.ys[dy], here.xs[dx]
        add_rest(y, x)
        if dy:
            rest_over["y", dy, dx] = push(rc.at[y, :, x], ry.at[dy, dx], rys.at[dy, dx], ryr.at[dy, dx], here.y_peers[dy])

    def rest_y(dx):
        x = here.xs[dx]
        for dy in range(1, batches):
            rest_over["y", dy, dx].wait()

            def one(z, _):
                summed(rc, (b, z, x), ry, (dy, dx, z))
                return 0

            lax.fori_loop(0, outer, one, 0)
        if dx:
            rest_over["x", dx] = push(rc.at[b, :, x], rx.at[dx], rxs.at[dx], rxr.at[dx], here.x_peers[dx])

    fold_block(order[0])
    if with_rest:
        for dy in yorder[:-1]:
            for dx in xorder:
                rest_core(dy, dx)
    fold_block(order[1])
    finish_block(order[0])
    if with_rest:
        for dx in xorder:
            rest_core(0, dx)
    for n in range(2, outer):
        fold_block(order[n])
        finish_block(order[n - 1])
        if with_rest and n == 2:
            for dx in xorder[:-1]:
                rest_y(dx)
    finish_block(order[-1])
    if with_rest:
        rest_y(0)
        for d in range(1, across):
            rest_over["x", d].wait()

            def one(z, _):
                summed(rc, (b, z, a), rx, (d, z))
                return 0

            lax.fori_loop(0, outer, one, 0)
        waits.append(carry(rc.at[b, :, a], rest_out, local.at[3]))
    own.wait()
    for copy in waits:
        copy.wait()


def fold_heads(dq, dk, dv, terms, batches, inner, ident):
    outer, rows, width = dq.shape
    across = inner // 2
    piece = jax.ShapeDtypeStruct(dq.shape, dq.dtype)
    with_rest = terms is not None
    args = (dq, dk, dv)
    specs = [ANYWHERE, IN_VMEM, IN_VMEM]
    shapes = (piece, piece, piece)
    scratch = [pltpu.VMEM((2, outer, across, rows, width), bf16)] * 2 + [pltpu.VMEM((2, outer, rows, width), bf16)]
    scratch += [DMA((outer,))] * 2 + [DMA((2, outer))] * 2 + [DMA((2, outer, across))] * 4 + [DMA((4,))]
    if with_rest:
        args += (terms,)
        specs += [IN_VMEM]
        tail = terms.shape[4:]
        shapes += (jax.ShapeDtypeStruct((outer,) + tail, bf16),)
        scratch += [pltpu.VMEM((batches, outer, across) + tail, bf16), pltpu.VMEM((batches, across, outer) + tail, bf16), pltpu.VMEM((across, outer) + tail, bf16)]
        scratch += [DMA((batches, across))] * 4 + [DMA((across,))] * 2
    return pl.pallas_call(
        functools.partial(fold_kernel, batches, inner, with_rest),
        out_shape=shapes,
        in_specs=specs,
        out_specs=(ANYWHERE,) * len(shapes),
        scratch_shapes=scratch,
        compiler_params=remote_params(ident, ROOM),
        name="fold_heads",
    )(*args)


def last_kernel(batches, outer, inner, terms, line, small, near_out, rest_out, small_out, rc, ry, rx, rz, lz, sc, sx, sy, sz, cs, cr, ys, yr, xs, xr, zs, zr, ls, lr, ss, sr):
    across = inner // 2
    here = Place(batches, outer, inner)
    o, a, b, c = here.o, here.a, here.batch, here.c
    greet(here.z_peers[1:] + here.x_peers[1:] + here.y_peers[1:] + [here.twin])
    half = terms.shape[4] // 2
    parts = [pl.ds(0, half), pl.ds(half, half)]
    xorder = list(range(1, across)) + [0]
    yorder = list(range(1, batches)) + [0]
    twin = {}
    for dy in yorder:
        for dx in xorder:
            y, x = here.ys[dy], here.xs[dx]
            twin[dy, dx] = push(terms.at[y, :, x, 1 - c], rc.at[y, :, x], cs.at[dy, dx], cr.at[dy, dx], here.twin)
    small_copy = push(small, sc, ss.at[0], sr.at[0], here.twin)
    line_copies = [push(line.at[here.zs[t]], lz.at[t], ls.at[t], lr.at[t], here.z_peers[t]) for t in range(1, outer)]
    over = {}

    def add_all(into_at, more, more_at):
        def one(z, _):
            summed(rc, into_at(z), more, more_at(z))
            return 0

        lax.fori_loop(0, outer, one, 0)

    for dy in yorder:
        for dx in xorder:
            twin[dy, dx].wait()
            y, x = here.ys[dy], here.xs[dx]
            add_all(lambda z: (y, z, x), terms, lambda z: (y, z, x, c))
            if dy:
                over["y", 0, dy, dx] = push(rc.at[y, :, x, parts[0]], ry.at[dy, dx, :, parts[0]], ys.at[0, dy, dx], yr.at[0, dy, dx], here.y_peers[dy])
            if dx:
                over["x", 1, dy, dx] = push(rc.at[y, :, x, parts[1]], rx.at[dx, dy, :, parts[1]], xs.at[1, dy, dx], xr.at[1, dy, dx], here.x_peers[dx])
    small_copy.wait()
    sc[...] = sc[...] + small[...]
    small_x = []
    for d in range(1, across):
        small_x.append(push(sc, sx.at[a], ss.at[d], sr.at[d], here.x_peers[d]))
    sx[a] = sc[...]
    for dx in xorder:
        x = here.xs[dx]
        for dy in range(1, batches):
            over["y", 0, dy, dx].wait()
            add_all(lambda z: (b, z, x, parts[0]), ry, lambda z: (dy, dx, z, parts[0]))
        if dx:
            over["x", 0, 0, dx] = push(rc.at[b, :, x, parts[0]], rx.at[dx, 0, :, parts[0]], xs.at[0, 0, dx], xr.at[0, 0, dx], here.x_peers[dx])
    for dy in yorder:
        y = here.ys[dy]
        for dx in range(1, across):
            over["x", 1, dy, dx].wait()
            add_all(lambda z: (y, z, a, parts[1]), rx, lambda z: (dx, dy, z, parts[1]))
        if dy:
            over["y", 1, dy, 0] = push(rc.at[y, :, a, parts[1]], ry.at[dy, 0, :, parts[1]], ys.at[1, dy, 0], yr.at[1, dy, 0], here.y_peers[dy])
    for copy in small_x:
        copy.wait()
    total = sx[0]
    for x in range(1, across):
        total = total + sx[x]
    sc[...] = total
    small_y = []
    for d in range(1, batches):
        small_y.append(push(sc, sy.at[b], ss.at[across + d], sr.at[across + d], here.y_peers[d]))
    sy[b] = total
    z_copies = {}
    for dx in range(1, across):
        over["x", 0, 0, dx].wait()
        add_all(lambda z: (b, z, a, parts[0]), rx, lambda z: (dx, 0, z, parts[0]))
    for t in range(1, outer):
        z_copies[0, t] = push(rc.at[b, here.zs[t], a, parts[0]], rz.at[t, parts[0]], zs.at[0, t], zr.at[0, t], here.z_peers[t])
    for dy in range(1, batches):
        over["y", 1, dy, 0].wait()
        add_all(lambda z: (b, z, a, parts[1]), ry, lambda z: (dy, 0, z, parts[1]))
    for t in range(1, outer):
        z_copies[1, t] = push(rc.at[b, here.zs[t], a, parts[1]], rz.at[t, parts[1]], zs.at[1, t], zr.at[1, t], here.z_peers[t])
    for copy in small_y:
        copy.wait()
    total = sy[0]
    for y in range(1, batches):
        total = total + sy[y]
    sc[...] = total
    small_z = []
    for t in range(1, outer):
        small_z.append(push(sc, sz.at[o], ss.at[across + batches + t], sr.at[across + batches + t], here.z_peers[t]))
    sz[o] = total
    sums = line[o].astype(f32)
    for t in range(1, outer):
        line_copies[t - 1].wait()
        sums = sums + lz[t].astype(f32)
    rest_out[...] = sums
    for p in (0, 1):
        sums = rc[b, o, a, parts[p]].astype(f32)
        for t in range(1, outer):
            z_copies[p, t].wait()
            sums = sums + rz[t, parts[p]].astype(f32)
        near_out[parts[p]] = sums
    for copy in small_z:
        copy.wait()
    total = sz[0]
    for z in range(1, outer):
        total = total + sz[z]
    small_out[...] = total


def reduce_last(terms, line, small, batches, outer, inner, ident):
    across = inner // 2
    tail = terms.shape[4:]
    buf = pltpu.VMEM
    scratch = [
        buf((batches, outer, across) + tail, bf16),
        buf((batches, across, outer) + tail, bf16),
        buf((across, batches, outer) + tail, bf16),
        buf((outer,) + tail, bf16),
        buf(line.shape, bf16),
        buf(small.shape, f32),
        buf((across,) + small.shape, f32),
        buf((batches,) + small.shape, f32),
        buf((outer,) + small.shape, f32),
    ]
    scratch += [DMA((batches, across))] * 2 + [DMA((2, batches, across))] * 4 + [DMA((2, outer))] * 2 + [DMA((outer,))] * 2
    scratch += [DMA((across + batches + outer,))] * 2
    return pl.pallas_call(
        functools.partial(last_kernel, batches, outer, inner),
        out_shape=(
            jax.ShapeDtypeStruct(tail, f32),
            jax.ShapeDtypeStruct(line.shape[1:], f32),
            jax.ShapeDtypeStruct(small.shape, f32),
        ),
        in_specs=[IN_VMEM] * 3,
        out_specs=(IN_VMEM,) * 3,
        scratch_shapes=scratch,
        compiler_params=remote_params(ident, ROOM),
        name="reduce_last",
    )(terms, line, small)


beta_one = 0.9
beta_two = 0.999
adam_eps = 1e-08
learn_rate = 0.01
decay_rate = 0.1
adam_step = 10


def layer_norm(values, gain, shift):
    center = values - jnp.mean(values, -1, keepdims=True)
    spread = jnp.mean(center * center, -1, keepdims=True)
    return center * lax.rsqrt(spread + 1e-05) * gain + shift


def gelu_tanh(values):
    inner = 0.7978845608028654 * (values + 0.044715 * values * values * values)
    return 0.5 * values * (1.0 + jnp.tanh(inner))


def angles(positions):
    freq = 10000.0 ** (-jnp.arange(HEAD // 2, dtype=jnp.float32) * 2.0 / HEAD)
    turned = positions.astype(jnp.float32)[:, None] * freq[None, :]
    return (jnp.cos(turned), jnp.sin(turned))


def rotate(tensor, cosine, sine, direction):
    first = tensor[..., : HEAD // 2]
    second = tensor[..., HEAD // 2 :]
    cosine = cosine[None, :, None, :]
    sine = direction * sine[None, :, None, :]
    return jnp.concatenate([first * cosine - second * sine, first * sine + second * cosine], -1)


def split_small(vector):
    gain_one = vector[0:D]
    gain_two = vector[D : 2 * D]
    shift_one = vector[2 * D : 3 * D]
    shift_two = vector[3 * D : 4 * D]
    bias_qkv = vector[4 * D : 7 * D]
    bias_out = vector[7 * D : 8 * D]
    bias_up = vector[8 * D : 8 * D + FF]
    bias_down = vector[8 * D + FF : 9 * D + FF]
    mixing = vector[9 * D + FF :]
    return (
        gain_one,
        gain_two,
        shift_one,
        shift_two,
        bias_qkv,
        bias_out,
        bias_up,
        bias_down,
        mixing,
    )


def adam(param, grad, first, second, decay):
    first_new = beta_one * first + (1.0 - beta_one) * grad
    second_new = beta_two * second + (1.0 - beta_two) * grad * grad
    fix_one = 1.0 - beta_one**adam_step
    fix_two = 1.0 - beta_two**adam_step
    update = first_new / fix_one / (jnp.sqrt(second_new / fix_two) + adam_eps)
    return (-learn_rate * (update + decay * param), first_new)


def body(
    tokens_in,
    earlier_outs,
    out_cotangent,
    seq_lengths,
    qkv_weight,
    out_weight,
    up_weight,
    down_weight,
    qkv_first,
    qkv_second,
    out_first,
    out_second,
    up_first,
    up_second,
    down_first,
    down_second,
    small_params,
    small_first,
    small_second,
):
    groups = tokens_in.shape[0]
    rows = tokens_in.shape[1]
    count_rows = groups * rows
    heads = D // HEAD
    seq_count = lax.axis_size("seq")
    seq_rank = lax.axis_index("seq")
    first_row = seq_rank * rows
    query_pos = first_row + jnp.arange(rows, dtype=jnp.int32)
    last_row = first_row + rows - 1
    batches = lax.axis_size("batch")
    devices = batches * seq_count
    outer = math.gcd(seq_count, D // HEAD)
    inner = seq_count // outer
    share = D // devices
    tall = share % 8 == 0 and inner % 2 == 0

    def by_rows(shard):
        return shard.astype(bf16).reshape(share, -1, D).transpose(1, 0, 2).reshape(-1, D)

    def by_blocks(gathered):
        return gathered.reshape(devices, -1, share, D).transpose(1, 0, 2, 3).reshape(-1, D, D)

    near = jnp.concatenate([by_rows(qkv_weight), by_rows(out_weight)], 0)
    rest = jnp.concatenate([by_rows(up_weight), down_weight.astype(bf16)], 0)
    mine = jnp.sum(seq_lengths)
    if tall:
        near_all, rest_line, counts = gather_first(near, rest, jnp.full((8, 128), mine, jnp.int32), batches, outer, inner, 1)
        total = jnp.sum(counts[:, 0, 0])
    else:
        near_all = lax.all_gather(near, ("batch", "seq"), axis=0)
        total = lax.psum(mine, "batch")
    mats = by_blocks(near_all)
    slots = groups * lax.axis_size("batch") * rows * seq_count
    live = (query_pos[None, :] < seq_lengths[:, None]).astype(jnp.float32)
    scale = live * (slots / total.astype(jnp.float32))
    mat_qkv = mats[:3].transpose(1, 0, 2).reshape(D, 3 * D)
    mat_out = mats[3]
    gain_one, gain_two, shift_one, shift_two, bias_qkv, bias_out, bias_up, bias_down, mixing = (
        split_small(small_params)
    )
    tokens = tokens_in.reshape(count_rows, D).astype(jnp.float32)
    normed_one, pull_one = jax.vjp(layer_norm, tokens, gain_one, shift_one)
    normed_one_low = normed_one.astype(jnp.bfloat16)
    joined = jnp.dot(normed_one_low, mat_qkv, preferred_element_type=jnp.float32) + bias_qkv
    cosine, sine = angles(query_pos)
    query_low = rotate(joined[:, :D].reshape(groups, rows, heads, HEAD), cosine, sine, 1.0).astype(
        jnp.bfloat16
    )
    key_low = (
        rotate(joined[:, D : 2 * D].reshape(groups, rows, heads, HEAD), cosine, sine, 1.0)
        .astype(jnp.bfloat16)
        .reshape(groups, rows, D)
    )
    value_low = joined[:, 2 * D :].astype(jnp.bfloat16).reshape(groups, rows, D)

    per = heads // outer

    def to_heads(value):
        return value.reshape(groups, rows, outer, per * HEAD).transpose(2, 1, 0, 3).reshape(outer, rows, groups * per * HEAD)

    def from_heads(value):
        return value.reshape(outer, rows, groups, per * HEAD).transpose(2, 1, 0, 3).reshape(count_rows, D)

    sent = (to_heads(query_low), to_heads(key_low), to_heads(value_low))
    if tall:
        q_mine, k_mine, v_mine, rest_all = spread_heads(*sent, rest_line, batches, inner, 2)
    else:
        q_mine, k_mine, v_mine = spread_heads(*sent, None, batches, inner, 2)
        rest_all = lax.all_gather(rest, ("batch", "seq"), axis=0)
    rest_all = rest_all.reshape(devices, -1, D)
    split = rest.shape[0] // 2
    mat_up = by_blocks(rest_all[:, :split]).transpose(1, 0, 2).reshape(D, FF)
    mat_down = rest_all[:, split:].reshape(FF, D)
    k_mine = k_mine.reshape(seq_count * rows, groups * per * HEAD)
    v_mine = v_mine.reshape(seq_count * rows, groups * per * HEAD)
    span = math.gcd(seq_count * rows, 1024)
    o_mine, o_turned, log_total = flash_fwd(seq_lengths, q_mine, k_mine, v_mine, groups, per, inner, span)
    attended_low = from_heads(swap_outer(o_mine, batches, inner, 3))
    branch = jnp.dot(attended_low, mat_out, preferred_element_type=jnp.float32) + bias_out
    middle = tokens + branch
    normed_two, pull_two = jax.vjp(layer_norm, middle, gain_two, shift_two)
    normed_two_low = normed_two.astype(jnp.bfloat16)
    hidden = jnp.dot(normed_two_low, mat_up, preferred_element_type=jnp.float32) + bias_up
    active, pull_gelu = jax.vjp(gelu_tanh, hidden)
    active_low = active.astype(jnp.bfloat16)
    layer_out = (
        middle + jnp.dot(active_low, mat_down, preferred_element_type=jnp.float32) + bias_down
    )
    earlier_count = earlier_outs.shape[0]
    earlier_rows = earlier_outs.reshape(earlier_count, count_rows, D)
    mixture = mixing[0] * layer_out + mixing[1] * tokens
    for earlier_index in range(earlier_count):
        mixture = mixture + mixing[2 + earlier_index] * earlier_rows[earlier_index].astype(
            jnp.float32
        )
    mixed = mixture.astype(jnp.bfloat16).reshape(groups, rows, D)
    grad_rows = (out_cotangent.astype(jnp.float32) * scale[..., None]).reshape(count_rows, D)
    mixing_terms = [jnp.sum(grad_rows * layer_out), jnp.sum(grad_rows * tokens)]
    for earlier_index in range(earlier_count):
        mixing_terms.append(jnp.sum(grad_rows * earlier_rows[earlier_index].astype(jnp.float32)))
    mixing_grad = jnp.stack(mixing_terms)
    result_grad = mixing[0] * grad_rows
    result_low = result_grad.astype(jnp.bfloat16)
    down_term = jnp.einsum("nf,nd->fd", active_low, result_low, preferred_element_type=jnp.float32)
    bias_down_grad = jnp.sum(result_low.astype(jnp.float32), 0)
    active_grad = jnp.einsum("nd,fd->nf", result_low, mat_down, preferred_element_type=jnp.float32)
    hidden_low = pull_gelu(active_grad)[0].astype(jnp.bfloat16)
    up_term = jnp.einsum(
        "nd,nf->df", normed_two_low, hidden_low, preferred_element_type=jnp.float32
    )
    bias_up_grad = jnp.sum(hidden_low.astype(jnp.float32), 0)
    normed_two_grad = jnp.einsum(
        "nf,df->nd", hidden_low, mat_up, preferred_element_type=jnp.float32
    )
    middle_part, gain_two_grad, shift_two_grad = pull_two(normed_two_grad)
    middle_grad = result_grad + middle_part
    branch_low = middle_grad.astype(jnp.bfloat16)
    out_term = jnp.einsum("nd,ne->de", attended_low, branch_low, preferred_element_type=jnp.float32)
    bias_out_grad = jnp.sum(branch_low.astype(jnp.float32), 0)
    attended_grad = jnp.einsum(
        "ne,de->nd", branch_low, mat_out, preferred_element_type=jnp.float32
    ).astype(jnp.bfloat16)
    grad_mine = swap_outer(to_heads(attended_grad), batches, inner, 4)
    block_pos = (jnp.arange(outer) * inner + seq_rank % inner)[:, None] * rows + jnp.arange(rows)[None, :]
    freq = 10000.0 ** (-jnp.arange(HEAD // 2, dtype=jnp.float32) * 2.0 / HEAD)
    turned = block_pos.astype(jnp.float32)[:, None, :] * freq[None, :, None]
    dq_mine, dk_mine, dv_mine = flash_bwd(
        seq_lengths, q_mine, k_mine, v_mine, grad_mine, o_turned, log_total, jnp.cos(turned), jnp.sin(turned), groups, per, inner, math.gcd(seq_count * rows, 512)
    )
    pieces = (outer, inner, rows, groups * per * HEAD)
    def by_owner(term):
        return term.astype(bf16).reshape(devices, share, -1, D).transpose(0, 2, 1, 3).reshape(devices, -1, D)

    rest_terms = jnp.concatenate([by_owner(up_term), down_term.astype(bf16).reshape(devices, -1, D)], 1)
    if tall:
        spread_terms = rest_terms.reshape((batches, outer, inner // 2, 2) + rest_terms.shape[1:])
        dq_home, dk_home, dv_home, rest_back = fold_heads(dq_mine, dk_mine.reshape(pieces), dv_mine.reshape(pieces), spread_terms, batches, inner, 5)
    else:
        dq_home, dk_home, dv_home = fold_heads(dq_mine, dk_mine.reshape(pieces), dv_mine.reshape(pieces), None, batches, inner, 5)
    key_grad = from_heads(dk_home).astype(jnp.float32)
    query_back = from_heads(dq_home)
    key_back = rotate(key_grad.reshape(groups, rows, heads, HEAD), cosine, sine, -1.0).reshape(
        count_rows, D
    )
    joined_low = jnp.concatenate(
        [query_back, key_back.astype(jnp.bfloat16), from_heads(dv_home)], -1
    )
    qkv_term = jnp.einsum(
        "nd,nf->df", normed_one_low, joined_low, preferred_element_type=jnp.float32
    )
    bias_qkv_grad = jnp.sum(joined_low.astype(jnp.float32), 0)
    normed_one_grad = jnp.einsum(
        "nf,df->nd", joined_low, mat_qkv, preferred_element_type=jnp.float32
    )
    input_part, gain_one_grad, shift_one_grad = pull_one(normed_one_grad)
    input_grad = (mixing[1] * grad_rows + middle_grad + input_part).reshape(groups, rows, D)
    small_local = jnp.concatenate(
        [
            gain_one_grad,
            gain_two_grad,
            shift_one_grad,
            shift_two_grad,
            bias_qkv_grad,
            bias_out_grad,
            bias_up_grad,
            bias_down_grad,
            mixing_grad,
        ]
    )
    near_terms = jnp.concatenate([by_owner(qkv_term), by_owner(out_term)], 1)
    if tall:
        near_terms = near_terms.reshape((batches, outer, inner // 2, 2) + near_terms.shape[1:])
        count = small_local.shape[0]
        lines = -(-count // 1024) * 8
        small_rows = jnp.pad(small_local, (0, lines * 128 - count)).reshape(lines, 128)
        near_grad, rest_grad, small_rows = reduce_last(near_terms, rest_back, small_rows, batches, outer, inner, 6)
        small_grad = small_rows.reshape(-1)[:count]
    else:
        near_grad = lax.psum_scatter(near_terms, ("batch", "seq"), scatter_dimension=0).astype(f32)
        rest_grad = lax.psum_scatter(rest_terms, ("batch", "seq"), scatter_dimension=0).astype(f32)
        small_grad = lax.psum(small_local, ("batch", "seq"))

    def as_shard(part):
        return part.reshape(-1, share, D).transpose(1, 0, 2).reshape(share, -1)

    qkv_grad, out_grad = as_shard(near_grad[: 3 * share]), near_grad[3 * share :]
    up_grad, down_grad = as_shard(rest_grad[:split]), rest_grad[split:]
    qkv_step, qkv_first_new = adam(qkv_weight, qkv_grad, qkv_first, qkv_second, decay_rate)
    out_step, out_first_new = adam(out_weight, out_grad, out_first, out_second, decay_rate)
    up_step, up_first_new = adam(up_weight, up_grad, up_first, up_second, decay_rate)
    down_step, down_first_new = adam(down_weight, down_grad, down_first, down_second, decay_rate)
    small_step, small_first_new = adam(small_params, small_grad, small_first, small_second, 0.0)
    return (
        mixed,
        input_grad,
        qkv_grad,
        out_grad,
        up_grad,
        down_grad,
        small_grad,
        qkv_step,
        out_step,
        up_step,
        down_step,
        small_step,
        qkv_first_new,
        out_first_new,
        up_first_new,
        down_first_new,
        small_first_new,
    )


def solution(mesh):
    placed = (
        P("batch", "seq", None),
        P(None, "batch", "seq", None),
        P("batch", "seq", None),
        P("batch"),
        P(("batch", "seq"), None),
        P(("batch", "seq"), None),
        P(("batch", "seq"), None),
        P(("batch", "seq"), None),
        P(("batch", "seq"), None),
        P(("batch", "seq"), None),
        P(("batch", "seq"), None),
        P(("batch", "seq"), None),
        P(("batch", "seq"), None),
        P(("batch", "seq"), None),
        P(("batch", "seq"), None),
        P(("batch", "seq"), None),
        P(),
        P(),
        P(),
    )
    return jax.shard_map(
        body,
        mesh=mesh,
        in_specs=placed,
        out_specs=(
            P("batch", "seq", None),
            P("batch", "seq", None),
            P(("batch", "seq"), None),
            P(("batch", "seq"), None),
            P(("batch", "seq"), None),
            P(("batch", "seq"), None),
            P(),
            P(("batch", "seq"), None),
            P(("batch", "seq"), None),
            P(("batch", "seq"), None),
            P(("batch", "seq"), None),
            P(),
            P(("batch", "seq"), None),
            P(("batch", "seq"), None),
            P(("batch", "seq"), None),
            P(("batch", "seq"), None),
            P(),
        ),
        check_vma=False,
    )
```

```python
import functools
import math

import jax
import jax.numpy as jnp
from jax import lax
from jax.experimental import pallas as pl
from jax.experimental.pallas import tpu as pltpu
from jax.sharding import PartitionSpec as P

D = 768
FF = 3072
HEAD = 64
BLOCKS = FF // D
VECTORS = 9 + BLOCKS
bf16 = jnp.bfloat16
f32 = jnp.float32
NEG = -1e30

beta_one = 0.9
beta_two = 0.999
adam_eps = 1e-08
learn_rate = 0.01
decay_rate = 0.1
adam_step = 10

MESH = pl.DeviceIdType.MESH
ANYWHERE = pl.BlockSpec(memory_space=pl.ANY)
IN_VMEM = pl.BlockSpec(memory_space=pltpu.VMEM)
IN_SMEM = pl.BlockSpec(memory_space=pltpu.SMEM)
DMA = pltpu.SemaphoreType.DMA
ROOM = 56 << 20

UNITS = ((0, 1, 4), (2, 3, 5))


def mm(a, b):
    return lax.dot_general(a, b, (((1,), (0,)), ((), ())), preferred_element_type=f32)


def mm_nt(a, b):
    return lax.dot_general(a, b, (((1,), (1,)), ((), ())), preferred_element_type=f32)


def params():
    return pltpu.CompilerParams(vmem_limit_bytes=ROOM)


def remote_params(ident, vmem=None):
    return pltpu.CompilerParams(collective_id=ident, has_side_effects=True, vmem_limit_bytes=vmem)


class Place:
    def __init__(self, batches, outer, inner):
        self.batch = lax.axis_index("batch")
        rank = lax.axis_index("seq")
        self.o = lax.div(rank, inner)
        self.j = lax.rem(rank, inner)
        self.a = lax.div(self.j, 2)
        self.c = lax.rem(rank, 2)
        across = inner // 2
        self.zs = [lax.rem(self.o + t, outer) for t in range(outer)]
        self.xs = [lax.rem(self.a + t, across) for t in range(across)]
        self.ys = [lax.rem(self.batch + t, batches) for t in range(batches)]
        self.z_from = [lax.rem(self.o + outer - t, outer) for t in range(outer)]
        self.x_from = [lax.rem(self.a + across - t, across) for t in range(across)]
        self.y_from = [lax.rem(self.batch + batches - t, batches) for t in range(batches)]
        self.z_peers = [(self.batch, z * inner + self.j) for z in self.zs]
        self.x_peers = [(self.batch, self.o * inner + x * 2 + self.c) for x in self.xs]
        self.y_peers = [(y, rank) for y in self.ys]
        self.twin = (self.batch, self.o * inner + self.a * 2 + (1 - self.c))


def greet(peers):
    barrier = pltpu.get_barrier_semaphore()
    for peer in peers:
        pl.semaphore_signal(barrier, inc=1, device_id=peer, device_id_type=MESH)
    pl.semaphore_wait(barrier, len(peers))


def push(src, dst, send, recv, peer):
    copy = pltpu.make_async_remote_copy(
        src_ref=src, dst_ref=dst, send_sem=send, recv_sem=recv, device_id=peer, device_id_type=MESH
    )
    copy.start()
    return copy


def carry(src, dst, sem):
    copy = pltpu.make_async_copy(src, dst, sem)
    copy.start()
    return copy


def normalize(values):
    center = values - jnp.mean(values, -1, keepdims=True)
    inverse = lax.rsqrt(jnp.mean(center * center, -1, keepdims=True) + 1e-05)
    return center * inverse, inverse


def normalize_back(grad, hat, inverse, gain):
    scaled = grad * gain
    part = scaled - jnp.mean(scaled, -1, keepdims=True) - hat * jnp.mean(scaled * hat, -1, keepdims=True)
    return part * inverse


def turn(value, cosine, sine):
    lane = lax.broadcasted_iota(jnp.int32, value.shape, 1)
    other = jnp.where(lax.rem(lane, HEAD) < HEAD // 2, pltpu.roll(value, 128 - HEAD // 2, 1), pltpu.roll(value, HEAD // 2, 1))
    return value * cosine + other * sine


def put_heads(write, tiles_of, outer):
    for o in range(outer):
        first = 3 * o * HEAD
        odd = first % 128 != 0
        pair = (first + HEAD if odd else first) // 128
        single = (first if odd else first + 128) // 128
        write(o, 0, tiles_of(0, pair))
        write(o, 1, tiles_of(1, pair))
        one, two = tiles_of(0, single), tiles_of(1, single)
        if odd:
            one = pltpu.roll(one, HEAD, 1)
        else:
            two = pltpu.roll(two, HEAD, 1)
        lane = lax.broadcasted_iota(jnp.int32, one.shape, 1)
        write(o, 2, jnp.where(lane < HEAD, one, two))


def take_heads(read, g, outer):
    tiles = [None] * (outer * 3 // 2)
    for o in range(0, outer, 2):
        base = 3 * o * HEAD // 128
        tiles[base] = read(o, g)
        tiles[base + 2] = read(o + 1, g)
        low, high = read(o, 2), read(o + 1, 2)
        if g == 0:
            high = pltpu.roll(high, HEAD, 1)
        else:
            low = pltpu.roll(low, HEAD, 1)
        lane = lax.broadcasted_iota(jnp.int32, low.shape, 1)
        tiles[base + 1] = jnp.where(lane < HEAD, low, high)
    return tiles


def first_kernel(batches, outer, inner, first_row, *refs):
    refs = list(refs)

    def take(n):
        got = refs[:n]
        del refs[:n]
        return got

    qkv, out, up, down, lens, mixing, tokens, cot, earlier, vecs, count = take(11)
    near_all, up_line, down_line, counts, normed, mixture, dots = take(7)
    own, got, near, up_bit, down_bit, queue = take(6)
    zs, zr, xs, xr, ys, yr, cs, cr, us, ur, ds, dr, ns, nr, ts, tr, local, es = refs
    across = inner // 2
    here = Place(batches, outer, inner)
    o, a, b, c = here.o, here.a, here.batch, here.c
    earlier_count, tall, _ = earlier.shape
    groups = lens.shape[0]
    rows = tall // groups
    fetches = {}
    for e in range(2):
        fetches[e] = carry(earlier.at[e], queue.at[e], es.at[e])
    for block in range(4):
        own[block] = qkv[:, block * D : block * D + D] if block < 3 else out[...]
        own[4 + block] = up[:, block * D : block * D + D]
    greet(here.z_peers[1:] + here.x_peers[1:] + here.y_peers[1:] + [here.twin])
    theirs = 2 * (1 - c)
    swaps = [
        push(own.at[pl.ds(theirs, 2)], got.at[0], ts.at[0], tr.at[0], here.twin),
        push(own.at[pl.ds(4 + theirs, 2)], got.at[1], ts.at[1], tr.at[1], here.twin),
    ]
    waits = [carry(count, counts.at[b], local.at[0])]
    for d in range(1, batches):
        waits.append(push(count, counts.at[b], ns.at[d], nr.at[d], here.y_peers[d]))
    down_bit[...] = down[...].astype(bf16)

    def joined(kind, p):
        mine, other = own[4 * kind + 2 * c + p], got[kind, p]
        low = jnp.where(c == 0, mine, other)
        high = jnp.where(c == 0, other, mine)
        return jnp.concatenate([low, high], 0).astype(bf16)

    def slot(p, y, z, x):
        return near_all.at[2 * c + p, y, z, x]

    arrivals = {}

    def onward(source, p, y, z, x, t, dx, dy):
        to = slot(p, y, z, x)
        if dx == 0 and (dy == 0 or p == 1):
            for d in range(1, across):
                key = (p, t, d, dy)
                arrivals["x", key] = push(source, to, xs.at[key], xr.at[key], here.x_peers[d])
        if dy == 0 and (dx == 0 or p == 0):
            for d in range(1, batches):
                key = (p, t, dx, d)
                arrivals["y", key] = push(source, to, ys.at[key], yr.at[key], here.y_peers[d])
        key = (p, t, dx, dy)
        waits.append(push(source, to, cs.at[key], cr.at[key], here.twin))

    swaps[0].wait()
    copies = {}
    for p in (0, 1):
        near[p] = joined(0, p)
        for t in range(1, outer):
            copies[t, p] = push(near.at[p], slot(p, b, o, a), zs.at[t, p], zr.at[t, p], here.z_peers[t])
        onward(near.at[p], p, b, o, a, 0, 0, 0)
        waits.append(carry(near.at[p], slot(p, b, o, a), local.at[1 + p]))
    swaps[1].wait()
    for p in (0, 1):
        up_bit[p] = joined(1, p)
    for t in range(1, outer):
        waits.append(push(up_bit, up_line.at[:, o], us.at[t], ur.at[t], here.z_peers[t]))
        waits.append(push(down_bit, down_line.at[o], ds.at[t], dr.at[t], here.z_peers[t]))
    waits.append(carry(up_bit, up_line.at[:, o], local.at[3]))
    waits.append(carry(down_bit, down_line.at[o], local.at[4]))

    def live_rows(value):
        row = lax.broadcasted_iota(jnp.int32, (rows, 1), 0) + first_row(rows)
        parts = [jnp.where(row < lens[g], value[g * rows : g * rows + rows], 0.0) for g in range(groups)]
        return jnp.concatenate(parts, 0)

    def normal():
        wide = tokens[...].astype(f32)
        hat, _ = normalize(wide)
        normed[...] = (hat * vecs[0:1] + vecs[2:3]).astype(bf16)
        grad = live_rows(cot[...].astype(f32))
        dots[...] = jnp.zeros(dots.shape, f32)
        dots[1:2] = jnp.sum(grad * wide, 0, keepdims=True)
        mixture[...] = mixing[1] * wide

    def mix(e):
        fetches[e].wait()
        wide = queue[e % 2].astype(f32)
        grad = live_rows(cot[...].astype(f32))
        dots[2 + e : 3 + e] = jnp.sum(grad * wide, 0, keepdims=True)
        mixture[...] = mixture[...] + mixing[2 + e] * wide
        if e + 2 < earlier_count:
            fetches[e + 2] = carry(earlier.at[e + 2], queue.at[e % 2], es.at[e + 2])

    steps = [normal] + [functools.partial(mix, e) for e in range(earlier_count)]

    def work(n=1):
        for _ in range(n):
            if steps:
                steps.pop(0)()

    for t in range(1, outer):
        for p in (0, 1):
            copies[t, p].wait()
            onward(slot(p, b, here.z_from[t], a), p, b, here.z_from[t], a, t, 0, 0)
    work(1)
    for t in range(outer):
        z = here.z_from[t]
        for d in range(1, across):
            arrivals["x", (0, t, d, 0)].wait()
            onward(slot(0, b, z, here.x_from[d]), 0, b, z, here.x_from[d], t, d, 0)
        for d in range(1, batches):
            arrivals["y", (1, t, 0, d)].wait()
            onward(slot(1, here.y_from[d], z, a), 1, here.y_from[d], z, a, t, 0, d)
        work(1)
    for t in range(outer):
        z = here.z_from[t]
        for dx in range(across):
            for dy in range(1, batches):
                arrivals["y", (0, t, dx, dy)].wait()
                onward(slot(0, here.y_from[dy], z, here.x_from[dx]), 0, here.y_from[dy], z, here.x_from[dx], t, dx, dy)
        for dy in range(batches):
            for dx in range(1, across):
                arrivals["x", (1, t, dx, dy)].wait()
                onward(slot(1, here.y_from[dy], z, here.x_from[dx]), 1, here.y_from[dy], z, here.x_from[dx], t, dx, dy)
        work(1)
    work(len(steps))
    for copy in waits:
        copy.wait()


def gather_first(qkv, out, up, down, lens, mixing, tokens, cot, earlier, vecs, count, batches, outer, inner, ident):
    across = inner // 2
    share = qkv.shape[0]
    tall = tokens.shape[0]

    def first_row(rows):
        return lax.axis_index("seq") * rows

    grid = (batches, outer, across)
    return pl.pallas_call(
        functools.partial(first_kernel, batches, outer, inner, first_row),
        out_shape=(
            jax.ShapeDtypeStruct((4,) + grid + (2 * share, D), bf16),
            jax.ShapeDtypeStruct((2, outer, 2 * share, D), bf16),
            jax.ShapeDtypeStruct((outer, BLOCKS * share, D), bf16),
            jax.ShapeDtypeStruct((batches,) + count.shape, count.dtype),
            jax.ShapeDtypeStruct((tall, D), bf16),
            jax.ShapeDtypeStruct((tall, D), f32),
            jax.ShapeDtypeStruct((16, D), f32),
        ),
        in_specs=[IN_VMEM] * 4 + [IN_SMEM] * 2 + [IN_VMEM] * 2 + [ANYWHERE, IN_VMEM, ANYWHERE],
        out_specs=(ANYWHERE,) * 4 + (IN_VMEM,) * 3,
        scratch_shapes=[
            pltpu.VMEM((8, share, D), f32),
            pltpu.VMEM((2, 2, share, D), f32),
            pltpu.VMEM((2, 2 * share, D), bf16),
            pltpu.VMEM((2, 2 * share, D), bf16),
            pltpu.VMEM((BLOCKS * share, D), bf16),
            pltpu.VMEM((2, tall, D), bf16),
        ]
        + [DMA((outer, 2))] * 2
        + [DMA((2, outer, across, batches))] * 6
        + [DMA((outer,))] * 4
        + [DMA((batches,))] * 2
        + [DMA((2,))] * 2
        + [DMA((5,)), DMA((earlier.shape[0],))],
        compiler_params=remote_params(ident, ROOM),
        name="gather_first",
    )(qkv, out, up, down, lens, mixing, tokens, cot, earlier, vecs, count)


def spread_kernel(batches, outer, inner, with_rest, *refs):
    refs = list(refs)

    def take(n):
        got = refs[:n]
        del refs[:n]
        return got

    normed, near, vecs, cosine, sine = take(5)
    lines = take(2) if with_rest else []
    q_all, k_all, v_all = take(3)
    alls = take(2) if with_rest else []
    q, k, v, work = take(4)
    qs, qr, zs, zr, xs, xr, cs, cr, local = take(9)
    across = inner // 2
    here = Place(batches, outer, inner)
    o, a, b, c, j = here.o, here.a, here.batch, here.c, here.j
    rows = cosine.shape[0]
    greet(here.z_peers[1:] + here.x_peers[1:] + [here.twin] + (here.y_peers[1:] if with_rest else []))
    waits, rest_x, rest_y = [], [], []

    def rest_slot(i, y, x):
        if i == 0:
            return alls[0].at[pl.ds(2 * c, 2), y, :, x]
        return alls[1].at[y, :, x, c]

    if with_rest:
        ax, axr, ay, ayr, ac, acr, alocal = refs
        for i in (0, 1):
            waits.append(carry(lines[i], rest_slot(i, b, a), alocal.at[i]))
            for d in range(1, across):
                rest_x.append((i, d, push(lines[i], rest_slot(i, b, a), ax.at[i, d], axr.at[i, d], here.x_peers[d])))
            for d in range(1, batches):
                rest_y.append((i, 0, d, push(lines[i], rest_slot(i, b, a), ay.at[i, 0, d], ayr.at[i, 0, d], here.y_peers[d])))
            waits.append(push(lines[i], rest_slot(i, b, a), ac.at[i, 0, 0], acr.at[i, 0, 0], here.twin))

    def rest_across():
        i, d, copy = rest_x.pop(0)
        copy.wait()
        piece = rest_slot(i, b, here.x_from[d])
        for e in range(1, batches):
            rest_y.append((i, d, e, push(piece, piece, ay.at[i, d, e], ayr.at[i, d, e], here.y_peers[e])))
        waits.append(push(piece, piece, ac.at[i, d, 0], acr.at[i, d, 0], here.twin))

    def rest_twin():
        i, d, e, copy = rest_y.pop(0)
        copy.wait()
        piece = rest_slot(i, here.y_from[e], here.x_from[d])
        waits.append(push(piece, piece, ac.at[i, d, e], acr.at[i, d, e], here.twin))

    def project(block, into, rotated):
        work[...] = mm(normed[...], near[block]) + vecs[4 + block : 5 + block]

        def tiles_of(g, tile):
            value = work[g * rows : g * rows + rows, 128 * tile : 128 * tile + 128]
            return turn(value, cosine[...], sine[...]) if rotated else value

        def write(target, tile, value):
            into[target, :, 128 * tile : 128 * tile + 128] = value.astype(bf16)

        put_heads(write, tiles_of, outer)

    arriving, own = [], []
    for i, (block, into, dest) in enumerate(((1, k, k_all), (2, v, v_all))):
        project(block, into, i == 0)
        for t in range(1, outer):
            copy = push(into.at[here.zs[t]], dest.at[o, j], zs.at[i, t], zr.at[i, t], here.z_peers[t])
            arriving.append((i, t, copy))
        waits.append(carry(into.at[o], dest.at[o, j], local.at[i]))
        own.append((i, 0, None))
    project(0, q, True)
    for t in range(1, outer):
        waits.append(push(q.at[here.zs[t]], q_all.at[o], qs.at[t], qr.at[t], here.z_peers[t]))
    waits.append(carry(q.at[o], q_all.at[o], local.at[2]))
    late = []
    order = own + arriving
    for n, (i, t, copy) in enumerate(order):
        dest = (k_all, v_all)[i]
        place = dest.at[here.z_from[t], j]
        source = (k, v)[i].at[o] if copy is None else place
        if copy is not None:
            copy.wait()
        for d in range(1, across):
            late.append((i, t, d, push(source, place, xs.at[i, t, d], xr.at[i, t, d], here.x_peers[d])))
        waits.append(push(source, place, cs.at[i, t, 0], cr.at[i, t, 0], here.twin))
        while len(late) > (across - 1 if n < len(order) - 1 else 0):
            li, lt, ld, waited = late.pop(0)
            waited.wait()
            moved = (k_all, v_all)[li].at[here.z_from[lt], here.x_from[ld] * 2 + c]
            waits.append(push(moved, moved, cs.at[li, lt, ld], cr.at[li, lt, ld], here.twin))
        if rest_x and n >= 2:
            rest_across()
    while rest_x:
        rest_across()
    while rest_y:
        rest_twin()
    for copy in waits:
        copy.wait()


def spread_heads(normed, near, vecs, cosine, sine, lines, batches, outer, inner, ident):
    rows = cosine.shape[0]
    across = inner // 2
    width = 2 * D // outer
    with_rest = bool(lines)
    piece = jax.ShapeDtypeStruct((outer, rows, width), bf16)
    full = jax.ShapeDtypeStruct((outer, inner, rows, width), bf16)
    shapes = (piece, full, full)
    scratch = [pltpu.VMEM((outer, rows, width), bf16)] * 3 + [pltpu.VMEM(normed.shape, f32)]
    scratch += [DMA((outer,))] * 2 + [DMA((2, outer))] * 2 + [DMA((2, outer, across))] * 4 + [DMA((3,))]
    if with_rest:
        shapes += (
            jax.ShapeDtypeStruct((4, batches, outer, across) + lines[0].shape[2:], bf16),
            jax.ShapeDtypeStruct((batches, outer, across, 2) + lines[1].shape[1:], bf16),
        )
        scratch += [DMA((2, across))] * 2 + [DMA((2, across, batches))] * 4 + [DMA((2,))]
    return pl.pallas_call(
        functools.partial(spread_kernel, batches, outer, inner, with_rest),
        out_shape=shapes,
        in_specs=[IN_VMEM] * 5 + [ANYWHERE] * len(lines),
        out_specs=(ANYWHERE,) * len(shapes),
        scratch_shapes=scratch,
        compiler_params=remote_params(ident, ROOM),
        name="spread_heads",
    )(normed, near, vecs, cosine, sine, *lines)


def swap_kernel(batches, inner, x, out, send, recv, local):
    outer = x.shape[0]
    here = Place(batches, outer, inner)
    greet(here.z_peers[1:])
    own = carry(x.at[here.o], out.at[here.o], local)
    copies = []
    for t in range(1, outer):
        copies.append(push(x.at[here.zs[t]], out.at[here.o], send.at[t], recv.at[t], here.z_peers[t]))
    own.wait()
    for copy in copies:
        copy.wait()


def swap_outer(x, batches, inner, ident):
    outer = x.shape[0]
    return pl.pallas_call(
        functools.partial(swap_kernel, batches, inner),
        out_shape=jax.ShapeDtypeStruct(x.shape, x.dtype),
        in_specs=[ANYWHERE],
        out_specs=ANYWHERE,
        scratch_shapes=[DMA((outer,)), DMA((outer,)), DMA],
        compiler_params=remote_params(ident),
        name="swap_heads",
    )(x)


def half_rows(block_t, half):
    z = jnp.zeros((HEAD, block_t.shape[1]), block_t.dtype)
    if half == 0:
        return jnp.concatenate([block_t[:HEAD], z], 0)
    return jnp.concatenate([z, block_t[HEAD:]], 0)


def attend_kernel(groups, per, span, inner, lens, q, k, v, o, ot, lse, vt, qt, m_s, l_s):
    outer, rows, width = q.shape
    units = groups * per
    total = k.shape[0]
    j = lax.rem(lax.axis_index("seq"), inner)
    blk = math.gcd(total, 512)

    def turn_v(i, _):
        at = pl.ds(pl.multiple_of(i * blk, blk), blk)
        for t in range(width // 128):
            lanes = slice(128 * t, 128 * t + 128)
            vt[lanes, at] = v[at, lanes].T
        return 0

    lax.fori_loop(0, total // blk, turn_v, 0)

    def one(z, _):
        first = (z * inner + j) * rows
        for t in range(width // 128):
            lanes = slice(128 * t, 128 * t + 128)
            turned = (q[z, :, lanes] * 0.125).astype(bf16).T
            for half in range(2):
                qt[2 * t + half] = half_rows(turned, half)
        for g in range(groups):
            length = lens[g]
            for u in UNITS[g]:
                ot[z, HEAD * u : HEAD * u + HEAD, :] = jnp.zeros((HEAD, rows), f32)
            m_s[...] = jnp.full(m_s.shape, NEG, f32)
            l_s[...] = jnp.zeros(l_s.shape, f32)

            def step(c, masked):
                at = pl.ds(pl.multiple_of(c * span, span), span)
                if masked:
                    key = c * span + lax.broadcasted_iota(jnp.int32, (span, rows), 0)
                    query = first + lax.broadcasted_iota(jnp.int32, (span, rows), 1)
                    allowed = (key <= query) & (key < length)
                scores, tops, news, shares, sums = [], [], [], [], []
                for h in range(per):
                    u = UNITS[g][h]
                    s = mm(k[at, 128 * (u // 2) : 128 * (u // 2) + 128], qt[u])
                    scores.append(jnp.where(allowed, s, NEG) if masked else s)
                for h in range(per):
                    tops.append(m_s[h : h + 1])
                    news.append(jnp.maximum(tops[h], jnp.max(scores[h], 0, keepdims=True)))
                for h in range(per):
                    p = jnp.exp(scores[h] - news[h])
                    sums.append(jnp.sum(p, 0, keepdims=True))
                    shares.append(p.astype(bf16))
                for h in range(per):
                    u = UNITS[g][h]
                    alpha = jnp.exp(tops[h] - news[h])
                    l_s[h : h + 1] = l_s[h : h + 1] * alpha + sums[h]
                    m_s[h : h + 1] = news[h]
                    span_u = slice(HEAD * u, HEAD * u + HEAD)
                    ot[z, span_u, :] = ot[z, span_u, :] * alpha + mm(vt[span_u, at], shares[h])

            whole = jnp.minimum(first, length) // span
            count = (jnp.minimum(first + rows, length) + span - 1) // span

            def full_step(c, _):
                step(c, False)
                return 0

            def edge_step(c, _):
                step(c, True)
                return 0

            lax.fori_loop(0, whole, full_step, 0)
            lax.fori_loop(whole, count, edge_step, 0)
            for h in range(per):
                u = UNITS[g][h]
                span_u = slice(HEAD * u, HEAD * u + HEAD)
                total_exp = l_s[h : h + 1]
                ot[z, span_u, :] = ot[z, span_u, :] / total_exp
                lse[z, u : u + 1, :] = m_s[h : h + 1] + jnp.log(total_exp)
        for t in range(width // 128):
            lanes = slice(128 * t, 128 * t + 128)
            o[z, :, lanes] = ot[z, lanes, :].T.astype(bf16)
        return 0

    lax.fori_loop(0, outer, one, 0)


def attend(lens, q, k, v, groups, per, inner, span):
    outer, rows, width = q.shape
    units = groups * per
    total = k.shape[0]
    vm = IN_VMEM
    return pl.pallas_call(
        functools.partial(attend_kernel, groups, per, span, inner),
        out_shape=(
            jax.ShapeDtypeStruct((outer, rows, width), bf16),
            jax.ShapeDtypeStruct((outer, width, rows), f32),
            jax.ShapeDtypeStruct((outer, 8, rows), f32),
        ),
        in_specs=[IN_SMEM, vm, vm, vm],
        out_specs=(vm, vm, vm),
        scratch_shapes=[
            pltpu.VMEM((width, total), bf16),
            pltpu.VMEM((units, 128, rows), bf16),
            pltpu.VMEM((8, rows), f32),
            pltpu.VMEM((8, rows), f32),
        ],
        compiler_params=params(),
        name="attend",
    )(lens, q, k, v)


def attend_back_kernel(groups, per, span, inner, lens, q, k, v, do, ot, lse, cos, sin, dq, dk, dv, kt, qt, dot_t, qz, dz, rd, dqt, dks, dvs):
    outer, rows, width = q.shape
    units = groups * per
    total = k.shape[0]
    j = lax.rem(lax.axis_index("seq"), inner)
    blk = math.gcd(total, 512)

    def prepare(i, _):
        at = pl.ds(pl.multiple_of(i * blk, blk), blk)
        for t in range(width // 128):
            lanes = slice(128 * t, 128 * t + 128)
            kt[lanes, at] = k[at, lanes].T
        dks[at, :] = jnp.zeros((blk, width), f32)
        dvs[at, :] = jnp.zeros((blk, width), f32)
        return 0

    lax.fori_loop(0, total // blk, prepare, 0)

    def one(z, _):
        first = (z * inner + j) * rows
        low = lax.broadcasted_iota(jnp.int32, (rows, 128), 1) < HEAD
        for t in range(width // 128):
            lanes = slice(128 * t, 128 * t + 128)
            small = (q[z, :, lanes] * 0.125).astype(bf16)
            grad = do[z, :, lanes]
            turned = small.T
            grad_t = grad.T
            prod = grad_t.astype(f32) * ot[z, lanes, :]
            for half in range(2):
                u = 2 * t + half
                qt[u] = half_rows(turned, half)
                dot_t[u] = half_rows(grad_t, half)
                keep = low if half == 0 else ~low
                qz[u] = jnp.where(keep, small, jnp.zeros_like(small))
                dz[u] = jnp.where(keep, grad, jnp.zeros_like(grad))
                rd[u : u + 1, :] = jnp.sum(prod[HEAD * half : HEAD * half + HEAD], 0, keepdims=True)
        dqt[...] = jnp.zeros(dqt.shape, f32)
        for g in range(groups):
            length = lens[g]

            def step(c, masked):
                at = pl.ds(pl.multiple_of(c * span, span), span)
                if masked:
                    key = c * span + lax.broadcasted_iota(jnp.int32, (span, rows), 0)
                    query = first + lax.broadcasted_iota(jnp.int32, (span, rows), 1)
                    allowed = (key <= query) & (key < length)
                for h in range(per):
                    u = UNITS[g][h]
                    lanes = slice(128 * (u // 2), 128 * (u // 2) + 128)
                    span_u = slice(HEAD * u, HEAD * u + HEAD)
                    s = mm(k[at, lanes], qt[u])
                    p = jnp.exp(s - lse[z, u : u + 1, :])
                    if masked:
                        p = jnp.where(allowed, p, 0.0)
                    dp = mm(v[at, lanes], dot_t[u])
                    ds = (p * (dp - rd[u : u + 1, :])).astype(bf16)
                    dvs[at, lanes] += mm(p.astype(bf16), dz[u])
                    dks[at, lanes] += mm(ds, qz[u])
                    dqt[span_u, :] += mm(kt[span_u, at], ds)

            live = first < length
            whole = jnp.where(live, jnp.minimum(first, length) // span, 0)
            count = jnp.where(live, (jnp.minimum(first + rows, length) + span - 1) // span, 0)

            def full_step(c, _):
                step(c, False)
                return 0

            def edge_step(c, _):
                step(c, True)
                return 0

            lax.fori_loop(0, whole, full_step, 0)
            lax.fori_loop(whole, count, edge_step, 0)
        cosine = cos[z]
        sine = sin[z]
        for t in range(width // 128):
            parts = []
            for half in range(2):
                u = 2 * t + half
                a = dqt[HEAD * u : HEAD * u + 32, :] * 0.125
                b = dqt[HEAD * u + 32 : HEAD * u + 64, :] * 0.125
                parts.append(a * cosine + b * sine)
                parts.append(b * cosine - a * sine)
            dq[z, :, 128 * t : 128 * t + 128] = jnp.concatenate(parts, 0).T.astype(bf16)
        return 0

    lax.fori_loop(0, outer, one, 0)

    def finish(i, _):
        at = pl.ds(pl.multiple_of(i * blk, blk), blk)
        dk[at, :] = dks[at, :].astype(bf16)
        dv[at, :] = dvs[at, :].astype(bf16)
        return 0

    lax.fori_loop(0, total // blk, finish, 0)


def attend_back(lens, q, k, v, do, ot, lse, cos, sin, groups, per, inner, span):
    outer, rows, width = q.shape
    units = groups * per
    total = k.shape[0]
    vm = IN_VMEM
    return pl.pallas_call(
        functools.partial(attend_back_kernel, groups, per, span, inner),
        out_shape=(
            jax.ShapeDtypeStruct((outer, rows, width), bf16),
            jax.ShapeDtypeStruct((total, width), bf16),
            jax.ShapeDtypeStruct((total, width), bf16),
        ),
        in_specs=[IN_SMEM] + [vm] * 8,
        out_specs=(vm, vm, vm),
        scratch_shapes=[
            pltpu.VMEM((width, total), bf16),
            pltpu.VMEM((units, 128, rows), bf16),
            pltpu.VMEM((units, 128, rows), bf16),
            pltpu.VMEM((units, rows, 128), bf16),
            pltpu.VMEM((units, rows, 128), bf16),
            pltpu.VMEM((8, rows), f32),
            pltpu.VMEM((width, rows), f32),
            pltpu.VMEM((total, width), f32),
            pltpu.VMEM((total, width), f32),
        ],
        compiler_params=params(),
        name="attend_back",
    )(lens, q, k, v, do, ot, lse, cos, sin)


def middle_kernel(outer, home, tokens, cot, mixture, dots, near, up, down, vecs, lens, mixing, total, mixed, sent, middle_grad, out_term, up_terms, down_terms, sums, attended, middle, hat_s, low_s, low_t, result_s, acc, back, weights, sems):
    tall = tokens.shape[0]
    groups = lens.shape[0]
    rows = tall // groups
    fetch_out = carry(near.at[3], weights.at[0], sems.at[0])
    fetch_up = carry(up, weights.at[pl.ds(1, BLOCKS)], sems.at[1])
    fetch_down = carry(down, weights.at[pl.ds(1 + BLOCKS, BLOCKS)], sems.at[2])
    for g in range(groups):
        tiles = take_heads(lambda o, t: home[o, :, 128 * t : 128 * t + 128].astype(f32), g, outer)
        for i, tile in enumerate(tiles):
            attended[g * rows : g * rows + rows, 128 * i : 128 * i + 128] = tile.astype(bf16)
    fetch_out.wait()
    value = tokens[...].astype(f32) + (mm(attended[...], weights[0]) + vecs[7:8])
    middle[...] = value
    hat, inverse = normalize(value)
    hat_s[...] = hat
    low = (hat * vecs[1:2] + vecs[3:4]).astype(bf16)
    low_s[...] = low
    low_t[...] = low.T
    slots = lax.axis_size("batch") * lax.axis_size("seq") * tall
    scale = slots / total[0].astype(f32)
    row = lax.broadcasted_iota(jnp.int32, (rows, 1), 0) + lax.axis_index("seq") * rows
    live = jnp.concatenate([jnp.where(row < lens[g], scale, 0.0) for g in range(groups)], 0)
    grad = cot[...].astype(f32) * live
    result = (mixing[0] * grad).astype(bf16)
    result_s[...] = result
    sums[...] = jnp.zeros(sums.shape, f32)
    sums[8 + BLOCKS : 9 + BLOCKS] = jnp.sum(result.astype(f32), 0, keepdims=True)
    acc[...] = jnp.zeros(acc.shape, f32)
    back[...] = jnp.zeros(back.shape, f32)
    fetch_up.wait()
    fetch_down.wait()

    def block(i, _):
        up_i = weights[1 + i]
        down_i = weights[1 + BLOCKS + i]
        hidden = mm(low_s[...], up_i) + vecs[pl.ds(8 + i, 1)]
        square = hidden * hidden
        bend = jnp.tanh(0.7978845608028654 * (hidden + 0.044715 * square * hidden))
        half = 0.5 * (1.0 + bend)
        active = (hidden * half).astype(bf16)
        slope = half + 0.5 * hidden * (1.0 - bend * bend) * (0.7978845608028654 * (1.0 + 3.0 * 0.044715 * square))
        acc[...] += mm(active, down_i)
        down_terms[i] = mm(active.T, result_s[...]).astype(bf16)
        hidden_grad = (slope * mm_nt(result_s[...], down_i)).astype(bf16)
        sums[pl.ds(8 + i, 1)] = jnp.sum(hidden_grad.astype(f32), 0, keepdims=True)
        up_terms[i] = mm(low_t[...], hidden_grad).astype(bf16)
        back[...] += mm_nt(hidden_grad, up_i)
        return 0

    lax.fori_loop(0, BLOCKS, block, 0)
    layer_out = middle[...] + acc[...] + vecs[8 + BLOCKS : 9 + BLOCKS]
    mixed[...] = (mixture[...] + mixing[0] * layer_out).astype(bf16)
    grad = cot[...].astype(f32) * live
    sums[VECTORS : VECTORS + 1] = jnp.sum(grad * layer_out, 0, keepdims=True)
    hat = hat_s[...]
    inner_grad = back[...]
    sums[1:2] = jnp.sum(inner_grad * hat, 0, keepdims=True)
    sums[3:4] = jnp.sum(inner_grad, 0, keepdims=True)
    total_grad = mixing[0] * grad + normalize_back(inner_grad, hat, inverse, vecs[1:2])
    middle_grad[...] = total_grad
    branch = total_grad.astype(bf16)
    sums[7:8] = jnp.sum(branch.astype(f32), 0, keepdims=True)
    out_term[...] = mm(attended[...].T, branch).astype(bf16)
    acc[...] = mm_nt(branch, weights[0])

    def write(target, tile, value):
        sent[target, :, 128 * tile : 128 * tile + 128] = value.astype(bf16)

    put_heads(write, lambda g, t: acc[g * rows : g * rows + rows, 128 * t : 128 * t + 128], outer)


def middle_layer(home, tokens, cot, mixture, dots, near, up, down, vecs, lens, mixing, total, outer):
    tall = tokens.shape[0]
    wide = pltpu.VMEM((tall, D), f32)
    low = pltpu.VMEM((tall, D), bf16)
    return pl.pallas_call(
        functools.partial(middle_kernel, outer),
        out_shape=(
            jax.ShapeDtypeStruct((tall, D), bf16),
            jax.ShapeDtypeStruct(home.shape, bf16),
            jax.ShapeDtypeStruct((tall, D), f32),
            jax.ShapeDtypeStruct((D, D), bf16),
            jax.ShapeDtypeStruct((BLOCKS, D, D), bf16),
            jax.ShapeDtypeStruct((BLOCKS, D, D), bf16),
            jax.ShapeDtypeStruct((16, D), f32),
        ),
        in_specs=[IN_VMEM] * 5 + [ANYWHERE] * 3 + [IN_VMEM] + [IN_SMEM] * 3,
        out_specs=(IN_VMEM,) * 7,
        scratch_shapes=[
            low, wide, wide, low, pltpu.VMEM((D, tall), bf16), low, wide, wide,
            pltpu.VMEM((1 + 2 * BLOCKS, D, D), bf16), DMA((3,)),
        ],
        compiler_params=params(),
        name="middle_layer",
    )(home, tokens, cot, mixture, dots, near, up, down, vecs, lens, mixing, total)


def back_kernel(outer, dq, dk, dv, cosine, sine, normed, tokens, near, vecs, cot, lens, mixing, total, middle_grad, out_term, sums, dots, input_grad, terms, small, joined, low_t):
    tall = tokens.shape[0]
    groups = lens.shape[0]
    rows = tall // groups
    for g in range(groups):
        for n, source in enumerate((dq, dk, dv)):
            tiles = take_heads(lambda o, t: source[o, :, 128 * t : 128 * t + 128].astype(f32), g, outer)
            for i, tile in enumerate(tiles):
                if n == 1:
                    tile = turn(tile, cosine[...], -sine[...])
                joined[n, g * rows : g * rows + rows, 128 * i : 128 * i + 128] = tile.astype(bf16)
    low_t[...] = normed[...].T
    small[...] = sums[...]
    back = jnp.zeros((tall, D), f32)
    for n in range(3):
        low = joined[n]
        small[4 + n : 5 + n] = jnp.sum(low.astype(f32), 0, keepdims=True)
        terms[n] = mm(low_t[...], low).astype(bf16)
        back = back + mm_nt(low, near[n])
    terms[3] = out_term[...]
    hat, inverse = normalize(tokens[...].astype(f32))
    small[0:1] = jnp.sum(back * hat, 0, keepdims=True)
    small[2:3] = jnp.sum(back, 0, keepdims=True)
    slots = lax.axis_size("batch") * lax.axis_size("seq") * tall
    scale = slots / total[0].astype(f32)
    row = lax.broadcasted_iota(jnp.int32, (rows, 1), 0) + lax.axis_index("seq") * rows
    live = jnp.concatenate([jnp.where(row < lens[g], scale, 0.0) for g in range(groups)], 0)
    grad = cot[...].astype(f32) * live
    input_grad[...] = mixing[1] * grad + middle_grad[...] + normalize_back(back, hat, inverse, vecs[0:1])
    lane = lax.broadcasted_iota(jnp.int32, (1, D), 1)
    line = jnp.where(lane == 0, jnp.sum(sums[VECTORS : VECTORS + 1], 1, keepdims=True), 0.0)
    for i in range(1, mixing.shape[0]):
        line = line + jnp.where(lane == i, scale * jnp.sum(dots[i : i + 1], 1, keepdims=True), 0.0)
    small[VECTORS : VECTORS + 1] = line


def back_layer(dq, dk, dv, cosine, sine, normed, tokens, near, vecs, cot, lens, mixing, total, middle_grad, out_term, sums, dots, outer):
    tall = tokens.shape[0]
    return pl.pallas_call(
        functools.partial(back_kernel, outer),
        out_shape=(
            jax.ShapeDtypeStruct((tall, D), f32),
            jax.ShapeDtypeStruct((4, D, D), bf16),
            jax.ShapeDtypeStruct((16, D), f32),
        ),
        in_specs=[IN_VMEM] * 10 + [IN_SMEM] * 3 + [IN_VMEM] * 4,
        out_specs=(IN_VMEM,) * 3,
        scratch_shapes=[pltpu.VMEM((3, tall, D), bf16), pltpu.VMEM((D, tall), bf16)],
        compiler_params=params(),
        name="back_layer",
    )(dq, dk, dv, cosine, sine, normed, tokens, near, vecs, cot, lens, mixing, total, middle_grad, out_term, sums, dots)


def adam(param, grad, first, second, decay):
    first_new = beta_one * first + (1.0 - beta_one) * grad
    second_new = beta_two * second + (1.0 - beta_two) * grad * grad
    fix_one = 1.0 - beta_one**adam_step
    fix_two = 1.0 - beta_two**adam_step
    update = first_new / fix_one / (jnp.sqrt(second_new / fix_two) + adam_eps)
    return (-learn_rate * (update + decay * param), first_new)


def adam_kernel(near, up, down, *refs):
    given, results = refs[:12], refs[12:]
    starts = (0, 3, 0, None)
    for n in range(4):
        param, first, second = given[3 * n : 3 * n + 3]
        grad_out, step_out, first_out = results[3 * n : 3 * n + 3]
        count = param.shape[1] // D if n < 3 else 1
        for i in range(count):
            lanes = slice(i * D, i * D + D)
            grad = down[...] if n == 3 else (up if n == 2 else near)[starts[n] + i]
            grad_out[:, lanes] = grad
            step_out[:, lanes], first_out[:, lanes] = adam(param[:, lanes], grad, first[:, lanes], second[:, lanes], decay_rate)


def adam_all(near, up, down, given):
    shapes = []
    for n in range(4):
        shapes += [jax.ShapeDtypeStruct(given[3 * n].shape, f32)] * 3
    return pl.pallas_call(
        adam_kernel,
        out_shape=tuple(shapes),
        in_specs=[IN_VMEM] * 15,
        out_specs=(IN_VMEM,) * 12,
        compiler_params=params(),
        name="adam_all",
    )(near, up, down, *given)


def summed(into, index, more, other):
    into[index] = (into[index].astype(f32) + more[other].astype(f32)).astype(bf16)


def fold_kernel(batches, inner, with_rest, *refs):
    refs = list(refs)

    def take(n):
        got = refs[:n]
        del refs[:n]
        return got

    dq, dk, dv = take(3)
    terms = take(2) if with_rest else []
    dq_all, dk_all, dv_all = take(3)
    rest_out = take(2) if with_rest else []
    cbuf, xbuf, done, qs, qr, zs, zr, xs, xr, cs, cr, local = take(12)
    outer = dq.shape[0]
    across = inner // 2
    here = Place(batches, outer, inner)
    o, a, b, c = here.o, here.a, here.batch, here.c
    greet(here.z_peers[1:] + here.x_peers[1:] + [here.twin] + (here.y_peers[1:] if with_rest else []))
    waits = [carry(dq.at[o], dq_all.at[o], local.at[0])]
    given = (dk, dv)
    results = (dk_all, dv_all)
    order = [t % outer for t in range(1, outer + 1)]
    xorder = list(range(1, across)) + [0]
    yorder = list(range(1, batches)) + [0]
    to_twin, rest_over = {}, {}

    def give_block(t):
        for i in (0, 1):
            for d in xorder:
                z, x = here.zs[t], here.xs[d]
                to_twin[i, t, d] = push(given[i].at[z, x * 2 + 1 - c], cbuf.at[i, z, x], cs.at[i, t, d], cr.at[i, t, d], here.twin)

    if with_rest:
        bufs = (refs[0:3], refs[3:6])
        rest_sem, rcs, rcr, rys, ryr, rxs, rxr = refs[6:]

    def theirs(i, y, x, core):
        if i == 0:
            return terms[0].at[pl.ds(2 * core, 2), y, :, x]
        return terms[1].at[y, :, x, core]

    def give_rest(i, dy, dx):
        y, x = here.ys[dy], here.xs[dx]
        rest_over["c", i, dy, dx] = push(theirs(i, y, x, 1 - c), bufs[i][0].at[y, x], rcs.at[i, dy, dx], rcr.at[i, dy, dx], here.twin)

    give_block(order[0])
    if with_rest:
        for dy in yorder:
            for dx in xorder:
                for i in (0, 1):
                    give_rest(i, dy, dx)
    for t in order[1:]:
        give_block(t)
    for t in range(1, outer):
        waits.append(push(dq.at[here.zs[t]], dq_all.at[o], qs.at[t], qr.at[t], here.z_peers[t]))
    over = {}

    def fold_block(t):
        for i in (0, 1):
            for d in xorder:
                to_twin[i, t, d].wait()
                z, x = here.zs[t], here.xs[d]
                summed(cbuf, (i, z, x), given[i], (z, x * 2 + c))
                if d:
                    over[i, t, d] = push(cbuf.at[i, z, x], xbuf.at[i, z, d], xs.at[i, t, d], xr.at[i, t, d], here.x_peers[d])

    def finish_block(t):
        for i in (0, 1):
            z = here.zs[t]
            total = cbuf[i, z, a].astype(f32)
            for d in range(1, across):
                over[i, t, d].wait()
                total = total + xbuf[i, z, d].astype(f32)
            done[i, z] = total.astype(bf16)
            if t:
                waits.append(push(done.at[i, z], results[i].at[o], zs.at[i, t], zr.at[i, t], here.z_peers[t]))
            else:
                waits.append(carry(done.at[i, z], results[i].at[o], local.at[1 + i]))

    def each(i, add):
        if i == 0:

            def one(n, _):
                add((lax.div(n, outer), lax.rem(n, outer)))
                return 0

            lax.fori_loop(0, 2 * outer, one, 0)
        else:

            def one(z, _):
                add((z,))
                return 0

            lax.fori_loop(0, outer, one, 0)

    def rest_core(dy, dx):
        y, x = here.ys[dy], here.xs[dx]
        for i in (0, 1):
            rest_over["c", i, dy, dx].wait()
            into = bufs[i][0]
            if i == 0:
                each(0, lambda at: summed(into, (y, x) + at, terms[0], (2 * c + at[0], y, at[1], x)))
            else:
                each(1, lambda at: summed(into, (y, x) + at, terms[1], (y, at[0], x, c)))
            if dy:
                rest_over["y", i, dy, dx] = push(into.at[y, x], bufs[i][1].at[dy, dx], rys.at[i, dy, dx], ryr.at[i, dy, dx], here.y_peers[dy])

    def rest_y(dx):
        x = here.xs[dx]
        for i in (0, 1):
            into, more = bufs[i][0], bufs[i][1]
            for dy in range(1, batches):
                rest_over["y", i, dy, dx].wait()
                each(i, lambda at: summed(into, (b, x) + at, more, (dy, dx) + at))
            if dx:
                rest_over["x", i, dx] = push(into.at[b, x], bufs[i][2].at[dx], rxs.at[i, dx], rxr.at[i, dx], here.x_peers[dx])

    fold_block(order[0])
    if with_rest:
        for dy in yorder[:-1]:
            for dx in xorder:
                rest_core(dy, dx)
    fold_block(order[1])
    finish_block(order[0])
    if with_rest:
        for dx in xorder:
            rest_core(0, dx)
    for n in range(2, outer):
        fold_block(order[n])
        finish_block(order[n - 1])
        if with_rest and n == 2:
            for dx in xorder[:-1]:
                rest_y(dx)
    finish_block(order[-1])
    if with_rest:
        rest_y(0)
        for i in (0, 1):
            into, more = bufs[i][0], bufs[i][2]
            for d in range(1, across):
                rest_over["x", i, d].wait()
                each(i, lambda at: summed(into, (b, a) + at, more, (d,) + at))
            waits.append(carry(into.at[b, a], rest_out[i], rest_sem.at[i]))
    for copy in waits:
        copy.wait()


def fold_heads(dq, dk, dv, terms, batches, inner, ident):
    outer, rows, width = dq.shape
    across = inner // 2
    piece = jax.ShapeDtypeStruct(dq.shape, dq.dtype)
    with_rest = bool(terms)
    shapes = (piece, piece, piece)
    scratch = [pltpu.VMEM((2, outer, across, rows, width), bf16)] * 2 + [pltpu.VMEM((2, outer, rows, width), bf16)]
    scratch += [DMA((outer,))] * 2 + [DMA((2, outer))] * 2 + [DMA((2, outer, across))] * 4 + [DMA((3,))]
    if with_rest:
        for tail in ((2, outer) + terms[0].shape[4:], (outer,) + terms[1].shape[4:]):
            shapes += (jax.ShapeDtypeStruct(tail, bf16),)
            scratch += [pltpu.VMEM((batches, across) + tail, bf16)] * 2 + [pltpu.VMEM((across,) + tail, bf16)]
        scratch += [DMA((2,))]
        scratch += [DMA((2, batches, across))] * 4 + [DMA((2, across))] * 2
    return pl.pallas_call(
        functools.partial(fold_kernel, batches, inner, with_rest),
        out_shape=shapes,
        in_specs=[ANYWHERE] + [IN_VMEM] * (2 + len(terms)),
        out_specs=(ANYWHERE,) * len(shapes),
        scratch_shapes=scratch,
        compiler_params=remote_params(ident, ROOM),
        name="fold_heads",
    )(dq, dk, dv, *terms)


def last_kernel(batches, outer, inner, *refs):
    refs = list(refs)

    def take(n):
        got = refs[:n]
        del refs[:n]
        return got

    terms, up_line, down_line, small = take(4)
    near_out, up_out, down_out, small_out = take(4)
    rc, ry, rx, rz, uz, dz, kept, sc, sx, sy, sz = take(11)
    cs, cr, ys, yr, xs, xr, zs, zr, us, ur, ds, dr, fs, fr, ss, sr = refs
    across = inner // 2
    here = Place(batches, outer, inner)
    o, a, b, c = here.o, here.a, here.batch, here.c
    share = near_out.shape[1]
    greet(here.z_peers[1:] + here.x_peers[1:] + here.y_peers[1:] + [here.twin])
    xorder = list(range(1, across)) + [0]
    yorder = list(range(1, batches)) + [0]
    over = {}
    for p, dy, dx in [(p, dy, dx) for dy in yorder for dx in xorder for p in (0, 1)]:
        y, x = here.ys[dy], here.xs[dx]
        over["c", p, dy, dx] = push(terms.at[2 * (1 - c) + p, y, :, x], rc.at[p, y, x], cs.at[p, dy, dx], cr.at[p, dy, dx], here.twin)
    small_copy = push(small, sc, ss.at[0], sr.at[0], here.twin)
    line_copies = {}
    for t in range(1, outer):
        line_copies[0, t] = push(up_line.at[:, here.zs[t]], uz.at[t], us.at[t], ur.at[t], here.z_peers[t])
        line_copies[1, t] = push(down_line.at[here.zs[t]], dz.at[t], ds.at[t], dr.at[t], here.z_peers[t])

    def add_all(into_at, more, more_at):
        def one(z, _):
            summed(rc, into_at + (z,), more, more_at(z))
            return 0

        lax.fori_loop(0, outer, one, 0)

    def core(p, dy, dx):
        y, x = here.ys[dy], here.xs[dx]
        over["c", p, dy, dx].wait()
        add_all((p, y, x), terms, lambda z: (2 * c + p, y, z, x))
        if p == 0 and dy:
            over["y", 0, dy, dx] = push(rc.at[0, y, x], ry.at[0, dy, dx], ys.at[0, dy, dx], yr.at[0, dy, dx], here.y_peers[dy])
        if p == 1 and dx:
            over["x", 1, dy, dx] = push(rc.at[1, y, x], rx.at[1, dx, dy], xs.at[1, dy, dx], xr.at[1, dy, dx], here.x_peers[dx])

    for dy in yorder:
        for dx in xorder:
            for p in (0, 1):
                core(p, dy, dx)
    small_copy.wait()
    sc[...] = sc[...] + small[...]
    small_x = [push(sc, sx.at[a], ss.at[d], sr.at[d], here.x_peers[d]) for d in range(1, across)]
    sx[a] = sc[...]
    for dx in xorder:
        x = here.xs[dx]
        for dy in range(1, batches):
            over["y", 0, dy, dx].wait()
            add_all((0, b, x), ry, lambda z: (0, dy, dx, z))
        if dx:
            over["x", 0, 0, dx] = push(rc.at[0, b, x], rx.at[0, dx, 0], xs.at[0, 0, dx], xr.at[0, 0, dx], here.x_peers[dx])
    for dy in yorder:
        y = here.ys[dy]
        for dx in range(1, across):
            over["x", 1, dy, dx].wait()
            add_all((1, y, a), rx, lambda z: (1, dx, dy, z))
        if dy:
            over["y", 1, dy, 0] = push(rc.at[1, y, a], ry.at[1, dy, 0], ys.at[1, dy, 0], yr.at[1, dy, 0], here.y_peers[dy])
    for copy in small_x:
        copy.wait()
    total = sx[0]
    for x in range(1, across):
        total = total + sx[x]
    sc[...] = total
    sy[b] = total
    small_y = [push(sc, sy.at[b], ss.at[across + d], sr.at[across + d], here.y_peers[d]) for d in range(1, batches)]
    z_copies = {}
    for dx in range(1, across):
        over["x", 0, 0, dx].wait()
        add_all((0, b, a), rx, lambda z: (0, dx, 0, z))
    for t in range(1, outer):
        z_copies[0, t] = push(rc.at[0, b, a, here.zs[t]], rz.at[0, t], zs.at[0, t], zr.at[0, t], here.z_peers[t])
    for dy in range(1, batches):
        over["y", 1, dy, 0].wait()
        add_all((1, b, a), ry, lambda z: (1, dy, 0, z))
    for t in range(1, outer):
        z_copies[1, t] = push(rc.at[1, b, a, here.zs[t]], rz.at[1, t], zs.at[1, t], zr.at[1, t], here.z_peers[t])
    for copy in small_y:
        copy.wait()
    total = sy[0]
    for y in range(1, batches):
        total = total + sy[y]
    sc[...] = total
    sz[o] = total
    small_z = [
        push(sc, sz.at[o], ss.at[across + batches + t], sr.at[across + batches + t], here.z_peers[t]) for t in range(1, outer)
    ]
    sums = down_line[o].astype(f32)
    for t in range(1, outer):
        line_copies[1, t].wait()
        sums = sums + dz[t].astype(f32)
    down_out[...] = sums
    for t in range(1, outer):
        line_copies[0, t].wait()
    give = pl.multiple_of(share * (1 - c), 8)
    rest_sends, near_sends = [], []
    for p in (0, 1):
        sums = up_line[p, o].astype(f32)
        for t in range(1, outer):
            sums = sums + uz[t, p].astype(f32)
        kept[1, p] = sums
    rest_sends.append(push(kept.at[1, :, pl.ds(give, share)], up_out.at[pl.ds(2 * c, 2)], fs.at[1], fr.at[1], here.twin))
    for p in (0, 1):
        sums = rc[p, b, a, o].astype(f32)
        for t in range(1, outer):
            z_copies[p, t].wait()
            sums = sums + rz[p, t].astype(f32)
        kept[0, p] = sums
    near_sends.append(push(kept.at[0, :, pl.ds(give, share)], near_out.at[pl.ds(2 * c, 2)], fs.at[0], fr.at[0], here.twin))
    for p in (0, 1):
        for kind, dest in enumerate((near_out, up_out)):
            value = kept[kind, p]
            dest[2 * c + p] = jnp.where(c == 0, value[:share], value[share:])
    for copy in small_z:
        copy.wait()
    total = sz[0]
    for z in range(1, outer):
        total = total + sz[z]
    small_out[...] = total
    for copy in rest_sends + near_sends:
        copy.wait()


def reduce_last(terms, up_line, down_line, small, batches, outer, inner, ident):
    across = inner // 2
    tail = terms.shape[4:]
    share = tail[0] // 2
    buf = pltpu.VMEM
    scratch = [
        buf((2, batches, across, outer) + tail, bf16),
        buf((2, batches, across, outer) + tail, bf16),
        buf((2, across, batches, outer) + tail, bf16),
        buf((2, outer) + tail, bf16),
        buf((outer, 2) + tail, bf16),
        buf(down_line.shape, bf16),
        buf((2, 2) + tail, f32),
        buf(small.shape, f32),
        buf((across,) + small.shape, f32),
        buf((batches,) + small.shape, f32),
        buf((outer,) + small.shape, f32),
    ]
    scratch += [DMA((2, batches, across))] * 6 + [DMA((2, outer))] * 2 + [DMA((outer,))] * 4 + [DMA((2,))] * 2
    scratch += [DMA((across + batches + outer,))] * 2
    return pl.pallas_call(
        functools.partial(last_kernel, batches, outer, inner),
        out_shape=(
            jax.ShapeDtypeStruct((4, share, D), f32),
            jax.ShapeDtypeStruct((4, share, D), f32),
            jax.ShapeDtypeStruct(down_line.shape[1:], f32),
            jax.ShapeDtypeStruct(small.shape, f32),
        ),
        in_specs=[IN_VMEM] * 4,
        out_specs=(IN_VMEM,) * 4,
        scratch_shapes=scratch,
        compiler_params=remote_params(ident, ROOM),
        name="reduce_last",
    )(terms, up_line, down_line, small)


def body(
    tokens_in,
    earlier_outs,
    out_cotangent,
    seq_lengths,
    qkv_weight,
    out_weight,
    up_weight,
    down_weight,
    qkv_first,
    qkv_second,
    out_first,
    out_second,
    up_first,
    up_second,
    down_first,
    down_second,
    small_params,
    small_first,
    small_second,
):
    groups, rows, _ = tokens_in.shape
    tall = groups * rows
    batches = lax.axis_size("batch")
    seq_count = lax.axis_size("seq")
    seq_rank = lax.axis_index("seq")
    devices = batches * seq_count
    outer = math.gcd(seq_count, D // HEAD)
    inner = seq_count // outer
    per = D // HEAD // outer
    length = seq_count * rows
    width = groups * per * HEAD
    share = D // devices
    remote = share % 8 == 0
    everywhere = ("batch", "seq")
    grid = (batches, outer, inner // 2)

    tokens = tokens_in.reshape(tall, D)
    cot = out_cotangent.reshape(tall, D)
    earlier = earlier_outs.reshape(-1, tall, D)
    vecs = jnp.pad(small_params[: VECTORS * D].reshape(VECTORS, D), ((0, 16 - VECTORS), (0, 0)))
    mixing = small_params[VECTORS * D :]
    mine = jnp.sum(seq_lengths)

    freq = 10000.0 ** (-jnp.arange(HEAD // 2, dtype=f32) * 2.0 / HEAD)
    query_pos = seq_rank * rows + jnp.arange(rows, dtype=jnp.int32)
    turned = query_pos.astype(f32)[:, None] * freq[None, :]
    cosine, sine = jnp.cos(turned), jnp.sin(turned)
    cosine = jnp.concatenate([cosine] * 4, 1)
    sine = jnp.concatenate([-sine, sine] * 2, 1)
    block_pos = (jnp.arange(outer) * inner + seq_rank % inner)[:, None] * rows + jnp.arange(rows)[None, :]
    block_turned = block_pos.astype(f32)[:, None, :] * freq[None, :, None]
    block_cos, block_sin = jnp.cos(block_turned), jnp.sin(block_turned)

    def by_rows(shard):
        return shard.astype(bf16).reshape(share, -1, D).transpose(1, 0, 2)

    def by_blocks(gathered):
        return gathered.transpose(1, 0, 2, 3).reshape(-1, D, D)

    if remote:
        near, up_line, down_line, counts, normed, mixture, dots = gather_first(
            qkv_weight, out_weight, up_weight, down_weight, seq_lengths, mixing, tokens, cot, earlier, vecs,
            jnp.full((8, 128), mine, jnp.int32), batches, outer, inner, 1,
        )
        near = near.reshape(4, D, D)
        total = jnp.sum(counts[:, 0, 0]).reshape(1)
        q, k, v, up, down = spread_heads(normed, near, vecs, cosine, sine, (up_line, down_line), batches, outer, inner, 2)
        up, down = up.reshape(BLOCKS, D, D), down.reshape(BLOCKS, D, D)
    else:
        near = by_blocks(lax.all_gather(jnp.concatenate([by_rows(qkv_weight), by_rows(out_weight)], 0), everywhere, axis=0))
        up = by_blocks(lax.all_gather(by_rows(up_weight), everywhere, axis=0))
        down = lax.all_gather(down_weight.astype(bf16), everywhere, axis=0).reshape(BLOCKS, D, D)
        total = lax.psum(mine, "batch").reshape(1)
        wide = tokens.astype(f32)
        normed = (normalize(wide)[0] * vecs[0] + vecs[2]).astype(bf16)
        live = (query_pos[None, :] < seq_lengths[:, None]).astype(f32).reshape(tall, 1)
        terms = [tokens] + [earlier[i] for i in range(earlier.shape[0])]
        mixture = sum(mixing[1 + i] * term.astype(f32) for i, term in enumerate(terms))
        sums = [jnp.sum(cot.astype(f32) * live * term.astype(f32), 0) for term in terms]
        dots = jnp.pad(jnp.stack(sums), ((1, 15 - len(sums)), (0, 0)))
        q, k, v = spread_heads(normed, near, vecs, cosine, sine, (), batches, outer, inner, 2)

    k, v = k.reshape(length, width), v.reshape(length, width)
    attended, turned_out, log_total = attend(seq_lengths, q, k, v, groups, per, inner, math.gcd(length, 1024))
    home = swap_outer(attended, batches, inner, 3)
    mixed, sent, middle_grad, out_term, up_terms, down_terms, sums = middle_layer(
        home, tokens, cot, mixture, dots, near, up, down, vecs, seq_lengths, mixing, total, outer
    )
    grad_mine = swap_outer(sent, batches, inner, 4)
    dq, dk, dv = attend_back(
        seq_lengths, q, k, v, grad_mine, turned_out, log_total, block_cos, block_sin, groups, per, inner, math.gcd(length, 512)
    )
    pieces = (outer, inner, rows, width)
    dk, dv = dk.reshape(pieces), dv.reshape(pieces)
    if remote:
        blocked = (up_terms.reshape((4,) + grid + (2 * share, D)), down_terms.reshape(grid + (2, BLOCKS * share, D)))
        dq, dk, dv, up_back, down_back = fold_heads(dq, dk, dv, blocked, batches, inner, 5)
    else:
        dq, dk, dv = fold_heads(dq, dk, dv, (), batches, inner, 5)
    input_grad, near_terms, small = back_layer(
        dq, dk, dv, cosine, sine, normed, tokens, near, vecs, cot, seq_lengths, mixing, total, middle_grad, out_term, sums, dots, outer
    )
    if remote:
        near_grad, up_grad, down_grad, small = reduce_last(
            near_terms.reshape((4,) + grid + (2 * share, D)), up_back, down_back, small, batches, outer, inner, 6
        )
    else:

        def scattered(terms):
            return lax.psum_scatter(terms.reshape(-1, devices, share, D), everywhere, scatter_dimension=1).astype(f32)

        near_grad, up_grad = scattered(near_terms), scattered(up_terms)
        down_grad = lax.psum_scatter(down_terms.reshape(devices, -1, D), everywhere, scatter_dimension=0).astype(f32)
        small = lax.psum(small, everywhere)
    small_grad = small.reshape(-1)[: small_params.shape[0]]
    small_step, small_first_new = adam(small_params, small_grad, small_first, small_second, 0.0)
    (
        qkv_grad, qkv_step, qkv_first_new, out_grad, out_step, out_first_new,
        up_grad, up_step, up_first_new, down_grad, down_step, down_first_new,
    ) = adam_all(
        near_grad, up_grad, down_grad,
        (qkv_weight, qkv_first, qkv_second, out_weight, out_first, out_second,
         up_weight, up_first, up_second, down_weight, down_first, down_second),
    )
    return (
        mixed.reshape(tokens_in.shape),
        input_grad.reshape(tokens_in.shape),
        qkv_grad,
        out_grad,
        up_grad,
        down_grad,
        small_grad,
        qkv_step,
        out_step,
        up_step,
        down_step,
        small_step,
        qkv_first_new,
        out_first_new,
        up_first_new,
        down_first_new,
        small_first_new,
    )


def solution(mesh):
    placed = (
        P("batch", "seq", None),
        P(None, "batch", "seq", None),
        P("batch", "seq", None),
        P("batch"),
        P(("batch", "seq"), None),
        P(("batch", "seq"), None),
        P(("batch", "seq"), None),
        P(("batch", "seq"), None),
        P(("batch", "seq"), None),
        P(("batch", "seq"), None),
        P(("batch", "seq"), None),
        P(("batch", "seq"), None),
        P(("batch", "seq"), None),
        P(("batch", "seq"), None),
        P(("batch", "seq"), None),
        P(("batch", "seq"), None),
        P(),
        P(),
        P(),
    )
    return jax.shard_map(
        body,
        mesh=mesh,
        in_specs=placed,
        out_specs=(
            P("batch", "seq", None),
            P("batch", "seq", None),
            P(("batch", "seq"), None),
            P(("batch", "seq"), None),
            P(("batch", "seq"), None),
            P(("batch", "seq"), None),
            P(),
            P(("batch", "seq"), None),
            P(("batch", "seq"), None),
            P(("batch", "seq"), None),
            P(("batch", "seq"), None),
            P(),
            P(("batch", "seq"), None),
            P(("batch", "seq"), None),
            P(("batch", "seq"), None),
            P(("batch", "seq"), None),
            P(),
        ),
        check_vma=False,
    )
```

```python
import functools
import math

import jax
import jax.numpy as jnp
from jax import lax
from jax.experimental import pallas as pl
from jax.experimental.pallas import tpu as pltpu
from jax.sharding import PartitionSpec as P

D = 768
FF = 3072
HEAD = 64
BLOCKS = FF // D
VECTORS = 9 + BLOCKS
bf16 = jnp.bfloat16
f32 = jnp.float32
NEG = -1e30

beta_one = 0.9
beta_two = 0.999
adam_eps = 1e-08
learn_rate = 0.01
decay_rate = 0.1
adam_step = 10

MESH = pl.DeviceIdType.MESH
ANYWHERE = pl.BlockSpec(memory_space=pl.ANY)
IN_VMEM = pl.BlockSpec(memory_space=pltpu.VMEM)
IN_SMEM = pl.BlockSpec(memory_space=pltpu.SMEM)
DMA = pltpu.SemaphoreType.DMA
ROOM = 56 << 20

UNITS = ((0, 1, 4), (2, 3, 5))


def mm(a, b):
    return lax.dot_general(a, b, (((1,), (0,)), ((), ())), preferred_element_type=f32)


def mm_nt(a, b):
    return lax.dot_general(a, b, (((1,), (1,)), ((), ())), preferred_element_type=f32)


def params():
    return pltpu.CompilerParams(vmem_limit_bytes=ROOM)


def remote_params(ident, vmem=None):
    return pltpu.CompilerParams(collective_id=ident, has_side_effects=True, vmem_limit_bytes=vmem)


class Place:
    def __init__(self, batches, outer, inner):
        self.batch = lax.axis_index("batch")
        rank = lax.axis_index("seq")
        self.o = lax.div(rank, inner)
        self.j = lax.rem(rank, inner)
        self.a = lax.div(self.j, 2)
        self.c = lax.rem(rank, 2)
        across = inner // 2
        self.zs = [lax.rem(self.o + t, outer) for t in range(outer)]
        self.xs = [lax.rem(self.a + t, across) for t in range(across)]
        self.ys = [lax.rem(self.batch + t, batches) for t in range(batches)]
        self.z_from = [lax.rem(self.o + outer - t, outer) for t in range(outer)]
        self.x_from = [lax.rem(self.a + across - t, across) for t in range(across)]
        self.y_from = [lax.rem(self.batch + batches - t, batches) for t in range(batches)]
        self.z_peers = [(self.batch, z * inner + self.j) for z in self.zs]
        self.x_peers = [(self.batch, self.o * inner + x * 2 + self.c) for x in self.xs]
        self.y_peers = [(y, rank) for y in self.ys]
        self.twin = (self.batch, self.o * inner + self.a * 2 + (1 - self.c))


def greet(peers):
    barrier = pltpu.get_barrier_semaphore()
    for peer in peers:
        pl.semaphore_signal(barrier, inc=1, device_id=peer, device_id_type=MESH)
    pl.semaphore_wait(barrier, len(peers))


def push(src, dst, send, recv, peer):
    copy = pltpu.make_async_remote_copy(
        src_ref=src, dst_ref=dst, send_sem=send, recv_sem=recv, device_id=peer, device_id_type=MESH
    )
    copy.start()
    return copy


def carry(src, dst, sem):
    copy = pltpu.make_async_copy(src, dst, sem)
    copy.start()
    return copy


def normalize(values):
    center = values - jnp.mean(values, -1, keepdims=True)
    inverse = lax.rsqrt(jnp.mean(center * center, -1, keepdims=True) + 1e-05)
    return center * inverse, inverse


def normalize_back(grad, hat, inverse, gain):
    scaled = grad * gain
    part = scaled - jnp.mean(scaled, -1, keepdims=True) - hat * jnp.mean(scaled * hat, -1, keepdims=True)
    return part * inverse


def turn(value, cosine, sine):
    lane = lax.broadcasted_iota(jnp.int32, value.shape, 1)
    other = jnp.where(lax.rem(lane, HEAD) < HEAD // 2, pltpu.roll(value, 128 - HEAD // 2, 1), pltpu.roll(value, HEAD // 2, 1))
    return value * cosine + other * sine


def put_heads(write, tiles_of, outer):
    for o in range(outer):
        first = 3 * o * HEAD
        odd = first % 128 != 0
        pair = (first + HEAD if odd else first) // 128
        single = (first if odd else first + 128) // 128
        write(o, 0, tiles_of(0, pair))
        write(o, 1, tiles_of(1, pair))
        one, two = tiles_of(0, single), tiles_of(1, single)
        if odd:
            one = pltpu.roll(one, HEAD, 1)
        else:
            two = pltpu.roll(two, HEAD, 1)
        lane = lax.broadcasted_iota(jnp.int32, one.shape, 1)
        write(o, 2, jnp.where(lane < HEAD, one, two))


def take_heads(read, g, outer):
    tiles = [None] * (outer * 3 // 2)
    for o in range(0, outer, 2):
        base = 3 * o * HEAD // 128
        tiles[base] = read(o, g)
        tiles[base + 2] = read(o + 1, g)
        low, high = read(o, 2), read(o + 1, 2)
        if g == 0:
            high = pltpu.roll(high, HEAD, 1)
        else:
            low = pltpu.roll(low, HEAD, 1)
        lane = lax.broadcasted_iota(jnp.int32, low.shape, 1)
        tiles[base + 1] = jnp.where(lane < HEAD, low, high)
    return tiles


def fold_single(value, odd):
    half = value.shape[0] // 2
    top, bottom = value[:half], value[half:]
    lane = lax.broadcasted_iota(jnp.int32, top.shape, 1)
    if odd:
        return jnp.where(lane < HEAD, pltpu.roll(top, HEAD, 1), bottom)
    return jnp.where(lane < HEAD, top, pltpu.roll(bottom, HEAD, 1))


def unfold_single(value, high):
    turned = pltpu.roll(value, HEAD, 1)
    return jnp.concatenate([turned, value] if high else [value, turned], 0)


def unfold_heads(read, rows, outer):
    tiles = [None] * (outer * 3 // 2)
    for o in range(0, outer, 2):
        base = 3 * o * HEAD // 128
        first, second = read(o), read(o + 1)
        tiles[base] = first[:rows]
        tiles[base + 2] = second[:rows]
        low, high = unfold_single(first[rows:], False), unfold_single(second[rows:], True)
        lane = lax.broadcasted_iota(jnp.int32, low.shape, 1)
        tiles[base + 1] = jnp.where(lane < HEAD, low, high)
    return tiles


def fold_heads_of(write, tile_of, outer):
    for o in range(outer):
        first = 3 * o * HEAD
        odd = first % 128 != 0
        pair = (first + HEAD if odd else first) // 128
        single = (first if odd else first + 128) // 128
        write(o, jnp.concatenate([tile_of(pair), fold_single(tile_of(single), odd)], 0))


def first_kernel(batches, outer, inner, first_row, *refs):
    refs = list(refs)

    def take(n):
        got = refs[:n]
        del refs[:n]
        return got

    qkv, out, up, down, lens, mixing, tokens, cot, earlier, vecs = take(10)
    near_all, up_line, down_line, counts, normed, mixture, dots = take(7)
    own, got, near, up_bit, down_bit, queue, count = take(7)
    zs, zr, xs, xr, ys, yr, cs, cr, us, ur, ds, dr, ns, nr, ts, tr, local, es = refs
    across = inner // 2
    here = Place(batches, outer, inner)
    o, a, b, c = here.o, here.a, here.batch, here.c
    earlier_count, tall, _ = earlier.shape
    groups = lens.shape[0]
    rows = tall // groups
    fetches = {}
    for e in range(2):
        fetches[e] = carry(earlier.at[e], queue.at[e], es.at[e])
    for block in range(4):
        own[block] = qkv[:, block * D : block * D + D] if block < 3 else out[...]
        own[4 + block] = up[:, block * D : block * D + D]
    here_count = lens[0]
    for g in range(1, groups):
        here_count = here_count + lens[g]
    count[...] = jnp.zeros(count.shape, jnp.int32) + here_count
    greet(here.z_peers[1:] + here.x_peers[1:] + here.y_peers[1:] + [here.twin])
    theirs = 2 * (1 - c)
    swaps = [
        push(own.at[pl.ds(theirs, 2)], got.at[0], ts.at[0], tr.at[0], here.twin),
        push(own.at[pl.ds(4 + theirs, 2)], got.at[1], ts.at[1], tr.at[1], here.twin),
    ]
    waits = [carry(count, counts.at[b], local.at[0])]
    for d in range(1, batches):
        waits.append(push(count, counts.at[b], ns.at[d], nr.at[d], here.y_peers[d]))
    down_bit[...] = down[...].astype(bf16)

    def joined(kind, p):
        mine, other = own[4 * kind + 2 * c + p], got[kind, p]
        low = jnp.where(c == 0, mine, other)
        high = jnp.where(c == 0, other, mine)
        return jnp.concatenate([low, high], 0).astype(bf16)

    def slot(p, y, z, x):
        return near_all.at[2 * c + p, y, z, x]

    arrivals = {}

    def onward(source, p, y, z, x, t, dx, dy):
        to = slot(p, y, z, x)
        if dx == 0 and (dy == 0 or p == 1):
            for d in range(1, across):
                key = (p, t, d, dy)
                arrivals["x", key] = push(source, to, xs.at[key], xr.at[key], here.x_peers[d])
        if dy == 0 and (dx == 0 or p == 0):
            for d in range(1, batches):
                key = (p, t, dx, d)
                arrivals["y", key] = push(source, to, ys.at[key], yr.at[key], here.y_peers[d])
        key = (p, t, dx, dy)
        waits.append(push(source, to, cs.at[key], cr.at[key], here.twin))

    swaps[0].wait()
    copies = {}
    for p in (0, 1):
        near[p] = joined(0, p)
        for t in range(1, outer):
            copies[t, p] = push(near.at[p], slot(p, b, o, a), zs.at[t, p], zr.at[t, p], here.z_peers[t])
        onward(near.at[p], p, b, o, a, 0, 0, 0)
        waits.append(carry(near.at[p], slot(p, b, o, a), local.at[1 + p]))
    swaps[1].wait()
    for p in (0, 1):
        up_bit[p] = joined(1, p)
    for t in range(1, outer):
        waits.append(push(up_bit, up_line.at[:, o], us.at[t], ur.at[t], here.z_peers[t]))
        waits.append(push(down_bit, down_line.at[o], ds.at[t], dr.at[t], here.z_peers[t]))
    waits.append(carry(up_bit, up_line.at[:, o], local.at[3]))
    waits.append(carry(down_bit, down_line.at[o], local.at[4]))

    def live_rows(value):
        row = lax.broadcasted_iota(jnp.int32, (rows, 1), 0) + first_row(rows)
        parts = [jnp.where(row < lens[g], value[g * rows : g * rows + rows], 0.0) for g in range(groups)]
        return jnp.concatenate(parts, 0)

    def normal():
        wide = tokens[...].astype(f32)
        hat, _ = normalize(wide)
        normed[...] = (hat * vecs[0:1] + vecs[2:3]).astype(bf16)
        grad = live_rows(cot[...].astype(f32))
        dots[...] = jnp.zeros(dots.shape, f32)
        dots[1:2] = jnp.sum(grad * wide, 0, keepdims=True)
        mixture[...] = mixing[1] * wide

    def mix(e):
        fetches[e].wait()
        wide = queue[e % 2].astype(f32)
        grad = live_rows(cot[...].astype(f32))
        dots[2 + e : 3 + e] = jnp.sum(grad * wide, 0, keepdims=True)
        mixture[...] = mixture[...] + mixing[2 + e] * wide
        if e + 2 < earlier_count:
            fetches[e + 2] = carry(earlier.at[e + 2], queue.at[e % 2], es.at[e + 2])

    steps = [normal] + [functools.partial(mix, e) for e in range(earlier_count)]

    def work(n=1):
        for _ in range(n):
            if steps:
                steps.pop(0)()

    for t in range(1, outer):
        for p in (0, 1):
            copies[t, p].wait()
            onward(slot(p, b, here.z_from[t], a), p, b, here.z_from[t], a, t, 0, 0)
    work(1)
    for t in range(outer):
        z = here.z_from[t]
        for d in range(1, across):
            arrivals["x", (0, t, d, 0)].wait()
            onward(slot(0, b, z, here.x_from[d]), 0, b, z, here.x_from[d], t, d, 0)
        for d in range(1, batches):
            arrivals["y", (1, t, 0, d)].wait()
            onward(slot(1, here.y_from[d], z, a), 1, here.y_from[d], z, a, t, 0, d)
        work(1)
    for t in range(outer):
        z = here.z_from[t]
        for dx in range(across):
            for dy in range(1, batches):
                arrivals["y", (0, t, dx, dy)].wait()
                onward(slot(0, here.y_from[dy], z, here.x_from[dx]), 0, here.y_from[dy], z, here.x_from[dx], t, dx, dy)
        for dy in range(batches):
            for dx in range(1, across):
                arrivals["x", (1, t, dx, dy)].wait()
                onward(slot(1, here.y_from[dy], z, here.x_from[dx]), 1, here.y_from[dy], z, here.x_from[dx], t, dx, dy)
        work(1)
    work(len(steps))
    for copy in waits:
        copy.wait()


def gather_first(qkv, out, up, down, lens, mixing, tokens, cot, earlier, vecs, batches, outer, inner, ident):
    across = inner // 2
    share = qkv.shape[0]
    tall = tokens.shape[0]

    def first_row(rows):
        return lax.axis_index("seq") * rows

    grid = (batches, outer, across)
    return pl.pallas_call(
        functools.partial(first_kernel, batches, outer, inner, first_row),
        out_shape=(
            jax.ShapeDtypeStruct((4,) + grid + (2 * share, D), bf16),
            jax.ShapeDtypeStruct((2, outer, 2 * share, D), bf16),
            jax.ShapeDtypeStruct((outer, BLOCKS * share, D), bf16),
            jax.ShapeDtypeStruct((batches, 8, 128), jnp.int32),
            jax.ShapeDtypeStruct((tall, D), bf16),
            jax.ShapeDtypeStruct((tall, D), f32),
            jax.ShapeDtypeStruct((16, D), f32),
        ),
        in_specs=[IN_VMEM] * 4 + [IN_SMEM] * 2 + [IN_VMEM] * 2 + [ANYWHERE, IN_VMEM],
        out_specs=(ANYWHERE,) * 4 + (IN_VMEM,) * 3,
        scratch_shapes=[
            pltpu.VMEM((8, share, D), f32),
            pltpu.VMEM((2, 2, share, D), f32),
            pltpu.VMEM((2, 2 * share, D), bf16),
            pltpu.VMEM((2, 2 * share, D), bf16),
            pltpu.VMEM((BLOCKS * share, D), bf16),
            pltpu.VMEM((2, tall, D), bf16),
            pltpu.VMEM((8, 128), jnp.int32),
        ]
        + [DMA((outer, 2))] * 2
        + [DMA((2, outer, across, batches))] * 6
        + [DMA((outer,))] * 4
        + [DMA((batches,))] * 2
        + [DMA((2,))] * 2
        + [DMA((5,)), DMA((earlier.shape[0],))],
        compiler_params=remote_params(ident, ROOM),
        name="gather_first",
    )(qkv, out, up, down, lens, mixing, tokens, cot, earlier, vecs)


def spread_kernel(batches, outer, inner, with_rest, *refs):
    refs = list(refs)

    def take(n):
        got = refs[:n]
        del refs[:n]
        return got

    normed, near, vecs, cosine, sine = take(5)
    lines = take(2) if with_rest else []
    q_all, k_all, v_all = take(3)
    alls = take(2) if with_rest else []
    q, k, v, work = take(4)
    qs, qr, zs, zr, xs, xr, cs, cr, local = take(9)
    across = inner // 2
    here = Place(batches, outer, inner)
    o, a, b, c, j = here.o, here.a, here.batch, here.c, here.j
    rows = cosine.shape[0]
    greet(here.z_peers[1:] + here.x_peers[1:] + [here.twin] + (here.y_peers[1:] if with_rest else []))
    waits, rest_x, rest_y = [], [], []

    def rest_slot(i, y, x):
        if i == 0:
            return alls[0].at[pl.ds(2 * c, 2), y, :, x]
        return alls[1].at[y, :, x, c]

    if with_rest:
        ax, axr, ay, ayr, ac, acr, alocal = refs
        for i in (0, 1):
            waits.append(carry(lines[i], rest_slot(i, b, a), alocal.at[i]))
            for d in range(1, across):
                rest_x.append((i, d, push(lines[i], rest_slot(i, b, a), ax.at[i, d], axr.at[i, d], here.x_peers[d])))
            for d in range(1, batches):
                rest_y.append((i, 0, d, push(lines[i], rest_slot(i, b, a), ay.at[i, 0, d], ayr.at[i, 0, d], here.y_peers[d])))
            waits.append(push(lines[i], rest_slot(i, b, a), ac.at[i, 0, 0], acr.at[i, 0, 0], here.twin))

    def rest_across():
        i, d, copy = rest_x.pop(0)
        copy.wait()
        piece = rest_slot(i, b, here.x_from[d])
        for e in range(1, batches):
            rest_y.append((i, d, e, push(piece, piece, ay.at[i, d, e], ayr.at[i, d, e], here.y_peers[e])))
        waits.append(push(piece, piece, ac.at[i, d, 0], acr.at[i, d, 0], here.twin))

    def rest_twin():
        i, d, e, copy = rest_y.pop(0)
        copy.wait()
        piece = rest_slot(i, here.y_from[e], here.x_from[d])
        waits.append(push(piece, piece, ac.at[i, d, e], acr.at[i, d, e], here.twin))

    def project(block, into, rotated):
        work[...] = mm(normed[...], near[block]) + vecs[4 + block : 5 + block]

        def tiles_of(g, tile):
            value = work[g * rows : g * rows + rows, 128 * tile : 128 * tile + 128]
            return turn(value, cosine[...], sine[...]) if rotated else value

        def write(target, tile, value):
            into[target, :, 128 * tile : 128 * tile + 128] = value.astype(bf16)

        put_heads(write, tiles_of, outer)

    arriving, own = [], []
    for i, (block, into, dest) in enumerate(((1, k, k_all), (2, v, v_all))):
        project(block, into, i == 0)
        for t in range(1, outer):
            copy = push(into.at[here.zs[t]], dest.at[o, j], zs.at[i, t], zr.at[i, t], here.z_peers[t])
            arriving.append((i, t, copy))
        waits.append(carry(into.at[o], dest.at[o, j], local.at[i]))
        own.append((i, 0, None))
    project(0, q, True)
    for t in range(1, outer):
        waits.append(push(q.at[here.zs[t]], q_all.at[o], qs.at[t], qr.at[t], here.z_peers[t]))
    waits.append(carry(q.at[o], q_all.at[o], local.at[2]))
    late = []
    order = own + arriving
    for n, (i, t, copy) in enumerate(order):
        dest = (k_all, v_all)[i]
        place = dest.at[here.z_from[t], j]
        source = (k, v)[i].at[o] if copy is None else place
        if copy is not None:
            copy.wait()
        for d in range(1, across):
            late.append((i, t, d, push(source, place, xs.at[i, t, d], xr.at[i, t, d], here.x_peers[d])))
        waits.append(push(source, place, cs.at[i, t, 0], cr.at[i, t, 0], here.twin))
        while len(late) > (across - 1 if n < len(order) - 1 else 0):
            li, lt, ld, waited = late.pop(0)
            waited.wait()
            moved = (k_all, v_all)[li].at[here.z_from[lt], here.x_from[ld] * 2 + c]
            waits.append(push(moved, moved, cs.at[li, lt, ld], cr.at[li, lt, ld], here.twin))
        if rest_x and n >= 2:
            rest_across()
    while rest_x:
        rest_across()
    while rest_y:
        rest_twin()
    for copy in waits:
        copy.wait()


def spread_heads(normed, near, vecs, cosine, sine, lines, batches, outer, inner, ident):
    rows = cosine.shape[0]
    across = inner // 2
    width = 2 * D // outer
    with_rest = bool(lines)
    piece = jax.ShapeDtypeStruct((outer, rows, width), bf16)
    full = jax.ShapeDtypeStruct((outer, inner, rows, width), bf16)
    shapes = (piece, full, full)
    scratch = [pltpu.VMEM((outer, rows, width), bf16)] * 3 + [pltpu.VMEM(normed.shape, f32)]
    scratch += [DMA((outer,))] * 2 + [DMA((2, outer))] * 2 + [DMA((2, outer, across))] * 4 + [DMA((3,))]
    if with_rest:
        shapes += (
            jax.ShapeDtypeStruct((4, batches, outer, across) + lines[0].shape[2:], bf16),
            jax.ShapeDtypeStruct((batches, outer, across, 2) + lines[1].shape[1:], bf16),
        )
        scratch += [DMA((2, across))] * 2 + [DMA((2, across, batches))] * 4 + [DMA((2,))]
    return pl.pallas_call(
        functools.partial(spread_kernel, batches, outer, inner, with_rest),
        out_shape=shapes,
        in_specs=[IN_VMEM] * 5 + [ANYWHERE] * len(lines),
        out_specs=(ANYWHERE,) * len(shapes),
        scratch_shapes=scratch,
        compiler_params=remote_params(ident, ROOM),
        name="spread_heads",
    )(normed, near, vecs, cosine, sine, *lines)


def half_rows(block_t, half):
    z = jnp.zeros((HEAD, block_t.shape[1]), block_t.dtype)
    if half == 0:
        return jnp.concatenate([block_t[:HEAD], z], 0)
    return jnp.concatenate([z, block_t[HEAD:]], 0)


def attend_kernel(groups, per, span, inner, lens, q, k, v, o, ot, lse, vt, qt, m_s, l_s):
    outer, rows, width = q.shape
    units = groups * per
    total = k.shape[0]
    j = lax.rem(lax.axis_index("seq"), inner)
    blk = math.gcd(total, 512)

    def turn_v(i, _):
        at = pl.ds(pl.multiple_of(i * blk, blk), blk)
        for t in range(width // 128):
            lanes = slice(128 * t, 128 * t + 128)
            vt[lanes, at] = v[at, lanes].T
        return 0

    lax.fori_loop(0, total // blk, turn_v, 0)

    def one(z, _):
        first = (z * inner + j) * rows
        for t in range(width // 128):
            lanes = slice(128 * t, 128 * t + 128)
            turned = (q[z, :, lanes] * 0.125).astype(bf16).T
            for half in range(2):
                qt[2 * t + half] = half_rows(turned, half)
        for g in range(groups):
            length = lens[g]
            for u in UNITS[g]:
                ot[z, HEAD * u : HEAD * u + HEAD, :] = jnp.zeros((HEAD, rows), f32)
            m_s[...] = jnp.full(m_s.shape, NEG, f32)
            l_s[...] = jnp.zeros(l_s.shape, f32)

            def step(c, masked):
                at = pl.ds(pl.multiple_of(c * span, span), span)
                if masked:
                    key = c * span + lax.broadcasted_iota(jnp.int32, (span, rows), 0)
                    query = first + lax.broadcasted_iota(jnp.int32, (span, rows), 1)
                    allowed = (key <= query) & (key < length)
                scores, tops, news, shares, sums = [], [], [], [], []
                for h in range(per):
                    u = UNITS[g][h]
                    s = mm(k[at, 128 * (u // 2) : 128 * (u // 2) + 128], qt[u])
                    scores.append(jnp.where(allowed, s, NEG) if masked else s)
                for h in range(per):
                    tops.append(m_s[h : h + 1])
                    news.append(jnp.maximum(tops[h], jnp.max(scores[h], 0, keepdims=True)))
                for h in range(per):
                    p = jnp.exp(scores[h] - news[h])
                    sums.append(jnp.sum(p, 0, keepdims=True))
                    shares.append(p.astype(bf16))
                for h in range(per):
                    u = UNITS[g][h]
                    alpha = jnp.exp(tops[h] - news[h])
                    l_s[h : h + 1] = l_s[h : h + 1] * alpha + sums[h]
                    m_s[h : h + 1] = news[h]
                    span_u = slice(HEAD * u, HEAD * u + HEAD)
                    ot[z, span_u, :] = ot[z, span_u, :] * alpha + mm(vt[span_u, at], shares[h])

            whole = jnp.minimum(first, length) // span
            count = (jnp.minimum(first + rows, length) + span - 1) // span

            def full_step(c, _):
                step(c, False)
                return 0

            def edge_step(c, _):
                step(c, True)
                return 0

            lax.fori_loop(0, whole, full_step, 0)
            lax.fori_loop(whole, count, edge_step, 0)
            for h in range(per):
                u = UNITS[g][h]
                span_u = slice(HEAD * u, HEAD * u + HEAD)
                total_exp = l_s[h : h + 1]
                ot[z, span_u, :] = ot[z, span_u, :] / total_exp
                lse[z, u : u + 1, :] = m_s[h : h + 1] + jnp.log(total_exp)
        for g in range(groups):
            pair, single = HEAD * UNITS[g][0], HEAD * UNITS[g][2]
            o[z, g, :rows, :] = ot[z, pair : pair + 128, :].T.astype(bf16)
            halves = [ot[z, single : single + HEAD, : rows // 2], ot[z, single : single + HEAD, rows // 2 :]]
            o[z, g, rows:, :] = jnp.concatenate(halves, 0).T.astype(bf16)
        return 0

    lax.fori_loop(0, outer, one, 0)


def attend(lens, q, k, v, groups, per, inner, span):
    outer, rows, width = q.shape
    units = groups * per
    total = k.shape[0]
    vm = IN_VMEM
    return pl.pallas_call(
        functools.partial(attend_kernel, groups, per, span, inner),
        out_shape=(
            jax.ShapeDtypeStruct((outer, groups, rows + rows // 2, 128), bf16),
            jax.ShapeDtypeStruct((outer, width, rows), f32),
            jax.ShapeDtypeStruct((outer, 8, rows), f32),
        ),
        in_specs=[IN_SMEM, vm, vm, vm],
        out_specs=(vm, vm, vm),
        scratch_shapes=[
            pltpu.VMEM((width, total), bf16),
            pltpu.VMEM((units, 128, rows), bf16),
            pltpu.VMEM((8, rows), f32),
            pltpu.VMEM((8, rows), f32),
        ],
        compiler_params=params(),
        name="attend",
    )(lens, q, k, v)


def attend_back_kernel(groups, per, span, inner, lens, q, k, v, do, ot, lse, cos, sin, dq, dk, dv, kt, qt, dot_t, qz, dz, rd, dqt, dks, dvs):
    outer, rows, width = q.shape
    units = groups * per
    total = k.shape[0]
    j = lax.rem(lax.axis_index("seq"), inner)
    blk = math.gcd(total, 512)

    def prepare(i, _):
        at = pl.ds(pl.multiple_of(i * blk, blk), blk)
        for t in range(width // 128):
            lanes = slice(128 * t, 128 * t + 128)
            kt[lanes, at] = k[at, lanes].T
        dks[at, :] = jnp.zeros((blk, width), f32)
        dvs[at, :] = jnp.zeros((blk, width), f32)
        return 0

    lax.fori_loop(0, total // blk, prepare, 0)

    def one(z, _):
        first = (z * inner + j) * rows
        low = lax.broadcasted_iota(jnp.int32, (rows, 128), 1) < HEAD
        for t in range(width // 128):
            lanes = slice(128 * t, 128 * t + 128)
            small = (q[z, :, lanes] * 0.125).astype(bf16)
            turned = small.T
            for half in range(2):
                u = 2 * t + half
                qt[u] = half_rows(turned, half)
                keep = low if half == 0 else ~low
                qz[u] = jnp.where(keep, small, jnp.zeros_like(small))
        for g in range(groups):
            pair = do[z, g, :rows, :]
            single = do[z, g, rows:, :]
            pair_t, single_t = pair.T, single.T
            single_t = jnp.concatenate([single_t[:HEAD], single_t[HEAD:]], 1)
            blank = jnp.zeros_like(single_t)
            wide = unfold_single(single.astype(f32), g == 1)
            for half in range(2):
                u = UNITS[g][half]
                dot_t[u] = half_rows(pair_t, half)
                dz[u] = jnp.where(low if half == 0 else ~low, pair, jnp.zeros_like(pair))
            u = UNITS[g][2]
            dot_t[u] = jnp.concatenate([single_t, blank] if g == 0 else [blank, single_t], 0)
            dz[u] = jnp.where(low if g == 0 else ~low, wide, 0.0).astype(bf16)
            for h in range(per):
                u = UNITS[g][h]
                span_u = slice(HEAD * u, HEAD * u + HEAD)
                grad_t = single_t if h == 2 else pair_t[HEAD * h : HEAD * h + HEAD]
                rd[u : u + 1, :] = jnp.sum(grad_t.astype(f32) * ot[z, span_u, :], 0, keepdims=True)
        dqt[...] = jnp.zeros(dqt.shape, f32)
        for g in range(groups):
            length = lens[g]

            def step(c, masked):
                at = pl.ds(pl.multiple_of(c * span, span), span)
                if masked:
                    key = c * span + lax.broadcasted_iota(jnp.int32, (span, rows), 0)
                    query = first + lax.broadcasted_iota(jnp.int32, (span, rows), 1)
                    allowed = (key <= query) & (key < length)
                for h in range(per):
                    u = UNITS[g][h]
                    lanes = slice(128 * (u // 2), 128 * (u // 2) + 128)
                    span_u = slice(HEAD * u, HEAD * u + HEAD)
                    s = mm(k[at, lanes], qt[u])
                    p = jnp.exp(s - lse[z, u : u + 1, :])
                    if masked:
                        p = jnp.where(allowed, p, 0.0)
                    dp = mm(v[at, lanes], dot_t[u])
                    ds = (p * (dp - rd[u : u + 1, :])).astype(bf16)
                    dvs[at, lanes] += mm(p.astype(bf16), dz[u])
                    dks[at, lanes] += mm(ds, qz[u])
                    dqt[span_u, :] += mm(kt[span_u, at], ds)

            live = first < length
            whole = jnp.where(live, jnp.minimum(first, length) // span, 0)
            count = jnp.where(live, (jnp.minimum(first + rows, length) + span - 1) // span, 0)

            def full_step(c, _):
                step(c, False)
                return 0

            def edge_step(c, _):
                step(c, True)
                return 0

            lax.fori_loop(0, whole, full_step, 0)
            lax.fori_loop(whole, count, edge_step, 0)
        cosine = cos[z]
        sine = sin[z]
        for t in range(width // 128):
            parts = []
            for half in range(2):
                u = 2 * t + half
                a = dqt[HEAD * u : HEAD * u + 32, :] * 0.125
                b = dqt[HEAD * u + 32 : HEAD * u + 64, :] * 0.125
                parts.append(a * cosine + b * sine)
                parts.append(b * cosine - a * sine)
            dq[z, :, 128 * t : 128 * t + 128] = jnp.concatenate(parts, 0).T.astype(bf16)
        return 0

    lax.fori_loop(0, outer, one, 0)

    def finish(i, _):
        at = pl.ds(pl.multiple_of(i * blk, blk), blk)
        dk[at, :] = dks[at, :].astype(bf16)
        dv[at, :] = dvs[at, :].astype(bf16)
        return 0

    lax.fori_loop(0, total // blk, finish, 0)


def attend_back(lens, q, k, v, do, ot, lse, cos, sin, groups, per, inner, span):
    outer, rows, width = q.shape
    units = groups * per
    total = k.shape[0]
    vm = IN_VMEM
    return pl.pallas_call(
        functools.partial(attend_back_kernel, groups, per, span, inner),
        out_shape=(
            jax.ShapeDtypeStruct((outer, rows, width), bf16),
            jax.ShapeDtypeStruct((total, width), bf16),
            jax.ShapeDtypeStruct((total, width), bf16),
        ),
        in_specs=[IN_SMEM] + [vm] * 8,
        out_specs=(vm, vm, vm),
        scratch_shapes=[
            pltpu.VMEM((width, total), bf16),
            pltpu.VMEM((units, 128, rows), bf16),
            pltpu.VMEM((units, 128, rows), bf16),
            pltpu.VMEM((units, rows, 128), bf16),
            pltpu.VMEM((units, rows, 128), bf16),
            pltpu.VMEM((8, rows), f32),
            pltpu.VMEM((width, rows), f32),
            pltpu.VMEM((total, width), f32),
            pltpu.VMEM((total, width), f32),
        ],
        compiler_params=params(),
        name="attend_back",
    )(lens, q, k, v, do, ot, lse, cos, sin)


def middle_kernel(batches, outer, inner, *refs):
    refs = list(refs)

    def take(n):
        got = refs[:n]
        del refs[:n]
        return got

    o_mine, near, up, down, tokens, cot, mixture, counts, vecs, lens, mixing = take(11)
    mixed, grad_mine, middle_grad, out_term, up_terms, down_terms, sums = take(7)
    home, sent, attended, middle, low_s, result_s, slope_s, active_s, hidden_s, acc, back, weights = take(12)
    fetch, hs, hr, gs, gr, local = refs
    tall = tokens.shape[0]
    groups = lens.shape[0]
    rows = tall // groups
    here = Place(batches, outer, inner)
    o = here.o
    fetches = [
        carry(down, weights.at[pl.ds(1 + BLOCKS, BLOCKS)], fetch.at[0]),
        carry(near.at[3], weights.at[0], fetch.at[1]),
        carry(up, weights.at[pl.ds(1, BLOCKS)], fetch.at[2]),
    ]
    greet(here.z_peers[1:])
    coming, waits = {}, []
    for g in range(groups):
        coming[g] = [carry(o_mine.at[o, g], home.at[o, g], local.at[0, g])]
        for t in range(1, outer):
            coming[g].append(push(o_mine.at[here.zs[t], g], home.at[o, g], hs.at[g, t], hr.at[g, t], here.z_peers[t]))
    count = counts[0, 0:1, 0:1]
    for y in range(1, batches):
        count = count + counts[y, 0:1, 0:1]
    slots = lax.axis_size("batch") * lax.axis_size("seq") * tall
    scale = slots / count.astype(f32)
    row = lax.broadcasted_iota(jnp.int32, (rows, 1), 0) + lax.axis_index("seq") * rows

    def grad_of(g):
        return cot[g * rows : g * rows + rows, :].astype(f32) * jnp.where(row < lens[g], scale, 0.0)

    sums[...] = jnp.zeros(sums.shape, f32)
    for g in range(groups):
        here_rows = slice(g * rows, g * rows + rows)
        result = (mixing[0] * grad_of(g)).astype(bf16)
        result_s[here_rows] = result
        sums[8 + BLOCKS : 9 + BLOCKS] = sums[8 + BLOCKS : 9 + BLOCKS] + jnp.sum(result.astype(f32), 0, keepdims=True)
    fetches[0].wait()

    def early(i, _):
        slope_s[i] = mm_nt(result_s[...], weights[1 + BLOCKS + i])
        return 0

    lax.fori_loop(0, BLOCKS, early, 0)
    for g in range(groups):
        here_rows = slice(g * rows, g * rows + rows)
        for copy in coming[g]:
            copy.wait()
        tiles = unfold_heads(lambda p: home[p, g].astype(f32), rows, outer)
        for i, tile in enumerate(tiles):
            attended[here_rows, 128 * i : 128 * i + 128] = tile.astype(bf16)
        if g == 0:
            fetches[1].wait()
        value = tokens[here_rows].astype(f32) + (mm(attended[here_rows], weights[0]) + vecs[7:8])
        middle[here_rows] = value
        hat, inverse = normalize(value)
        low_s[here_rows] = (hat * vecs[1:2] + vecs[3:4]).astype(bf16)
        acc[here_rows] = jnp.zeros((rows, D), f32)
        back[...] = jnp.zeros((rows, D), f32)
        if g == 0:
            fetches[2].wait()

        def block(i, _):
            hidden = mm(low_s[here_rows], weights[1 + i]) + vecs[pl.ds(8 + i, 1)]
            square = hidden * hidden
            bend = jnp.tanh(0.7978845608028654 * (hidden + 0.044715 * square * hidden))
            half = 0.5 * (1.0 + bend)
            active = (hidden * half).astype(bf16)
            active_s[i, here_rows] = active
            slope = half + 0.5 * hidden * (1.0 - bend * bend) * (0.7978845608028654 * (1.0 + 3.0 * 0.044715 * square))
            hidden_grad = (slope * slope_s[i, here_rows]).astype(bf16)
            hidden_s[i, here_rows] = hidden_grad
            sums[pl.ds(8 + i, 1)] = sums[pl.ds(8 + i, 1)] + jnp.sum(hidden_grad.astype(f32), 0, keepdims=True)
            back[...] += mm_nt(hidden_grad, weights[1 + i])
            acc[here_rows] += mm(active, weights[1 + BLOCKS + i])
            return 0

        lax.fori_loop(0, BLOCKS, block, 0)
        inner_grad = back[...]
        sums[1:2] = sums[1:2] + jnp.sum(inner_grad * hat, 0, keepdims=True)
        sums[3:4] = sums[3:4] + jnp.sum(inner_grad, 0, keepdims=True)
        total_grad = mixing[0] * grad_of(g) + normalize_back(inner_grad, hat, inverse, vecs[1:2])
        middle_grad[here_rows] = total_grad
        branch = total_grad.astype(bf16)
        sums[7:8] = sums[7:8] + jnp.sum(branch.astype(f32), 0, keepdims=True)
        back[...] = mm_nt(branch, weights[0])

        def write(target, value):
            sent[target, g] = value.astype(bf16)

        fold_heads_of(write, lambda t: back[:, 128 * t : 128 * t + 128], outer)
        for t in range(1, outer):
            waits.append(push(sent.at[here.zs[t], g], grad_mine.at[o, g], gs.at[g, t], gr.at[g, t], here.z_peers[t]))
        waits.append(carry(sent.at[o, g], grad_mine.at[o, g], local.at[1, g]))

    low_t = low_s[...].T

    def late(i, _):
        down_terms[i] = mm(active_s[i].T, result_s[...]).astype(bf16)
        up_terms[i] = mm(low_t, hidden_s[i]).astype(bf16)
        return 0

    lax.fori_loop(0, BLOCKS, late, 0)
    out_term[...] = mm(attended[...].T, middle_grad[...].astype(bf16)).astype(bf16)
    for g in range(groups):
        here_rows = slice(g * rows, g * rows + rows)
        layer_out = middle[here_rows] + acc[here_rows] + vecs[8 + BLOCKS : 9 + BLOCKS]
        mixed[here_rows] = (mixture[here_rows] + mixing[0] * layer_out).astype(bf16)
        sums[VECTORS : VECTORS + 1] = sums[VECTORS : VECTORS + 1] + jnp.sum(grad_of(g) * layer_out, 0, keepdims=True)
    for copy in waits:
        copy.wait()


def middle_layer(o_mine, near, up, down, tokens, cot, mixture, counts, vecs, lens, mixing, batches, outer, inner, ident):
    tall = tokens.shape[0]
    groups = lens.shape[0]
    wide = pltpu.VMEM((tall, D), f32)
    low = pltpu.VMEM((tall, D), bf16)
    hidden = pltpu.VMEM((BLOCKS, tall, D), bf16)
    return pl.pallas_call(
        functools.partial(middle_kernel, batches, outer, inner),
        out_shape=(
            jax.ShapeDtypeStruct((tall, D), bf16),
            jax.ShapeDtypeStruct(o_mine.shape, bf16),
            jax.ShapeDtypeStruct((tall, D), f32),
            jax.ShapeDtypeStruct((D, D), bf16),
            jax.ShapeDtypeStruct((BLOCKS, D, D), bf16),
            jax.ShapeDtypeStruct((BLOCKS, D, D), bf16),
            jax.ShapeDtypeStruct((16, D), f32),
        ),
        in_specs=[ANYWHERE] * 4 + [IN_VMEM] * 5 + [IN_SMEM] * 2,
        out_specs=(IN_VMEM, ANYWHERE) + (IN_VMEM,) * 5,
        scratch_shapes=[
            pltpu.VMEM(o_mine.shape, bf16), pltpu.VMEM(o_mine.shape, bf16),
            low, wide, low, low, pltpu.VMEM((BLOCKS, tall, D), f32), hidden, hidden,
            wide, pltpu.VMEM((tall // groups, D), f32),
            pltpu.VMEM((1 + 2 * BLOCKS, D, D), bf16), DMA((3,)),
        ]
        + [DMA((groups, outer))] * 4
        + [DMA((2, groups))],
        compiler_params=remote_params(ident, ROOM),
        name="middle_layer",
    )(o_mine, near, up, down, tokens, cot, mixture, counts, vecs, lens, mixing)


def back_kernel(outer, dq, dk, dv, cosine, sine, normed, tokens, near, vecs, cot, counts, lens, mixing, middle_grad, out_term, sums, dots, input_grad, terms, small, joined, low_t):
    tall = tokens.shape[0]
    groups = lens.shape[0]
    rows = tall // groups
    for g in range(groups):
        for n, source in enumerate((dq, dk, dv)):
            tiles = take_heads(lambda o, t: source[o, :, 128 * t : 128 * t + 128].astype(f32), g, outer)
            for i, tile in enumerate(tiles):
                if n == 1:
                    tile = turn(tile, cosine[...], -sine[...])
                joined[n, g * rows : g * rows + rows, 128 * i : 128 * i + 128] = tile.astype(bf16)
    low_t[...] = normed[...].T
    small[...] = sums[...]
    back = jnp.zeros((tall, D), f32)
    for n in range(3):
        low = joined[n]
        small[4 + n : 5 + n] = jnp.sum(low.astype(f32), 0, keepdims=True)
        terms[n] = mm(low_t[...], low).astype(bf16)
        back = back + mm_nt(low, near[n])
    terms[3] = out_term[...]
    hat, inverse = normalize(tokens[...].astype(f32))
    small[0:1] = jnp.sum(back * hat, 0, keepdims=True)
    small[2:3] = jnp.sum(back, 0, keepdims=True)
    slots = lax.axis_size("batch") * lax.axis_size("seq") * tall
    count = counts[0, 0:1, 0:1]
    for y in range(1, counts.shape[0]):
        count = count + counts[y, 0:1, 0:1]
    scale = slots / count.astype(f32)
    row = lax.broadcasted_iota(jnp.int32, (rows, 1), 0) + lax.axis_index("seq") * rows
    live = jnp.concatenate([jnp.where(row < lens[g], scale, 0.0) for g in range(groups)], 0)
    grad = cot[...].astype(f32) * live
    input_grad[...] = mixing[1] * grad + middle_grad[...] + normalize_back(back, hat, inverse, vecs[0:1])
    lane = lax.broadcasted_iota(jnp.int32, (1, D), 1)
    line = jnp.where(lane == 0, jnp.sum(sums[VECTORS : VECTORS + 1], 1, keepdims=True), 0.0)
    for i in range(1, mixing.shape[0]):
        line = line + jnp.where(lane == i, scale * jnp.sum(dots[i : i + 1], 1, keepdims=True), 0.0)
    small[VECTORS : VECTORS + 1] = line


def back_layer(dq, dk, dv, cosine, sine, normed, tokens, near, vecs, cot, counts, lens, mixing, middle_grad, out_term, sums, dots, outer):
    tall = tokens.shape[0]
    return pl.pallas_call(
        functools.partial(back_kernel, outer),
        out_shape=(
            jax.ShapeDtypeStruct((tall, D), f32),
            jax.ShapeDtypeStruct((4, D, D), bf16),
            jax.ShapeDtypeStruct((16, D), f32),
        ),
        in_specs=[IN_VMEM] * 11 + [IN_SMEM] * 2 + [IN_VMEM] * 4,
        out_specs=(IN_VMEM,) * 3,
        scratch_shapes=[pltpu.VMEM((3, tall, D), bf16), pltpu.VMEM((D, tall), bf16)],
        compiler_params=params(),
        name="back_layer",
    )(dq, dk, dv, cosine, sine, normed, tokens, near, vecs, cot, counts, lens, mixing, middle_grad, out_term, sums, dots)


def adam(param, grad, first, second, decay):
    first_new = beta_one * first + (1.0 - beta_one) * grad
    second_new = beta_two * second + (1.0 - beta_two) * grad * grad
    fix_one = 1.0 - beta_one**adam_step
    fix_two = 1.0 - beta_two**adam_step
    update = first_new / fix_one / (jnp.sqrt(second_new / fix_two) + adam_eps)
    return (-learn_rate * (update + decay * param), first_new)


def adam_kernel(near, up, down, *refs):
    given, results = refs[:12], refs[12:]
    starts = (0, 3, 0, None)
    for n in range(4):
        param, first, second = given[3 * n : 3 * n + 3]
        grad_out, step_out, first_out = results[3 * n : 3 * n + 3]
        count = param.shape[1] // D if n < 3 else 1
        for i in range(count):
            lanes = slice(i * D, i * D + D)
            grad = down[...] if n == 3 else (up if n == 2 else near)[starts[n] + i]
            grad_out[:, lanes] = grad
            step_out[:, lanes], first_out[:, lanes] = adam(param[:, lanes], grad, first[:, lanes], second[:, lanes], decay_rate)


def adam_all(near, up, down, given):
    shapes = []
    for n in range(4):
        shapes += [jax.ShapeDtypeStruct(given[3 * n].shape, f32)] * 3
    return pl.pallas_call(
        adam_kernel,
        out_shape=tuple(shapes),
        in_specs=[IN_VMEM] * 15,
        out_specs=(IN_VMEM,) * 12,
        compiler_params=params(),
        name="adam_all",
    )(near, up, down, *given)


def summed(into, index, more, other):
    into[index] = (into[index].astype(f32) + more[other].astype(f32)).astype(bf16)


def fold_kernel(batches, inner, with_rest, *refs):
    refs = list(refs)

    def take(n):
        got = refs[:n]
        del refs[:n]
        return got

    dq, dk, dv = take(3)
    terms = take(2) if with_rest else []
    dq_all, dk_all, dv_all = take(3)
    rest_out = take(2) if with_rest else []
    cbuf, xbuf, done, qs, qr, zs, zr, xs, xr, cs, cr, local = take(12)
    outer = dq.shape[0]
    across = inner // 2
    here = Place(batches, outer, inner)
    o, a, b, c = here.o, here.a, here.batch, here.c
    greet(here.z_peers[1:] + here.x_peers[1:] + [here.twin] + (here.y_peers[1:] if with_rest else []))
    waits = [carry(dq.at[o], dq_all.at[o], local.at[0])]
    given = (dk, dv)
    results = (dk_all, dv_all)
    order = [t % outer for t in range(1, outer + 1)]
    xorder = list(range(1, across)) + [0]
    yorder = list(range(1, batches)) + [0]
    to_twin, rest_over = {}, {}

    def give_block(t):
        for i in (0, 1):
            for d in xorder:
                z, x = here.zs[t], here.xs[d]
                to_twin[i, t, d] = push(given[i].at[z, x * 2 + 1 - c], cbuf.at[i, z, x], cs.at[i, t, d], cr.at[i, t, d], here.twin)

    if with_rest:
        bufs = (refs[0:3], refs[3:6])
        rest_sem, rcs, rcr, rys, ryr, rxs, rxr = refs[6:]

    def theirs(i, y, x, core):
        if i == 0:
            return terms[0].at[pl.ds(2 * core, 2), y, :, x]
        return terms[1].at[y, :, x, core]

    def give_rest(i, dy, dx):
        y, x = here.ys[dy], here.xs[dx]
        rest_over["c", i, dy, dx] = push(theirs(i, y, x, 1 - c), bufs[i][0].at[y, x], rcs.at[i, dy, dx], rcr.at[i, dy, dx], here.twin)

    give_block(order[0])
    if with_rest:
        for dy in yorder:
            for dx in xorder:
                for i in (0, 1):
                    give_rest(i, dy, dx)
    for t in order[1:]:
        give_block(t)
    for t in range(1, outer):
        waits.append(push(dq.at[here.zs[t]], dq_all.at[o], qs.at[t], qr.at[t], here.z_peers[t]))
    over = {}

    def fold_block(t):
        for i in (0, 1):
            for d in xorder:
                to_twin[i, t, d].wait()
                z, x = here.zs[t], here.xs[d]
                summed(cbuf, (i, z, x), given[i], (z, x * 2 + c))
                if d:
                    over[i, t, d] = push(cbuf.at[i, z, x], xbuf.at[i, z, d], xs.at[i, t, d], xr.at[i, t, d], here.x_peers[d])

    def finish_block(t):
        for i in (0, 1):
            z = here.zs[t]
            total = cbuf[i, z, a].astype(f32)
            for d in range(1, across):
                over[i, t, d].wait()
                total = total + xbuf[i, z, d].astype(f32)
            done[i, z] = total.astype(bf16)
            if t:
                waits.append(push(done.at[i, z], results[i].at[o], zs.at[i, t], zr.at[i, t], here.z_peers[t]))
            else:
                waits.append(carry(done.at[i, z], results[i].at[o], local.at[1 + i]))

    def each(i, add):
        if i == 0:

            def one(n, _):
                add((lax.div(n, outer), lax.rem(n, outer)))
                return 0

            lax.fori_loop(0, 2 * outer, one, 0)
        else:

            def one(z, _):
                add((z,))
                return 0

            lax.fori_loop(0, outer, one, 0)

    def rest_core(dy, dx):
        y, x = here.ys[dy], here.xs[dx]
        for i in (0, 1):
            rest_over["c", i, dy, dx].wait()
            into = bufs[i][0]
            if i == 0:
                each(0, lambda at: summed(into, (y, x) + at, terms[0], (2 * c + at[0], y, at[1], x)))
            else:
                each(1, lambda at: summed(into, (y, x) + at, terms[1], (y, at[0], x, c)))
            if dy:
                rest_over["y", i, dy, dx] = push(into.at[y, x], bufs[i][1].at[dy, dx], rys.at[i, dy, dx], ryr.at[i, dy, dx], here.y_peers[dy])

    def rest_y(dx):
        x = here.xs[dx]
        for i in (0, 1):
            into, more = bufs[i][0], bufs[i][1]
            for dy in range(1, batches):
                rest_over["y", i, dy, dx].wait()
                each(i, lambda at: summed(into, (b, x) + at, more, (dy, dx) + at))
            if dx:
                rest_over["x", i, dx] = push(into.at[b, x], bufs[i][2].at[dx], rxs.at[i, dx], rxr.at[i, dx], here.x_peers[dx])

    fold_block(order[0])
    if with_rest:
        for dy in yorder[:-1]:
            for dx in xorder:
                rest_core(dy, dx)
    fold_block(order[1])
    finish_block(order[0])
    if with_rest:
        for dx in xorder:
            rest_core(0, dx)
    for n in range(2, outer):
        fold_block(order[n])
        finish_block(order[n - 1])
        if with_rest and n == 2:
            for dx in xorder[:-1]:
                rest_y(dx)
    finish_block(order[-1])
    if with_rest:
        rest_y(0)
        for i in (0, 1):
            into, more = bufs[i][0], bufs[i][2]
            for d in range(1, across):
                rest_over["x", i, d].wait()
                each(i, lambda at: summed(into, (b, a) + at, more, (d,) + at))
            waits.append(carry(into.at[b, a], rest_out[i], rest_sem.at[i]))
    for copy in waits:
        copy.wait()


def fold_heads(dq, dk, dv, terms, batches, inner, ident):
    outer, rows, width = dq.shape
    across = inner // 2
    piece = jax.ShapeDtypeStruct(dq.shape, dq.dtype)
    with_rest = bool(terms)
    shapes = (piece, piece, piece)
    scratch = [pltpu.VMEM((2, outer, across, rows, width), bf16)] * 2 + [pltpu.VMEM((2, outer, rows, width), bf16)]
    scratch += [DMA((outer,))] * 2 + [DMA((2, outer))] * 2 + [DMA((2, outer, across))] * 4 + [DMA((3,))]
    if with_rest:
        for tail in ((2, outer) + terms[0].shape[4:], (outer,) + terms[1].shape[4:]):
            shapes += (jax.ShapeDtypeStruct(tail, bf16),)
            scratch += [pltpu.VMEM((batches, across) + tail, bf16)] * 2 + [pltpu.VMEM((across,) + tail, bf16)]
        scratch += [DMA((2,))]
        scratch += [DMA((2, batches, across))] * 4 + [DMA((2, across))] * 2
    return pl.pallas_call(
        functools.partial(fold_kernel, batches, inner, with_rest),
        out_shape=shapes,
        in_specs=[ANYWHERE] + [IN_VMEM] * (2 + len(terms)),
        out_specs=(ANYWHERE,) * len(shapes),
        scratch_shapes=scratch,
        compiler_params=remote_params(ident, ROOM),
        name="fold_heads",
    )(dq, dk, dv, *terms)


def last_kernel(batches, outer, inner, *refs):
    refs = list(refs)

    def take(n):
        got = refs[:n]
        del refs[:n]
        return got

    terms, up_line, down_line, small = take(4)
    near_out, up_out, down_out, small_out = take(4)
    rc, ry, rx, rz, uz, dz, kept, sc, sx, sy, sz = take(11)
    cs, cr, ys, yr, xs, xr, zs, zr, us, ur, ds, dr, fs, fr, ss, sr = refs
    across = inner // 2
    here = Place(batches, outer, inner)
    o, a, b, c = here.o, here.a, here.batch, here.c
    share = near_out.shape[1]
    greet(here.z_peers[1:] + here.x_peers[1:] + here.y_peers[1:] + [here.twin])
    xorder = list(range(1, across)) + [0]
    yorder = list(range(1, batches)) + [0]
    over = {}
    for p, dy, dx in [(p, dy, dx) for dy in yorder for dx in xorder for p in (0, 1)]:
        y, x = here.ys[dy], here.xs[dx]
        over["c", p, dy, dx] = push(terms.at[2 * (1 - c) + p, y, :, x], rc.at[p, y, x], cs.at[p, dy, dx], cr.at[p, dy, dx], here.twin)
    small_copy = push(small, sc, ss.at[0], sr.at[0], here.twin)
    line_copies = {}
    for t in range(1, outer):
        line_copies[0, t] = push(up_line.at[:, here.zs[t]], uz.at[t], us.at[t], ur.at[t], here.z_peers[t])
        line_copies[1, t] = push(down_line.at[here.zs[t]], dz.at[t], ds.at[t], dr.at[t], here.z_peers[t])

    def add_all(into_at, more, more_at):
        def one(z, _):
            summed(rc, into_at + (z,), more, more_at(z))
            return 0

        lax.fori_loop(0, outer, one, 0)

    def core(p, dy, dx):
        y, x = here.ys[dy], here.xs[dx]
        over["c", p, dy, dx].wait()
        add_all((p, y, x), terms, lambda z: (2 * c + p, y, z, x))
        if p == 0 and dy:
            over["y", 0, dy, dx] = push(rc.at[0, y, x], ry.at[0, dy, dx], ys.at[0, dy, dx], yr.at[0, dy, dx], here.y_peers[dy])
        if p == 1 and dx:
            over["x", 1, dy, dx] = push(rc.at[1, y, x], rx.at[1, dx, dy], xs.at[1, dy, dx], xr.at[1, dy, dx], here.x_peers[dx])

    for dy in yorder:
        for dx in xorder:
            for p in (0, 1):
                core(p, dy, dx)
    small_copy.wait()
    sc[...] = sc[...] + small[...]
    small_x = [push(sc, sx.at[a], ss.at[d], sr.at[d], here.x_peers[d]) for d in range(1, across)]
    sx[a] = sc[...]
    for dx in xorder:
        x = here.xs[dx]
        for dy in range(1, batches):
            over["y", 0, dy, dx].wait()
            add_all((0, b, x), ry, lambda z: (0, dy, dx, z))
        if dx:
            over["x", 0, 0, dx] = push(rc.at[0, b, x], rx.at[0, dx, 0], xs.at[0, 0, dx], xr.at[0, 0, dx], here.x_peers[dx])
    for dy in yorder:
        y = here.ys[dy]
        for dx in range(1, across):
            over["x", 1, dy, dx].wait()
            add_all((1, y, a), rx, lambda z: (1, dx, dy, z))
        if dy:
            over["y", 1, dy, 0] = push(rc.at[1, y, a], ry.at[1, dy, 0], ys.at[1, dy, 0], yr.at[1, dy, 0], here.y_peers[dy])
    for copy in small_x:
        copy.wait()
    total = sx[0]
    for x in range(1, across):
        total = total + sx[x]
    sc[...] = total
    sy[b] = total
    small_y = [push(sc, sy.at[b], ss.at[across + d], sr.at[across + d], here.y_peers[d]) for d in range(1, batches)]
    z_copies = {}
    for dx in range(1, across):
        over["x", 0, 0, dx].wait()
        add_all((0, b, a), rx, lambda z: (0, dx, 0, z))
    for t in range(1, outer):
        z_copies[0, t] = push(rc.at[0, b, a, here.zs[t]], rz.at[0, t], zs.at[0, t], zr.at[0, t], here.z_peers[t])
    for dy in range(1, batches):
        over["y", 1, dy, 0].wait()
        add_all((1, b, a), ry, lambda z: (1, dy, 0, z))
    for t in range(1, outer):
        z_copies[1, t] = push(rc.at[1, b, a, here.zs[t]], rz.at[1, t], zs.at[1, t], zr.at[1, t], here.z_peers[t])
    for copy in small_y:
        copy.wait()
    total = sy[0]
    for y in range(1, batches):
        total = total + sy[y]
    sc[...] = total
    sz[o] = total
    small_z = [
        push(sc, sz.at[o], ss.at[across + batches + t], sr.at[across + batches + t], here.z_peers[t]) for t in range(1, outer)
    ]
    sums = down_line[o].astype(f32)
    for t in range(1, outer):
        line_copies[1, t].wait()
        sums = sums + dz[t].astype(f32)
    down_out[...] = sums
    for t in range(1, outer):
        line_copies[0, t].wait()
    give = pl.multiple_of(share * (1 - c), 8)
    rest_sends, near_sends = [], []
    for p in (0, 1):
        sums = up_line[p, o].astype(f32)
        for t in range(1, outer):
            sums = sums + uz[t, p].astype(f32)
        kept[1, p] = sums
    rest_sends.append(push(kept.at[1, :, pl.ds(give, share)], up_out.at[pl.ds(2 * c, 2)], fs.at[1], fr.at[1], here.twin))
    for p in (0, 1):
        sums = rc[p, b, a, o].astype(f32)
        for t in range(1, outer):
            z_copies[p, t].wait()
            sums = sums + rz[p, t].astype(f32)
        kept[0, p] = sums
    near_sends.append(push(kept.at[0, :, pl.ds(give, share)], near_out.at[pl.ds(2 * c, 2)], fs.at[0], fr.at[0], here.twin))
    for p in (0, 1):
        for kind, dest in enumerate((near_out, up_out)):
            value = kept[kind, p]
            dest[2 * c + p] = jnp.where(c == 0, value[:share], value[share:])
    for copy in small_z:
        copy.wait()
    total = sz[0]
    for z in range(1, outer):
        total = total + sz[z]
    small_out[...] = total
    for copy in rest_sends + near_sends:
        copy.wait()


def reduce_last(terms, up_line, down_line, small, batches, outer, inner, ident):
    across = inner // 2
    tail = terms.shape[4:]
    share = tail[0] // 2
    buf = pltpu.VMEM
    scratch = [
        buf((2, batches, across, outer) + tail, bf16),
        buf((2, batches, across, outer) + tail, bf16),
        buf((2, across, batches, outer) + tail, bf16),
        buf((2, outer) + tail, bf16),
        buf((outer, 2) + tail, bf16),
        buf(down_line.shape, bf16),
        buf((2, 2) + tail, f32),
        buf(small.shape, f32),
        buf((across,) + small.shape, f32),
        buf((batches,) + small.shape, f32),
        buf((outer,) + small.shape, f32),
    ]
    scratch += [DMA((2, batches, across))] * 6 + [DMA((2, outer))] * 2 + [DMA((outer,))] * 4 + [DMA((2,))] * 2
    scratch += [DMA((across + batches + outer,))] * 2
    return pl.pallas_call(
        functools.partial(last_kernel, batches, outer, inner),
        out_shape=(
            jax.ShapeDtypeStruct((4, share, D), f32),
            jax.ShapeDtypeStruct((4, share, D), f32),
            jax.ShapeDtypeStruct(down_line.shape[1:], f32),
            jax.ShapeDtypeStruct(small.shape, f32),
        ),
        in_specs=[IN_VMEM] * 4,
        out_specs=(IN_VMEM,) * 4,
        scratch_shapes=scratch,
        compiler_params=remote_params(ident, ROOM),
        name="reduce_last",
    )(terms, up_line, down_line, small)


def body(
    tokens_in,
    earlier_outs,
    out_cotangent,
    seq_lengths,
    qkv_weight,
    out_weight,
    up_weight,
    down_weight,
    qkv_first,
    qkv_second,
    out_first,
    out_second,
    up_first,
    up_second,
    down_first,
    down_second,
    small_params,
    small_first,
    small_second,
):
    groups, rows, _ = tokens_in.shape
    tall = groups * rows
    batches = lax.axis_size("batch")
    seq_count = lax.axis_size("seq")
    seq_rank = lax.axis_index("seq")
    devices = batches * seq_count
    outer = math.gcd(seq_count, D // HEAD)
    inner = seq_count // outer
    per = D // HEAD // outer
    length = seq_count * rows
    width = groups * per * HEAD
    share = D // devices
    remote = share % 8 == 0
    everywhere = ("batch", "seq")
    grid = (batches, outer, inner // 2)

    tokens = tokens_in.reshape(tall, D)
    cot = out_cotangent.reshape(tall, D)
    earlier = earlier_outs.reshape(-1, tall, D)
    vecs = jnp.pad(small_params[: VECTORS * D].reshape(VECTORS, D), ((0, 16 - VECTORS), (0, 0)))
    mixing = small_params[VECTORS * D :]

    freq = 10000.0 ** (-jnp.arange(HEAD // 2, dtype=f32) * 2.0 / HEAD)
    query_pos = seq_rank * rows + jnp.arange(rows, dtype=jnp.int32)
    turned = query_pos.astype(f32)[:, None] * freq[None, :]
    cosine, sine = jnp.cos(turned), jnp.sin(turned)
    cosine = jnp.concatenate([cosine] * 4, 1)
    sine = jnp.concatenate([-sine, sine] * 2, 1)
    block_pos = (jnp.arange(outer) * inner + seq_rank % inner)[:, None] * rows + jnp.arange(rows)[None, :]
    block_turned = block_pos.astype(f32)[:, None, :] * freq[None, :, None]
    block_cos, block_sin = jnp.cos(block_turned), jnp.sin(block_turned)

    def by_rows(shard):
        return shard.astype(bf16).reshape(share, -1, D).transpose(1, 0, 2)

    def by_blocks(gathered):
        return gathered.transpose(1, 0, 2, 3).reshape(-1, D, D)

    if remote:
        near, up_line, down_line, counts, normed, mixture, dots = gather_first(
            qkv_weight, out_weight, up_weight, down_weight, seq_lengths, mixing, tokens, cot, earlier, vecs,
            batches, outer, inner, 1,
        )
        near = near.reshape(4, D, D)
        q, k, v, up, down = spread_heads(normed, near, vecs, cosine, sine, (up_line, down_line), batches, outer, inner, 2)
        up, down = up.reshape(BLOCKS, D, D), down.reshape(BLOCKS, D, D)
    else:
        near = by_blocks(lax.all_gather(jnp.concatenate([by_rows(qkv_weight), by_rows(out_weight)], 0), everywhere, axis=0))
        up = by_blocks(lax.all_gather(by_rows(up_weight), everywhere, axis=0))
        down = lax.all_gather(down_weight.astype(bf16), everywhere, axis=0).reshape(BLOCKS, D, D)
        counts = jnp.full((1, 8, 128), lax.psum(jnp.sum(seq_lengths), "batch"), jnp.int32)
        wide = tokens.astype(f32)
        normed = (normalize(wide)[0] * vecs[0] + vecs[2]).astype(bf16)
        live = (query_pos[None, :] < seq_lengths[:, None]).astype(f32).reshape(tall, 1)
        terms = [tokens] + [earlier[i] for i in range(earlier.shape[0])]
        mixture = sum(mixing[1 + i] * term.astype(f32) for i, term in enumerate(terms))
        sums = [jnp.sum(cot.astype(f32) * live * term.astype(f32), 0) for term in terms]
        dots = jnp.pad(jnp.stack(sums), ((1, 15 - len(sums)), (0, 0)))
        q, k, v = spread_heads(normed, near, vecs, cosine, sine, (), batches, outer, inner, 2)

    k, v = k.reshape(length, width), v.reshape(length, width)
    attended, turned_out, log_total = attend(seq_lengths, q, k, v, groups, per, inner, math.gcd(length, 1024))
    mixed, grad_mine, middle_grad, out_term, up_terms, down_terms, sums = middle_layer(
        attended, near, up, down, tokens, cot, mixture, counts, vecs, seq_lengths, mixing, batches, outer, inner, 3
    )
    dq, dk, dv = attend_back(
        seq_lengths, q, k, v, grad_mine, turned_out, log_total, block_cos, block_sin, groups, per, inner, math.gcd(length, 512)
    )
    pieces = (outer, inner, rows, width)
    dk, dv = dk.reshape(pieces), dv.reshape(pieces)
    if remote:
        blocked = (up_terms.reshape((4,) + grid + (2 * share, D)), down_terms.reshape(grid + (2, BLOCKS * share, D)))
        dq, dk, dv, up_back, down_back = fold_heads(dq, dk, dv, blocked, batches, inner, 5)
    else:
        dq, dk, dv = fold_heads(dq, dk, dv, (), batches, inner, 5)
    input_grad, near_terms, small = back_layer(
        dq, dk, dv, cosine, sine, normed, tokens, near, vecs, cot, counts, seq_lengths, mixing, middle_grad, out_term, sums, dots, outer
    )
    if remote:
        near_grad, up_grad, down_grad, small = reduce_last(
            near_terms.reshape((4,) + grid + (2 * share, D)), up_back, down_back, small, batches, outer, inner, 6
        )
    else:

        def scattered(terms):
            return lax.psum_scatter(terms.reshape(-1, devices, share, D), everywhere, scatter_dimension=1).astype(f32)

        near_grad, up_grad = scattered(near_terms), scattered(up_terms)
        down_grad = lax.psum_scatter(down_terms.reshape(devices, -1, D), everywhere, scatter_dimension=0).astype(f32)
        small = lax.psum(small, everywhere)
    small_grad = small.reshape(-1)[: small_params.shape[0]]
    small_step, small_first_new = adam(small_params, small_grad, small_first, small_second, 0.0)
    (
        qkv_grad, qkv_step, qkv_first_new, out_grad, out_step, out_first_new,
        up_grad, up_step, up_first_new, down_grad, down_step, down_first_new,
    ) = adam_all(
        near_grad, up_grad, down_grad,
        (qkv_weight, qkv_first, qkv_second, out_weight, out_first, out_second,
         up_weight, up_first, up_second, down_weight, down_first, down_second),
    )
    return (
        mixed.reshape(tokens_in.shape),
        input_grad.reshape(tokens_in.shape),
        qkv_grad,
        out_grad,
        up_grad,
        down_grad,
        small_grad,
        qkv_step,
        out_step,
        up_step,
        down_step,
        small_step,
        qkv_first_new,
        out_first_new,
        up_first_new,
        down_first_new,
        small_first_new,
    )


def solution(mesh):
    placed = (
        P("batch", "seq", None),
        P(None, "batch", "seq", None),
        P("batch", "seq", None),
        P("batch"),
        P(("batch", "seq"), None),
        P(("batch", "seq"), None),
        P(("batch", "seq"), None),
        P(("batch", "seq"), None),
        P(("batch", "seq"), None),
        P(("batch", "seq"), None),
        P(("batch", "seq"), None),
        P(("batch", "seq"), None),
        P(("batch", "seq"), None),
        P(("batch", "seq"), None),
        P(("batch", "seq"), None),
        P(("batch", "seq"), None),
        P(),
        P(),
        P(),
    )
    return jax.shard_map(
        body,
        mesh=mesh,
        in_specs=placed,
        out_specs=(
            P("batch", "seq", None),
            P("batch", "seq", None),
            P(("batch", "seq"), None),
            P(("batch", "seq"), None),
            P(("batch", "seq"), None),
            P(("batch", "seq"), None),
            P(),
            P(("batch", "seq"), None),
            P(("batch", "seq"), None),
            P(("batch", "seq"), None),
            P(("batch", "seq"), None),
            P(),
            P(("batch", "seq"), None),
            P(("batch", "seq"), None),
            P(("batch", "seq"), None),
            P(("batch", "seq"), None),
            P(),
        ),
        check_vma=False,
    )
```

```python
import functools
import math

import jax
import jax.numpy as jnp
from jax import lax
from jax.experimental import pallas as pl
from jax.experimental.pallas import tpu as pltpu
from jax.sharding import PartitionSpec as P

D = 768
FF = 3072
HEAD = 64
BLOCKS = FF // D
VECTORS = 9 + BLOCKS
bf16 = jnp.bfloat16
f32 = jnp.float32
NEG = -1e30

beta_one = 0.9
beta_two = 0.999
adam_eps = 1e-08
learn_rate = 0.01
decay_rate = 0.1
adam_step = 10

MESH = pl.DeviceIdType.MESH
ANYWHERE = pl.BlockSpec(memory_space=pl.ANY)
IN_VMEM = pl.BlockSpec(memory_space=pltpu.VMEM)
IN_SMEM = pl.BlockSpec(memory_space=pltpu.SMEM)
DMA = pltpu.SemaphoreType.DMA
ROOM = 56 << 20

def mm(a, b):
    return lax.dot_general(a, b, (((1,), (0,)), ((), ())), preferred_element_type=f32)


def mm_nt(a, b):
    return lax.dot_general(a, b, (((1,), (1,)), ((), ())), preferred_element_type=f32)


def params():
    return pltpu.CompilerParams(vmem_limit_bytes=ROOM)


def remote_params(ident, vmem=None):
    return pltpu.CompilerParams(collective_id=ident, has_side_effects=True, vmem_limit_bytes=vmem)


class Place:
    def __init__(self, batches, outer, inner):
        self.batch = lax.axis_index("batch")
        rank = lax.axis_index("seq")
        self.o = lax.div(rank, inner)
        self.j = lax.rem(rank, inner)
        self.a = lax.div(self.j, 2)
        self.c = lax.rem(rank, 2)
        across = inner // 2
        self.zs = [lax.rem(self.o + t, outer) for t in range(outer)]
        self.xs = [lax.rem(self.a + t, across) for t in range(across)]
        self.ys = [lax.rem(self.batch + t, batches) for t in range(batches)]
        self.z_from = [lax.rem(self.o + outer - t, outer) for t in range(outer)]
        self.x_from = [lax.rem(self.a + across - t, across) for t in range(across)]
        self.y_from = [lax.rem(self.batch + batches - t, batches) for t in range(batches)]
        self.z_peers = [(self.batch, z * inner + self.j) for z in self.zs]
        self.x_peers = [(self.batch, self.o * inner + x * 2 + self.c) for x in self.xs]
        self.y_peers = [(y, rank) for y in self.ys]
        self.twin = (self.batch, self.o * inner + self.a * 2 + (1 - self.c))


def greet(peers):
    barrier = pltpu.get_barrier_semaphore()
    for peer in peers:
        pl.semaphore_signal(barrier, inc=1, device_id=peer, device_id_type=MESH)
    pl.semaphore_wait(barrier, len(peers))


def push(src, dst, send, recv, peer):
    copy = pltpu.make_async_remote_copy(
        src_ref=src, dst_ref=dst, send_sem=send, recv_sem=recv, device_id=peer, device_id_type=MESH
    )
    copy.start()
    return copy


def carry(src, dst, sem):
    copy = pltpu.make_async_copy(src, dst, sem)
    copy.start()
    return copy


def normalize(values):
    center = values - jnp.mean(values, -1, keepdims=True)
    inverse = lax.rsqrt(jnp.mean(center * center, -1, keepdims=True) + 1e-05)
    return center * inverse, inverse


def normalize_back(grad, hat, inverse, gain):
    scaled = grad * gain
    part = scaled - jnp.mean(scaled, -1, keepdims=True) - hat * jnp.mean(scaled * hat, -1, keepdims=True)
    return part * inverse


def turn(value, cosine, sine):
    lane = lax.broadcasted_iota(jnp.int32, value.shape, 1)
    other = jnp.where(lax.rem(lane, HEAD) < HEAD // 2, pltpu.roll(value, 128 - HEAD // 2, 1), pltpu.roll(value, HEAD // 2, 1))
    return value * cosine + other * sine


def fold_single(value, odd):
    half = value.shape[0] // 2
    top, bottom = value[:half], value[half:]
    lane = lax.broadcasted_iota(jnp.int32, top.shape, 1)
    if odd:
        return jnp.where(lane < HEAD, pltpu.roll(top, HEAD, 1), bottom)
    return jnp.where(lane < HEAD, top, pltpu.roll(bottom, HEAD, 1))


def unfold_single(value, high):
    turned = pltpu.roll(value, HEAD, 1)
    return jnp.concatenate([turned, value] if high else [value, turned], 0)


def unfold_heads(read, rows, outer):
    tiles = [None] * (outer * 3 // 2)
    for o in range(0, outer, 2):
        base = 3 * o * HEAD // 128
        first, second = read(o), read(o + 1)
        tiles[base] = first[:rows]
        tiles[base + 2] = second[:rows]
        low, high = unfold_single(first[rows:], False), unfold_single(second[rows:], True)
        lane = lax.broadcasted_iota(jnp.int32, low.shape, 1)
        tiles[base + 1] = jnp.where(lane < HEAD, low, high)
    return tiles


def fold_heads_of(write, tile_of, outer):
    for o in range(outer):
        first = 3 * o * HEAD
        odd = first % 128 != 0
        pair = (first + HEAD if odd else first) // 128
        single = (first if odd else first + 128) // 128
        write(o, jnp.concatenate([tile_of(pair), fold_single(tile_of(single), odd)], 0))


def packed_rows(vector, z):
    pairs, singles = [], []
    for n in range(3):
        base = n * D + 3 * z * HEAD
        odd = base % 128 != 0
        first = base + HEAD if odd else base
        pairs.append(vector[first : first + 128])
        single = vector[base : base + HEAD] if odd else vector[base + 128 : base + 192]
        singles.append(jnp.concatenate([single, jnp.zeros_like(single)]))
    return pairs + singles


def lane_half(core):
    return pl.ds(pl.multiple_of(core * (D // 2), 128), D // 2)


def packed_tiles(read, z):
    pairs, singles = [], []
    for n in range(3):
        base = n * D + 3 * z * HEAD
        odd = base % 128 != 0
        pairs.append(read(base + HEAD if odd else base))
        single = read(base - HEAD if odd else base + 128)
        singles.append(pltpu.roll(single, HEAD, 1) if odd else single)
    return pairs + singles


class Line:
    def __init__(self, here, outer, inner, slot, own_send, hand_send, recv):
        self.here, self.outer, self.slot = here, outer, slot
        self.own_send, self.hand_send, self.recv = own_send, hand_send, recv
        self.inner = inner
        self.sends = []
        self.table = [sorted((s for s in range(outer) if s != i), key=lambda s: (abs(s - i), s)) for i in range(outer)]

    def origin(self, n):
        if n == 0:
            return self.here.o
        found = 0
        for i in range(self.outer):
            found = found + (self.here.o == i).astype(jnp.int32) * self.table[i][n - 1]
        return found

    def peer(self, z):
        return (self.here.batch, z * self.inner + self.here.j)

    def send(self, source, key, s, to, sem):
        there = jnp.clip(to, 0, self.outer - 1)
        copy = pltpu.make_async_remote_copy(
            src_ref=source,
            dst_ref=self.slot(key, s),
            send_sem=sem,
            recv_sem=self.recv.at[key, s],
            device_id=self.peer(there),
            device_id_type=MESH,
        )
        valid = (to >= 0) & (to < self.outer)

        @pl.when(valid)
        def _():
            copy.start()

        self.sends.append((valid, copy))

    def start(self, key, source):
        o = self.here.o
        self.send(source, key, o, o + 1, self.own_send.at[key, 0])
        self.send(source, key, o, o - 1, self.own_send.at[key, 1])

    def arrive(self, key, n):
        o, s = self.here.o, self.origin(n)
        place = self.slot(key, s)
        pltpu.make_async_remote_copy(
            src_ref=place,
            dst_ref=place,
            send_sem=self.hand_send.at[key, n],
            recv_sem=self.recv.at[key, s],
            device_id=self.here.twin,
            device_id_type=MESH,
        ).wait_recv()
        step = 1 - 2 * (s > o).astype(jnp.int32)
        self.send(place, key, s, o + step, self.hand_send.at[key, n])
        return s

    def finish(self):
        for valid, copy in self.sends:

            @pl.when(valid)
            def _(copy=copy):
                copy.wait_send()


def start_kernel(batches, outer, inner, *refs):
    refs = list(refs)

    def take(n):
        got = refs[:n]
        del refs[:n]
        return got

    qkv, out, up, down, lens, mixing, tokens, cot, earlier, vecs, packed_bias, cos_t, sin_t = take(13)
    mine, normed, q_all, k_all, v_all, out_all, up_all, down_all, counts, mixture, dots, o_mine, ot, lse = take(14)
    own, got, near, up_bit, out_bit, down_bit, queue, count, wide_s, cosine, sine = take(11)
    zs, zr, xs, xr, ys, yr, cs, cr, ts, tr, ns, nr, local, es = take(14)
    nls, nlf, nlr, rls, rlf, rlr, rxs, rxr, rys, ryr, rcs, rcr, axs, axr, acs, acr = take(16)
    attend_refs = refs
    across = inner // 2
    here = Place(batches, outer, inner)
    o, a, b, c, j = here.o, here.a, here.batch, here.c, here.j
    earlier_count, tall, _ = earlier.shape
    groups = lens.shape[0]
    rows = tall // groups
    fetches = {e: carry(earlier.at[e], queue.at[e], es.at[e]) for e in range(2)}
    for g in range(groups):
        hat, _ = normalize(tokens[g * rows : g * rows + rows].astype(f32))
        normed[g, o] = (hat * vecs[0:1] + vecs[2:3]).astype(bf16)
    for z in range(outer):
        for i, tile in enumerate(packed_tiles(lambda lane: qkv[:, lane : lane + 128], z)):
            own[z, :, 128 * i : 128 * i + 128] = tile
    for i in range(BLOCKS):
        own[outer + 1 + i] = up[:, i * D : i * D + D]
    own[outer] = out[...]
    here_count = lens[0]
    for g in range(1, groups):
        here_count = here_count + lens[g]
    count[...] = jnp.zeros(count.shape, jnp.int32) + here_count
    greet(here.z_peers[1:] + here.x_peers[1:] + here.y_peers[1:] + [here.twin])
    give = lane_half(1 - c)
    keep = lane_half(c)
    near_count = outer + 1
    swaps = [
        push(own.at[pl.ds(0, near_count), :, give], got.at[pl.ds(0, near_count), :, pl.ds(0, D // 2)], ts.at[0], tr.at[0], here.twin),
        push(own.at[pl.ds(near_count + 2 * (1 - c), 2)], got.at[pl.ds(near_count, 2)], ts.at[1], tr.at[1], here.twin),
    ]
    line = Line(here, outer, inner, lambda g, s: normed.at[g, s], nls, nlf, nlr)
    line.start(0, normed.at[0, o])
    waits = [carry(count, counts.at[b], local.at[0])]
    for d in range(1, batches):
        waits.append(push(count, counts.at[b], ns.at[d], nr.at[d], here.y_peers[d]))

    def joined(own_part, other):
        low = jnp.where(c == 0, own_part, other)
        high = jnp.where(c == 0, other, own_part)
        return jnp.concatenate([low, high], 0).astype(bf16)

    def slot(y, z, x):
        return mine.at[y, z, x, :, keep]

    arrivals, twins = {}, []

    def onward(source, y, z, x, t, dx, dy):
        to = slot(y, z, x)
        if dx == 0 and dy == 0:
            for d in range(1, across):
                arrivals["x", t, d] = push(source, to, xs.at[t, d], xr.at[t, d], here.x_peers[d])
        if dy == 0:
            for d in range(1, batches):
                arrivals["y", t, dx, d] = push(source, to, ys.at[t, dx, d], yr.at[t, dx, d], here.y_peers[d])
        twins.append(push(source, to, cs.at[t, dx, dy], cr.at[t, dx, dy], here.twin))

    swaps[0].wait()
    for z in range(outer + 1):
        own_part = jnp.where(c == 0, own[z, :, : D // 2], own[z, :, D // 2 :])
        value = joined(own_part, got[z, :, : D // 2])
        if z < outer:
            near[z] = value
        else:
            out_bit[...] = value
    copies = {}
    for t in range(1, outer):
        copies[t] = push(near.at[here.zs[t]], slot(b, o, a), zs.at[t], zr.at[t], here.z_peers[t])
    twins.append(carry(near.at[o], slot(b, o, a), local.at[1]))
    onward(near.at[o], b, o, a, 0, 0, 0)
    swaps[1].wait()
    for p in (0, 1):
        up_bit[p] = joined(own[near_count + 2 * c + p], got[near_count + p])
    down_bit[...] = down[...].astype(bf16)
    for t in range(1, outer):
        copies[t].wait()
        onward(slot(b, here.z_from[t], a), b, here.z_from[t], a, t, 0, 0)

    bits = (up_bit, down_bit, out_bit)

    def rest_slot(i, y, z, x):
        if i == 0:
            return up_all.at[pl.ds(2 * c, 2), y, z, x]
        if i == 1:
            return down_all.at[y, z, x, c]
        return out_all.at[y, z, x, :, keep]

    rest_x, rest_y = [], []
    rest = Line(here, outer, inner, lambda i, s: rest_slot(i, b, s, a), rls, rlf, rlr)

    def rest_onward(i, n, s, source):
        to = rest_slot(i, b, s, a)
        for d in range(1, across):
            rest_x.append((i, n, s, d, push(source, to, rxs.at[i, n, d], rxr.at[i, n, d], here.x_peers[d])))
        for d in range(1, batches):
            rest_y.append((i, n, s, 0, d, push(source, to, rys.at[i, n, 0, d], ryr.at[i, n, 0, d], here.y_peers[d])))
        waits.append(push(source, to, rcs.at[i, n, 0, 0], rcr.at[i, n, 0, 0], here.twin))

    def rest_line(n):
        for i in range(3):
            s = rest.arrive(i, n)
            rest_onward(i, n, s, rest_slot(i, b, s, a))

    def rest_across():
        if rest_x:
            i, n, s, d, copy = rest_x.pop(0)
            copy.wait()
            piece = rest_slot(i, b, s, here.x_from[d])
            for e in range(1, batches):
                rest_y.append((i, n, s, d, e, push(piece, piece, rys.at[i, n, d, e], ryr.at[i, n, d, e], here.y_peers[e])))
            waits.append(push(piece, piece, rcs.at[i, n, d, 0], rcr.at[i, n, d, 0], here.twin))

    def rest_twin():
        if rest_y:
            i, n, s, d, e, copy = rest_y.pop(0)
            copy.wait()
            piece = rest_slot(i, here.y_from[e], s, here.x_from[d])
            waits.append(push(piece, piece, rcs.at[i, n, d, e], rcr.at[i, n, d, e], here.twin))

    late = {0: [], 1: []}
    spread = {0: [], 1: []}

    def project(g, n, s):
        wide_s[...] = mm(normed[g, s], mine[...].reshape(D, D)) + packed_bias[pl.ds(o, 1)]
        for i, dest in enumerate((q_all, k_all, v_all)):
            pair, single = wide_s[:, 128 * i : 128 * i + 128], wide_s[:, 384 + 128 * i : 512 + 128 * i]
            if i < 2:
                pair, single = turn(pair, cosine[s], sine[s]), turn(single, cosine[s], sine[s])
            value = jnp.concatenate([pair, fold_single(single, False)], 0).astype(bf16)
            if i == 0:
                q_all[g, s] = value
            else:
                dest[g, s, j] = value
        for i, dest in enumerate((k_all, v_all)):
            piece = dest.at[g, s, j]
            for d in range(1, across):
                late[g].append((i, n, s, d, push(piece, piece, axs.at[g, i, n, d], axr.at[g, i, n, d], here.x_peers[d])))
            spread[g].append(push(piece, piece, acs.at[g, i, n, 0], acr.at[g, i, n, 0], here.twin))

    def settle(g, count):
        for _ in range(count):
            if late[g]:
                i, n, s, d, copy = late[g].pop(0)
                copy.wait()
                piece = (k_all, v_all)[i].at[g, s, here.x_from[d] * 2 + c]
                spread[g].append(push(piece, piece, acs.at[g, i, n, d], acr.at[g, i, n, d], here.twin))

    def arrive(g, n):
        project(g, n, line.arrive(g, n))

    def live_rows(value):
        row = lax.broadcasted_iota(jnp.int32, (rows, 1), 0) + lax.axis_index("seq") * rows
        parts = [jnp.where(row < lens[g], value[g * rows : g * rows + rows], 0.0) for g in range(groups)]
        return jnp.concatenate(parts, 0)

    def plain():
        wide = tokens[...].astype(f32)
        grad = live_rows(cot[...].astype(f32))
        dots[...] = jnp.zeros(dots.shape, f32)
        dots[1:2] = jnp.sum(grad * wide, 0, keepdims=True)
        mixture[...] = mixing[1] * wide

    def mix(e):
        fetches[e].wait()
        wide = queue[e % 2].astype(f32)
        grad = live_rows(cot[...].astype(f32))
        dots[2 + e : 3 + e] = jnp.sum(grad * wide, 0, keepdims=True)
        mixture[...] = mixture[...] + mixing[2 + e] * wide
        if e + 2 < earlier_count:
            fetches[e + 2] = carry(earlier.at[e + 2], queue.at[e % 2], es.at[e + 2])

    steps = [plain] + [functools.partial(mix, e) for e in range(earlier_count)]

    def work(n=1):
        for _ in range(n):
            if steps:
                steps.pop(0)()

    for z in range(outer):
        cosine[z] = jnp.concatenate([cos_t[z]] * 4, 0).T
        sine[z] = jnp.concatenate([-sin_t[z], sin_t[z]] * 2, 0).T
    first = line.arrive(0, 1)
    for t in range(outer):
        for d in range(1, across):
            arrivals["x", t, d].wait()
            z, x = here.z_from[t], here.x_from[d]
            onward(slot(b, z, x), b, z, x, t, d, 0)
    for i in range(3):
        waits.append(carry(bits[i], rest_slot(i, b, o, a), local.at[2 + i]))
        rest_onward(i, 0, o, bits[i])
    for t in range(outer):
        for dx in range(across):
            for dy in range(1, batches):
                arrivals["y", t, dx, dy].wait()
                y, z, x = here.y_from[dy], here.z_from[t], here.x_from[dx]
                onward(slot(y, z, x), y, z, x, t, dx, dy)
    second = line.arrive(0, 2)
    for i in range(3):
        rest.start(i, bits[i])
    for copy in twins:
        copy.wait()
    project(0, 0, o)
    project(0, 1, first)
    project(0, 2, second)
    for n in range(3, outer):
        arrive(0, n)
    line.start(1, normed.at[1, o])
    settle(0, 2)
    rest_line(1)
    work(3)
    settle(0, 2)
    rest_line(2)
    settle(0, 2 * outer * across)
    project(1, 0, o)
    for copy in spread[0]:
        copy.wait()
    events = [
        lambda: rest_line(3) if outer > 3 else None,
        lambda: (rest_across(), rest_across(), rest_across()),
        lambda: arrive(1, 1),
        lambda: (settle(1, 2), rest_across(), rest_across(), rest_across()),
        lambda: (rest_twin(), rest_twin(), rest_twin()),
        lambda: arrive(1, 2),
        lambda: (settle(1, 2), rest_across(), rest_across(), rest_across()),
        lambda: (rest_twin(), rest_twin(), rest_twin()),
    ]
    attend_group(0, outer, inner, lens, q_all, k_all, v_all, o_mine, ot, lse, attend_refs, here, events)
    while events:
        events.pop(0)()
    work(4)
    for n in range(3, outer):
        arrive(1, n)
    while rest_x:
        rest_across()
    settle(1, 2 * outer * across)
    work(len(steps))
    for copy in spread[1]:
        copy.wait()
    events = [lambda: (rest_twin(), rest_twin(), rest_twin())] * 8
    attend_group(1, outer, inner, lens, q_all, k_all, v_all, o_mine, ot, lse, attend_refs, here, events)
    while rest_y:
        rest_twin()
    line.finish()
    rest.finish()
    for copy in waits:
        copy.wait()


def start_layer(qkv, out, up, down, lens, mixing, tokens, cot, earlier, vecs, packed_bias, cos_t, sin_t, batches, outer, inner, ident):
    across = inner // 2
    share = qkv.shape[0]
    tall = tokens.shape[0]
    groups = lens.shape[0]
    rows = tall // groups
    grid = (batches, outer, across)
    folded = rows + rows // 2
    buf = pltpu.VMEM
    return pl.pallas_call(
        functools.partial(start_kernel, batches, outer, inner),
        out_shape=(
            jax.ShapeDtypeStruct(grid + (2 * share, D), bf16),
            jax.ShapeDtypeStruct((groups, outer, rows, D), bf16),
            jax.ShapeDtypeStruct((groups, outer, folded, 128), bf16),
            jax.ShapeDtypeStruct((groups, outer, inner, folded, 128), bf16),
            jax.ShapeDtypeStruct((groups, outer, inner, folded, 128), bf16),
            jax.ShapeDtypeStruct(grid + (2 * share, D), bf16),
            jax.ShapeDtypeStruct((BLOCKS,) + grid + (2 * share, D), bf16),
            jax.ShapeDtypeStruct(grid + (2, BLOCKS * share, D), bf16),
            jax.ShapeDtypeStruct((batches, 8, 128), jnp.int32),
            jax.ShapeDtypeStruct((tall, D), f32),
            jax.ShapeDtypeStruct((16, D), f32),
            jax.ShapeDtypeStruct((outer, groups, folded, 128), bf16),
            jax.ShapeDtypeStruct((groups, outer, 3 * HEAD, rows), f32),
            jax.ShapeDtypeStruct((groups, outer, 8, rows), f32),
        ),
        in_specs=[IN_VMEM] * 4 + [IN_SMEM] * 2 + [IN_VMEM] * 2 + [ANYWHERE] + [IN_VMEM] * 4,
        out_specs=(IN_VMEM,) * 5 + (ANYWHERE,) * 4 + (IN_VMEM,) * 5,
        scratch_shapes=[
            buf((outer + 1 + BLOCKS, share, D), f32),
            buf((outer + 3, share, D), f32),
            buf((outer, 2 * share, D // 2), bf16),
            buf((2, 2 * share, D), bf16),
            buf((2 * share, D // 2), bf16),
            buf((BLOCKS * share, D), bf16),
            buf((2, tall, D), bf16),
            buf((8, 128), jnp.int32),
            buf((rows, D), f32),
            buf((outer, rows, 128), f32),
            buf((outer, rows, 128), f32),
        ]
        + [DMA((outer,))] * 2
        + [DMA((outer, across))] * 2
        + [DMA((outer, across, batches))] * 4
        + [DMA((2,))] * 2
        + [DMA((batches,))] * 2
        + [DMA((5,)), DMA((earlier.shape[0],))]
        + [DMA((groups, 2)), DMA((groups, outer)), DMA((groups, outer))]
        + [DMA((3, 2)), DMA((3, outer)), DMA((3, outer))]
        + [DMA((3, outer, across))] * 2
        + [DMA((3, outer, across, batches))] * 4
        + [DMA((groups, 2, outer, across))] * 4
        + attend_scratch(outer, inner, rows),
        compiler_params=remote_params(ident, ROOM),
        name="start_layer",
    )(qkv, out, up, down, lens, mixing, tokens, cot, earlier, vecs, packed_bias, cos_t, sin_t)


class Exchange:
    def __init__(self, here, pair, q, alls, q_all, sems, local, first_local):
        self.here, self.pair, self.q, self.alls, self.q_all = here, pair, q, alls, q_all
        self.qs, self.qr, self.zs, self.zr, self.xs, self.xr, self.cs, self.cr = sems
        self.local, self.first_local = local, first_local
        self.outer, self.across = len(here.zs), len(here.xs)
        self.arriving = {0: [], 1: []}
        self.late = {0: [], 1: []}
        self.waits = {0: [], 1: []}

    def send_pair(self, g):
        here = self.here
        for i in (0, 1):
            source, dest = self.pair[i], self.alls[i]
            for t in range(1, self.outer):
                copy = push(source.at[g, here.zs[t]], dest.at[g, here.o, here.j], self.zs.at[g, i, t], self.zr.at[g, i, t], here.z_peers[t])
                self.arriving[g].append((i, t, copy))
            place = dest.at[g, here.o, here.j]
            self.waits[g].append(carry(source.at[g, here.o], place, self.local.at[self.first_local + 3 * g + i]))
            self.onward(g, i, 0, source.at[g, here.o], place)

    def send_query(self, g):
        here = self.here
        for t in range(1, self.outer):
            self.waits[g].append(push(self.q.at[g, here.zs[t]], self.q_all.at[g, here.o], self.qs.at[g, t], self.qr.at[g, t], here.z_peers[t]))
        self.waits[g].append(carry(self.q.at[g, here.o], self.q_all.at[g, here.o], self.local.at[self.first_local + 3 * g + 2]))

    def onward(self, g, i, t, source, place):
        here = self.here
        for d in range(1, self.across):
            copy = push(source, place, self.xs.at[g, i, t, d], self.xr.at[g, i, t, d], here.x_peers[d])
            self.late[g].append((i, t, d, copy))
        self.waits[g].append(push(source, place, self.cs.at[g, i, t, 0], self.cr.at[g, i, t, 0], here.twin))

    def settle(self, g, left):
        here = self.here
        while len(self.late[g]) > left:
            i, t, d, copy = self.late[g].pop(0)
            copy.wait()
            moved = self.alls[i].at[g, here.z_from[t], here.x_from[d] * 2 + here.c]
            self.waits[g].append(push(moved, moved, self.cs.at[g, i, t, d], self.cr.at[g, i, t, d], here.twin))

    def arrive(self, g):
        i, t, copy = self.arriving[g].pop(0)
        copy.wait()
        place = self.alls[i].at[g, self.here.z_from[t], self.here.j]
        self.onward(g, i, t, place, place)
        self.settle(g, self.across - 1)

    def finish(self, g):
        for copy in self.waits[g]:
            copy.wait()


def exchange_scratch(groups, outer, across):
    return [DMA((groups, outer))] * 2 + [DMA((groups, 2, outer))] * 2 + [DMA((groups, 2, outer, across))] * 4


def turned_parts(block, rows):
    pair = block[:rows].T
    single = block[rows:].T
    single = jnp.concatenate([single[:HEAD], single[HEAD:]], 1)
    blank = jnp.zeros_like(single)
    stack = lambda *parts: jnp.concatenate(parts, 0)
    return stack(pair[:HEAD], blank), stack(blank, pair[HEAD:]), stack(single, blank), stack(blank, single)


def attend_scratch(outer, inner, rows):
    span = inner * rows
    return [
        pltpu.VMEM((outer, 128, span), bf16),
        pltpu.VMEM((outer, 128, span // 2), bf16),
        pltpu.VMEM((outer, span, 128), f32),
        pltpu.VMEM((4, 128, rows), bf16),
        pltpu.VMEM((8, rows), f32),
        pltpu.VMEM((8, rows), f32),
    ]


def bias_rows(bias, lens, g, outer, span):
    for c in range(outer):
        key = c * span + lax.broadcasted_iota(jnp.int32, (span, 128), 0)
        bias[c] = jnp.where(key < lens[g], 0.0, NEG)


def attend_group(g, outer, inner, lens, q_all, k_all, v_all, o_mine, ot, lse, scratch, here, events):
    vt, vft, bias, qt, m_s, l_s = scratch
    folded = q_all.shape[2]
    rows = folded * 2 // 3
    span = inner * rows
    half = rows // 2
    tiles = rows // 128
    bias_rows(bias, lens, g, outer, span)
    for c in range(outer):
        vt[c] = v_all[g, c, :, :rows, :].reshape(span, 128).T
        vft[c] = v_all[g, c, :, rows:, :].reshape(span // 2, 128).T
    for z in range(outer):
        first = (z * inner + here.j) * rows
        for n, part in enumerate(turned_parts((q_all[g, z] * 0.125).astype(bf16), rows)):
            qt[n] = part
        ot[g, z] = jnp.zeros((3 * HEAD, rows), f32)
        m_s[...] = jnp.full(m_s.shape, NEG, f32)
        l_s[...] = jnp.zeros(l_s.shape, f32)

        def step(c, masked):
            pair = k_all[g, c, :, :rows, :].reshape(span, 128)
            single = k_all[g, c, :, rows:, :].reshape(span // 2, 128)
            low = bias[c]
            low_parts = low.reshape(inner, rows, 128)
            shut = (low, low, low_parts[:, :half].reshape(span // 2, 128), low_parts[:, half:].reshape(span // 2, 128))
            lhs = (pair, pair, single, single)
            scores = []
            for n in range(4):
                s = mm(lhs[n], qt[n]) + jnp.concatenate([shut[n]] * tiles, 1)
                if masked:
                    key = lax.broadcasted_iota(jnp.int32, s.shape, 0)
                    if n >= 2:
                        key = lax.div(key, half) * rows + lax.rem(key, half) + (n - 2) * half
                    query = first + lax.broadcasted_iota(jnp.int32, s.shape, 1)
                    s = jnp.where(key + c * span <= query, s, NEG)
                scores.append(s)
            own = ((0,), (1,), (2, 3))
            tops = [m_s[h : h + 1] for h in range(3)]
            news = []
            for h in range(3):
                top = tops[h]
                for n in own[h]:
                    top = jnp.maximum(top, jnp.max(scores[n], 0, keepdims=True))
                news.append(top)
            shares, sums = [], [0.0, 0.0, 0.0]
            for h in range(3):
                for n in own[h]:
                    p = jnp.exp(scores[n] - news[h])
                    sums[h] = sums[h] + jnp.sum(p, 0, keepdims=True)
                    shares.append(p.astype(bf16))
            for h in range(3):
                alpha = jnp.exp(tops[h] - news[h])
                l_s[h : h + 1] = l_s[h : h + 1] * alpha + sums[h]
                m_s[h : h + 1] = news[h]
                at = slice(HEAD * h, HEAD * h + HEAD)
                if h < 2:
                    out = mm(vt[c, at, :], shares[h])
                else:
                    out = mm(vft[c, :HEAD, :], shares[2]) + mm(vft[c, HEAD:, :], shares[3])
                ot[g, z, at, :] = ot[g, z, at, :] * alpha + out

        def full_step(c, _):
            step(c, False)
            return 0

        if z:
            lax.fori_loop(0, z, full_step, 0)
        if events:
            events.pop(0)()
        step(z, True)
        if events:
            events.pop(0)()
        for h in range(3):
            at = slice(HEAD * h, HEAD * h + HEAD)
            total = l_s[h : h + 1]
            ot[g, z, at, :] = ot[g, z, at, :] / total
            lse[g, z, h : h + 1, :] = m_s[h : h + 1] + jnp.log(total)
        o_mine[z, g, :rows, :] = ot[g, z, :128, :].T.astype(bf16)
        halves = [ot[g, z, 128:, :half], ot[g, z, 128:, half:]]
        o_mine[z, g, rows:, :] = jnp.concatenate(halves, 0).T.astype(bf16)


def spread_kernel(batches, outer, inner, *refs):
    refs = list(refs)

    def take(n):
        got = refs[:n]
        del refs[:n]
        return got

    normed, near, vecs, lens, cosine, sine = take(6)
    q_all, k_all, v_all, o_mine, ot, lse = take(6)
    q, k, v, wide_s, local = take(5)
    sems = take(8)
    here = Place(batches, outer, inner)
    rows = cosine.shape[0]
    groups = lens.shape[0]
    greet(here.z_peers[1:] + here.x_peers[1:] + [here.twin])

    def project(block, into, rotated):
        wide_s[...] = mm(normed[...], near[block]) + vecs[4 + block : 5 + block]
        for g in range(groups):

            def tile_of(tile):
                value = wide_s[g * rows : g * rows + rows, 128 * tile : 128 * tile + 128]
                return turn(value, cosine[...], sine[...]) if rotated else value

            def write(target, value):
                into[g, target] = value.astype(bf16)

            fold_heads_of(write, tile_of, outer)

    exchange = Exchange(here, (k, v), q, (k_all, v_all), q_all, sems, local, 0)
    for block, into in ((1, k), (2, v), (0, q)):
        project(block, into, block != 2)
    for g in range(groups):
        exchange.send_pair(g)
        exchange.send_query(g)
    for g in range(groups):
        for _ in range(2 * (outer - 1)):
            exchange.arrive(g)
        exchange.settle(g, 0)
        exchange.finish(g)
    for g in range(groups):
        attend_group(g, outer, inner, lens, q_all, k_all, v_all, o_mine, ot, lse, refs, here, [])


def spread_heads(normed, near, vecs, lens, cosine, sine, batches, outer, inner, ident):
    rows = cosine.shape[0]
    groups = lens.shape[0]
    folded = rows + rows // 2
    piece = (groups, outer, folded, 128)
    full = jax.ShapeDtypeStruct((groups, outer, inner, folded, 128), bf16)
    shapes = (
        jax.ShapeDtypeStruct(piece, bf16),
        full,
        full,
        jax.ShapeDtypeStruct((outer, groups, folded, 128), bf16),
        jax.ShapeDtypeStruct((groups, outer, 3 * HEAD, rows), f32),
        jax.ShapeDtypeStruct((groups, outer, 8, rows), f32),
    )
    return pl.pallas_call(
        functools.partial(spread_kernel, batches, outer, inner),
        out_shape=shapes,
        in_specs=[IN_VMEM] * 3 + [IN_SMEM] + [IN_VMEM] * 2,
        out_specs=(IN_VMEM,) * len(shapes),
        scratch_shapes=[pltpu.VMEM(piece, bf16)] * 3
        + [pltpu.VMEM(normed.shape, f32), DMA((3 * groups,))]
        + exchange_scratch(groups, outer, inner // 2)
        + attend_scratch(outer, inner, rows),
        compiler_params=remote_params(ident, ROOM),
        name="spread_heads",
    )(normed, near, vecs, lens, cosine, sine)


def attend_back_kernel(outer, inner, lens, q, k, v, do, ot, lse, cos, sin, dq, dk, dv, kt, kft, qt, dot_t, qz, dz, rd, dqt, dks, dvs):
    groups, _, folded, _ = q.shape
    rows = folded * 2 // 3
    half = rows // 2
    span = inner * rows
    j = lax.rem(lax.axis_index("seq"), inner)
    low = lax.broadcasted_iota(jnp.int32, (rows, 128), 1) < HEAD

    def spread_parts(into, block):
        pair = block[:rows]
        single = block[rows:].astype(f32)
        blank = jnp.zeros_like(pair)
        into[0] = jnp.where(low, pair, blank)
        into[1] = jnp.where(low, blank, pair)
        into[2] = jnp.where(low, unfold_single(single, False), 0.0).astype(bf16)
        into[3] = jnp.where(low, 0.0, unfold_single(single, True)).astype(bf16)

    for g in range(groups):
        length = lens[g]
        for c in range(outer):
            kt[c] = k[g, c, :, :rows, :].reshape(span, 128).T
            kft[c] = k[g, c, :, rows:, :].reshape(span // 2, 128).T
        dks[...] = jnp.zeros(dks.shape, f32)
        dvs[...] = jnp.zeros(dvs.shape, f32)

        def one(z, _):
            first = (z * inner + j) * rows
            small = (q[g, z] * 0.125).astype(bf16)
            grad = do[z, g]
            for n, part in enumerate(turned_parts(small, rows)):
                qt[n] = part
            grads = turned_parts(grad, rows)
            for n, part in enumerate(grads):
                dot_t[n] = part
            spread_parts(qz, small)
            spread_parts(dz, grad)
            for h in range(3):
                part = grads[h][HEAD * (h % 2) : HEAD * (h % 2) + HEAD]
                rd[h : h + 1, :] = jnp.sum(part.astype(f32) * ot[g, z, HEAD * h : HEAD * h + HEAD, :], 0, keepdims=True)
            dqt[...] = jnp.zeros(dqt.shape, f32)

            def step(c, masked):
                pair = k[g, c, :, :rows, :].reshape(span, 128)
                single = k[g, c, :, rows:, :].reshape(span // 2, 128)
                v_pair = v[g, c, :, :rows, :].reshape(span, 128)
                v_single = v[g, c, :, rows:, :].reshape(span // 2, 128)
                lhs = (pair, pair, single, single)
                values = (v_pair, v_pair, v_single, v_single)
                for n in range(4):
                    h = min(n, 2)
                    s = mm(lhs[n], qt[n])
                    p = jnp.exp(s - lse[g, z, h : h + 1, :])
                    if masked:
                        key = lax.broadcasted_iota(jnp.int32, s.shape, 0)
                        if n >= 2:
                            key = lax.div(key, half) * rows + lax.rem(key, half) + (n - 2) * half
                        key = key + c * span
                        query = first + lax.broadcasted_iota(jnp.int32, s.shape, 1)
                        p = jnp.where((key <= query) & (key < length), p, 0.0)
                    dp = mm(values[n], dot_t[n])
                    ds = (p * (dp - rd[h : h + 1, :])).astype(bf16)
                    dv_part = mm(p.astype(bf16), dz[n])
                    dk_part = mm(ds, qz[n])
                    at = slice(HEAD * h, HEAD * h + HEAD)
                    if n < 2:
                        dvs[c, :, :rows, :] += dv_part.reshape(inner, rows, 128)
                        dks[c, :, :rows, :] += dk_part.reshape(inner, rows, 128)
                        dqt[at, :] += mm(kt[c, at, :], ds)
                    else:
                        dvs[c, :, rows:, :] += dv_part.reshape(inner, half, 128)
                        dks[c, :, rows:, :] += dk_part.reshape(inner, half, 128)
                        dqt[at, :] += mm(kft[c, HEAD * (n - 2) : HEAD * (n - 1), :], ds)

            live = first < length
            whole = jnp.where(live, jnp.minimum(z, lax.div(length, span)), 0)
            count = jnp.where(live, jnp.minimum(z + 1, lax.div(length + span - 1, span)), 0)

            def full_step(c, _):
                step(c, False)
                return 0

            def edge_step(c, _):
                step(c, True)
                return 0

            lax.fori_loop(0, whole, full_step, 0)
            lax.fori_loop(whole, count, edge_step, 0)
            parts = []
            for h in range(3):
                a = dqt[HEAD * h : HEAD * h + 32, :] * 0.125
                b = dqt[HEAD * h + 32 : HEAD * h + 64, :] * 0.125
                parts.append(a * cos[z] + b * sin[z])
                parts.append(b * cos[z] - a * sin[z])
            dq[g, z, :rows, :] = jnp.concatenate(parts[:4], 0).T.astype(bf16)
            single = jnp.concatenate(parts[4:], 0)
            dq[g, z, rows:, :] = jnp.concatenate([single[:, :half], single[:, half:]], 0).T.astype(bf16)
            return 0

        lax.fori_loop(0, outer, one, 0)
        for c in range(outer):
            dk[g, c] = dks[c].astype(bf16)
            dv[g, c] = dvs[c].astype(bf16)


def attend_back(lens, q, k, v, do, ot, lse, cos, sin, inner):
    groups, outer, folded, _ = q.shape
    rows = folded * 2 // 3
    span = inner * rows
    vm = IN_VMEM
    return pl.pallas_call(
        functools.partial(attend_back_kernel, outer, inner),
        out_shape=(
            jax.ShapeDtypeStruct(q.shape, bf16),
            jax.ShapeDtypeStruct(k.shape, bf16),
            jax.ShapeDtypeStruct(v.shape, bf16),
        ),
        in_specs=[IN_SMEM] + [vm] * 8,
        out_specs=(vm, vm, vm),
        scratch_shapes=[
            pltpu.VMEM((outer, 128, span), bf16),
            pltpu.VMEM((outer, 128, span // 2), bf16),
            pltpu.VMEM((4, 128, rows), bf16),
            pltpu.VMEM((4, 128, rows), bf16),
            pltpu.VMEM((4, rows, 128), bf16),
            pltpu.VMEM((4, rows, 128), bf16),
            pltpu.VMEM((8, rows), f32),
            pltpu.VMEM((3 * HEAD, rows), f32),
            pltpu.VMEM((outer, inner, folded, 128), f32),
            pltpu.VMEM((outer, inner, folded, 128), f32),
        ],
        compiler_params=params(),
        name="attend_back",
    )(lens, q, k, v, do, ot, lse, cos, sin)


def middle_kernel(batches, outer, inner, *refs):
    refs = list(refs)

    def take(n):
        got = refs[:n]
        del refs[:n]
        return got

    o_mine, out, up, down, tokens, cot, mixture, counts, vecs, lens, mixing = take(11)
    mixed, grad_mine, middle_grad, out_term, up_terms, down_terms, sums = take(7)
    home, sent, attended, middle, low_s, result_s, slope_s, active_s, hidden_s, acc, back, weights = take(12)
    fetch, hs, hr, gs, gr, local = refs
    tall = tokens.shape[0]
    groups = lens.shape[0]
    rows = tall // groups
    here = Place(batches, outer, inner)
    o = here.o
    fetches = [
        carry(down, weights.at[pl.ds(1 + BLOCKS, BLOCKS)], fetch.at[0]),
        carry(out, weights.at[0], fetch.at[1]),
        carry(up, weights.at[pl.ds(1, BLOCKS)], fetch.at[2]),
    ]
    greet(here.z_peers[1:])
    coming, waits = {}, []
    for g in range(groups):
        coming[g] = [carry(o_mine.at[o, g], home.at[o, g], local.at[0, g])]
        for t in range(1, outer):
            coming[g].append(push(o_mine.at[here.zs[t], g], home.at[o, g], hs.at[g, t], hr.at[g, t], here.z_peers[t]))
    count = counts[0, 0:1, 0:1]
    for y in range(1, batches):
        count = count + counts[y, 0:1, 0:1]
    slots = lax.axis_size("batch") * lax.axis_size("seq") * tall
    scale = slots / count.astype(f32)
    row = lax.broadcasted_iota(jnp.int32, (rows, 1), 0) + lax.axis_index("seq") * rows

    def grad_of(g):
        return cot[g * rows : g * rows + rows, :].astype(f32) * jnp.where(row < lens[g], scale, 0.0)

    sums[...] = jnp.zeros(sums.shape, f32)
    for g in range(groups):
        here_rows = slice(g * rows, g * rows + rows)
        result = (mixing[0] * grad_of(g)).astype(bf16)
        result_s[here_rows] = result
        sums[8 + BLOCKS : 9 + BLOCKS] = sums[8 + BLOCKS : 9 + BLOCKS] + jnp.sum(result.astype(f32), 0, keepdims=True)
    fetches[0].wait()

    def early(i, _):
        slope_s[i] = mm_nt(result_s[...], weights[1 + BLOCKS + i])
        return 0

    lax.fori_loop(0, BLOCKS, early, 0)
    for g in range(groups):
        here_rows = slice(g * rows, g * rows + rows)
        for copy in coming[g]:
            copy.wait()
        tiles = unfold_heads(lambda p: home[p, g].astype(f32), rows, outer)
        for i, tile in enumerate(tiles):
            attended[here_rows, 128 * i : 128 * i + 128] = tile.astype(bf16)
        if g == 0:
            fetches[1].wait()
        value = tokens[here_rows].astype(f32) + (mm(attended[here_rows], weights[0]) + vecs[7:8])
        middle[here_rows] = value
        hat, inverse = normalize(value)
        low_s[here_rows] = (hat * vecs[1:2] + vecs[3:4]).astype(bf16)
        acc[here_rows] = jnp.zeros((rows, D), f32)
        back[...] = jnp.zeros((rows, D), f32)
        if g == 0:
            fetches[2].wait()

        def block(i, _):
            hidden = mm(low_s[here_rows], weights[1 + i]) + vecs[pl.ds(8 + i, 1)]
            square = hidden * hidden
            bend = jnp.tanh(0.7978845608028654 * (hidden + 0.044715 * square * hidden))
            half = 0.5 * (1.0 + bend)
            active = (hidden * half).astype(bf16)
            active_s[i, here_rows] = active
            slope = half + 0.5 * hidden * (1.0 - bend * bend) * (0.7978845608028654 * (1.0 + 3.0 * 0.044715 * square))
            hidden_grad = (slope * slope_s[i, here_rows]).astype(bf16)
            hidden_s[i, here_rows] = hidden_grad
            sums[pl.ds(8 + i, 1)] = sums[pl.ds(8 + i, 1)] + jnp.sum(hidden_grad.astype(f32), 0, keepdims=True)
            back[...] += mm_nt(hidden_grad, weights[1 + i])
            acc[here_rows] += mm(active, weights[1 + BLOCKS + i])
            return 0

        lax.fori_loop(0, BLOCKS, block, 0)
        inner_grad = back[...]
        sums[1:2] = sums[1:2] + jnp.sum(inner_grad * hat, 0, keepdims=True)
        sums[3:4] = sums[3:4] + jnp.sum(inner_grad, 0, keepdims=True)
        total_grad = mixing[0] * grad_of(g) + normalize_back(inner_grad, hat, inverse, vecs[1:2])
        middle_grad[here_rows] = total_grad
        branch = total_grad.astype(bf16)
        sums[7:8] = sums[7:8] + jnp.sum(branch.astype(f32), 0, keepdims=True)
        back[...] = mm_nt(branch, weights[0])

        def write(target, value):
            sent[target, g] = value.astype(bf16)

        fold_heads_of(write, lambda t: back[:, 128 * t : 128 * t + 128], outer)
        for t in range(1, outer):
            waits.append(push(sent.at[here.zs[t], g], grad_mine.at[o, g], gs.at[g, t], gr.at[g, t], here.z_peers[t]))
        waits.append(carry(sent.at[o, g], grad_mine.at[o, g], local.at[1, g]))

    low_t = low_s[...].T

    def late(i, _):
        down_terms[i] = mm(active_s[i].T, result_s[...]).astype(bf16)
        up_terms[i] = mm(low_t, hidden_s[i]).astype(bf16)
        return 0

    lax.fori_loop(0, BLOCKS, late, 0)
    out_term[...] = mm(attended[...].T, middle_grad[...].astype(bf16)).astype(bf16)
    for g in range(groups):
        here_rows = slice(g * rows, g * rows + rows)
        layer_out = middle[here_rows] + acc[here_rows] + vecs[8 + BLOCKS : 9 + BLOCKS]
        mixed[here_rows] = (mixture[here_rows] + mixing[0] * layer_out).astype(bf16)
        sums[VECTORS : VECTORS + 1] = sums[VECTORS : VECTORS + 1] + jnp.sum(grad_of(g) * layer_out, 0, keepdims=True)
    for copy in waits:
        copy.wait()


def middle_layer(o_mine, out, up, down, tokens, cot, mixture, counts, vecs, lens, mixing, batches, outer, inner, ident):
    tall = tokens.shape[0]
    groups = lens.shape[0]
    wide = pltpu.VMEM((tall, D), f32)
    low = pltpu.VMEM((tall, D), bf16)
    hidden = pltpu.VMEM((BLOCKS, tall, D), bf16)
    return pl.pallas_call(
        functools.partial(middle_kernel, batches, outer, inner),
        out_shape=(
            jax.ShapeDtypeStruct((tall, D), bf16),
            jax.ShapeDtypeStruct(o_mine.shape, bf16),
            jax.ShapeDtypeStruct((tall, D), f32),
            jax.ShapeDtypeStruct((D, D), bf16),
            jax.ShapeDtypeStruct((BLOCKS, D, D), bf16),
            jax.ShapeDtypeStruct((BLOCKS, D, D), bf16),
            jax.ShapeDtypeStruct((16, D), f32),
        ),
        in_specs=[ANYWHERE] * 4 + [IN_VMEM] * 5 + [IN_SMEM] * 2,
        out_specs=(IN_VMEM, ANYWHERE) + (IN_VMEM,) * 5,
        scratch_shapes=[
            pltpu.VMEM(o_mine.shape, bf16), pltpu.VMEM(o_mine.shape, bf16),
            low, wide, low, low, pltpu.VMEM((BLOCKS, tall, D), f32), hidden, hidden,
            wide, pltpu.VMEM((tall // groups, D), f32),
            pltpu.VMEM((1 + 2 * BLOCKS, D, D), bf16), DMA((3,)),
        ]
        + [DMA((groups, outer))] * 4
        + [DMA((2, groups))],
        compiler_params=remote_params(ident, ROOM),
        name="middle_layer",
    )(o_mine, out, up, down, tokens, cot, mixture, counts, vecs, lens, mixing)


def back_kernel(outer, dq, dk, dv, cosine, sine, normed, tokens, near, vecs, cot, counts, lens, mixing, middle_grad, out_term, sums, dots, input_grad, terms, small, joined, low_t):
    tall = tokens.shape[0]
    groups = lens.shape[0]
    rows = tall // groups
    for g in range(groups):
        for n, source in enumerate((dq, dk, dv)):
            tiles = unfold_heads(lambda p: source[g, p].astype(f32), rows, outer)
            for i, tile in enumerate(tiles):
                if n == 1:
                    tile = turn(tile, cosine[...], -sine[...])
                joined[n, g * rows : g * rows + rows, 128 * i : 128 * i + 128] = tile.astype(bf16)
    low_t[...] = normed[...].T
    small[...] = sums[...]
    back = jnp.zeros((tall, D), f32)
    for n in range(3):
        low = joined[n]
        small[4 + n : 5 + n] = jnp.sum(low.astype(f32), 0, keepdims=True)
        terms[n] = mm(low_t[...], low).astype(bf16)
        back = back + mm_nt(low, near[n])
    terms[3] = out_term[...]
    hat, inverse = normalize(tokens[...].astype(f32))
    small[0:1] = jnp.sum(back * hat, 0, keepdims=True)
    small[2:3] = jnp.sum(back, 0, keepdims=True)
    slots = lax.axis_size("batch") * lax.axis_size("seq") * tall
    count = counts[0, 0:1, 0:1]
    for y in range(1, counts.shape[0]):
        count = count + counts[y, 0:1, 0:1]
    scale = slots / count.astype(f32)
    row = lax.broadcasted_iota(jnp.int32, (rows, 1), 0) + lax.axis_index("seq") * rows
    live = jnp.concatenate([jnp.where(row < lens[g], scale, 0.0) for g in range(groups)], 0)
    grad = cot[...].astype(f32) * live
    input_grad[...] = mixing[1] * grad + middle_grad[...] + normalize_back(back, hat, inverse, vecs[0:1])
    lane = lax.broadcasted_iota(jnp.int32, (1, D), 1)
    line = jnp.where(lane == 0, jnp.sum(sums[VECTORS : VECTORS + 1], 1, keepdims=True), 0.0)
    for i in range(1, mixing.shape[0]):
        line = line + jnp.where(lane == i, scale * jnp.sum(dots[i : i + 1], 1, keepdims=True), 0.0)
    small[VECTORS : VECTORS + 1] = line


def back_layer(dq, dk, dv, cosine, sine, normed, tokens, near, vecs, cot, counts, lens, mixing, middle_grad, out_term, sums, dots, outer):
    tall = tokens.shape[0]
    return pl.pallas_call(
        functools.partial(back_kernel, outer),
        out_shape=(
            jax.ShapeDtypeStruct((tall, D), f32),
            jax.ShapeDtypeStruct((4, D, D), bf16),
            jax.ShapeDtypeStruct((16, D), f32),
        ),
        in_specs=[IN_VMEM] * 11 + [IN_SMEM] * 2 + [IN_VMEM] * 4,
        out_specs=(IN_VMEM,) * 3,
        scratch_shapes=[pltpu.VMEM((3, tall, D), bf16), pltpu.VMEM((D, tall), bf16)],
        compiler_params=params(),
        name="back_layer",
    )(dq, dk, dv, cosine, sine, normed, tokens, near, vecs, cot, counts, lens, mixing, middle_grad, out_term, sums, dots)


def adam(param, grad, first, second, decay):
    first_new = beta_one * first + (1.0 - beta_one) * grad
    second_new = beta_two * second + (1.0 - beta_two) * grad * grad
    fix_one = 1.0 - beta_one**adam_step
    fix_two = 1.0 - beta_two**adam_step
    update = first_new / fix_one / (jnp.sqrt(second_new / fix_two) + adam_eps)
    return (-learn_rate * (update + decay * param), first_new)


def adam_kernel(packed, near, up, down, out, *refs):
    given, results = refs[:12], refs[12:]
    for n in range(4):
        param, first, second = given[3 * n : 3 * n + 3]
        grad_out, step_out, first_out = results[3 * n : 3 * n + 3]
        for i in range(param.shape[1] // D):
            lanes = slice(i * D, i * D + D)
            if n == 0 and packed:
                grad = jnp.concatenate(plain_tiles(lambda z: near[z], i, near.shape[0]), 1)
            else:
                grad = near[i] if n == 0 else out[...] if n == 1 else up[i] if n == 2 else down[...]
            grad_out[:, lanes] = grad
            step_out[:, lanes], first_out[:, lanes] = adam(param[:, lanes], grad, first[:, lanes], second[:, lanes], decay_rate)


def adam_all(packed, near, up, down, out, given):
    shapes = []
    for n in range(4):
        shapes += [jax.ShapeDtypeStruct(given[3 * n].shape, f32)] * 3
    return pl.pallas_call(
        functools.partial(adam_kernel, packed),
        out_shape=tuple(shapes),
        in_specs=[IN_VMEM] * 16,
        out_specs=(IN_VMEM,) * 12,
        compiler_params=params(),
        name="adam_all",
    )(near, up, down, out, *given)


def summed(into, index, more, other):
    into[index] = (into[index].astype(f32) + more[other].astype(f32)).astype(bf16)


def fold_kernel(batches, inner, dq, dk, dv, dq_all, dk_all, dv_all, cbuf, xbuf, done, qs, qr, zs, zr, xs, xr, cs, cr, local):
    outer = dq.shape[1]
    across = inner // 2
    here = Place(batches, outer, inner)
    o, a, c = here.o, here.a, here.c
    greet(here.z_peers[1:] + here.x_peers[1:] + [here.twin])
    waits = [carry(dq.at[:, o], dq_all.at[:, o], local.at[0])]
    given = (dk, dv)
    results = (dk_all, dv_all)
    order = [t % outer for t in range(1, outer + 1)]
    xorder = list(range(1, across)) + [0]
    to_twin, over = {}, {}
    for t in order:
        for i in (0, 1):
            for d in xorder:
                z, x = here.zs[t], here.xs[d]
                to_twin[i, t, d] = push(given[i].at[:, z, x * 2 + 1 - c], cbuf.at[i, z, x], cs.at[i, t, d], cr.at[i, t, d], here.twin)
    for t in range(1, outer):
        waits.append(push(dq.at[:, here.zs[t]], dq_all.at[:, o], qs.at[t], qr.at[t], here.z_peers[t]))
    for t in order:
        for i in (0, 1):
            for d in xorder:
                to_twin[i, t, d].wait()
                z, x = here.zs[t], here.xs[d]
                for g in range(dq.shape[0]):
                    summed(cbuf, (i, z, x, g), given[i], (g, z, x * 2 + c))
                if d:
                    over[i, t, d] = push(cbuf.at[i, z, x], xbuf.at[i, z, d], xs.at[i, t, d], xr.at[i, t, d], here.x_peers[d])
    for t in order:
        for i in (0, 1):
            z = here.zs[t]
            total = cbuf[i, z, a].astype(f32)
            for d in range(1, across):
                over[i, t, d].wait()
                total = total + xbuf[i, z, d].astype(f32)
            done[i, z] = total.astype(bf16)
            if t:
                waits.append(push(done.at[i, z], results[i].at[:, o], zs.at[i, t], zr.at[i, t], here.z_peers[t]))
            else:
                waits.append(carry(done.at[i, z], results[i].at[:, o], local.at[1 + i]))
    for copy in waits:
        copy.wait()


def fold_heads(dq, dk, dv, batches, inner, ident):
    groups, outer = dq.shape[:2]
    tail = (groups,) + dq.shape[2:]
    across = inner // 2
    piece = jax.ShapeDtypeStruct(dq.shape, dq.dtype)
    scratch = [pltpu.VMEM((2, outer, across) + tail, bf16)] * 2 + [pltpu.VMEM((2, outer) + tail, bf16)]
    scratch += [DMA((outer,))] * 2 + [DMA((2, outer))] * 2 + [DMA((2, outer, across))] * 4 + [DMA((3,))]
    return pl.pallas_call(
        functools.partial(fold_kernel, batches, inner),
        out_shape=(piece, piece, piece),
        in_specs=[ANYWHERE] + [IN_VMEM] * 2,
        out_specs=(ANYWHERE,) * 3,
        scratch_shapes=scratch,
        compiler_params=remote_params(ident, ROOM),
        name="fold_heads",
    )(dq, dk, dv)


def finish_kernel(batches, outer, inner, *refs):
    refs = list(refs)

    def take(n):
        got = refs[:n]
        del refs[:n]
        return got

    dq, dk, dv, up_terms, down_terms, out_terms, mine, normed, tokens, cot, middle_grad = take(11)
    counts, vecs, sums, dots, cos_t, sin_t, lens, mixing = take(8)
    input_grad, near_out, up_out, down_out, out_out, small_out = take(6)
    cosine, sine, gm, gt, gx, partial, from_left, from_right, weight_grad = take(9)
    rm, rt, ry, rx, rz = take(3), take(3), take(3), take(3), take(3)
    terms_n, nc, na, ny, nx, nz, kept, kept_out, kept_n = take(9)
    small, sc, sx, sy, sz = take(5)
    gls, gcs, gcr, gxs, gxr, hrs, hrr, hls, hlr = take(9)
    rls, rcs, rcr, rys, ryr, rxs, rxr, rzs, rzr = take(9)
    ncs, ncr, nys, nyr, nxs, nxr, nzs, nzr, fs, fr, ss, sr = refs
    across = inner // 2
    here = Place(batches, outer, inner)
    o, a, b, c, j = here.o, here.a, here.batch, here.c, here.j
    tall = tokens.shape[0]
    groups = lens.shape[0]
    rows = tall // groups
    share = down_out.shape[0] // BLOCKS
    table = [sorted((s for s in range(outer) if s != i), key=lambda s: (abs(s - i), s)) + [i] for i in range(outer)]
    give, keep = lane_half(1 - c), lane_half(c)

    def layer(n):
        if n == outer - 1:
            return o
        found = 0
        for i in range(outer):
            found = found + (o == i).astype(jnp.int32) * table[i][outer - 2 - n]
        return found

    for z in range(outer):
        cosine[z] = jnp.concatenate([cos_t[z]] * 4, 0).T
        sine[z] = jnp.concatenate([-sin_t[z], sin_t[z]] * 2, 0).T
    greet(here.z_peers[1:] + here.x_peers[1:] + here.y_peers[1:] + [here.twin])
    given = (dk, dv)
    over = {}
    order = [(g, n) for g in range(groups) for n in range(outer)]

    def give_piece(g, n):
        s = layer(n)
        for i in (0, 1):
            for d in range(across):
                x = here.xs[d]
                over["own", g, n, i, d] = carry(given[i].at[g, s, x * 2 + c], gm.at[g, n, i, d], gls.at[g, n, i, d])
                over["twin", g, n, i, d] = push(
                    given[i].at[g, s, x * 2 + 1 - c], gt.at[g, n, i, d], gcs.at[g, n, i, d], gcr.at[g, n, i, d], here.twin
                )

    def theirs(i, y, x, core):
        if i == 0:
            return up_terms.at[pl.ds(2 * core, 2), y, :, x]
        if i == 1:
            return down_terms.at[y, :, x, core]
        return out_terms.at[y, :, x, :, lane_half(core)]

    corners = [(dy, dx) for dy in list(range(1, batches)) + [0] for dx in list(range(1, across)) + [0]]

    def give_rest(dy, dx):
        y, x = here.ys[dy], here.xs[dx]
        for i in range(3):
            over["rown", i, dy, dx] = carry(theirs(i, y, x, c), rm[i].at[dy, dx], rls.at[i, dy, dx])
            over["rtwin", i, dy, dx] = push(
                theirs(i, y, x, 1 - c), rt[i].at[dy, dx], rcs.at[i, dy, dx], rcr.at[i, dy, dx], here.twin
            )

    for n in range(outer):
        give_piece(0, n)
        if n < len(corners):
            give_rest(*corners[n])
    for corner in corners[outer:]:
        give_rest(*corner)
    for n in range(outer):
        give_piece(1, n)

    def fold_core(g, n):
        for i in (0, 1):
            for d in list(range(1, across)) + [0]:
                over["own", g, n, i, d].wait()
                over["twin", g, n, i, d].wait()
                gm[g, n, i, d] = (gm[g, n, i, d].astype(f32) + gt[g, n, i, d].astype(f32)).astype(bf16)
                if d:
                    over["x", g, n, i, d] = push(
                        gm.at[g, n, i, d], gx.at[g, n, i, d], gxs.at[g, n, i, d], gxr.at[g, n, i, d], here.x_peers[d]
                    )

    small[...] = jnp.zeros(small.shape, f32)
    small[0:16] = sums[...]
    weight_grad[...] = jnp.zeros(weight_grad.shape, f32)
    lane = lax.broadcasted_iota(jnp.int32, (rows, 128), 1)

    def halves(value):
        return value[:rows], jnp.where(lane < HEAD, unfold_single(value[rows:], False), 0.0)

    def piece(g, n):
        s = layer(n)
        totals = [dq[g, s].astype(f32)]
        for i in (0, 1):
            total = gm[g, n, i, 0].astype(f32)
            for d in range(1, across):
                over["x", g, n, i, d].wait()
                total = total + gx[g, n, i, d].astype(f32)
            totals.append(total)
        pairs, singles = [], []
        for i, total in enumerate(totals):
            pair, single = halves(total)
            if i == 1:
                pair, single = turn(pair, cosine[s], -sine[s]), turn(single, cosine[s], -sine[s])
                single = jnp.where(lane < HEAD, single, 0.0)
            pairs.append(pair)
            singles.append(single)
        joined = jnp.concatenate(pairs + singles, 1).astype(bf16)
        small[pl.ds(16 + o, 1)] = small[pl.ds(16 + o, 1)] + jnp.sum(joined.astype(f32), 0, keepdims=True)
        partial[g, n] = mm_nt(joined, mine[...].reshape(D, D)).astype(bf16)
        weight_grad[...] += mm(normed[g, s].T, joined)

    line_sends = []

    def hand(g, n):
        if n == outer - 1:
            return
        s = layer(n)
        for buf, sends, recvs, step, outside, away in (
            (from_left, hrs, hrr, 1, o > 0, o < s),
            (from_right, hls, hlr, -1, o < outer - 1, o > s),
        ):
            to = jnp.clip(o + step, 0, outer - 1)
            copy = pltpu.make_async_remote_copy(
                src_ref=buf.at[g, s],
                dst_ref=buf.at[g, s],
                send_sem=sends.at[g, s],
                recv_sem=recvs.at[g, s],
                device_id=(b, to * inner + j),
                device_id_type=MESH,
            )

            @pl.when(away & outside)
            def _(copy=copy, buf=buf):
                copy.wait_recv()
                buf[g, s] = (buf[g, s].astype(f32) + partial[g, n].astype(f32)).astype(bf16)

            @pl.when(away & jnp.logical_not(outside))
            def _(buf=buf):
                buf[g, s] = partial[g, n]

            @pl.when(away)
            def _(copy=copy):
                copy.start()

            line_sends.append((away, copy))

    slots = lax.axis_size("batch") * lax.axis_size("seq") * tall
    count = counts[0, 0:1, 0:1]
    for y in range(1, batches):
        count = count + counts[y, 0:1, 0:1]
    scale = slots / count.astype(f32)
    row = lax.broadcasted_iota(jnp.int32, (rows, 1), 0) + lax.axis_index("seq") * rows

    def arrive(g):
        back = partial[g, outer - 1].astype(f32)
        for buf, recvs, outside in ((from_left, hrr, o > 0), (from_right, hlr, o < outer - 1)):
            copy = pltpu.make_async_remote_copy(
                src_ref=buf.at[g, o],
                dst_ref=buf.at[g, o],
                send_sem=hrs.at[g, o],
                recv_sem=recvs.at[g, o],
                device_id=here.twin,
                device_id_type=MESH,
            )

            @pl.when(outside)
            def _(copy=copy):
                copy.wait_recv()

            back = back + jnp.where(outside, buf[g, o].astype(f32), 0.0)
        at = slice(g * rows, g * rows + rows)
        hat, inverse = normalize(tokens[at].astype(f32))
        small[0:1] = small[0:1] + jnp.sum(back * hat, 0, keepdims=True)
        small[2:3] = small[2:3] + jnp.sum(back, 0, keepdims=True)
        grad = cot[at].astype(f32) * jnp.where(row < lens[g], scale, 0.0)
        input_grad[at] = mixing[1] * grad + middle_grad[at] + normalize_back(back, hat, inverse, vecs[0:1])

    def each(i, add):
        if i == 0:

            def one(n, _):
                add((lax.div(n, outer), lax.rem(n, outer)))
                return 0

            lax.fori_loop(0, 2 * outer, one, 0)
        else:

            def one(z, _):
                add((z,))
                return 0

            lax.fori_loop(0, outer, one, 0)

    def plus(into, at, more, other):
        into[at] = (into[at].astype(f32) + more[other].astype(f32)).astype(bf16)

    def rest_core(dy, dx):
        for i in range(3):
            over["rown", i, dy, dx].wait()
            over["rtwin", i, dy, dx].wait()
            each(i, lambda at: plus(rm[i], (dy, dx) + at, rt[i], (dy, dx) + at))
            if dy:
                over["ry", i, dy, dx] = push(
                    rm[i].at[dy, dx], ry[i].at[dy - 1, dx], rys.at[i, dy, dx], ryr.at[i, dy, dx], here.y_peers[dy]
                )

    def rest_y(dx):
        for i in range(3):
            for dy in range(1, batches):
                over["ry", i, dy, dx].wait()
                each(i, lambda at: plus(rm[i], (0, dx) + at, ry[i], (dy - 1, dx) + at))
            if dx:
                over["rx", i, dx] = push(rm[i].at[0, dx], rx[i].at[dx - 1], rxs.at[i, dx], rxr.at[i, dx], here.x_peers[dx])

    def line_piece(i, z):
        return rm[i].at[0, 0, :, z] if i == 0 else rm[i].at[0, 0, z]

    def rest_x():
        for i in range(3):
            for d in range(1, across):
                over["rx", i, d].wait()
                each(i, lambda at: plus(rm[i], (0, 0) + at, rx[i], (d - 1,) + at))
            for t in range(1, outer):
                over["rz", i, t] = push(line_piece(i, here.zs[t]), rz[i].at[t], rzs.at[i, t], rzr.at[i, t], here.z_peers[t])

    ends = []

    def rest_last():
        for i in range(3):
            for t in range(1, outer):
                over["rz", i, t].wait()
        for p in (0, 1):
            total = rm[0][0, 0, p, o].astype(f32)
            for t in range(1, outer):
                total = total + rz[0][t, p].astype(f32)
            kept[p] = total
        total, total_out = rm[1][0, 0, o].astype(f32), rm[2][0, 0, o].astype(f32)
        for t in range(1, outer):
            total = total + rz[1][t].astype(f32)
            total_out = total_out + rz[2][t].astype(f32)
        down_out[...] = total
        kept_out[...] = total_out
        theirs_rows = pl.ds(pl.multiple_of(share * (1 - c), 8), share)
        ends.append(push(kept.at[:, theirs_rows], up_out.at[pl.ds(2 * c, 2)], fs.at[0], fr.at[0], here.twin))
        ends.append(push(kept_out.at[theirs_rows], out_out.at[:, keep], fs.at[1], fr.at[1], here.twin))
        for p in (0, 1):
            value = kept[p]
            up_out[2 * c + p] = jnp.where(c == 0, value[:share], value[share:])
        value = kept_out[...]
        out_out[:, keep] = jnp.where(c == 0, value[:share], value[share:])

    events = [functools.partial(rest_core, *corner) for corner in corners]
    events += [functools.partial(rest_y, dx) for dx in list(range(1, across)) + [0]] + [rest_x]

    def event():
        if events:
            events.pop(0)()

    fold_core(*order[0])
    event()
    fold_core(*order[1])
    event()
    for n, at in enumerate(order):
        piece(*at)
        if n + 2 < len(order):
            fold_core(*order[n + 2])
        if n >= 1:
            hand(*order[n - 1])
        if n in (1, 3, 5, 6, 7):
            event()
    hand(*order[-1])

    terms_n[...] = weight_grad[...].reshape(terms_n.shape).astype(bf16)
    near_core = push(terms_n.at[:, :, :, :, give], nc, ncs, ncr, here.twin)
    while events:
        event()
    arrive(0)
    near_core.wait()

    def fold_near(i, _):
        y, z, x = lax.div(i, outer * across), lax.rem(lax.div(i, across), outer), lax.rem(i, across)
        value = terms_n[y, z, x]
        own_half = jnp.where(c == 0, value[:, : D // 2], value[:, D // 2 :])
        na[y, z, x] = (own_half.astype(f32) + nc[y, z, x].astype(f32)).astype(bf16)
        return 0

    lax.fori_loop(0, batches * outer * across, fold_near, 0)
    near_y = [push(na.at[here.ys[d]], ny.at[d - 1], nys.at[d], nyr.at[d], here.y_peers[d]) for d in range(1, batches)]
    rest_last()
    for d in range(1, batches):
        near_y[d - 1].wait()

        def add_y(i, _):
            z, x = lax.div(i, across), lax.rem(i, across)
            plus(na, (b, z, x), ny, (d - 1, z, x))
            return 0

        lax.fori_loop(0, outer * across, add_y, 0)
    near_x = [
        push(na.at[b, :, here.xs[d]], nx.at[d - 1], nxs.at[d], nxr.at[d], here.x_peers[d]) for d in range(1, across)
    ]
    arrive(1)
    lane_wide = lax.broadcasted_iota(jnp.int32, (1, D), 1)
    line = jnp.where(lane_wide == 0, jnp.sum(sums[VECTORS : VECTORS + 1], 1, keepdims=True), 0.0)
    for i in range(1, mixing.shape[0]):
        line = line + jnp.where(lane_wide == i, scale * jnp.sum(dots[i : i + 1], 1, keepdims=True), 0.0)
    small[VECTORS : VECTORS + 1] = line
    small_copy = push(small, sc, ss.at[0], sr.at[0], here.twin)
    for d in range(1, across):
        near_x[d - 1].wait()

        def add_x(z, _):
            plus(na, (b, z, a), nx, (d - 1, z))
            return 0

        lax.fori_loop(0, outer, add_x, 0)
    near_z = [push(na.at[b, here.zs[t], a], nz.at[o], nzs.at[t], nzr.at[t], here.z_peers[t]) for t in range(1, outer)]
    nz[o] = na[b, o, a]
    small_copy.wait()
    sc[...] = sc[...] + small[...]
    sx[a] = sc[...]
    copies = [push(sc, sx.at[a], ss.at[d], sr.at[d], here.x_peers[d]) for d in range(1, across)]
    for copy in copies:
        copy.wait()
    total = sx[0]
    for x in range(1, across):
        total = total + sx[x]
    sc[...] = total
    sy[b] = total
    copies = [push(sc, sy.at[b], ss.at[across + d], sr.at[across + d], here.y_peers[d]) for d in range(1, batches)]
    for copy in near_z:
        copy.wait()
    for z in range(outer):
        kept_n[z] = nz[z].astype(f32)
    theirs_rows = pl.ds(pl.multiple_of(share * (1 - c), 8), share)
    ends.append(push(kept_n.at[:, theirs_rows], near_out.at[:, :, keep], fs.at[2], fr.at[2], here.twin))
    for z in range(outer):
        value = kept_n[z]
        near_out[z, :, keep] = jnp.where(c == 0, value[:share], value[share:])
    for copy in copies:
        copy.wait()
    total = sy[0]
    for y in range(1, batches):
        total = total + sy[y]
    sc[...] = total
    sz[o] = total
    copies = [
        push(sc, sz.at[o], ss.at[across + batches + t], sr.at[across + batches + t], here.z_peers[t]) for t in range(1, outer)
    ]
    for copy in copies:
        copy.wait()
    total = sz[0]
    for z in range(1, outer):
        total = total + sz[z]
    small_out[...] = total[:16]
    for n in range(3):
        small_out[4 + n : 5 + n] = jnp.concatenate(plain_tiles(lambda z: total[16 + z : 17 + z], n, outer), 1)
    for copy in ends:
        copy.wait()
    for away, copy in line_sends:

        @pl.when(away)
        def _(copy=copy):
            copy.wait_send()


def plain_tiles(read, n, outer):
    tiles = []
    for z in range(0, outer, 2):
        even, odd = read(z), read(z + 1)
        pair, single = slice(128 * n, 128 * n + 128), slice(384 + 128 * n, 512 + 128 * n)
        lane = lax.broadcasted_iota(jnp.int32, even[:, single].shape, 1)
        middle = jnp.where(lane < HEAD, even[:, single], pltpu.roll(odd[:, single], HEAD, 1))
        tiles += [even[:, pair], middle, odd[:, pair]]
    return tiles


def finish_layer(
    dq, dk, dv, up_terms, down_terms, out_terms, mine, normed, tokens, cot, middle_grad, counts, vecs, sums, dots, cos_t, sin_t,
    lens, mixing, batches, outer, inner, ident,
):
    across = inner // 2
    tall = tokens.shape[0]
    groups = lens.shape[0]
    rows = tall // groups
    folded = dq.shape[2]
    wide = out_terms.shape[3]
    share = wide // 2
    low = lambda *shape: pltpu.VMEM(shape, bf16)
    full = lambda *shape: pltpu.VMEM(shape, f32)
    tails = ((2, outer, wide, D), (outer, BLOCKS * share, D), (outer, wide, D // 2))
    ends = ((2, wide, D), (BLOCKS * share, D), (wide, D // 2))
    grid = (batches, outer, across)
    scratch = [
        full(outer, rows, 128),
        full(outer, rows, 128),
        low(groups, outer, 2, across, folded, 128),
        low(groups, outer, 2, across, folded, 128),
        low(groups, outer, 2, across, folded, 128),
        low(groups, outer, rows, D),
        low(groups, outer, rows, D),
        low(groups, outer, rows, D),
        full(D, D),
    ]
    scratch += [low(batches, across, *tail) for tail in tails]
    scratch += [low(batches, across, *tail) for tail in tails]
    scratch += [low(batches - 1, across, *tail) for tail in tails]
    scratch += [low(across - 1, *tail) for tail in tails]
    scratch += [low(outer, *end) for end in ends]
    scratch += [
        low(*grid, wide, D),
        low(*grid, wide, D // 2),
        low(*grid, wide, D // 2),
        low(batches - 1, outer, across, wide, D // 2),
        low(across - 1, outer, wide, D // 2),
        low(outer, wide, D // 2),
        full(2, wide, D),
        full(wide, D // 2),
        full(outer, wide, D // 2),
        full(24, D),
        full(24, D),
        full(across, 24, D),
        full(batches, 24, D),
        full(outer, 24, D),
    ]
    scratch += [DMA((groups, outer, 2, across))] * 5 + [DMA((groups, outer))] * 4
    scratch += [DMA((3, batches, across))] * 5 + [DMA((3, across))] * 2 + [DMA((3, outer))] * 2
    scratch += [DMA] * 2 + [DMA((batches,))] * 2 + [DMA((across,))] * 2 + [DMA((outer,))] * 2 + [DMA((3,))] * 2
    scratch += [DMA((across + batches + outer,))] * 2
    return pl.pallas_call(
        functools.partial(finish_kernel, batches, outer, inner),
        out_shape=(
            jax.ShapeDtypeStruct((tall, D), f32),
            jax.ShapeDtypeStruct((outer, share, D), f32),
            jax.ShapeDtypeStruct((BLOCKS, share, D), f32),
            jax.ShapeDtypeStruct((BLOCKS * share, D), f32),
            jax.ShapeDtypeStruct((share, D), f32),
            jax.ShapeDtypeStruct((16, D), f32),
        ),
        in_specs=[IN_VMEM] + [ANYWHERE] * 5 + [IN_VMEM] * 11 + [IN_SMEM] * 2,
        out_specs=(IN_VMEM,) * 6,
        scratch_shapes=scratch,
        compiler_params=remote_params(ident, 60 << 20),
        name="finish_layer",
    )(
        dq, dk, dv, up_terms, down_terms, out_terms, mine, normed, tokens, cot, middle_grad, counts, vecs, sums, dots, cos_t, sin_t,
        lens, mixing,
    )


def body(
    tokens_in,
    earlier_outs,
    out_cotangent,
    seq_lengths,
    qkv_weight,
    out_weight,
    up_weight,
    down_weight,
    qkv_first,
    qkv_second,
    out_first,
    out_second,
    up_first,
    up_second,
    down_first,
    down_second,
    small_params,
    small_first,
    small_second,
):
    groups, rows, _ = tokens_in.shape
    tall = groups * rows
    batches = lax.axis_size("batch")
    seq_count = lax.axis_size("seq")
    seq_rank = lax.axis_index("seq")
    devices = batches * seq_count
    outer = math.gcd(seq_count, D // HEAD)
    inner = seq_count // outer
    share = D // devices
    remote = share % 8 == 0
    everywhere = ("batch", "seq")
    grid = (batches, outer, inner // 2)

    tokens = tokens_in.reshape(tall, D)
    cot = out_cotangent.reshape(tall, D)
    earlier = earlier_outs.reshape(-1, tall, D)
    vecs = jnp.pad(small_params[: VECTORS * D].reshape(VECTORS, D), ((0, 16 - VECTORS), (0, 0)))
    mixing = small_params[VECTORS * D :]

    freq = 10000.0 ** (-jnp.arange(HEAD // 2, dtype=f32) * 2.0 / HEAD)
    query_pos = seq_rank * rows + jnp.arange(rows, dtype=jnp.int32)
    turned = query_pos.astype(f32)[:, None] * freq[None, :]
    cosine = jnp.concatenate([jnp.cos(turned)] * 4, 1)
    sine = jnp.concatenate([-jnp.sin(turned), jnp.sin(turned)] * 2, 1)
    block_pos = (jnp.arange(outer) * inner + seq_rank % inner)[:, None] * rows + jnp.arange(rows)[None, :]
    block_turned = block_pos.astype(f32)[:, None, :] * freq[None, :, None]
    block_cos, block_sin = jnp.cos(block_turned), jnp.sin(block_turned)

    def by_rows(shard):
        return shard.astype(bf16).reshape(share, -1, D).transpose(1, 0, 2)

    def by_blocks(gathered):
        return gathered.transpose(1, 0, 2, 3).reshape(-1, D, D)

    if remote:
        packed_bias = jnp.stack([
            jnp.concatenate(packed_rows(small_params[4 * D : 7 * D], z)) for z in range(outer)
        ])
        packed_bias = jnp.pad(packed_bias, ((0, 8 - outer), (0, 0)))
        mine, normed, q, k, v, out, up, down, counts, mixture, dots, attended, turned_out, log_total = start_layer(
            qkv_weight, out_weight, up_weight, down_weight, seq_lengths, mixing, tokens, cot, earlier, vecs, packed_bias,
            block_cos, block_sin, batches, outer, inner, 1,
        )
        out, up, down = out.reshape(D, D), up.reshape(BLOCKS, D, D), down.reshape(BLOCKS, D, D)
    else:
        near = by_blocks(lax.all_gather(jnp.concatenate([by_rows(qkv_weight), by_rows(out_weight)], 0), everywhere, axis=0))
        out = near[3]
        up = by_blocks(lax.all_gather(by_rows(up_weight), everywhere, axis=0))
        down = lax.all_gather(down_weight.astype(bf16), everywhere, axis=0).reshape(BLOCKS, D, D)
        counts = jnp.full((1, 8, 128), lax.psum(jnp.sum(seq_lengths), "batch"), jnp.int32)
        wide = tokens.astype(f32)
        normed = (normalize(wide)[0] * vecs[0] + vecs[2]).astype(bf16)
        live = (query_pos[None, :] < seq_lengths[:, None]).astype(f32).reshape(tall, 1)
        terms = [tokens] + [earlier[i] for i in range(earlier.shape[0])]
        mixture = sum(mixing[1 + i] * term.astype(f32) for i, term in enumerate(terms))
        sums = [jnp.sum(cot.astype(f32) * live * term.astype(f32), 0) for term in terms]
        dots = jnp.pad(jnp.stack(sums), ((1, 15 - len(sums)), (0, 0)))
        q, k, v, attended, turned_out, log_total = spread_heads(
            normed, near, vecs, seq_lengths, cosine, sine, batches, outer, inner, 2
        )

    mixed, grad_mine, middle_grad, out_term, up_terms, down_terms, sums = middle_layer(
        attended, out, up, down, tokens, cot, mixture, counts, vecs, seq_lengths, mixing, batches, outer, inner, 3
    )
    dq, dk, dv = attend_back(seq_lengths, q, k, v, grad_mine, turned_out, log_total, block_cos, block_sin, inner)
    if remote:
        pieces = grid + (2 * share, D)
        input_grad, near_grad, up_grad, down_grad, out_grad, small = finish_layer(
            dq, dk, dv, up_terms.reshape((BLOCKS,) + pieces), down_terms.reshape(grid + (2, BLOCKS * share, D)), out_term.reshape(pieces),
            mine, normed, tokens, cot, middle_grad, counts, vecs, sums, dots, block_cos, block_sin, seq_lengths, mixing,
            batches, outer, inner, 4,
        )
    else:

        def scattered(terms):
            return lax.psum_scatter(terms.reshape(-1, devices, share, D), everywhere, scatter_dimension=1).astype(f32)

        dq, dk, dv = fold_heads(dq, dk, dv, batches, inner, 5)
        input_grad, near_terms, small = back_layer(
            dq, dk, dv, cosine, sine, normed, tokens, near, vecs, cot, counts, seq_lengths, mixing, middle_grad, out_term, sums, dots, outer
        )
        near_grad, up_grad = scattered(near_terms), scattered(up_terms)
        out_grad = near_grad[3]
        down_grad = lax.psum_scatter(down_terms.reshape(devices, -1, D), everywhere, scatter_dimension=0).astype(f32)
        small = lax.psum(small, everywhere)
    small_grad = small.reshape(-1)[: small_params.shape[0]]
    small_step, small_first_new = adam(small_params, small_grad, small_first, small_second, 0.0)
    (
        qkv_grad, qkv_step, qkv_first_new, out_grad, out_step, out_first_new,
        up_grad, up_step, up_first_new, down_grad, down_step, down_first_new,
    ) = adam_all(
        remote, near_grad, up_grad, down_grad, out_grad,
        (qkv_weight, qkv_first, qkv_second, out_weight, out_first, out_second,
         up_weight, up_first, up_second, down_weight, down_first, down_second),
    )
    return (
        mixed.reshape(tokens_in.shape),
        input_grad.reshape(tokens_in.shape),
        qkv_grad,
        out_grad,
        up_grad,
        down_grad,
        small_grad,
        qkv_step,
        out_step,
        up_step,
        down_step,
        small_step,
        qkv_first_new,
        out_first_new,
        up_first_new,
        down_first_new,
        small_first_new,
    )


def solution(mesh):
    placed = (
        P("batch", "seq", None),
        P(None, "batch", "seq", None),
        P("batch", "seq", None),
        P("batch"),
        P(("batch", "seq"), None),
        P(("batch", "seq"), None),
        P(("batch", "seq"), None),
        P(("batch", "seq"), None),
        P(("batch", "seq"), None),
        P(("batch", "seq"), None),
        P(("batch", "seq"), None),
        P(("batch", "seq"), None),
        P(("batch", "seq"), None),
        P(("batch", "seq"), None),
        P(("batch", "seq"), None),
        P(("batch", "seq"), None),
        P(),
        P(),
        P(),
    )
    return jax.shard_map(
        body,
        mesh=mesh,
        in_specs=placed,
        out_specs=(
            P("batch", "seq", None),
            P("batch", "seq", None),
            P(("batch", "seq"), None),
            P(("batch", "seq"), None),
            P(("batch", "seq"), None),
            P(("batch", "seq"), None),
            P(),
            P(("batch", "seq"), None),
            P(("batch", "seq"), None),
            P(("batch", "seq"), None),
            P(("batch", "seq"), None),
            P(),
            P(("batch", "seq"), None),
            P(("batch", "seq"), None),
            P(("batch", "seq"), None),
            P(("batch", "seq"), None),
            P(),
        ),
        check_vma=False,
    )
```

```python
import functools
import math

import jax
import jax.numpy as jnp
from jax import lax
from jax.experimental import pallas as pl
from jax.experimental.pallas import tpu as pltpu
from jax.sharding import PartitionSpec as P

D = 768
FF = 3072
HEAD = 64
BLOCKS = FF // D
VECTORS = 9 + BLOCKS
bf16 = jnp.bfloat16
f32 = jnp.float32
NEG = -1e30

beta_one = 0.9
beta_two = 0.999
adam_eps = 1e-08
learn_rate = 0.01
decay_rate = 0.1
adam_step = 10

MESH = pl.DeviceIdType.MESH
ANYWHERE = pl.BlockSpec(memory_space=pl.ANY)
IN_VMEM = pl.BlockSpec(memory_space=pltpu.VMEM)
IN_SMEM = pl.BlockSpec(memory_space=pltpu.SMEM)
DMA = pltpu.SemaphoreType.DMA
ROOM = 56 << 20

def mm(a, b):
    return lax.dot_general(a, b, (((1,), (0,)), ((), ())), preferred_element_type=f32)


def mm_nt(a, b):
    return lax.dot_general(a, b, (((1,), (1,)), ((), ())), preferred_element_type=f32)


def params():
    return pltpu.CompilerParams(vmem_limit_bytes=ROOM)


def remote_params(ident, vmem=None):
    return pltpu.CompilerParams(collective_id=ident, has_side_effects=True, vmem_limit_bytes=vmem)


class Place:
    def __init__(self, batches, outer, inner):
        self.batch = lax.axis_index("batch")
        rank = lax.axis_index("seq")
        self.o = lax.div(rank, inner)
        self.j = lax.rem(rank, inner)
        self.a = lax.div(self.j, 2)
        self.c = lax.rem(rank, 2)
        across = inner // 2
        self.zs = [lax.rem(self.o + t, outer) for t in range(outer)]
        self.xs = [lax.rem(self.a + t, across) for t in range(across)]
        self.ys = [lax.rem(self.batch + t, batches) for t in range(batches)]
        self.z_from = [lax.rem(self.o + outer - t, outer) for t in range(outer)]
        self.x_from = [lax.rem(self.a + across - t, across) for t in range(across)]
        self.y_from = [lax.rem(self.batch + batches - t, batches) for t in range(batches)]
        self.z_peers = [(self.batch, z * inner + self.j) for z in self.zs]
        self.x_peers = [(self.batch, self.o * inner + x * 2 + self.c) for x in self.xs]
        self.y_peers = [(y, rank) for y in self.ys]
        self.twin = (self.batch, self.o * inner + self.a * 2 + (1 - self.c))


def greet(peers):
    barrier = pltpu.get_barrier_semaphore()
    for peer in peers:
        pl.semaphore_signal(barrier, inc=1, device_id=peer, device_id_type=MESH)
    pl.semaphore_wait(barrier, len(peers))


def push(src, dst, send, recv, peer):
    copy = pltpu.make_async_remote_copy(
        src_ref=src, dst_ref=dst, send_sem=send, recv_sem=recv, device_id=peer, device_id_type=MESH
    )
    copy.start()
    return copy


def carry(src, dst, sem):
    copy = pltpu.make_async_copy(src, dst, sem)
    copy.start()
    return copy


def normalize(values):
    center = values - jnp.mean(values, -1, keepdims=True)
    inverse = lax.rsqrt(jnp.mean(center * center, -1, keepdims=True) + 1e-05)
    return center * inverse, inverse


def normalize_back(grad, hat, inverse, gain):
    scaled = grad * gain
    part = scaled - jnp.mean(scaled, -1, keepdims=True) - hat * jnp.mean(scaled * hat, -1, keepdims=True)
    return part * inverse


def turn(value, cosine, sine):
    lane = lax.broadcasted_iota(jnp.int32, value.shape, 1)
    other = jnp.where(lax.rem(lane, HEAD) < HEAD // 2, pltpu.roll(value, 128 - HEAD // 2, 1), pltpu.roll(value, HEAD // 2, 1))
    return value * cosine + other * sine


def fold_single(value, odd):
    half = value.shape[0] // 2
    top, bottom = value[:half], value[half:]
    lane = lax.broadcasted_iota(jnp.int32, top.shape, 1)
    if odd:
        return jnp.where(lane < HEAD, pltpu.roll(top, HEAD, 1), bottom)
    return jnp.where(lane < HEAD, top, pltpu.roll(bottom, HEAD, 1))


def unfold_single(value, high):
    turned = pltpu.roll(value, HEAD, 1)
    return jnp.concatenate([turned, value] if high else [value, turned], 0)


def unfold_heads(read, rows, outer):
    tiles = [None] * (outer * 3 // 2)
    for o in range(0, outer, 2):
        base = 3 * o * HEAD // 128
        first, second = read(o), read(o + 1)
        tiles[base] = first[:rows]
        tiles[base + 2] = second[:rows]
        low, high = unfold_single(first[rows:], False), unfold_single(second[rows:], True)
        lane = lax.broadcasted_iota(jnp.int32, low.shape, 1)
        tiles[base + 1] = jnp.where(lane < HEAD, low, high)
    return tiles


def fold_heads_of(write, tile_of, outer):
    for o in range(outer):
        first = 3 * o * HEAD
        odd = first % 128 != 0
        pair = (first + HEAD if odd else first) // 128
        single = (first if odd else first + 128) // 128
        write(o, jnp.concatenate([tile_of(pair), fold_single(tile_of(single), odd)], 0))


def packed_rows(vector, z):
    pairs, singles = [], []
    for n in range(3):
        base = n * D + 3 * z * HEAD
        odd = base % 128 != 0
        first = base + HEAD if odd else base
        pairs.append(vector[first : first + 128])
        single = vector[base : base + HEAD] if odd else vector[base + 128 : base + 192]
        singles.append(jnp.concatenate([single, jnp.zeros_like(single)]))
    return pairs + singles


def lane_half(core):
    return pl.ds(pl.multiple_of(core * (D // 2), 128), D // 2)


def packed_tiles(read, z):
    pairs, singles = [], []
    for n in range(3):
        base = n * D + 3 * z * HEAD
        odd = base % 128 != 0
        pairs.append(read(base + HEAD if odd else base))
        single = read(base - HEAD if odd else base + 128)
        singles.append(pltpu.roll(single, HEAD, 1) if odd else single)
    return pairs + singles


class Line:
    def __init__(self, here, outer, inner, slot, own_send, hand_send, recv):
        self.here, self.outer, self.slot = here, outer, slot
        self.own_send, self.hand_send, self.recv = own_send, hand_send, recv
        self.inner = inner
        self.sends = []
        self.table = [sorted((s for s in range(outer) if s != i), key=lambda s: (abs(s - i), s)) for i in range(outer)]

    def origin(self, n):
        if n == 0:
            return self.here.o
        found = 0
        for i in range(self.outer):
            found = found + (self.here.o == i).astype(jnp.int32) * self.table[i][n - 1]
        return found

    def peer(self, z):
        return (self.here.batch, z * self.inner + self.here.j)

    def send(self, source, key, s, to, sem):
        there = jnp.clip(to, 0, self.outer - 1)
        copy = pltpu.make_async_remote_copy(
            src_ref=source,
            dst_ref=self.slot(key, s),
            send_sem=sem,
            recv_sem=self.recv.at[key, s],
            device_id=self.peer(there),
            device_id_type=MESH,
        )
        valid = (to >= 0) & (to < self.outer)

        @pl.when(valid)
        def _():
            copy.start()

        self.sends.append((valid, copy))

    def start(self, key, source):
        o = self.here.o
        self.send(source, key, o, o + 1, self.own_send.at[key, 0])
        self.send(source, key, o, o - 1, self.own_send.at[key, 1])

    def arrive(self, key, n):
        o, s = self.here.o, self.origin(n)
        place = self.slot(key, s)
        pltpu.make_async_remote_copy(
            src_ref=place,
            dst_ref=place,
            send_sem=self.hand_send.at[key, n],
            recv_sem=self.recv.at[key, s],
            device_id=self.here.twin,
            device_id_type=MESH,
        ).wait_recv()
        step = 1 - 2 * (s > o).astype(jnp.int32)
        self.send(place, key, s, o + step, self.hand_send.at[key, n])
        return s

    def finish(self):
        for valid, copy in self.sends:

            @pl.when(valid)
            def _(copy=copy):
                copy.wait_send()


def start_kernel(batches, outer, inner, *refs):
    refs = list(refs)

    def take(n):
        got = refs[:n]
        del refs[:n]
        return got

    qkv, out, up, down, lens, mixing, tokens, cot, earlier, vecs, packed_bias, cos_t, sin_t = take(13)
    mine, normed, q_all, k_all, v_all, out_all, up_all, down_all, counts, mixture, dots, o_mine, ot, lse = take(14)
    own, got, near, up_bit, out_bit, down_bit, queue, count, wide_s, cosine, sine = take(11)
    zs, zr, xs, xr, ys, yr, cs, cr, ts, tr, ns, nr, local, es = take(14)
    nls, nlf, nlr, rls, rlf, rlr, rxs, rxr, rys, ryr, rcs, rcr, axs, axr, acs, acr = take(16)
    attend_refs = refs
    across = inner // 2
    here = Place(batches, outer, inner)
    o, a, b, c, j = here.o, here.a, here.batch, here.c, here.j
    earlier_count, tall, _ = earlier.shape
    groups = lens.shape[0]
    rows = tall // groups
    fetches = {e: carry(earlier.at[e], queue.at[e], es.at[e]) for e in range(2)}
    for g in range(groups):
        hat, _ = normalize(tokens[g * rows : g * rows + rows].astype(f32))
        normed[g, o] = (hat * vecs[0:1] + vecs[2:3]).astype(bf16)
    for z in range(outer):
        for i, tile in enumerate(packed_tiles(lambda lane: qkv[:, lane : lane + 128], z)):
            own[z, :, 128 * i : 128 * i + 128] = tile
    for i in range(BLOCKS):
        own[outer + 1 + i] = up[:, i * D : i * D + D]
    own[outer] = out[...]
    here_count = lens[0]
    for g in range(1, groups):
        here_count = here_count + lens[g]
    count[...] = jnp.zeros(count.shape, jnp.int32) + here_count
    greet(here.z_peers[1:] + here.x_peers[1:] + here.y_peers[1:] + [here.twin])
    give = lane_half(1 - c)
    keep = lane_half(c)
    near_count = outer + 1
    swaps = [
        push(own.at[pl.ds(0, near_count), :, give], got.at[pl.ds(0, near_count), :, pl.ds(0, D // 2)], ts.at[0], tr.at[0], here.twin),
        push(own.at[pl.ds(near_count + 2 * (1 - c), 2)], got.at[pl.ds(near_count, 2)], ts.at[1], tr.at[1], here.twin),
    ]
    line = Line(here, outer, inner, lambda g, s: normed.at[g, s], nls, nlf, nlr)
    line.start(0, normed.at[0, o])
    waits = [carry(count, counts.at[b], local.at[0])]
    for d in range(1, batches):
        waits.append(push(count, counts.at[b], ns.at[d], nr.at[d], here.y_peers[d]))

    def joined(own_part, other):
        low = jnp.where(c == 0, own_part, other)
        high = jnp.where(c == 0, other, own_part)
        return jnp.concatenate([low, high], 0).astype(bf16)

    def slot(y, z, x):
        return mine.at[y, z, x, :, keep]

    arrivals, twins = {}, []

    def onward(source, y, z, x, t, dx, dy):
        to = slot(y, z, x)
        if dx == 0 and dy == 0:
            for d in range(1, across):
                arrivals["x", t, d] = push(source, to, xs.at[t, d], xr.at[t, d], here.x_peers[d])
        if dy == 0:
            for d in range(1, batches):
                arrivals["y", t, dx, d] = push(source, to, ys.at[t, dx, d], yr.at[t, dx, d], here.y_peers[d])
        twins.append(push(source, to, cs.at[t, dx, dy], cr.at[t, dx, dy], here.twin))

    swaps[0].wait()
    for z in range(outer + 1):
        own_part = jnp.where(c == 0, own[z, :, : D // 2], own[z, :, D // 2 :])
        value = joined(own_part, got[z, :, : D // 2])
        if z < outer:
            near[z] = value
        else:
            out_bit[...] = value
    copies = {}
    for t in range(1, outer):
        copies[t] = push(near.at[here.zs[t]], slot(b, o, a), zs.at[t], zr.at[t], here.z_peers[t])
    twins.append(carry(near.at[o], slot(b, o, a), local.at[1]))
    onward(near.at[o], b, o, a, 0, 0, 0)
    swaps[1].wait()
    for p in (0, 1):
        up_bit[p] = joined(own[near_count + 2 * c + p], got[near_count + p])
    down_bit[...] = down[...].astype(bf16)
    for t in range(1, outer):
        copies[t].wait()
        onward(slot(b, here.z_from[t], a), b, here.z_from[t], a, t, 0, 0)

    bits = (up_bit, down_bit, out_bit)

    def rest_slot(i, y, z, x):
        if i == 0:
            return up_all.at[pl.ds(2 * c, 2), y, z, x]
        if i == 1:
            return down_all.at[y, z, x, c]
        return out_all.at[y, z, x, :, keep]

    rest_x, rest_y = [], []
    rest = Line(here, outer, inner, lambda i, s: rest_slot(i, b, s, a), rls, rlf, rlr)

    def rest_onward(i, n, s, source):
        to = rest_slot(i, b, s, a)
        for d in range(1, across):
            rest_x.append((i, n, s, d, push(source, to, rxs.at[i, n, d], rxr.at[i, n, d], here.x_peers[d])))
        for d in range(1, batches):
            rest_y.append((i, n, s, 0, d, push(source, to, rys.at[i, n, 0, d], ryr.at[i, n, 0, d], here.y_peers[d])))
        waits.append(push(source, to, rcs.at[i, n, 0, 0], rcr.at[i, n, 0, 0], here.twin))

    def rest_line(n):
        for i in range(3):
            s = rest.arrive(i, n)
            rest_onward(i, n, s, rest_slot(i, b, s, a))

    def rest_across():
        if rest_x:
            i, n, s, d, copy = rest_x.pop(0)
            copy.wait()
            piece = rest_slot(i, b, s, here.x_from[d])
            for e in range(1, batches):
                rest_y.append((i, n, s, d, e, push(piece, piece, rys.at[i, n, d, e], ryr.at[i, n, d, e], here.y_peers[e])))
            waits.append(push(piece, piece, rcs.at[i, n, d, 0], rcr.at[i, n, d, 0], here.twin))

    def rest_twin():
        if rest_y:
            i, n, s, d, e, copy = rest_y.pop(0)
            copy.wait()
            piece = rest_slot(i, here.y_from[e], s, here.x_from[d])
            waits.append(push(piece, piece, rcs.at[i, n, d, e], rcr.at[i, n, d, e], here.twin))

    late = {0: [], 1: []}
    spread = {0: [], 1: []}

    def project(g, n, s):
        wide_s[...] = mm(normed[g, s], mine[...].reshape(D, D)) + packed_bias[pl.ds(o, 1)]
        for i, dest in enumerate((q_all, k_all, v_all)):
            pair, single = wide_s[:, 128 * i : 128 * i + 128], wide_s[:, 384 + 128 * i : 512 + 128 * i]
            if i < 2:
                pair, single = turn(pair, cosine[s], sine[s]), turn(single, cosine[s], sine[s])
            value = jnp.concatenate([pair, fold_single(single, False)], 0).astype(bf16)
            if i == 0:
                q_all[g, s] = value
            else:
                dest[g, s, j] = value
        for i, dest in enumerate((k_all, v_all)):
            piece = dest.at[g, s, j]
            for d in range(1, across):
                late[g].append((i, n, s, d, push(piece, piece, axs.at[g, i, n, d], axr.at[g, i, n, d], here.x_peers[d])))
            spread[g].append(push(piece, piece, acs.at[g, i, n, 0], acr.at[g, i, n, 0], here.twin))

    def settle(g, count):
        for _ in range(count):
            if late[g]:
                i, n, s, d, copy = late[g].pop(0)
                copy.wait()
                piece = (k_all, v_all)[i].at[g, s, here.x_from[d] * 2 + c]
                spread[g].append(push(piece, piece, acs.at[g, i, n, d], acr.at[g, i, n, d], here.twin))

    def arrive(g, n):
        project(g, n, line.arrive(g, n))

    def live_rows(value):
        row = lax.broadcasted_iota(jnp.int32, (rows, 1), 0) + lax.axis_index("seq") * rows
        parts = [jnp.where(row < lens[g], value[g * rows : g * rows + rows], 0.0) for g in range(groups)]
        return jnp.concatenate(parts, 0)

    def plain():
        wide = tokens[...].astype(f32)
        grad = live_rows(cot[...].astype(f32))
        dots[...] = jnp.zeros(dots.shape, f32)
        dots[1:2] = jnp.sum(grad * wide, 0, keepdims=True)
        mixture[...] = mixing[1] * wide

    def mix(e):
        fetches[e].wait()
        wide = queue[e % 2].astype(f32)
        grad = live_rows(cot[...].astype(f32))
        dots[2 + e : 3 + e] = jnp.sum(grad * wide, 0, keepdims=True)
        mixture[...] = mixture[...] + mixing[2 + e] * wide
        if e + 2 < earlier_count:
            fetches[e + 2] = carry(earlier.at[e + 2], queue.at[e % 2], es.at[e + 2])

    steps = [plain] + [functools.partial(mix, e) for e in range(earlier_count)]

    def work(n=1):
        for _ in range(n):
            if steps:
                steps.pop(0)()

    for z in range(outer):
        cosine[z] = jnp.concatenate([cos_t[z]] * 4, 0).T
        sine[z] = jnp.concatenate([-sin_t[z], sin_t[z]] * 2, 0).T
    first = line.arrive(0, 1)
    for t in range(outer):
        for d in range(1, across):
            arrivals["x", t, d].wait()
            z, x = here.z_from[t], here.x_from[d]
            onward(slot(b, z, x), b, z, x, t, d, 0)
    for i in range(3):
        waits.append(carry(bits[i], rest_slot(i, b, o, a), local.at[2 + i]))
        rest_onward(i, 0, o, bits[i])
    for t in range(outer):
        for dx in range(across):
            for dy in range(1, batches):
                arrivals["y", t, dx, dy].wait()
                y, z, x = here.y_from[dy], here.z_from[t], here.x_from[dx]
                onward(slot(y, z, x), y, z, x, t, dx, dy)
    second = line.arrive(0, 2)
    for i in range(3):
        rest.start(i, bits[i])
    for copy in twins:
        copy.wait()
    project(0, 0, o)
    project(0, 1, first)
    project(0, 2, second)
    for n in range(3, outer):
        arrive(0, n)
    line.start(1, normed.at[1, o])
    settle(0, 2)
    rest_line(1)
    work(3)
    settle(0, 2)
    rest_line(2)
    settle(0, 2 * outer * across)
    project(1, 0, o)
    for copy in spread[0]:
        copy.wait()
    events = [
        lambda: rest_line(3) if outer > 3 else None,
        lambda: (rest_across(), rest_across(), rest_across()),
        lambda: arrive(1, 1),
        lambda: (settle(1, 2), rest_across(), rest_across(), rest_across()),
        lambda: arrive(1, 2),
        lambda: (rest_twin(), rest_twin(), rest_twin()),
        lambda: (settle(1, 2), rest_across(), rest_across(), rest_across()),
        lambda: [arrive(1, n) for n in range(3, outer)],
    ]
    attend_group(0, outer, inner, lens, q_all, k_all, v_all, o_mine, ot, lse, attend_refs, here, events)
    while events:
        events.pop(0)()
    work(4)
    while rest_x:
        rest_across()
    settle(1, 2 * outer * across)
    work(len(steps))
    for copy in spread[1]:
        copy.wait()
    events = [lambda: (rest_twin(), rest_twin(), rest_twin())] * 8
    attend_group(1, outer, inner, lens, q_all, k_all, v_all, o_mine, ot, lse, attend_refs, here, events)
    while rest_y:
        rest_twin()
    line.finish()
    rest.finish()
    for copy in waits:
        copy.wait()


def start_layer(qkv, out, up, down, lens, mixing, tokens, cot, earlier, vecs, packed_bias, cos_t, sin_t, batches, outer, inner, ident):
    across = inner // 2
    share = qkv.shape[0]
    tall = tokens.shape[0]
    groups = lens.shape[0]
    rows = tall // groups
    grid = (batches, outer, across)
    folded = rows + rows // 2
    buf = pltpu.VMEM
    return pl.pallas_call(
        functools.partial(start_kernel, batches, outer, inner),
        out_shape=(
            jax.ShapeDtypeStruct(grid + (2 * share, D), bf16),
            jax.ShapeDtypeStruct((groups, outer, rows, D), bf16),
            jax.ShapeDtypeStruct((groups, outer, folded, 128), bf16),
            jax.ShapeDtypeStruct((groups, outer, inner, folded, 128), bf16),
            jax.ShapeDtypeStruct((groups, outer, inner, folded, 128), bf16),
            jax.ShapeDtypeStruct(grid + (2 * share, D), bf16),
            jax.ShapeDtypeStruct((BLOCKS,) + grid + (2 * share, D), bf16),
            jax.ShapeDtypeStruct(grid + (2, BLOCKS * share, D), bf16),
            jax.ShapeDtypeStruct((batches, 8, 128), jnp.int32),
            jax.ShapeDtypeStruct((tall, D), f32),
            jax.ShapeDtypeStruct((16, D), f32),
            jax.ShapeDtypeStruct((outer, groups, folded, 128), bf16),
            jax.ShapeDtypeStruct((groups, outer, 3 * HEAD, rows), f32),
            jax.ShapeDtypeStruct((groups, outer, 8, rows), f32),
        ),
        in_specs=[IN_VMEM] * 4 + [IN_SMEM] * 2 + [IN_VMEM] * 2 + [ANYWHERE] + [IN_VMEM] * 4,
        out_specs=(IN_VMEM,) * 5 + (ANYWHERE,) * 4 + (IN_VMEM,) * 5,
        scratch_shapes=[
            buf((outer + 1 + BLOCKS, share, D), f32),
            buf((outer + 3, share, D), f32),
            buf((outer, 2 * share, D // 2), bf16),
            buf((2, 2 * share, D), bf16),
            buf((2 * share, D // 2), bf16),
            buf((BLOCKS * share, D), bf16),
            buf((2, tall, D), bf16),
            buf((8, 128), jnp.int32),
            buf((rows, D), f32),
            buf((outer, rows, 128), f32),
            buf((outer, rows, 128), f32),
        ]
        + [DMA((outer,))] * 2
        + [DMA((outer, across))] * 2
        + [DMA((outer, across, batches))] * 4
        + [DMA((2,))] * 2
        + [DMA((batches,))] * 2
        + [DMA((5,)), DMA((earlier.shape[0],))]
        + [DMA((groups, 2)), DMA((groups, outer)), DMA((groups, outer))]
        + [DMA((3, 2)), DMA((3, outer)), DMA((3, outer))]
        + [DMA((3, outer, across))] * 2
        + [DMA((3, outer, across, batches))] * 4
        + [DMA((groups, 2, outer, across))] * 4
        + attend_scratch(outer, inner, rows),
        compiler_params=remote_params(ident, ROOM),
        name="start_layer",
    )(qkv, out, up, down, lens, mixing, tokens, cot, earlier, vecs, packed_bias, cos_t, sin_t)


class Exchange:
    def __init__(self, here, pair, q, alls, q_all, sems, local, first_local):
        self.here, self.pair, self.q, self.alls, self.q_all = here, pair, q, alls, q_all
        self.qs, self.qr, self.zs, self.zr, self.xs, self.xr, self.cs, self.cr = sems
        self.local, self.first_local = local, first_local
        self.outer, self.across = len(here.zs), len(here.xs)
        self.arriving = {0: [], 1: []}
        self.late = {0: [], 1: []}
        self.waits = {0: [], 1: []}

    def send_pair(self, g):
        here = self.here
        for i in (0, 1):
            source, dest = self.pair[i], self.alls[i]
            for t in range(1, self.outer):
                copy = push(source.at[g, here.zs[t]], dest.at[g, here.o, here.j], self.zs.at[g, i, t], self.zr.at[g, i, t], here.z_peers[t])
                self.arriving[g].append((i, t, copy))
            place = dest.at[g, here.o, here.j]
            self.waits[g].append(carry(source.at[g, here.o], place, self.local.at[self.first_local + 3 * g + i]))
            self.onward(g, i, 0, source.at[g, here.o], place)

    def send_query(self, g):
        here = self.here
        for t in range(1, self.outer):
            self.waits[g].append(push(self.q.at[g, here.zs[t]], self.q_all.at[g, here.o], self.qs.at[g, t], self.qr.at[g, t], here.z_peers[t]))
        self.waits[g].append(carry(self.q.at[g, here.o], self.q_all.at[g, here.o], self.local.at[self.first_local + 3 * g + 2]))

    def onward(self, g, i, t, source, place):
        here = self.here
        for d in range(1, self.across):
            copy = push(source, place, self.xs.at[g, i, t, d], self.xr.at[g, i, t, d], here.x_peers[d])
            self.late[g].append((i, t, d, copy))
        self.waits[g].append(push(source, place, self.cs.at[g, i, t, 0], self.cr.at[g, i, t, 0], here.twin))

    def settle(self, g, left):
        here = self.here
        while len(self.late[g]) > left:
            i, t, d, copy = self.late[g].pop(0)
            copy.wait()
            moved = self.alls[i].at[g, here.z_from[t], here.x_from[d] * 2 + here.c]
            self.waits[g].append(push(moved, moved, self.cs.at[g, i, t, d], self.cr.at[g, i, t, d], here.twin))

    def arrive(self, g):
        i, t, copy = self.arriving[g].pop(0)
        copy.wait()
        place = self.alls[i].at[g, self.here.z_from[t], self.here.j]
        self.onward(g, i, t, place, place)
        self.settle(g, self.across - 1)

    def finish(self, g):
        for copy in self.waits[g]:
            copy.wait()


def exchange_scratch(groups, outer, across):
    return [DMA((groups, outer))] * 2 + [DMA((groups, 2, outer))] * 2 + [DMA((groups, 2, outer, across))] * 4


def turned_parts(block, rows):
    pair = block[:rows].T
    single = block[rows:].T
    single = jnp.concatenate([single[:HEAD], single[HEAD:]], 1)
    blank = jnp.zeros_like(single)
    stack = lambda *parts: jnp.concatenate(parts, 0)
    return stack(pair[:HEAD], blank), stack(blank, pair[HEAD:]), stack(single, blank), stack(blank, single)


def attend_scratch(outer, inner, rows):
    span = inner * rows
    return [
        pltpu.VMEM((outer, 128, span), bf16),
        pltpu.VMEM((outer, 128, span // 2), bf16),
        pltpu.VMEM((outer, span, 128), f32),
        pltpu.VMEM((4, 128, rows), bf16),
        pltpu.VMEM((8, rows), f32),
        pltpu.VMEM((8, rows), f32),
    ]


def bias_rows(bias, lens, g, outer, span):
    for c in range(outer):
        key = c * span + lax.broadcasted_iota(jnp.int32, (span, 128), 0)
        bias[c] = jnp.where(key < lens[g], 0.0, NEG)


def attend_group(g, outer, inner, lens, q_all, k_all, v_all, o_mine, ot, lse, scratch, here, events):
    vt, vft, bias, qt, m_s, l_s = scratch
    folded = q_all.shape[2]
    rows = folded * 2 // 3
    span = inner * rows
    half = rows // 2
    tiles = rows // 128
    bias_rows(bias, lens, g, outer, span)
    for c in range(outer):
        vt[c] = v_all[g, c, :, :rows, :].reshape(span, 128).T
        vft[c] = v_all[g, c, :, rows:, :].reshape(span // 2, 128).T
    for z in range(outer):
        first = (z * inner + here.j) * rows
        for n, part in enumerate(turned_parts((q_all[g, z] * 0.125).astype(bf16), rows)):
            qt[n] = part
        ot[g, z] = jnp.zeros((3 * HEAD, rows), f32)
        m_s[...] = jnp.full(m_s.shape, NEG, f32)
        l_s[...] = jnp.zeros(l_s.shape, f32)

        def step(c, masked):
            pair = k_all[g, c, :, :rows, :].reshape(span, 128)
            single = k_all[g, c, :, rows:, :].reshape(span // 2, 128)
            low = bias[c]
            low_parts = low.reshape(inner, rows, 128)
            shut = (low, low, low_parts[:, :half].reshape(span // 2, 128), low_parts[:, half:].reshape(span // 2, 128))
            lhs = (pair, pair, single, single)
            scores = []
            for n in range(4):
                s = mm(lhs[n], qt[n]) + jnp.concatenate([shut[n]] * tiles, 1)
                if masked:
                    key = lax.broadcasted_iota(jnp.int32, s.shape, 0)
                    if n >= 2:
                        key = lax.div(key, half) * rows + lax.rem(key, half) + (n - 2) * half
                    query = first + lax.broadcasted_iota(jnp.int32, s.shape, 1)
                    s = jnp.where(key + c * span <= query, s, NEG)
                scores.append(s)
            own = ((0,), (1,), (2, 3))
            tops = [m_s[h : h + 1] for h in range(3)]
            news = []
            for h in range(3):
                top = tops[h]
                for n in own[h]:
                    top = jnp.maximum(top, jnp.max(scores[n], 0, keepdims=True))
                news.append(top)
            shares, sums = [], [0.0, 0.0, 0.0]
            for h in range(3):
                for n in own[h]:
                    p = jnp.exp(scores[n] - news[h])
                    sums[h] = sums[h] + jnp.sum(p, 0, keepdims=True)
                    shares.append(p.astype(bf16))
            for h in range(3):
                alpha = jnp.exp(tops[h] - news[h])
                l_s[h : h + 1] = l_s[h : h + 1] * alpha + sums[h]
                m_s[h : h + 1] = news[h]
                at = slice(HEAD * h, HEAD * h + HEAD)
                if h < 2:
                    out = mm(vt[c, at, :], shares[h])
                else:
                    out = mm(vft[c, :HEAD, :], shares[2]) + mm(vft[c, HEAD:, :], shares[3])
                ot[g, z, at, :] = ot[g, z, at, :] * alpha + out

        def full_step(c, _):
            step(c, False)
            return 0

        if z:
            lax.fori_loop(0, z, full_step, 0)
        if events:
            events.pop(0)()
        step(z, True)
        if events:
            events.pop(0)()
        for h in range(3):
            at = slice(HEAD * h, HEAD * h + HEAD)
            total = l_s[h : h + 1]
            ot[g, z, at, :] = ot[g, z, at, :] / total
            lse[g, z, h : h + 1, :] = m_s[h : h + 1] + jnp.log(total)
        o_mine[z, g, :rows, :] = ot[g, z, :128, :].T.astype(bf16)
        halves = [ot[g, z, 128:, :half], ot[g, z, 128:, half:]]
        o_mine[z, g, rows:, :] = jnp.concatenate(halves, 0).T.astype(bf16)


def spread_kernel(batches, outer, inner, *refs):
    refs = list(refs)

    def take(n):
        got = refs[:n]
        del refs[:n]
        return got

    normed, near, vecs, lens, cosine, sine = take(6)
    q_all, k_all, v_all, o_mine, ot, lse = take(6)
    q, k, v, wide_s, local = take(5)
    sems = take(8)
    here = Place(batches, outer, inner)
    rows = cosine.shape[0]
    groups = lens.shape[0]
    greet(here.z_peers[1:] + here.x_peers[1:] + [here.twin])

    def project(block, into, rotated):
        wide_s[...] = mm(normed[...], near[block]) + vecs[4 + block : 5 + block]
        for g in range(groups):

            def tile_of(tile):
                value = wide_s[g * rows : g * rows + rows, 128 * tile : 128 * tile + 128]
                return turn(value, cosine[...], sine[...]) if rotated else value

            def write(target, value):
                into[g, target] = value.astype(bf16)

            fold_heads_of(write, tile_of, outer)

    exchange = Exchange(here, (k, v), q, (k_all, v_all), q_all, sems, local, 0)
    for block, into in ((1, k), (2, v), (0, q)):
        project(block, into, block != 2)
    for g in range(groups):
        exchange.send_pair(g)
        exchange.send_query(g)
    for g in range(groups):
        for _ in range(2 * (outer - 1)):
            exchange.arrive(g)
        exchange.settle(g, 0)
        exchange.finish(g)
    for g in range(groups):
        attend_group(g, outer, inner, lens, q_all, k_all, v_all, o_mine, ot, lse, refs, here, [])


def spread_heads(normed, near, vecs, lens, cosine, sine, batches, outer, inner, ident):
    rows = cosine.shape[0]
    groups = lens.shape[0]
    folded = rows + rows // 2
    piece = (groups, outer, folded, 128)
    full = jax.ShapeDtypeStruct((groups, outer, inner, folded, 128), bf16)
    shapes = (
        jax.ShapeDtypeStruct(piece, bf16),
        full,
        full,
        jax.ShapeDtypeStruct((outer, groups, folded, 128), bf16),
        jax.ShapeDtypeStruct((groups, outer, 3 * HEAD, rows), f32),
        jax.ShapeDtypeStruct((groups, outer, 8, rows), f32),
    )
    return pl.pallas_call(
        functools.partial(spread_kernel, batches, outer, inner),
        out_shape=shapes,
        in_specs=[IN_VMEM] * 3 + [IN_SMEM] + [IN_VMEM] * 2,
        out_specs=(IN_VMEM,) * len(shapes),
        scratch_shapes=[pltpu.VMEM(piece, bf16)] * 3
        + [pltpu.VMEM(normed.shape, f32), DMA((3 * groups,))]
        + exchange_scratch(groups, outer, inner // 2)
        + attend_scratch(outer, inner, rows),
        compiler_params=remote_params(ident, ROOM),
        name="spread_heads",
    )(normed, near, vecs, lens, cosine, sine)


def attend_back_kernel(outer, inner, lens, q, k, v, do, ot, lse, cos, sin, dq, dk, dv, kt, kft, qt, dot_t, qz, dz, rd, dqt, dks, dvs):
    groups, _, folded, _ = q.shape
    rows = folded * 2 // 3
    half = rows // 2
    span = inner * rows
    j = lax.rem(lax.axis_index("seq"), inner)
    low = lax.broadcasted_iota(jnp.int32, (rows, 128), 1) < HEAD

    def spread_parts(into, block):
        pair = block[:rows]
        single = block[rows:].astype(f32)
        blank = jnp.zeros_like(pair)
        into[0] = jnp.where(low, pair, blank)
        into[1] = jnp.where(low, blank, pair)
        into[2] = jnp.where(low, unfold_single(single, False), 0.0).astype(bf16)
        into[3] = jnp.where(low, 0.0, unfold_single(single, True)).astype(bf16)

    for g in range(groups):
        length = lens[g]
        for c in range(outer):
            kt[c] = k[g, c, :, :rows, :].reshape(span, 128).T
            kft[c] = k[g, c, :, rows:, :].reshape(span // 2, 128).T
        dks[...] = jnp.zeros(dks.shape, f32)
        dvs[...] = jnp.zeros(dvs.shape, f32)

        def one(z, _):
            first = (z * inner + j) * rows
            small = (q[g, z] * 0.125).astype(bf16)
            grad = do[z, g]
            for n, part in enumerate(turned_parts(small, rows)):
                qt[n] = part
            grads = turned_parts(grad, rows)
            for n, part in enumerate(grads):
                dot_t[n] = part
            spread_parts(qz, small)
            spread_parts(dz, grad)
            for h in range(3):
                part = grads[h][HEAD * (h % 2) : HEAD * (h % 2) + HEAD]
                rd[h : h + 1, :] = jnp.sum(part.astype(f32) * ot[g, z, HEAD * h : HEAD * h + HEAD, :], 0, keepdims=True)
            dqt[...] = jnp.zeros(dqt.shape, f32)

            def step(c, masked):
                pair = k[g, c, :, :rows, :].reshape(span, 128)
                single = k[g, c, :, rows:, :].reshape(span // 2, 128)
                v_pair = v[g, c, :, :rows, :].reshape(span, 128)
                v_single = v[g, c, :, rows:, :].reshape(span // 2, 128)
                lhs = (pair, pair, single, single)
                values = (v_pair, v_pair, v_single, v_single)
                for n in range(4):
                    h = min(n, 2)
                    s = mm(lhs[n], qt[n])
                    p = jnp.exp(s - lse[g, z, h : h + 1, :])
                    if masked:
                        key = lax.broadcasted_iota(jnp.int32, s.shape, 0)
                        if n >= 2:
                            key = lax.div(key, half) * rows + lax.rem(key, half) + (n - 2) * half
                        key = key + c * span
                        query = first + lax.broadcasted_iota(jnp.int32, s.shape, 1)
                        p = jnp.where((key <= query) & (key < length), p, 0.0)
                    dp = mm(values[n], dot_t[n])
                    ds = (p * (dp - rd[h : h + 1, :])).astype(bf16)
                    dv_part = mm(p.astype(bf16), dz[n])
                    dk_part = mm(ds, qz[n])
                    at = slice(HEAD * h, HEAD * h + HEAD)
                    if n < 2:
                        dvs[c, :, :rows, :] += dv_part.reshape(inner, rows, 128)
                        dks[c, :, :rows, :] += dk_part.reshape(inner, rows, 128)
                        dqt[at, :] += mm(kt[c, at, :], ds)
                    else:
                        dvs[c, :, rows:, :] += dv_part.reshape(inner, half, 128)
                        dks[c, :, rows:, :] += dk_part.reshape(inner, half, 128)
                        dqt[at, :] += mm(kft[c, HEAD * (n - 2) : HEAD * (n - 1), :], ds)

            live = first < length
            whole = jnp.where(live, jnp.minimum(z, lax.div(length, span)), 0)
            count = jnp.where(live, jnp.minimum(z + 1, lax.div(length + span - 1, span)), 0)

            def full_step(c, _):
                step(c, False)
                return 0

            def edge_step(c, _):
                step(c, True)
                return 0

            lax.fori_loop(0, whole, full_step, 0)
            lax.fori_loop(whole, count, edge_step, 0)
            parts = []
            for h in range(3):
                a = dqt[HEAD * h : HEAD * h + 32, :] * 0.125
                b = dqt[HEAD * h + 32 : HEAD * h + 64, :] * 0.125
                parts.append(a * cos[z] + b * sin[z])
                parts.append(b * cos[z] - a * sin[z])
            dq[g, z, :rows, :] = jnp.concatenate(parts[:4], 0).T.astype(bf16)
            single = jnp.concatenate(parts[4:], 0)
            dq[g, z, rows:, :] = jnp.concatenate([single[:, :half], single[:, half:]], 0).T.astype(bf16)
            return 0

        lax.fori_loop(0, outer, one, 0)
        for c in range(outer):
            dk[g, c] = dks[c].astype(bf16)
            dv[g, c] = dvs[c].astype(bf16)


def attend_back(lens, q, k, v, do, ot, lse, cos, sin, inner):
    groups, outer, folded, _ = q.shape
    rows = folded * 2 // 3
    span = inner * rows
    vm = IN_VMEM
    return pl.pallas_call(
        functools.partial(attend_back_kernel, outer, inner),
        out_shape=(
            jax.ShapeDtypeStruct(q.shape, bf16),
            jax.ShapeDtypeStruct(k.shape, bf16),
            jax.ShapeDtypeStruct(v.shape, bf16),
        ),
        in_specs=[IN_SMEM] + [vm] * 8,
        out_specs=(vm, vm, vm),
        scratch_shapes=[
            pltpu.VMEM((outer, 128, span), bf16),
            pltpu.VMEM((outer, 128, span // 2), bf16),
            pltpu.VMEM((4, 128, rows), bf16),
            pltpu.VMEM((4, 128, rows), bf16),
            pltpu.VMEM((4, rows, 128), bf16),
            pltpu.VMEM((4, rows, 128), bf16),
            pltpu.VMEM((8, rows), f32),
            pltpu.VMEM((3 * HEAD, rows), f32),
            pltpu.VMEM((outer, inner, folded, 128), f32),
            pltpu.VMEM((outer, inner, folded, 128), f32),
        ],
        compiler_params=params(),
        name="attend_back",
    )(lens, q, k, v, do, ot, lse, cos, sin)


def middle_kernel(batches, outer, inner, *refs):
    refs = list(refs)

    def take(n):
        got = refs[:n]
        del refs[:n]
        return got

    o_mine, out, up, down, tokens, cot, mixture, counts, vecs, lens, mixing = take(11)
    mixed, grad_mine, middle_grad, out_term, up_terms, down_terms, sums = take(7)
    home, sent, attended, middle, low_s, result_s, slope_s, active_s, hidden_s, acc, back, weights = take(12)
    fetch, hs, hr, gs, gr, local = refs
    tall = tokens.shape[0]
    groups = lens.shape[0]
    rows = tall // groups
    here = Place(batches, outer, inner)
    o = here.o
    fetches = [
        carry(down, weights.at[pl.ds(1 + BLOCKS, BLOCKS)], fetch.at[0]),
        carry(out, weights.at[0], fetch.at[1]),
        carry(up, weights.at[pl.ds(1, BLOCKS)], fetch.at[2]),
    ]
    greet(here.z_peers[1:])
    coming, waits = {}, []
    for g in range(groups):
        coming[g] = [carry(o_mine.at[o, g], home.at[o, g], local.at[0, g])]
        for t in range(1, outer):
            coming[g].append(push(o_mine.at[here.zs[t], g], home.at[o, g], hs.at[g, t], hr.at[g, t], here.z_peers[t]))
    count = counts[0, 0:1, 0:1]
    for y in range(1, batches):
        count = count + counts[y, 0:1, 0:1]
    slots = lax.axis_size("batch") * lax.axis_size("seq") * tall
    scale = slots / count.astype(f32)
    row = lax.broadcasted_iota(jnp.int32, (rows, 1), 0) + lax.axis_index("seq") * rows

    def grad_of(g):
        return cot[g * rows : g * rows + rows, :].astype(f32) * jnp.where(row < lens[g], scale, 0.0)

    sums[...] = jnp.zeros(sums.shape, f32)
    for g in range(groups):
        here_rows = slice(g * rows, g * rows + rows)
        result = (mixing[0] * grad_of(g)).astype(bf16)
        result_s[here_rows] = result
        sums[8 + BLOCKS : 9 + BLOCKS] = sums[8 + BLOCKS : 9 + BLOCKS] + jnp.sum(result.astype(f32), 0, keepdims=True)
    fetches[0].wait()

    def early(i, _):
        slope_s[i] = mm_nt(result_s[...], weights[1 + BLOCKS + i])
        return 0

    lax.fori_loop(0, BLOCKS, early, 0)
    for g in range(groups):
        here_rows = slice(g * rows, g * rows + rows)
        for copy in coming[g]:
            copy.wait()
        tiles = unfold_heads(lambda p: home[p, g].astype(f32), rows, outer)
        for i, tile in enumerate(tiles):
            attended[here_rows, 128 * i : 128 * i + 128] = tile.astype(bf16)
        if g == 0:
            fetches[1].wait()
        value = tokens[here_rows].astype(f32) + (mm(attended[here_rows], weights[0]) + vecs[7:8])
        middle[here_rows] = value
        hat, inverse = normalize(value)
        low_s[here_rows] = (hat * vecs[1:2] + vecs[3:4]).astype(bf16)
        acc[here_rows] = jnp.zeros((rows, D), f32)
        back[...] = jnp.zeros((rows, D), f32)
        if g == 0:
            fetches[2].wait()

        def block(i, _):
            hidden = mm(low_s[here_rows], weights[1 + i]) + vecs[pl.ds(8 + i, 1)]
            square = hidden * hidden
            bend = jnp.tanh(0.7978845608028654 * (hidden + 0.044715 * square * hidden))
            half = 0.5 * (1.0 + bend)
            active = (hidden * half).astype(bf16)
            active_s[i, here_rows] = active
            slope = half + 0.5 * hidden * (1.0 - bend * bend) * (0.7978845608028654 * (1.0 + 3.0 * 0.044715 * square))
            hidden_grad = (slope * slope_s[i, here_rows]).astype(bf16)
            hidden_s[i, here_rows] = hidden_grad
            sums[pl.ds(8 + i, 1)] = sums[pl.ds(8 + i, 1)] + jnp.sum(hidden_grad.astype(f32), 0, keepdims=True)
            back[...] += mm_nt(hidden_grad, weights[1 + i])
            acc[here_rows] += mm(active, weights[1 + BLOCKS + i])
            return 0

        lax.fori_loop(0, BLOCKS, block, 0)
        inner_grad = back[...]
        sums[1:2] = sums[1:2] + jnp.sum(inner_grad * hat, 0, keepdims=True)
        sums[3:4] = sums[3:4] + jnp.sum(inner_grad, 0, keepdims=True)
        total_grad = mixing[0] * grad_of(g) + normalize_back(inner_grad, hat, inverse, vecs[1:2])
        middle_grad[here_rows] = total_grad
        branch = total_grad.astype(bf16)
        sums[7:8] = sums[7:8] + jnp.sum(branch.astype(f32), 0, keepdims=True)
        back[...] = mm_nt(branch, weights[0])

        def write(target, value):
            sent[target, g] = value.astype(bf16)

        fold_heads_of(write, lambda t: back[:, 128 * t : 128 * t + 128], outer)
        for t in range(1, outer):
            waits.append(push(sent.at[here.zs[t], g], grad_mine.at[o, g], gs.at[g, t], gr.at[g, t], here.z_peers[t]))
        waits.append(carry(sent.at[o, g], grad_mine.at[o, g], local.at[1, g]))

    low_t = low_s[...].T

    def late(i, _):
        down_terms[i] = mm(active_s[i].T, result_s[...]).astype(bf16)
        up_terms[i] = mm(low_t, hidden_s[i]).astype(bf16)
        return 0

    lax.fori_loop(0, BLOCKS, late, 0)
    out_term[...] = mm(attended[...].T, middle_grad[...].astype(bf16)).astype(bf16)
    for g in range(groups):
        here_rows = slice(g * rows, g * rows + rows)
        layer_out = middle[here_rows] + acc[here_rows] + vecs[8 + BLOCKS : 9 + BLOCKS]
        mixed[here_rows] = (mixture[here_rows] + mixing[0] * layer_out).astype(bf16)
        sums[VECTORS : VECTORS + 1] = sums[VECTORS : VECTORS + 1] + jnp.sum(grad_of(g) * layer_out, 0, keepdims=True)
    for copy in waits:
        copy.wait()


def middle_layer(o_mine, out, up, down, tokens, cot, mixture, counts, vecs, lens, mixing, batches, outer, inner, ident):
    tall = tokens.shape[0]
    groups = lens.shape[0]
    wide = pltpu.VMEM((tall, D), f32)
    low = pltpu.VMEM((tall, D), bf16)
    hidden = pltpu.VMEM((BLOCKS, tall, D), bf16)
    return pl.pallas_call(
        functools.partial(middle_kernel, batches, outer, inner),
        out_shape=(
            jax.ShapeDtypeStruct((tall, D), bf16),
            jax.ShapeDtypeStruct(o_mine.shape, bf16),
            jax.ShapeDtypeStruct((tall, D), f32),
            jax.ShapeDtypeStruct((D, D), bf16),
            jax.ShapeDtypeStruct((BLOCKS, D, D), bf16),
            jax.ShapeDtypeStruct((BLOCKS, D, D), bf16),
            jax.ShapeDtypeStruct((16, D), f32),
        ),
        in_specs=[ANYWHERE] * 4 + [IN_VMEM] * 5 + [IN_SMEM] * 2,
        out_specs=(IN_VMEM, ANYWHERE) + (IN_VMEM,) * 5,
        scratch_shapes=[
            pltpu.VMEM(o_mine.shape, bf16), pltpu.VMEM(o_mine.shape, bf16),
            low, wide, low, low, pltpu.VMEM((BLOCKS, tall, D), f32), hidden, hidden,
            wide, pltpu.VMEM((tall // groups, D), f32),
            pltpu.VMEM((1 + 2 * BLOCKS, D, D), bf16), DMA((3,)),
        ]
        + [DMA((groups, outer))] * 4
        + [DMA((2, groups))],
        compiler_params=remote_params(ident, ROOM),
        name="middle_layer",
    )(o_mine, out, up, down, tokens, cot, mixture, counts, vecs, lens, mixing)


def back_kernel(outer, dq, dk, dv, cosine, sine, normed, tokens, near, vecs, cot, counts, lens, mixing, middle_grad, out_term, sums, dots, input_grad, terms, small, joined, low_t):
    tall = tokens.shape[0]
    groups = lens.shape[0]
    rows = tall // groups
    for g in range(groups):
        for n, source in enumerate((dq, dk, dv)):
            tiles = unfold_heads(lambda p: source[g, p].astype(f32), rows, outer)
            for i, tile in enumerate(tiles):
                if n == 1:
                    tile = turn(tile, cosine[...], -sine[...])
                joined[n, g * rows : g * rows + rows, 128 * i : 128 * i + 128] = tile.astype(bf16)
    low_t[...] = normed[...].T
    small[...] = sums[...]
    back = jnp.zeros((tall, D), f32)
    for n in range(3):
        low = joined[n]
        small[4 + n : 5 + n] = jnp.sum(low.astype(f32), 0, keepdims=True)
        terms[n] = mm(low_t[...], low).astype(bf16)
        back = back + mm_nt(low, near[n])
    terms[3] = out_term[...]
    hat, inverse = normalize(tokens[...].astype(f32))
    small[0:1] = jnp.sum(back * hat, 0, keepdims=True)
    small[2:3] = jnp.sum(back, 0, keepdims=True)
    slots = lax.axis_size("batch") * lax.axis_size("seq") * tall
    count = counts[0, 0:1, 0:1]
    for y in range(1, counts.shape[0]):
        count = count + counts[y, 0:1, 0:1]
    scale = slots / count.astype(f32)
    row = lax.broadcasted_iota(jnp.int32, (rows, 1), 0) + lax.axis_index("seq") * rows
    live = jnp.concatenate([jnp.where(row < lens[g], scale, 0.0) for g in range(groups)], 0)
    grad = cot[...].astype(f32) * live
    input_grad[...] = mixing[1] * grad + middle_grad[...] + normalize_back(back, hat, inverse, vecs[0:1])
    lane = lax.broadcasted_iota(jnp.int32, (1, D), 1)
    line = jnp.where(lane == 0, jnp.sum(sums[VECTORS : VECTORS + 1], 1, keepdims=True), 0.0)
    for i in range(1, mixing.shape[0]):
        line = line + jnp.where(lane == i, scale * jnp.sum(dots[i : i + 1], 1, keepdims=True), 0.0)
    small[VECTORS : VECTORS + 1] = line


def back_layer(dq, dk, dv, cosine, sine, normed, tokens, near, vecs, cot, counts, lens, mixing, middle_grad, out_term, sums, dots, outer):
    tall = tokens.shape[0]
    return pl.pallas_call(
        functools.partial(back_kernel, outer),
        out_shape=(
            jax.ShapeDtypeStruct((tall, D), f32),
            jax.ShapeDtypeStruct((4, D, D), bf16),
            jax.ShapeDtypeStruct((16, D), f32),
        ),
        in_specs=[IN_VMEM] * 11 + [IN_SMEM] * 2 + [IN_VMEM] * 4,
        out_specs=(IN_VMEM,) * 3,
        scratch_shapes=[pltpu.VMEM((3, tall, D), bf16), pltpu.VMEM((D, tall), bf16)],
        compiler_params=params(),
        name="back_layer",
    )(dq, dk, dv, cosine, sine, normed, tokens, near, vecs, cot, counts, lens, mixing, middle_grad, out_term, sums, dots)


def adam(param, grad, first, second, decay):
    first_new = beta_one * first + (1.0 - beta_one) * grad
    second_new = beta_two * second + (1.0 - beta_two) * grad * grad
    fix_one = 1.0 - beta_one**adam_step
    fix_two = 1.0 - beta_two**adam_step
    update = first_new / fix_one / (jnp.sqrt(second_new / fix_two) + adam_eps)
    return (-learn_rate * (update + decay * param), first_new)


def adam_kernel(packed, near, up, down, out, *refs):
    given, results = refs[:12], refs[12:]
    for n in range(4):
        param, first, second = given[3 * n : 3 * n + 3]
        grad_out, step_out, first_out = results[3 * n : 3 * n + 3]
        for i in range(param.shape[1] // D):
            lanes = slice(i * D, i * D + D)
            if n == 0 and packed:
                grad = jnp.concatenate(plain_tiles(lambda z: near[z], i, near.shape[0]), 1)
            else:
                grad = near[i] if n == 0 else out[...] if n == 1 else up[i] if n == 2 else down[...]
            grad_out[:, lanes] = grad
            step_out[:, lanes], first_out[:, lanes] = adam(param[:, lanes], grad, first[:, lanes], second[:, lanes], decay_rate)


def adam_all(packed, near, up, down, out, given):
    shapes = []
    for n in range(4):
        shapes += [jax.ShapeDtypeStruct(given[3 * n].shape, f32)] * 3
    return pl.pallas_call(
        functools.partial(adam_kernel, packed),
        out_shape=tuple(shapes),
        in_specs=[IN_VMEM] * 16,
        out_specs=(IN_VMEM,) * 12,
        compiler_params=params(),
        name="adam_all",
    )(near, up, down, out, *given)


def summed(into, index, more, other):
    into[index] = (into[index].astype(f32) + more[other].astype(f32)).astype(bf16)


def fold_kernel(batches, inner, dq, dk, dv, dq_all, dk_all, dv_all, cbuf, xbuf, done, qs, qr, zs, zr, xs, xr, cs, cr, local):
    outer = dq.shape[1]
    across = inner // 2
    here = Place(batches, outer, inner)
    o, a, c = here.o, here.a, here.c
    greet(here.z_peers[1:] + here.x_peers[1:] + [here.twin])
    waits = [carry(dq.at[:, o], dq_all.at[:, o], local.at[0])]
    given = (dk, dv)
    results = (dk_all, dv_all)
    order = [t % outer for t in range(1, outer + 1)]
    xorder = list(range(1, across)) + [0]
    to_twin, over = {}, {}
    for t in order:
        for i in (0, 1):
            for d in xorder:
                z, x = here.zs[t], here.xs[d]
                to_twin[i, t, d] = push(given[i].at[:, z, x * 2 + 1 - c], cbuf.at[i, z, x], cs.at[i, t, d], cr.at[i, t, d], here.twin)
    for t in range(1, outer):
        waits.append(push(dq.at[:, here.zs[t]], dq_all.at[:, o], qs.at[t], qr.at[t], here.z_peers[t]))
    for t in order:
        for i in (0, 1):
            for d in xorder:
                to_twin[i, t, d].wait()
                z, x = here.zs[t], here.xs[d]
                for g in range(dq.shape[0]):
                    summed(cbuf, (i, z, x, g), given[i], (g, z, x * 2 + c))
                if d:
                    over[i, t, d] = push(cbuf.at[i, z, x], xbuf.at[i, z, d], xs.at[i, t, d], xr.at[i, t, d], here.x_peers[d])
    for t in order:
        for i in (0, 1):
            z = here.zs[t]
            total = cbuf[i, z, a].astype(f32)
            for d in range(1, across):
                over[i, t, d].wait()
                total = total + xbuf[i, z, d].astype(f32)
            done[i, z] = total.astype(bf16)
            if t:
                waits.append(push(done.at[i, z], results[i].at[:, o], zs.at[i, t], zr.at[i, t], here.z_peers[t]))
            else:
                waits.append(carry(done.at[i, z], results[i].at[:, o], local.at[1 + i]))
    for copy in waits:
        copy.wait()


def fold_heads(dq, dk, dv, batches, inner, ident):
    groups, outer = dq.shape[:2]
    tail = (groups,) + dq.shape[2:]
    across = inner // 2
    piece = jax.ShapeDtypeStruct(dq.shape, dq.dtype)
    scratch = [pltpu.VMEM((2, outer, across) + tail, bf16)] * 2 + [pltpu.VMEM((2, outer) + tail, bf16)]
    scratch += [DMA((outer,))] * 2 + [DMA((2, outer))] * 2 + [DMA((2, outer, across))] * 4 + [DMA((3,))]
    return pl.pallas_call(
        functools.partial(fold_kernel, batches, inner),
        out_shape=(piece, piece, piece),
        in_specs=[ANYWHERE] + [IN_VMEM] * 2,
        out_specs=(ANYWHERE,) * 3,
        scratch_shapes=scratch,
        compiler_params=remote_params(ident, ROOM),
        name="fold_heads",
    )(dq, dk, dv)


def finish_kernel(batches, outer, inner, *refs):
    refs = list(refs)

    def take(n):
        got = refs[:n]
        del refs[:n]
        return got

    dq, dk, dv, up_terms, down_terms, out_terms, mine, normed, tokens, cot, middle_grad = take(11)
    counts, vecs, sums, dots, cos_t, sin_t, lens, mixing = take(8)
    input_grad, near_out, up_out, down_out, out_out, small_out = take(6)
    cosine, sine, gm, gt, gx, partial, from_left, from_right, weight_grad = take(9)
    rm, rt, ry, rx, rz = take(3), take(3), take(3), take(3), take(3)
    terms_n, nc, na, ny, nx, nz, kept, kept_out, kept_n = take(9)
    small, sc, sx, sy, sz = take(5)
    gls, gcs, gcr, gxs, gxr, hrs, hrr, hls, hlr = take(9)
    rls, rcs, rcr, rys, ryr, rxs, rxr, rzs, rzr = take(9)
    ncs, ncr, nys, nyr, nxs, nxr, nzs, nzr, fs, fr, ss, sr = refs
    across = inner // 2
    here = Place(batches, outer, inner)
    o, a, b, c, j = here.o, here.a, here.batch, here.c, here.j
    tall = tokens.shape[0]
    groups = lens.shape[0]
    rows = tall // groups
    share = down_out.shape[0] // BLOCKS
    table = [sorted((s for s in range(outer) if s != i), key=lambda s: (abs(s - i), s)) + [i] for i in range(outer)]
    give, keep = lane_half(1 - c), lane_half(c)

    def layer(n):
        if n == outer - 1:
            return o
        found = 0
        for i in range(outer):
            found = found + (o == i).astype(jnp.int32) * table[i][outer - 2 - n]
        return found

    for z in range(outer):
        cosine[z] = jnp.concatenate([cos_t[z]] * 4, 0).T
        sine[z] = jnp.concatenate([-sin_t[z], sin_t[z]] * 2, 0).T
    greet(here.z_peers[1:] + here.x_peers[1:] + here.y_peers[1:] + [here.twin])
    given = (dk, dv)
    over = {}
    order = [(g, n) for g in range(groups) for n in range(outer)]

    def give_piece(g, n):
        s = layer(n)
        for i in (0, 1):
            for d in range(across):
                x = here.xs[d]
                over["own", g, n, i, d] = carry(given[i].at[g, s, x * 2 + c], gm.at[g, n, i, d], gls.at[g, n, i, d])
                over["twin", g, n, i, d] = push(
                    given[i].at[g, s, x * 2 + 1 - c], gt.at[g, n, i, d], gcs.at[g, n, i, d], gcr.at[g, n, i, d], here.twin
                )

    def theirs(i, y, x, core):
        if i == 0:
            return up_terms.at[pl.ds(2 * core, 2), y, :, x]
        if i == 1:
            return down_terms.at[y, :, x, core]
        return out_terms.at[y, :, x, :, lane_half(core)]

    corners = [(dy, dx) for dy in list(range(1, batches)) + [0] for dx in list(range(1, across)) + [0]]

    def give_rest(dy, dx):
        y, x = here.ys[dy], here.xs[dx]
        for i in range(3):
            over["rown", i, dy, dx] = carry(theirs(i, y, x, c), rm[i].at[dy, dx], rls.at[i, dy, dx])
            over["rtwin", i, dy, dx] = push(
                theirs(i, y, x, 1 - c), rt[i].at[dy, dx], rcs.at[i, dy, dx], rcr.at[i, dy, dx], here.twin
            )

    for n in range(outer):
        give_piece(0, n)
        if n < len(corners):
            give_rest(*corners[n])
    for corner in corners[outer:]:
        give_rest(*corner)
    for n in range(outer):
        give_piece(1, n)

    def fold_core(g, n):
        for i in (0, 1):
            for d in list(range(1, across)) + [0]:
                over["own", g, n, i, d].wait()
                over["twin", g, n, i, d].wait()
                gm[g, n, i, d] = (gm[g, n, i, d].astype(f32) + gt[g, n, i, d].astype(f32)).astype(bf16)
                if d:
                    over["x", g, n, i, d] = push(
                        gm.at[g, n, i, d], gx.at[g, n, i, d], gxs.at[g, n, i, d], gxr.at[g, n, i, d], here.x_peers[d]
                    )

    small[...] = jnp.zeros(small.shape, f32)
    small[0:16] = sums[...]
    weight_grad[...] = jnp.zeros(weight_grad.shape, f32)
    lane = lax.broadcasted_iota(jnp.int32, (rows, 128), 1)

    def halves(value):
        return value[:rows], jnp.where(lane < HEAD, unfold_single(value[rows:], False), 0.0)

    def piece(g, n):
        s = layer(n)
        totals = [dq[g, s].astype(f32)]
        for i in (0, 1):
            total = gm[g, n, i, 0].astype(f32)
            for d in range(1, across):
                over["x", g, n, i, d].wait()
                total = total + gx[g, n, i, d].astype(f32)
            totals.append(total)
        pairs, singles = [], []
        for i, total in enumerate(totals):
            pair, single = halves(total)
            if i == 1:
                pair, single = turn(pair, cosine[s], -sine[s]), turn(single, cosine[s], -sine[s])
                single = jnp.where(lane < HEAD, single, 0.0)
            pairs.append(pair)
            singles.append(single)
        joined = jnp.concatenate(pairs + singles, 1).astype(bf16)
        small[pl.ds(16 + o, 1)] = small[pl.ds(16 + o, 1)] + jnp.sum(joined.astype(f32), 0, keepdims=True)
        partial[g, n] = mm_nt(joined, mine[...].reshape(D, D)).astype(bf16)
        weight_grad[...] += mm(normed[g, s].T, joined)

    line_sends = []

    def hand(g, n):
        if n == outer - 1:
            return
        s = layer(n)
        for buf, sends, recvs, step, outside, away in (
            (from_left, hrs, hrr, 1, o > 0, o < s),
            (from_right, hls, hlr, -1, o < outer - 1, o > s),
        ):
            to = jnp.clip(o + step, 0, outer - 1)
            copy = pltpu.make_async_remote_copy(
                src_ref=buf.at[g, s],
                dst_ref=buf.at[g, s],
                send_sem=sends.at[g, s],
                recv_sem=recvs.at[g, s],
                device_id=(b, to * inner + j),
                device_id_type=MESH,
            )

            @pl.when(away & outside)
            def _(copy=copy, buf=buf):
                copy.wait_recv()
                buf[g, s] = (buf[g, s].astype(f32) + partial[g, n].astype(f32)).astype(bf16)

            @pl.when(away & jnp.logical_not(outside))
            def _(buf=buf):
                buf[g, s] = partial[g, n]

            @pl.when(away)
            def _(copy=copy):
                copy.start()

            line_sends.append((away, copy))

    slots = lax.axis_size("batch") * lax.axis_size("seq") * tall
    count = counts[0, 0:1, 0:1]
    for y in range(1, batches):
        count = count + counts[y, 0:1, 0:1]
    scale = slots / count.astype(f32)
    row = lax.broadcasted_iota(jnp.int32, (rows, 1), 0) + lax.axis_index("seq") * rows

    def arrive(g):
        back = partial[g, outer - 1].astype(f32)
        for buf, recvs, outside in ((from_left, hrr, o > 0), (from_right, hlr, o < outer - 1)):
            copy = pltpu.make_async_remote_copy(
                src_ref=buf.at[g, o],
                dst_ref=buf.at[g, o],
                send_sem=hrs.at[g, o],
                recv_sem=recvs.at[g, o],
                device_id=here.twin,
                device_id_type=MESH,
            )

            @pl.when(outside)
            def _(copy=copy):
                copy.wait_recv()

            back = back + jnp.where(outside, buf[g, o].astype(f32), 0.0)
        at = slice(g * rows, g * rows + rows)
        hat, inverse = normalize(tokens[at].astype(f32))
        small[0:1] = small[0:1] + jnp.sum(back * hat, 0, keepdims=True)
        small[2:3] = small[2:3] + jnp.sum(back, 0, keepdims=True)
        grad = cot[at].astype(f32) * jnp.where(row < lens[g], scale, 0.0)
        input_grad[at] = mixing[1] * grad + middle_grad[at] + normalize_back(back, hat, inverse, vecs[0:1])

    def each(i, add):
        if i == 0:

            def one(n, _):
                add((lax.div(n, outer), lax.rem(n, outer)))
                return 0

            lax.fori_loop(0, 2 * outer, one, 0)
        else:

            def one(z, _):
                add((z,))
                return 0

            lax.fori_loop(0, outer, one, 0)

    def plus(into, at, more, other):
        into[at] = (into[at].astype(f32) + more[other].astype(f32)).astype(bf16)

    def rest_core(dy, dx):
        for i in range(3):
            over["rown", i, dy, dx].wait()
            over["rtwin", i, dy, dx].wait()
            each(i, lambda at: plus(rm[i], (dy, dx) + at, rt[i], (dy, dx) + at))
        if dy and dx == min(1, across - 1):
            y_push(dy, dx)

    def y_push(dy, dx):
        for i in range(3):
            over["ry", i, dy, dx] = push(
                rm[i].at[dy, dx], ry[i].at[dy - 1, dx], rys.at[i, dy, dx], ryr.at[i, dy, dx], here.y_peers[dy]
            )

    def rest_y(dx):
        for i in range(3):
            for dy in range(1, batches):
                over["ry", i, dy, dx].wait()
        if dx:
            for dy in range(1, batches):
                y_push(dy, (dx + 1) % across)
        for i in range(3):
            for dy in range(1, batches):
                each(i, lambda at: plus(rm[i], (0, dx) + at, ry[i], (dy - 1, dx) + at))
            if dx:
                over["rx", i, dx] = push(rm[i].at[0, dx], rx[i].at[dx - 1], rxs.at[i, dx], rxr.at[i, dx], here.x_peers[dx])

    def line_piece(i, z):
        return rm[i].at[0, 0, :, z] if i == 0 else rm[i].at[0, 0, z]

    def rest_x():
        for i in range(3):
            for d in range(1, across):
                over["rx", i, d].wait()
                each(i, lambda at: plus(rm[i], (0, 0) + at, rx[i], (d - 1,) + at))
            for t in range(1, outer):
                over["rz", i, t] = push(line_piece(i, here.zs[t]), rz[i].at[t], rzs.at[i, t], rzr.at[i, t], here.z_peers[t])

    ends = []

    def rest_last():
        for i in range(3):
            for t in range(1, outer):
                over["rz", i, t].wait()
        for p in (0, 1):
            total = rm[0][0, 0, p, o].astype(f32)
            for t in range(1, outer):
                total = total + rz[0][t, p].astype(f32)
            kept[p] = total
        total, total_out = rm[1][0, 0, o].astype(f32), rm[2][0, 0, o].astype(f32)
        for t in range(1, outer):
            total = total + rz[1][t].astype(f32)
            total_out = total_out + rz[2][t].astype(f32)
        down_out[...] = total
        kept_out[...] = total_out
        theirs_rows = pl.ds(pl.multiple_of(share * (1 - c), 8), share)
        ends.append(push(kept.at[:, theirs_rows], up_out.at[pl.ds(2 * c, 2)], fs.at[0], fr.at[0], here.twin))
        ends.append(push(kept_out.at[theirs_rows], out_out.at[:, keep], fs.at[1], fr.at[1], here.twin))
        for p in (0, 1):
            value = kept[p]
            up_out[2 * c + p] = jnp.where(c == 0, value[:share], value[share:])
        value = kept_out[...]
        out_out[:, keep] = jnp.where(c == 0, value[:share], value[share:])

    events = [functools.partial(rest_core, *corner) for corner in corners]
    events += [functools.partial(rest_y, dx) for dx in list(range(1, across)) + [0]] + [rest_x]

    def event():
        if events:
            events.pop(0)()

    fold_core(*order[0])
    event()
    fold_core(*order[1])
    event()
    for n, at in enumerate(order):
        piece(*at)
        if n + 2 < len(order):
            fold_core(*order[n + 2])
        if n >= 1:
            hand(*order[n - 1])
        if n in (1, 3, 5):
            event()
    hand(*order[-1])

    terms_n[...] = weight_grad[...].reshape(terms_n.shape).astype(bf16)
    near_core = push(terms_n.at[:, :, :, :, give], nc, ncs, ncr, here.twin)
    while events:
        event()
    arrive(0)
    near_core.wait()

    def fold_near(i, _):
        y, z, x = lax.div(i, outer * across), lax.rem(lax.div(i, across), outer), lax.rem(i, across)
        value = terms_n[y, z, x]
        own_half = jnp.where(c == 0, value[:, : D // 2], value[:, D // 2 :])
        na[y, z, x] = (own_half.astype(f32) + nc[y, z, x].astype(f32)).astype(bf16)
        return 0

    lax.fori_loop(0, batches * outer * across, fold_near, 0)
    near_y = [push(na.at[here.ys[d]], ny.at[d - 1], nys.at[d], nyr.at[d], here.y_peers[d]) for d in range(1, batches)]
    for d in range(1, batches):
        near_y[d - 1].wait()

        def add_y(i, _):
            z, x = lax.div(i, across), lax.rem(i, across)
            plus(na, (b, z, x), ny, (d - 1, z, x))
            return 0

        lax.fori_loop(0, outer * across, add_y, 0)
    near_x = [
        push(na.at[b, :, here.xs[d]], nx.at[d - 1], nxs.at[d], nxr.at[d], here.x_peers[d]) for d in range(1, across)
    ]
    arrive(1)
    lane_wide = lax.broadcasted_iota(jnp.int32, (1, D), 1)
    line = jnp.where(lane_wide == 0, jnp.sum(sums[VECTORS : VECTORS + 1], 1, keepdims=True), 0.0)
    for i in range(1, mixing.shape[0]):
        line = line + jnp.where(lane_wide == i, scale * jnp.sum(dots[i : i + 1], 1, keepdims=True), 0.0)
    small[VECTORS : VECTORS + 1] = line
    small_copy = push(small, sc, ss.at[0], sr.at[0], here.twin)
    for d in range(1, across):
        near_x[d - 1].wait()

        def add_x(z, _):
            plus(na, (b, z, a), nx, (d - 1, z))
            return 0

        lax.fori_loop(0, outer, add_x, 0)
    near_z = [push(na.at[b, here.zs[t], a], nz.at[o], nzs.at[t], nzr.at[t], here.z_peers[t]) for t in range(1, outer)]
    nz[o] = na[b, o, a]
    small_copy.wait()
    sc[...] = sc[...] + small[...]
    sx[a] = sc[...]
    copies = [push(sc, sx.at[a], ss.at[d], sr.at[d], here.x_peers[d]) for d in range(1, across)]
    for copy in copies:
        copy.wait()
    total = sx[0]
    for x in range(1, across):
        total = total + sx[x]
    sc[...] = total
    sy[b] = total
    copies = [push(sc, sy.at[b], ss.at[across + d], sr.at[across + d], here.y_peers[d]) for d in range(1, batches)]
    rest_last()
    for copy in near_z:
        copy.wait()
    for z in range(outer):
        kept_n[z] = nz[z].astype(f32)
    theirs_rows = pl.ds(pl.multiple_of(share * (1 - c), 8), share)
    ends.append(push(kept_n.at[:, theirs_rows], near_out.at[:, :, keep], fs.at[2], fr.at[2], here.twin))
    for z in range(outer):
        value = kept_n[z]
        near_out[z, :, keep] = jnp.where(c == 0, value[:share], value[share:])
    for copy in copies:
        copy.wait()
    total = sy[0]
    for y in range(1, batches):
        total = total + sy[y]
    sc[...] = total
    sz[o] = total
    copies = [
        push(sc, sz.at[o], ss.at[across + batches + t], sr.at[across + batches + t], here.z_peers[t]) for t in range(1, outer)
    ]
    for copy in copies:
        copy.wait()
    total = sz[0]
    for z in range(1, outer):
        total = total + sz[z]
    small_out[...] = total[:16]
    for n in range(3):
        small_out[4 + n : 5 + n] = jnp.concatenate(plain_tiles(lambda z: total[16 + z : 17 + z], n, outer), 1)
    for copy in ends:
        copy.wait()
    for away, copy in line_sends:

        @pl.when(away)
        def _(copy=copy):
            copy.wait_send()


def plain_tiles(read, n, outer):
    tiles = []
    for z in range(0, outer, 2):
        even, odd = read(z), read(z + 1)
        pair, single = slice(128 * n, 128 * n + 128), slice(384 + 128 * n, 512 + 128 * n)
        lane = lax.broadcasted_iota(jnp.int32, even[:, single].shape, 1)
        middle = jnp.where(lane < HEAD, even[:, single], pltpu.roll(odd[:, single], HEAD, 1))
        tiles += [even[:, pair], middle, odd[:, pair]]
    return tiles


def finish_layer(
    dq, dk, dv, up_terms, down_terms, out_terms, mine, normed, tokens, cot, middle_grad, counts, vecs, sums, dots, cos_t, sin_t,
    lens, mixing, batches, outer, inner, ident,
):
    across = inner // 2
    tall = tokens.shape[0]
    groups = lens.shape[0]
    rows = tall // groups
    folded = dq.shape[2]
    wide = out_terms.shape[3]
    share = wide // 2
    low = lambda *shape: pltpu.VMEM(shape, bf16)
    full = lambda *shape: pltpu.VMEM(shape, f32)
    tails = ((2, outer, wide, D), (outer, BLOCKS * share, D), (outer, wide, D // 2))
    ends = ((2, wide, D), (BLOCKS * share, D), (wide, D // 2))
    grid = (batches, outer, across)
    scratch = [
        full(outer, rows, 128),
        full(outer, rows, 128),
        low(groups, outer, 2, across, folded, 128),
        low(groups, outer, 2, across, folded, 128),
        low(groups, outer, 2, across, folded, 128),
        low(groups, outer, rows, D),
        low(groups, outer, rows, D),
        low(groups, outer, rows, D),
        full(D, D),
    ]
    scratch += [low(batches, across, *tail) for tail in tails]
    scratch += [low(batches, across, *tail) for tail in tails]
    scratch += [low(batches - 1, across, *tail) for tail in tails]
    scratch += [low(across - 1, *tail) for tail in tails]
    scratch += [low(outer, *end) for end in ends]
    scratch += [
        low(*grid, wide, D),
        low(*grid, wide, D // 2),
        low(*grid, wide, D // 2),
        low(batches - 1, outer, across, wide, D // 2),
        low(across - 1, outer, wide, D // 2),
        low(outer, wide, D // 2),
        full(2, wide, D),
        full(wide, D // 2),
        full(outer, wide, D // 2),
        full(24, D),
        full(24, D),
        full(across, 24, D),
        full(batches, 24, D),
        full(outer, 24, D),
    ]
    scratch += [DMA((groups, outer, 2, across))] * 5 + [DMA((groups, outer))] * 4
    scratch += [DMA((3, batches, across))] * 5 + [DMA((3, across))] * 2 + [DMA((3, outer))] * 2
    scratch += [DMA] * 2 + [DMA((batches,))] * 2 + [DMA((across,))] * 2 + [DMA((outer,))] * 2 + [DMA((3,))] * 2
    scratch += [DMA((across + batches + outer,))] * 2
    return pl.pallas_call(
        functools.partial(finish_kernel, batches, outer, inner),
        out_shape=(
            jax.ShapeDtypeStruct((tall, D), f32),
            jax.ShapeDtypeStruct((outer, share, D), f32),
            jax.ShapeDtypeStruct((BLOCKS, share, D), f32),
            jax.ShapeDtypeStruct((BLOCKS * share, D), f32),
            jax.ShapeDtypeStruct((share, D), f32),
            jax.ShapeDtypeStruct((16, D), f32),
        ),
        in_specs=[IN_VMEM] + [ANYWHERE] * 5 + [IN_VMEM] * 11 + [IN_SMEM] * 2,
        out_specs=(IN_VMEM,) * 6,
        scratch_shapes=scratch,
        compiler_params=remote_params(ident, 60 << 20),
        name="finish_layer",
    )(
        dq, dk, dv, up_terms, down_terms, out_terms, mine, normed, tokens, cot, middle_grad, counts, vecs, sums, dots, cos_t, sin_t,
        lens, mixing,
    )


def body(
    tokens_in,
    earlier_outs,
    out_cotangent,
    seq_lengths,
    qkv_weight,
    out_weight,
    up_weight,
    down_weight,
    qkv_first,
    qkv_second,
    out_first,
    out_second,
    up_first,
    up_second,
    down_first,
    down_second,
    small_params,
    small_first,
    small_second,
):
    groups, rows, _ = tokens_in.shape
    tall = groups * rows
    batches = lax.axis_size("batch")
    seq_count = lax.axis_size("seq")
    seq_rank = lax.axis_index("seq")
    devices = batches * seq_count
    outer = math.gcd(seq_count, D // HEAD)
    inner = seq_count // outer
    share = D // devices
    remote = share % 8 == 0
    everywhere = ("batch", "seq")
    grid = (batches, outer, inner // 2)

    tokens = tokens_in.reshape(tall, D)
    cot = out_cotangent.reshape(tall, D)
    earlier = earlier_outs.reshape(-1, tall, D)
    vecs = jnp.pad(small_params[: VECTORS * D].reshape(VECTORS, D), ((0, 16 - VECTORS), (0, 0)))
    mixing = small_params[VECTORS * D :]

    freq = 10000.0 ** (-jnp.arange(HEAD // 2, dtype=f32) * 2.0 / HEAD)
    query_pos = seq_rank * rows + jnp.arange(rows, dtype=jnp.int32)
    turned = query_pos.astype(f32)[:, None] * freq[None, :]
    cosine = jnp.concatenate([jnp.cos(turned)] * 4, 1)
    sine = jnp.concatenate([-jnp.sin(turned), jnp.sin(turned)] * 2, 1)
    block_pos = (jnp.arange(outer) * inner + seq_rank % inner)[:, None] * rows + jnp.arange(rows)[None, :]
    block_turned = block_pos.astype(f32)[:, None, :] * freq[None, :, None]
    block_cos, block_sin = jnp.cos(block_turned), jnp.sin(block_turned)

    def by_rows(shard):
        return shard.astype(bf16).reshape(share, -1, D).transpose(1, 0, 2)

    def by_blocks(gathered):
        return gathered.transpose(1, 0, 2, 3).reshape(-1, D, D)

    if remote:
        packed_bias = jnp.stack([
            jnp.concatenate(packed_rows(small_params[4 * D : 7 * D], z)) for z in range(outer)
        ])
        packed_bias = jnp.pad(packed_bias, ((0, 8 - outer), (0, 0)))
        mine, normed, q, k, v, out, up, down, counts, mixture, dots, attended, turned_out, log_total = start_layer(
            qkv_weight, out_weight, up_weight, down_weight, seq_lengths, mixing, tokens, cot, earlier, vecs, packed_bias,
            block_cos, block_sin, batches, outer, inner, 1,
        )
        out, up, down = out.reshape(D, D), up.reshape(BLOCKS, D, D), down.reshape(BLOCKS, D, D)
    else:
        near = by_blocks(lax.all_gather(jnp.concatenate([by_rows(qkv_weight), by_rows(out_weight)], 0), everywhere, axis=0))
        out = near[3]
        up = by_blocks(lax.all_gather(by_rows(up_weight), everywhere, axis=0))
        down = lax.all_gather(down_weight.astype(bf16), everywhere, axis=0).reshape(BLOCKS, D, D)
        counts = jnp.full((1, 8, 128), lax.psum(jnp.sum(seq_lengths), "batch"), jnp.int32)
        wide = tokens.astype(f32)
        normed = (normalize(wide)[0] * vecs[0] + vecs[2]).astype(bf16)
        live = (query_pos[None, :] < seq_lengths[:, None]).astype(f32).reshape(tall, 1)
        terms = [tokens] + [earlier[i] for i in range(earlier.shape[0])]
        mixture = sum(mixing[1 + i] * term.astype(f32) for i, term in enumerate(terms))
        sums = [jnp.sum(cot.astype(f32) * live * term.astype(f32), 0) for term in terms]
        dots = jnp.pad(jnp.stack(sums), ((1, 15 - len(sums)), (0, 0)))
        q, k, v, attended, turned_out, log_total = spread_heads(
            normed, near, vecs, seq_lengths, cosine, sine, batches, outer, inner, 2
        )

    mixed, grad_mine, middle_grad, out_term, up_terms, down_terms, sums = middle_layer(
        attended, out, up, down, tokens, cot, mixture, counts, vecs, seq_lengths, mixing, batches, outer, inner, 3
    )
    dq, dk, dv = attend_back(seq_lengths, q, k, v, grad_mine, turned_out, log_total, block_cos, block_sin, inner)
    if remote:
        pieces = grid + (2 * share, D)
        input_grad, near_grad, up_grad, down_grad, out_grad, small = finish_layer(
            dq, dk, dv, up_terms.reshape((BLOCKS,) + pieces), down_terms.reshape(grid + (2, BLOCKS * share, D)), out_term.reshape(pieces),
            mine, normed, tokens, cot, middle_grad, counts, vecs, sums, dots, block_cos, block_sin, seq_lengths, mixing,
            batches, outer, inner, 4,
        )
    else:

        def scattered(terms):
            return lax.psum_scatter(terms.reshape(-1, devices, share, D), everywhere, scatter_dimension=1).astype(f32)

        dq, dk, dv = fold_heads(dq, dk, dv, batches, inner, 5)
        input_grad, near_terms, small = back_layer(
            dq, dk, dv, cosine, sine, normed, tokens, near, vecs, cot, counts, seq_lengths, mixing, middle_grad, out_term, sums, dots, outer
        )
        near_grad, up_grad = scattered(near_terms), scattered(up_terms)
        out_grad = near_grad[3]
        down_grad = lax.psum_scatter(down_terms.reshape(devices, -1, D), everywhere, scatter_dimension=0).astype(f32)
        small = lax.psum(small, everywhere)
    small_grad = small.reshape(-1)[: small_params.shape[0]]
    small_step, small_first_new = adam(small_params, small_grad, small_first, small_second, 0.0)
    (
        qkv_grad, qkv_step, qkv_first_new, out_grad, out_step, out_first_new,
        up_grad, up_step, up_first_new, down_grad, down_step, down_first_new,
    ) = adam_all(
        remote, near_grad, up_grad, down_grad, out_grad,
        (qkv_weight, qkv_first, qkv_second, out_weight, out_first, out_second,
         up_weight, up_first, up_second, down_weight, down_first, down_second),
    )
    return (
        mixed.reshape(tokens_in.shape),
        input_grad.reshape(tokens_in.shape),
        qkv_grad,
        out_grad,
        up_grad,
        down_grad,
        small_grad,
        qkv_step,
        out_step,
        up_step,
        down_step,
        small_step,
        qkv_first_new,
        out_first_new,
        up_first_new,
        down_first_new,
        small_first_new,
    )


def solution(mesh):
    placed = (
        P("batch", "seq", None),
        P(None, "batch", "seq", None),
        P("batch", "seq", None),
        P("batch"),
        P(("batch", "seq"), None),
        P(("batch", "seq"), None),
        P(("batch", "seq"), None),
        P(("batch", "seq"), None),
        P(("batch", "seq"), None),
        P(("batch", "seq"), None),
        P(("batch", "seq"), None),
        P(("batch", "seq"), None),
        P(("batch", "seq"), None),
        P(("batch", "seq"), None),
        P(("batch", "seq"), None),
        P(("batch", "seq"), None),
        P(),
        P(),
        P(),
    )
    return jax.shard_map(
        body,
        mesh=mesh,
        in_specs=placed,
        out_specs=(
            P("batch", "seq", None),
            P("batch", "seq", None),
            P(("batch", "seq"), None),
            P(("batch", "seq"), None),
            P(("batch", "seq"), None),
            P(("batch", "seq"), None),
            P(),
            P(("batch", "seq"), None),
            P(("batch", "seq"), None),
            P(("batch", "seq"), None),
            P(("batch", "seq"), None),
            P(),
            P(("batch", "seq"), None),
            P(("batch", "seq"), None),
            P(("batch", "seq"), None),
            P(("batch", "seq"), None),
            P(),
        ),
        check_vma=False,
    )
```

```python
import functools
import math

import jax
import jax.numpy as jnp
from jax import lax
from jax.experimental import pallas as pl
from jax.experimental.pallas import tpu as pltpu
from jax.sharding import PartitionSpec as P

D = 768
FF = 3072
HEAD = 64
BLOCKS = FF // D
VECTORS = 9 + BLOCKS
bf16 = jnp.bfloat16
f32 = jnp.float32
NEG = -1e30

beta_one = 0.9
beta_two = 0.999
adam_eps = 1e-08
learn_rate = 0.01
decay_rate = 0.1
adam_step = 10

MESH = pl.DeviceIdType.MESH
ANYWHERE = pl.BlockSpec(memory_space=pl.ANY)
IN_VMEM = pl.BlockSpec(memory_space=pltpu.VMEM)
IN_SMEM = pl.BlockSpec(memory_space=pltpu.SMEM)
DMA = pltpu.SemaphoreType.DMA
ROOM = 56 << 20

def mm(a, b):
    return lax.dot_general(a, b, (((1,), (0,)), ((), ())), preferred_element_type=f32)


def mm_nt(a, b):
    return lax.dot_general(a, b, (((1,), (1,)), ((), ())), preferred_element_type=f32)


def params():
    return pltpu.CompilerParams(vmem_limit_bytes=ROOM)


def remote_params(ident, vmem=None):
    return pltpu.CompilerParams(collective_id=ident, has_side_effects=True, vmem_limit_bytes=vmem)


class Place:
    def __init__(self, batches, outer, inner):
        self.batch = lax.axis_index("batch")
        rank = lax.axis_index("seq")
        self.o = lax.div(rank, inner)
        self.j = lax.rem(rank, inner)
        self.a = lax.div(self.j, 2)
        self.c = lax.rem(rank, 2)
        across = inner // 2
        self.zs = [lax.rem(self.o + t, outer) for t in range(outer)]
        self.xs = [lax.rem(self.a + t, across) for t in range(across)]
        self.ys = [lax.rem(self.batch + t, batches) for t in range(batches)]
        self.z_from = [lax.rem(self.o + outer - t, outer) for t in range(outer)]
        self.x_from = [lax.rem(self.a + across - t, across) for t in range(across)]
        self.y_from = [lax.rem(self.batch + batches - t, batches) for t in range(batches)]
        self.z_peers = [(self.batch, z * inner + self.j) for z in self.zs]
        self.x_peers = [(self.batch, self.o * inner + x * 2 + self.c) for x in self.xs]
        self.y_peers = [(y, rank) for y in self.ys]
        self.twin = (self.batch, self.o * inner + self.a * 2 + (1 - self.c))


def greet(peers):
    barrier = pltpu.get_barrier_semaphore()
    for peer in peers:
        pl.semaphore_signal(barrier, inc=1, device_id=peer, device_id_type=MESH)
    pl.semaphore_wait(barrier, len(peers))


def push(src, dst, send, recv, peer):
    copy = pltpu.make_async_remote_copy(
        src_ref=src, dst_ref=dst, send_sem=send, recv_sem=recv, device_id=peer, device_id_type=MESH
    )
    copy.start()
    return copy


def carry(src, dst, sem):
    copy = pltpu.make_async_copy(src, dst, sem)
    copy.start()
    return copy


def normalize(values):
    center = values - jnp.mean(values, -1, keepdims=True)
    inverse = lax.rsqrt(jnp.mean(center * center, -1, keepdims=True) + 1e-05)
    return center * inverse, inverse


def normalize_back(grad, hat, inverse, gain):
    scaled = grad * gain
    part = scaled - jnp.mean(scaled, -1, keepdims=True) - hat * jnp.mean(scaled * hat, -1, keepdims=True)
    return part * inverse


def turn(value, cosine, sine):
    lane = lax.broadcasted_iota(jnp.int32, value.shape, 1)
    other = jnp.where(lax.rem(lane, HEAD) < HEAD // 2, pltpu.roll(value, 128 - HEAD // 2, 1), pltpu.roll(value, HEAD // 2, 1))
    return value * cosine + other * sine


def fold_single(value, odd):
    half = value.shape[0] // 2
    top, bottom = value[:half], value[half:]
    lane = lax.broadcasted_iota(jnp.int32, top.shape, 1)
    if odd:
        return jnp.where(lane < HEAD, pltpu.roll(top, HEAD, 1), bottom)
    return jnp.where(lane < HEAD, top, pltpu.roll(bottom, HEAD, 1))


def unfold_single(value, high):
    turned = pltpu.roll(value, HEAD, 1)
    return jnp.concatenate([turned, value] if high else [value, turned], 0)


def unfold_heads(read, rows, outer):
    tiles = [None] * (outer * 3 // 2)
    for o in range(0, outer, 2):
        base = 3 * o * HEAD // 128
        first, second = read(o), read(o + 1)
        tiles[base] = first[:rows]
        tiles[base + 2] = second[:rows]
        low, high = unfold_single(first[rows:], False), unfold_single(second[rows:], True)
        lane = lax.broadcasted_iota(jnp.int32, low.shape, 1)
        tiles[base + 1] = jnp.where(lane < HEAD, low, high)
    return tiles


def fold_heads_of(write, tile_of, outer):
    for o in range(outer):
        first = 3 * o * HEAD
        odd = first % 128 != 0
        pair = (first + HEAD if odd else first) // 128
        single = (first if odd else first + 128) // 128
        write(o, jnp.concatenate([tile_of(pair), fold_single(tile_of(single), odd)], 0))


def lane_half(core):
    return pl.ds(pl.multiple_of(core * (D // 2), 128), D // 2)


def packed_tiles(read, z):
    pairs, singles = [], []
    for n in range(3):
        base = n * D + 3 * z * HEAD
        odd = base % 128 != 0
        pairs.append(read(base + HEAD if odd else base))
        single = read(base - HEAD if odd else base + 128)
        singles.append(pltpu.roll(single, HEAD, 1) if odd else single)
    return pairs + singles


class Line:
    def __init__(self, here, outer, inner, slot, own_send, hand_send, recv):
        self.here, self.outer, self.slot = here, outer, slot
        self.own_send, self.hand_send, self.recv = own_send, hand_send, recv
        self.inner = inner
        self.sends = []
        self.table = [sorted((s for s in range(outer) if s != i), key=lambda s: (abs(s - i), s)) for i in range(outer)]

    def origin(self, n):
        if n == 0:
            return self.here.o
        found = 0
        for i in range(self.outer):
            found = found + (self.here.o == i).astype(jnp.int32) * self.table[i][n - 1]
        return found

    def peer(self, z):
        return (self.here.batch, z * self.inner + self.here.j)

    def send(self, source, key, s, to, sem):
        there = jnp.clip(to, 0, self.outer - 1)
        copy = pltpu.make_async_remote_copy(
            src_ref=source,
            dst_ref=self.slot(key, s),
            send_sem=sem,
            recv_sem=self.recv.at[key, s],
            device_id=self.peer(there),
            device_id_type=MESH,
        )
        valid = (to >= 0) & (to < self.outer)

        @pl.when(valid)
        def _():
            copy.start()

        self.sends.append((valid, copy))

    def start(self, key, source):
        o = self.here.o
        self.send(source, key, o, o + 1, self.own_send.at[key, 0])
        self.send(source, key, o, o - 1, self.own_send.at[key, 1])

    def arrive(self, key, n):
        o, s = self.here.o, self.origin(n)
        place = self.slot(key, s)
        pltpu.make_async_remote_copy(
            src_ref=place,
            dst_ref=place,
            send_sem=self.hand_send.at[key, n],
            recv_sem=self.recv.at[key, s],
            device_id=self.here.twin,
            device_id_type=MESH,
        ).wait_recv()
        step = 1 - 2 * (s > o).astype(jnp.int32)
        self.send(place, key, s, o + step, self.hand_send.at[key, n])
        return s

    def finish(self):
        for valid, copy in self.sends:

            @pl.when(valid)
            def _(copy=copy):
                copy.wait_send()


def start_kernel(batches, outer, inner, *refs):
    refs = list(refs)

    def take(n):
        got = refs[:n]
        del refs[:n]
        return got

    qkv, out, up, down, lens, mixing, tokens, cot, earlier, vecs, cos_t, sin_t = take(12)
    mine, normed, q_all, k_all, v_all, out_all, up_all, down_all, counts, mixture, dots, o_mine, ot, lse = take(14)
    own, got, near, up_bit, out_bit, down_bit, queue, count, wide_s, cosine, sine, packed_bias = take(12)
    zs, zr, xs, xr, ys, yr, cs, cr, ts, tr, ns, nr, local, es = take(14)
    nls, nlf, nlr, rls, rlf, rlr, rxs, rxr, rys, ryr, rcs, rcr, axs, axr, acs, acr = take(16)
    attend_refs = refs
    across = inner // 2
    here = Place(batches, outer, inner)
    o, a, b, c, j = here.o, here.a, here.batch, here.c, here.j
    earlier_count, tall, _ = earlier.shape
    groups = lens.shape[0]
    rows = tall // groups
    fetches = {e: carry(earlier.at[e], queue.at[e], es.at[e]) for e in range(2)}
    for g in range(groups):
        hat, _ = normalize(tokens[g * rows : g * rows + rows].astype(f32))
        normed[g, o] = (hat * vecs[0:1] + vecs[2:3]).astype(bf16)
    for z in range(outer):
        for i, tile in enumerate(packed_tiles(lambda lane: qkv[:, lane : lane + 128], z)):
            own[z, :, 128 * i : 128 * i + 128] = tile
    for i in range(BLOCKS):
        own[outer + 1 + i] = up[:, i * D : i * D + D]
    own[outer] = out[...]
    here_count = lens[0]
    for g in range(1, groups):
        here_count = here_count + lens[g]
    count[...] = jnp.zeros(count.shape, jnp.int32) + here_count
    greet(here.z_peers[1:] + here.x_peers[1:] + here.y_peers[1:] + [here.twin])
    give = lane_half(1 - c)
    keep = lane_half(c)
    near_count = outer + 1
    swaps = [
        push(own.at[pl.ds(0, near_count), :, give], got.at[pl.ds(0, near_count), :, pl.ds(0, D // 2)], ts.at[0], tr.at[0], here.twin),
        push(own.at[pl.ds(near_count + 2 * (1 - c), 2)], got.at[pl.ds(near_count, 2)], ts.at[1], tr.at[1], here.twin),
    ]
    line = Line(here, outer, inner, lambda g, s: normed.at[g, s], nls, nlf, nlr)
    line.start(0, normed.at[0, o])
    waits = [carry(count, counts.at[b], local.at[0])]
    for d in range(1, batches):
        waits.append(push(count, counts.at[b], ns.at[d], nr.at[d], here.y_peers[d]))

    def joined(own_part, other):
        low = jnp.where(c == 0, own_part, other)
        high = jnp.where(c == 0, other, own_part)
        return jnp.concatenate([low, high], 0).astype(bf16)

    def slot(y, z, x):
        return mine.at[y, z, x, :, keep]

    arrivals, twins = {}, []

    def onward(source, y, z, x, t, dx, dy):
        to = slot(y, z, x)
        if dx == 0 and dy == 0:
            for d in range(1, across):
                arrivals["x", t, d] = push(source, to, xs.at[t, d], xr.at[t, d], here.x_peers[d])
        if dy == 0:
            for d in range(1, batches):
                arrivals["y", t, dx, d] = push(source, to, ys.at[t, dx, d], yr.at[t, dx, d], here.y_peers[d])
        twins.append(push(source, to, cs.at[t, dx, dy], cr.at[t, dx, dy], here.twin))

    swaps[0].wait()
    for z in range(outer + 1):
        own_part = jnp.where(c == 0, own[z, :, : D // 2], own[z, :, D // 2 :])
        value = joined(own_part, got[z, :, : D // 2])
        if z < outer:
            near[z] = value
        else:
            out_bit[...] = value
    copies = {}
    for t in range(1, outer):
        copies[t] = push(near.at[here.zs[t]], slot(b, o, a), zs.at[t], zr.at[t], here.z_peers[t])
    twins.append(carry(near.at[o], slot(b, o, a), local.at[1]))
    onward(near.at[o], b, o, a, 0, 0, 0)
    swaps[1].wait()
    for p in (0, 1):
        up_bit[p] = joined(own[near_count + 2 * c + p], got[near_count + p])
    down_bit[...] = down[...].astype(bf16)
    for t in range(1, outer):
        copies[t].wait()
        onward(slot(b, here.z_from[t], a), b, here.z_from[t], a, t, 0, 0)

    bits = (up_bit, down_bit, out_bit)

    def rest_slot(i, y, z, x):
        if i == 0:
            return up_all.at[pl.ds(2 * c, 2), y, z, x]
        if i == 1:
            return down_all.at[y, z, x, c]
        return out_all.at[y, z, x, :, keep]

    rest_x, rest_y = [], []
    rest = Line(here, outer, inner, lambda i, s: rest_slot(i, b, s, a), rls, rlf, rlr)

    def rest_onward(i, n, s, source):
        to = rest_slot(i, b, s, a)
        for d in range(1, across):
            rest_x.append((i, n, s, d, push(source, to, rxs.at[i, n, d], rxr.at[i, n, d], here.x_peers[d])))
        for d in range(1, batches):
            rest_y.append((i, n, s, 0, d, push(source, to, rys.at[i, n, 0, d], ryr.at[i, n, 0, d], here.y_peers[d])))
        waits.append(push(source, to, rcs.at[i, n, 0, 0], rcr.at[i, n, 0, 0], here.twin))

    def rest_line(n):
        for i in range(3):
            s = rest.arrive(i, n)
            rest_onward(i, n, s, rest_slot(i, b, s, a))

    def rest_across():
        if rest_x:
            i, n, s, d, copy = rest_x.pop(0)
            copy.wait()
            piece = rest_slot(i, b, s, here.x_from[d])
            for e in range(1, batches):
                rest_y.append((i, n, s, d, e, push(piece, piece, rys.at[i, n, d, e], ryr.at[i, n, d, e], here.y_peers[e])))
            waits.append(push(piece, piece, rcs.at[i, n, d, 0], rcr.at[i, n, d, 0], here.twin))

    def rest_twin():
        if rest_y:
            i, n, s, d, e, copy = rest_y.pop(0)
            copy.wait()
            piece = rest_slot(i, here.y_from[e], s, here.x_from[d])
            waits.append(push(piece, piece, rcs.at[i, n, d, e], rcr.at[i, n, d, e], here.twin))

    late = {0: [], 1: []}
    spread = {0: [], 1: []}

    def project(g, n, s):
        wide_s[...] = mm(normed[g, s], mine[...].reshape(D, D)) + packed_bias[pl.ds(o, 1)]
        for i, dest in enumerate((q_all, k_all, v_all)):
            pair, single = wide_s[:, 128 * i : 128 * i + 128], wide_s[:, 384 + 128 * i : 512 + 128 * i]
            if i < 2:
                pair, single = turn(pair, cosine[s], sine[s]), turn(single, cosine[s], sine[s])
            value = jnp.concatenate([pair, fold_single(single, False)], 0).astype(bf16)
            if i == 0:
                q_all[g, s] = value
            else:
                dest[g, s, j] = value
        for i, dest in enumerate((k_all, v_all)):
            piece = dest.at[g, s, j]
            for d in range(1, across):
                late[g].append((i, n, s, d, push(piece, piece, axs.at[g, i, n, d], axr.at[g, i, n, d], here.x_peers[d])))
            spread[g].append(push(piece, piece, acs.at[g, i, n, 0], acr.at[g, i, n, 0], here.twin))

    def settle(g, count):
        for _ in range(count):
            if late[g]:
                i, n, s, d, copy = late[g].pop(0)
                copy.wait()
                piece = (k_all, v_all)[i].at[g, s, here.x_from[d] * 2 + c]
                spread[g].append(push(piece, piece, acs.at[g, i, n, d], acr.at[g, i, n, d], here.twin))

    def arrive(g, n):
        project(g, n, line.arrive(g, n))

    def live_rows(value):
        row = lax.broadcasted_iota(jnp.int32, (rows, 1), 0) + lax.axis_index("seq") * rows
        parts = [jnp.where(row < lens[g], value[g * rows : g * rows + rows], 0.0) for g in range(groups)]
        return jnp.concatenate(parts, 0)

    def plain():
        wide = tokens[...].astype(f32)
        grad = live_rows(cot[...].astype(f32))
        dots[...] = jnp.zeros(dots.shape, f32)
        dots[1:2] = jnp.sum(grad * wide, 0, keepdims=True)
        mixture[...] = mixing[1] * wide

    def mix(e):
        fetches[e].wait()
        wide = queue[e % 2].astype(f32)
        grad = live_rows(cot[...].astype(f32))
        dots[2 + e : 3 + e] = jnp.sum(grad * wide, 0, keepdims=True)
        mixture[...] = mixture[...] + mixing[2 + e] * wide
        if e + 2 < earlier_count:
            fetches[e + 2] = carry(earlier.at[e + 2], queue.at[e % 2], es.at[e + 2])

    steps = [plain] + [functools.partial(mix, e) for e in range(earlier_count)]

    def work(n=1):
        for _ in range(n):
            if steps:
                steps.pop(0)()

    for z in range(outer):
        bias = packed_tiles(lambda lane: vecs[4 + lane // D : 5 + lane // D, lane % D : lane % D + 128], z)
        packed_bias[z : z + 1, :] = jnp.concatenate(bias, 1)
        cosine[z] = jnp.concatenate([cos_t[z]] * 4, 0).T
        sine[z] = jnp.concatenate([-sin_t[z], sin_t[z]] * 2, 0).T
    first = line.arrive(0, 1)
    for t in range(outer):
        for d in range(1, across):
            arrivals["x", t, d].wait()
            z, x = here.z_from[t], here.x_from[d]
            onward(slot(b, z, x), b, z, x, t, d, 0)
    for i in range(3):
        rest.start(i, bits[i])
    for i in range(3):
        waits.append(carry(bits[i], rest_slot(i, b, o, a), local.at[2 + i]))
        rest_onward(i, 0, o, bits[i])
    for t in range(outer):
        for dx in range(across):
            for dy in range(1, batches):
                arrivals["y", t, dx, dy].wait()
                y, z, x = here.y_from[dy], here.z_from[t], here.x_from[dx]
                onward(slot(y, z, x), y, z, x, t, dx, dy)
    second = line.arrive(0, 2)
    for _ in range(3):
        rest_across()
    for copy in twins:
        copy.wait()
    project(0, 0, o)
    project(0, 1, first)
    project(0, 2, second)
    for n in range(3, outer):
        arrive(0, n)
    line.start(1, normed.at[1, o])
    settle(0, 2)
    rest_line(1)
    work(3)
    settle(0, 2)
    rest_line(2)
    settle(0, 2 * outer * across)
    project(1, 0, o)
    for copy in spread[0]:
        copy.wait()
    events = [
        lambda: rest_line(3) if outer > 3 else None,
        lambda: (rest_across(), rest_across(), rest_across()),
        lambda: arrive(1, 1),
        lambda: (settle(1, 2), rest_across(), rest_across(), rest_across()),
        lambda: arrive(1, 2),
        lambda: (rest_twin(), rest_twin(), rest_twin()),
        lambda: (settle(1, 2), rest_across(), rest_across(), rest_across()),
        lambda: [arrive(1, n) for n in range(3, outer)],
    ]
    attend_group(0, outer, inner, lens, q_all, k_all, v_all, o_mine, ot, lse, attend_refs, here, events)
    while events:
        events.pop(0)()
    work(4)
    while rest_x:
        rest_across()
    settle(1, 2 * outer * across)
    work(len(steps))
    for copy in spread[1]:
        copy.wait()
    events = [lambda: (rest_twin(), rest_twin(), rest_twin())] * 8
    attend_group(1, outer, inner, lens, q_all, k_all, v_all, o_mine, ot, lse, attend_refs, here, events)
    while rest_y:
        rest_twin()
    line.finish()
    rest.finish()
    for copy in waits:
        copy.wait()


def start_layer(qkv, out, up, down, lens, mixing, tokens, cot, earlier, vecs, cos_t, sin_t, batches, outer, inner, ident):
    across = inner // 2
    share = qkv.shape[0]
    tall = tokens.shape[0]
    groups = lens.shape[0]
    rows = tall // groups
    grid = (batches, outer, across)
    folded = rows + rows // 2
    buf = pltpu.VMEM
    return pl.pallas_call(
        functools.partial(start_kernel, batches, outer, inner),
        out_shape=(
            jax.ShapeDtypeStruct(grid + (2 * share, D), bf16),
            jax.ShapeDtypeStruct((groups, outer, rows, D), bf16),
            jax.ShapeDtypeStruct((groups, outer, folded, 128), bf16),
            jax.ShapeDtypeStruct((groups, outer, inner, folded, 128), bf16),
            jax.ShapeDtypeStruct((groups, outer, inner, folded, 128), bf16),
            jax.ShapeDtypeStruct(grid + (2 * share, D), bf16),
            jax.ShapeDtypeStruct((BLOCKS,) + grid + (2 * share, D), bf16),
            jax.ShapeDtypeStruct(grid + (2, BLOCKS * share, D), bf16),
            jax.ShapeDtypeStruct((batches, 8, 128), jnp.int32),
            jax.ShapeDtypeStruct((tall, D), f32),
            jax.ShapeDtypeStruct((16, D), f32),
            jax.ShapeDtypeStruct((outer, groups, folded, 128), bf16),
            jax.ShapeDtypeStruct((groups, outer, 3 * HEAD, rows), f32),
            jax.ShapeDtypeStruct((groups, outer, 8, rows), f32),
        ),
        in_specs=[IN_VMEM] * 4 + [IN_SMEM] * 2 + [IN_VMEM] * 2 + [ANYWHERE] + [IN_VMEM] * 3,
        out_specs=(IN_VMEM,) * 5 + (ANYWHERE,) * 4 + (IN_VMEM,) * 5,
        scratch_shapes=[
            buf((outer + 1 + BLOCKS, share, D), f32),
            buf((outer + 3, share, D), f32),
            buf((outer, 2 * share, D // 2), bf16),
            buf((2, 2 * share, D), bf16),
            buf((2 * share, D // 2), bf16),
            buf((BLOCKS * share, D), bf16),
            buf((2, tall, D), bf16),
            buf((8, 128), jnp.int32),
            buf((rows, D), f32),
            buf((outer, rows, 128), f32),
            buf((outer, rows, 128), f32),
            buf((8, D), f32),
        ]
        + [DMA((outer,))] * 2
        + [DMA((outer, across))] * 2
        + [DMA((outer, across, batches))] * 4
        + [DMA((2,))] * 2
        + [DMA((batches,))] * 2
        + [DMA((5,)), DMA((earlier.shape[0],))]
        + [DMA((groups, 2)), DMA((groups, outer)), DMA((groups, outer))]
        + [DMA((3, 2)), DMA((3, outer)), DMA((3, outer))]
        + [DMA((3, outer, across))] * 2
        + [DMA((3, outer, across, batches))] * 4
        + [DMA((groups, 2, outer, across))] * 4
        + attend_scratch(outer, inner, rows),
        compiler_params=remote_params(ident, ROOM),
        name="start_layer",
    )(qkv, out, up, down, lens, mixing, tokens, cot, earlier, vecs, cos_t, sin_t)


class Exchange:
    def __init__(self, here, pair, q, alls, q_all, sems, local, first_local):
        self.here, self.pair, self.q, self.alls, self.q_all = here, pair, q, alls, q_all
        self.qs, self.qr, self.zs, self.zr, self.xs, self.xr, self.cs, self.cr = sems
        self.local, self.first_local = local, first_local
        self.outer, self.across = len(here.zs), len(here.xs)
        self.arriving = {0: [], 1: []}
        self.late = {0: [], 1: []}
        self.waits = {0: [], 1: []}

    def send_pair(self, g):
        here = self.here
        for i in (0, 1):
            source, dest = self.pair[i], self.alls[i]
            for t in range(1, self.outer):
                copy = push(source.at[g, here.zs[t]], dest.at[g, here.o, here.j], self.zs.at[g, i, t], self.zr.at[g, i, t], here.z_peers[t])
                self.arriving[g].append((i, t, copy))
            place = dest.at[g, here.o, here.j]
            self.waits[g].append(carry(source.at[g, here.o], place, self.local.at[self.first_local + 3 * g + i]))
            self.onward(g, i, 0, source.at[g, here.o], place)

    def send_query(self, g):
        here = self.here
        for t in range(1, self.outer):
            self.waits[g].append(push(self.q.at[g, here.zs[t]], self.q_all.at[g, here.o], self.qs.at[g, t], self.qr.at[g, t], here.z_peers[t]))
        self.waits[g].append(carry(self.q.at[g, here.o], self.q_all.at[g, here.o], self.local.at[self.first_local + 3 * g + 2]))

    def onward(self, g, i, t, source, place):
        here = self.here
        for d in range(1, self.across):
            copy = push(source, place, self.xs.at[g, i, t, d], self.xr.at[g, i, t, d], here.x_peers[d])
            self.late[g].append((i, t, d, copy))
        self.waits[g].append(push(source, place, self.cs.at[g, i, t, 0], self.cr.at[g, i, t, 0], here.twin))

    def settle(self, g, left):
        here = self.here
        while len(self.late[g]) > left:
            i, t, d, copy = self.late[g].pop(0)
            copy.wait()
            moved = self.alls[i].at[g, here.z_from[t], here.x_from[d] * 2 + here.c]
            self.waits[g].append(push(moved, moved, self.cs.at[g, i, t, d], self.cr.at[g, i, t, d], here.twin))

    def arrive(self, g):
        i, t, copy = self.arriving[g].pop(0)
        copy.wait()
        place = self.alls[i].at[g, self.here.z_from[t], self.here.j]
        self.onward(g, i, t, place, place)
        self.settle(g, self.across - 1)

    def finish(self, g):
        for copy in self.waits[g]:
            copy.wait()


def exchange_scratch(groups, outer, across):
    return [DMA((groups, outer))] * 2 + [DMA((groups, 2, outer))] * 2 + [DMA((groups, 2, outer, across))] * 4


def turned_parts(block, rows):
    pair = block[:rows].T
    single = block[rows:].T
    single = jnp.concatenate([single[:HEAD], single[HEAD:]], 1)
    blank = jnp.zeros_like(single)
    stack = lambda *parts: jnp.concatenate(parts, 0)
    return stack(pair[:HEAD], blank), stack(blank, pair[HEAD:]), stack(single, blank), stack(blank, single)


def attend_scratch(outer, inner, rows):
    span = inner * rows
    return [
        pltpu.VMEM((outer, 128, span), bf16),
        pltpu.VMEM((outer, 128, span // 2), bf16),
        pltpu.VMEM((outer, span, 128), f32),
        pltpu.VMEM((4, 128, rows), bf16),
        pltpu.VMEM((8, rows), f32),
        pltpu.VMEM((8, rows), f32),
    ]


def bias_rows(bias, lens, g, outer, span):
    for c in range(outer):
        key = c * span + lax.broadcasted_iota(jnp.int32, (span, 128), 0)
        bias[c] = jnp.where(key < lens[g], 0.0, NEG)


def attend_group(g, outer, inner, lens, q_all, k_all, v_all, o_mine, ot, lse, scratch, here, events):
    vt, vft, bias, qt, m_s, l_s = scratch
    folded = q_all.shape[2]
    rows = folded * 2 // 3
    span = inner * rows
    half = rows // 2
    tiles = rows // 128
    bias_rows(bias, lens, g, outer, span)
    for c in range(outer):
        vt[c] = v_all[g, c, :, :rows, :].reshape(span, 128).T
        vft[c] = v_all[g, c, :, rows:, :].reshape(span // 2, 128).T
    for z in range(outer):
        first = (z * inner + here.j) * rows
        for n, part in enumerate(turned_parts((q_all[g, z] * 0.125).astype(bf16), rows)):
            qt[n] = part
        ot[g, z] = jnp.zeros((3 * HEAD, rows), f32)
        m_s[...] = jnp.full(m_s.shape, NEG, f32)
        l_s[...] = jnp.zeros(l_s.shape, f32)

        def step(c, masked):
            pair = k_all[g, c, :, :rows, :].reshape(span, 128)
            single = k_all[g, c, :, rows:, :].reshape(span // 2, 128)
            low = bias[c]
            low_parts = low.reshape(inner, rows, 128)
            shut = (low, low, low_parts[:, :half].reshape(span // 2, 128), low_parts[:, half:].reshape(span // 2, 128))
            lhs = (pair, pair, single, single)
            scores = []
            for n in range(4):
                s = mm(lhs[n], qt[n]) + jnp.concatenate([shut[n]] * tiles, 1)
                if masked:
                    key = lax.broadcasted_iota(jnp.int32, s.shape, 0)
                    if n >= 2:
                        key = lax.div(key, half) * rows + lax.rem(key, half) + (n - 2) * half
                    query = first + lax.broadcasted_iota(jnp.int32, s.shape, 1)
                    s = jnp.where(key + c * span <= query, s, NEG)
                scores.append(s)
            own = ((0,), (1,), (2, 3))
            tops = [m_s[h : h + 1] for h in range(3)]
            news = []
            for h in range(3):
                top = tops[h]
                for n in own[h]:
                    top = jnp.maximum(top, jnp.max(scores[n], 0, keepdims=True))
                news.append(top)
            shares, sums = [], [0.0, 0.0, 0.0]
            for h in range(3):
                for n in own[h]:
                    p = jnp.exp(scores[n] - news[h])
                    sums[h] = sums[h] + jnp.sum(p, 0, keepdims=True)
                    shares.append(p.astype(bf16))
            for h in range(3):
                alpha = jnp.exp(tops[h] - news[h])
                l_s[h : h + 1] = l_s[h : h + 1] * alpha + sums[h]
                m_s[h : h + 1] = news[h]
                at = slice(HEAD * h, HEAD * h + HEAD)
                if h < 2:
                    out = mm(vt[c, at, :], shares[h])
                else:
                    out = mm(vft[c, :HEAD, :], shares[2]) + mm(vft[c, HEAD:, :], shares[3])
                ot[g, z, at, :] = ot[g, z, at, :] * alpha + out

        def full_step(c, _):
            step(c, False)
            return 0

        if z:
            lax.fori_loop(0, z, full_step, 0)
        if events:
            events.pop(0)()
        step(z, True)
        if events:
            events.pop(0)()
        for h in range(3):
            at = slice(HEAD * h, HEAD * h + HEAD)
            total = l_s[h : h + 1]
            ot[g, z, at, :] = ot[g, z, at, :] / total
            lse[g, z, h : h + 1, :] = m_s[h : h + 1] + jnp.log(total)
        o_mine[z, g, :rows, :] = ot[g, z, :128, :].T.astype(bf16)
        halves = [ot[g, z, 128:, :half], ot[g, z, 128:, half:]]
        o_mine[z, g, rows:, :] = jnp.concatenate(halves, 0).T.astype(bf16)


def spread_kernel(batches, outer, inner, *refs):
    refs = list(refs)

    def take(n):
        got = refs[:n]
        del refs[:n]
        return got

    normed, near, vecs, lens, cosine, sine = take(6)
    q_all, k_all, v_all, o_mine, ot, lse = take(6)
    q, k, v, wide_s, local = take(5)
    sems = take(8)
    here = Place(batches, outer, inner)
    rows = cosine.shape[0]
    groups = lens.shape[0]
    greet(here.z_peers[1:] + here.x_peers[1:] + [here.twin])

    def project(block, into, rotated):
        wide_s[...] = mm(normed[...], near[block]) + vecs[4 + block : 5 + block]
        for g in range(groups):

            def tile_of(tile):
                value = wide_s[g * rows : g * rows + rows, 128 * tile : 128 * tile + 128]
                return turn(value, cosine[...], sine[...]) if rotated else value

            def write(target, value):
                into[g, target] = value.astype(bf16)

            fold_heads_of(write, tile_of, outer)

    exchange = Exchange(here, (k, v), q, (k_all, v_all), q_all, sems, local, 0)
    for block, into in ((1, k), (2, v), (0, q)):
        project(block, into, block != 2)
    for g in range(groups):
        exchange.send_pair(g)
        exchange.send_query(g)
    for g in range(groups):
        for _ in range(2 * (outer - 1)):
            exchange.arrive(g)
        exchange.settle(g, 0)
        exchange.finish(g)
    for g in range(groups):
        attend_group(g, outer, inner, lens, q_all, k_all, v_all, o_mine, ot, lse, refs, here, [])


def spread_heads(normed, near, vecs, lens, cosine, sine, batches, outer, inner, ident):
    rows = cosine.shape[0]
    groups = lens.shape[0]
    folded = rows + rows // 2
    piece = (groups, outer, folded, 128)
    full = jax.ShapeDtypeStruct((groups, outer, inner, folded, 128), bf16)
    shapes = (
        jax.ShapeDtypeStruct(piece, bf16),
        full,
        full,
        jax.ShapeDtypeStruct((outer, groups, folded, 128), bf16),
        jax.ShapeDtypeStruct((groups, outer, 3 * HEAD, rows), f32),
        jax.ShapeDtypeStruct((groups, outer, 8, rows), f32),
    )
    return pl.pallas_call(
        functools.partial(spread_kernel, batches, outer, inner),
        out_shape=shapes,
        in_specs=[IN_VMEM] * 3 + [IN_SMEM] + [IN_VMEM] * 2,
        out_specs=(IN_VMEM,) * len(shapes),
        scratch_shapes=[pltpu.VMEM(piece, bf16)] * 3
        + [pltpu.VMEM(normed.shape, f32), DMA((3 * groups,))]
        + exchange_scratch(groups, outer, inner // 2)
        + attend_scratch(outer, inner, rows),
        compiler_params=remote_params(ident, ROOM),
        name="spread_heads",
    )(normed, near, vecs, lens, cosine, sine)


def attend_back_kernel(outer, inner, lens, q, k, v, do, ot, lse, cos, sin, dq, dk, dv, kt, kft, qt, dot_t, qz, dz, rd, dqt, dks, dvs):
    groups, _, folded, _ = q.shape
    rows = folded * 2 // 3
    half = rows // 2
    span = inner * rows
    j = lax.rem(lax.axis_index("seq"), inner)
    low = lax.broadcasted_iota(jnp.int32, (rows, 128), 1) < HEAD

    def spread_parts(into, block):
        pair = block[:rows]
        single = block[rows:].astype(f32)
        blank = jnp.zeros_like(pair)
        into[0] = jnp.where(low, pair, blank)
        into[1] = jnp.where(low, blank, pair)
        into[2] = jnp.where(low, unfold_single(single, False), 0.0).astype(bf16)
        into[3] = jnp.where(low, 0.0, unfold_single(single, True)).astype(bf16)

    for g in range(groups):
        length = lens[g]
        for c in range(outer):
            kt[c] = k[g, c, :, :rows, :].reshape(span, 128).T
            kft[c] = k[g, c, :, rows:, :].reshape(span // 2, 128).T
        dks[...] = jnp.zeros(dks.shape, f32)
        dvs[...] = jnp.zeros(dvs.shape, f32)

        def one(z, _):
            first = (z * inner + j) * rows
            small = (q[g, z] * 0.125).astype(bf16)
            grad = do[z, g]
            for n, part in enumerate(turned_parts(small, rows)):
                qt[n] = part
            grads = turned_parts(grad, rows)
            for n, part in enumerate(grads):
                dot_t[n] = part
            spread_parts(qz, small)
            spread_parts(dz, grad)
            for h in range(3):
                part = grads[h][HEAD * (h % 2) : HEAD * (h % 2) + HEAD]
                rd[h : h + 1, :] = jnp.sum(part.astype(f32) * ot[g, z, HEAD * h : HEAD * h + HEAD, :], 0, keepdims=True)
            dqt[...] = jnp.zeros(dqt.shape, f32)

            def step(c, masked):
                pair = k[g, c, :, :rows, :].reshape(span, 128)
                single = k[g, c, :, rows:, :].reshape(span // 2, 128)
                v_pair = v[g, c, :, :rows, :].reshape(span, 128)
                v_single = v[g, c, :, rows:, :].reshape(span // 2, 128)
                lhs = (pair, pair, single, single)
                values = (v_pair, v_pair, v_single, v_single)
                for n in range(4):
                    h = min(n, 2)
                    s = mm(lhs[n], qt[n])
                    p = jnp.exp(s - lse[g, z, h : h + 1, :])
                    if masked:
                        key = lax.broadcasted_iota(jnp.int32, s.shape, 0)
                        if n >= 2:
                            key = lax.div(key, half) * rows + lax.rem(key, half) + (n - 2) * half
                        key = key + c * span
                        query = first + lax.broadcasted_iota(jnp.int32, s.shape, 1)
                        p = jnp.where((key <= query) & (key < length), p, 0.0)
                    dp = mm(values[n], dot_t[n])
                    ds = (p * (dp - rd[h : h + 1, :])).astype(bf16)
                    dv_part = mm(p.astype(bf16), dz[n])
                    dk_part = mm(ds, qz[n])
                    at = slice(HEAD * h, HEAD * h + HEAD)
                    if n < 2:
                        dvs[c, :, :rows, :] += dv_part.reshape(inner, rows, 128)
                        dks[c, :, :rows, :] += dk_part.reshape(inner, rows, 128)
                        dqt[at, :] += mm(kt[c, at, :], ds)
                    else:
                        dvs[c, :, rows:, :] += dv_part.reshape(inner, half, 128)
                        dks[c, :, rows:, :] += dk_part.reshape(inner, half, 128)
                        dqt[at, :] += mm(kft[c, HEAD * (n - 2) : HEAD * (n - 1), :], ds)

            live = first < length
            whole = jnp.where(live, jnp.minimum(z, lax.div(length, span)), 0)
            count = jnp.where(live, jnp.minimum(z + 1, lax.div(length + span - 1, span)), 0)

            def full_step(c, _):
                step(c, False)
                return 0

            def edge_step(c, _):
                step(c, True)
                return 0

            lax.fori_loop(0, whole, full_step, 0)
            lax.fori_loop(whole, count, edge_step, 0)
            parts = []
            for h in range(3):
                a = dqt[HEAD * h : HEAD * h + 32, :] * 0.125
                b = dqt[HEAD * h + 32 : HEAD * h + 64, :] * 0.125
                parts.append(a * cos[z] + b * sin[z])
                parts.append(b * cos[z] - a * sin[z])
            dq[g, z, :rows, :] = jnp.concatenate(parts[:4], 0).T.astype(bf16)
            single = jnp.concatenate(parts[4:], 0)
            dq[g, z, rows:, :] = jnp.concatenate([single[:, :half], single[:, half:]], 0).T.astype(bf16)
            return 0

        lax.fori_loop(0, outer, one, 0)
        for c in range(outer):
            dk[g, c] = dks[c].astype(bf16)
            dv[g, c] = dvs[c].astype(bf16)


def attend_back(lens, q, k, v, do, ot, lse, cos, sin, inner):
    groups, outer, folded, _ = q.shape
    rows = folded * 2 // 3
    span = inner * rows
    vm = IN_VMEM
    return pl.pallas_call(
        functools.partial(attend_back_kernel, outer, inner),
        out_shape=(
            jax.ShapeDtypeStruct(q.shape, bf16),
            jax.ShapeDtypeStruct(k.shape, bf16),
            jax.ShapeDtypeStruct(v.shape, bf16),
        ),
        in_specs=[IN_SMEM] + [vm] * 8,
        out_specs=(vm, vm, vm),
        scratch_shapes=[
            pltpu.VMEM((outer, 128, span), bf16),
            pltpu.VMEM((outer, 128, span // 2), bf16),
            pltpu.VMEM((4, 128, rows), bf16),
            pltpu.VMEM((4, 128, rows), bf16),
            pltpu.VMEM((4, rows, 128), bf16),
            pltpu.VMEM((4, rows, 128), bf16),
            pltpu.VMEM((8, rows), f32),
            pltpu.VMEM((3 * HEAD, rows), f32),
            pltpu.VMEM((outer, inner, folded, 128), f32),
            pltpu.VMEM((outer, inner, folded, 128), f32),
        ],
        compiler_params=params(),
        name="attend_back",
    )(lens, q, k, v, do, ot, lse, cos, sin)


def middle_kernel(batches, outer, inner, *refs):
    refs = list(refs)

    def take(n):
        got = refs[:n]
        del refs[:n]
        return got

    o_mine, out, up, down, tokens, cot, mixture, counts, vecs, lens, mixing = take(11)
    mixed, grad_mine, middle_grad, out_term, up_terms, down_terms, sums = take(7)
    home, sent, attended, middle, low_s, result_s, slope_s, active_s, hidden_s, acc, back, weights = take(12)
    fetch, hs, hr, gs, gr, local = refs
    tall = tokens.shape[0]
    groups = lens.shape[0]
    rows = tall // groups
    here = Place(batches, outer, inner)
    o = here.o
    fetches = [
        carry(down, weights.at[pl.ds(1 + BLOCKS, BLOCKS)], fetch.at[0]),
        carry(out, weights.at[0], fetch.at[1]),
        carry(up, weights.at[pl.ds(1, BLOCKS)], fetch.at[2]),
    ]
    greet(here.z_peers[1:])
    coming, waits = {}, []
    for g in range(groups):
        coming[g] = [carry(o_mine.at[o, g], home.at[o, g], local.at[0, g])]
        for t in range(1, outer):
            coming[g].append(push(o_mine.at[here.zs[t], g], home.at[o, g], hs.at[g, t], hr.at[g, t], here.z_peers[t]))
    count = counts[0, 0:1, 0:1]
    for y in range(1, batches):
        count = count + counts[y, 0:1, 0:1]
    slots = lax.axis_size("batch") * lax.axis_size("seq") * tall
    scale = slots / count.astype(f32)
    row = lax.broadcasted_iota(jnp.int32, (rows, 1), 0) + lax.axis_index("seq") * rows

    def grad_of(g):
        return cot[g * rows : g * rows + rows, :].astype(f32) * jnp.where(row < lens[g], scale, 0.0)

    sums[...] = jnp.zeros(sums.shape, f32)
    for g in range(groups):
        here_rows = slice(g * rows, g * rows + rows)
        result = (mixing[0] * grad_of(g)).astype(bf16)
        result_s[here_rows] = result
        sums[8 + BLOCKS : 9 + BLOCKS] = sums[8 + BLOCKS : 9 + BLOCKS] + jnp.sum(result.astype(f32), 0, keepdims=True)
    fetches[0].wait()

    def early(i, _):
        slope_s[i] = mm_nt(result_s[...], weights[1 + BLOCKS + i])
        return 0

    lax.fori_loop(0, BLOCKS, early, 0)
    for g in range(groups):
        here_rows = slice(g * rows, g * rows + rows)
        for copy in coming[g]:
            copy.wait()
        tiles = unfold_heads(lambda p: home[p, g].astype(f32), rows, outer)
        for i, tile in enumerate(tiles):
            attended[here_rows, 128 * i : 128 * i + 128] = tile.astype(bf16)
        if g == 0:
            fetches[1].wait()
        value = tokens[here_rows].astype(f32) + (mm(attended[here_rows], weights[0]) + vecs[7:8])
        middle[here_rows] = value
        hat, inverse = normalize(value)
        low_s[here_rows] = (hat * vecs[1:2] + vecs[3:4]).astype(bf16)
        acc[here_rows] = jnp.zeros((rows, D), f32)
        back[...] = jnp.zeros((rows, D), f32)
        if g == 0:
            fetches[2].wait()

        def block(i, _):
            hidden = mm(low_s[here_rows], weights[1 + i]) + vecs[pl.ds(8 + i, 1)]
            square = hidden * hidden
            bend = jnp.tanh(0.7978845608028654 * (hidden + 0.044715 * square * hidden))
            half = 0.5 * (1.0 + bend)
            active = (hidden * half).astype(bf16)
            active_s[i, here_rows] = active
            slope = half + 0.5 * hidden * (1.0 - bend * bend) * (0.7978845608028654 * (1.0 + 3.0 * 0.044715 * square))
            hidden_grad = (slope * slope_s[i, here_rows]).astype(bf16)
            hidden_s[i, here_rows] = hidden_grad
            sums[pl.ds(8 + i, 1)] = sums[pl.ds(8 + i, 1)] + jnp.sum(hidden_grad.astype(f32), 0, keepdims=True)
            back[...] += mm_nt(hidden_grad, weights[1 + i])
            acc[here_rows] += mm(active, weights[1 + BLOCKS + i])
            return 0

        lax.fori_loop(0, BLOCKS, block, 0)
        inner_grad = back[...]
        sums[1:2] = sums[1:2] + jnp.sum(inner_grad * hat, 0, keepdims=True)
        sums[3:4] = sums[3:4] + jnp.sum(inner_grad, 0, keepdims=True)
        total_grad = mixing[0] * grad_of(g) + normalize_back(inner_grad, hat, inverse, vecs[1:2])
        middle_grad[here_rows] = total_grad
        branch = total_grad.astype(bf16)
        sums[7:8] = sums[7:8] + jnp.sum(branch.astype(f32), 0, keepdims=True)
        back[...] = mm_nt(branch, weights[0])

        def write(target, value):
            sent[target, g] = value.astype(bf16)

        fold_heads_of(write, lambda t: back[:, 128 * t : 128 * t + 128], outer)
        for t in range(1, outer):
            waits.append(push(sent.at[here.zs[t], g], grad_mine.at[o, g], gs.at[g, t], gr.at[g, t], here.z_peers[t]))
        waits.append(carry(sent.at[o, g], grad_mine.at[o, g], local.at[1, g]))

    low_t = low_s[...].T

    def late(i, _):
        down_terms[i] = mm(active_s[i].T, result_s[...]).astype(bf16)
        up_terms[i] = mm(low_t, hidden_s[i]).astype(bf16)
        return 0

    lax.fori_loop(0, BLOCKS, late, 0)
    out_term[...] = mm(attended[...].T, middle_grad[...].astype(bf16)).astype(bf16)
    for g in range(groups):
        here_rows = slice(g * rows, g * rows + rows)
        layer_out = middle[here_rows] + acc[here_rows] + vecs[8 + BLOCKS : 9 + BLOCKS]
        mixed[here_rows] = (mixture[here_rows] + mixing[0] * layer_out).astype(bf16)
        sums[VECTORS : VECTORS + 1] = sums[VECTORS : VECTORS + 1] + jnp.sum(grad_of(g) * layer_out, 0, keepdims=True)
    for copy in waits:
        copy.wait()


def middle_layer(o_mine, out, up, down, tokens, cot, mixture, counts, vecs, lens, mixing, batches, outer, inner, ident):
    tall = tokens.shape[0]
    groups = lens.shape[0]
    wide = pltpu.VMEM((tall, D), f32)
    low = pltpu.VMEM((tall, D), bf16)
    hidden = pltpu.VMEM((BLOCKS, tall, D), bf16)
    return pl.pallas_call(
        functools.partial(middle_kernel, batches, outer, inner),
        out_shape=(
            jax.ShapeDtypeStruct((tall, D), bf16),
            jax.ShapeDtypeStruct(o_mine.shape, bf16),
            jax.ShapeDtypeStruct((tall, D), f32),
            jax.ShapeDtypeStruct((D, D), bf16),
            jax.ShapeDtypeStruct((BLOCKS, D, D), bf16),
            jax.ShapeDtypeStruct((BLOCKS, D, D), bf16),
            jax.ShapeDtypeStruct((16, D), f32),
        ),
        in_specs=[ANYWHERE] * 4 + [IN_VMEM] * 5 + [IN_SMEM] * 2,
        out_specs=(IN_VMEM, ANYWHERE) + (IN_VMEM,) * 5,
        scratch_shapes=[
            pltpu.VMEM(o_mine.shape, bf16), pltpu.VMEM(o_mine.shape, bf16),
            low, wide, low, low, pltpu.VMEM((BLOCKS, tall, D), f32), hidden, hidden,
            wide, pltpu.VMEM((tall // groups, D), f32),
            pltpu.VMEM((1 + 2 * BLOCKS, D, D), bf16), DMA((3,)),
        ]
        + [DMA((groups, outer))] * 4
        + [DMA((2, groups))],
        compiler_params=remote_params(ident, ROOM),
        name="middle_layer",
    )(o_mine, out, up, down, tokens, cot, mixture, counts, vecs, lens, mixing)


def back_kernel(outer, dq, dk, dv, cosine, sine, normed, tokens, near, vecs, cot, counts, lens, mixing, middle_grad, out_term, sums, dots, input_grad, terms, small, joined, low_t):
    tall = tokens.shape[0]
    groups = lens.shape[0]
    rows = tall // groups
    for g in range(groups):
        for n, source in enumerate((dq, dk, dv)):
            tiles = unfold_heads(lambda p: source[g, p].astype(f32), rows, outer)
            for i, tile in enumerate(tiles):
                if n == 1:
                    tile = turn(tile, cosine[...], -sine[...])
                joined[n, g * rows : g * rows + rows, 128 * i : 128 * i + 128] = tile.astype(bf16)
    low_t[...] = normed[...].T
    small[...] = sums[...]
    back = jnp.zeros((tall, D), f32)
    for n in range(3):
        low = joined[n]
        small[4 + n : 5 + n] = jnp.sum(low.astype(f32), 0, keepdims=True)
        terms[n] = mm(low_t[...], low).astype(bf16)
        back = back + mm_nt(low, near[n])
    terms[3] = out_term[...]
    hat, inverse = normalize(tokens[...].astype(f32))
    small[0:1] = jnp.sum(back * hat, 0, keepdims=True)
    small[2:3] = jnp.sum(back, 0, keepdims=True)
    slots = lax.axis_size("batch") * lax.axis_size("seq") * tall
    count = counts[0, 0:1, 0:1]
    for y in range(1, counts.shape[0]):
        count = count + counts[y, 0:1, 0:1]
    scale = slots / count.astype(f32)
    row = lax.broadcasted_iota(jnp.int32, (rows, 1), 0) + lax.axis_index("seq") * rows
    live = jnp.concatenate([jnp.where(row < lens[g], scale, 0.0) for g in range(groups)], 0)
    grad = cot[...].astype(f32) * live
    input_grad[...] = mixing[1] * grad + middle_grad[...] + normalize_back(back, hat, inverse, vecs[0:1])
    lane = lax.broadcasted_iota(jnp.int32, (1, D), 1)
    line = jnp.where(lane == 0, jnp.sum(sums[VECTORS : VECTORS + 1], 1, keepdims=True), 0.0)
    for i in range(1, mixing.shape[0]):
        line = line + jnp.where(lane == i, scale * jnp.sum(dots[i : i + 1], 1, keepdims=True), 0.0)
    small[VECTORS : VECTORS + 1] = line


def back_layer(dq, dk, dv, cosine, sine, normed, tokens, near, vecs, cot, counts, lens, mixing, middle_grad, out_term, sums, dots, outer):
    tall = tokens.shape[0]
    return pl.pallas_call(
        functools.partial(back_kernel, outer),
        out_shape=(
            jax.ShapeDtypeStruct((tall, D), f32),
            jax.ShapeDtypeStruct((4, D, D), bf16),
            jax.ShapeDtypeStruct((16, D), f32),
        ),
        in_specs=[IN_VMEM] * 11 + [IN_SMEM] * 2 + [IN_VMEM] * 4,
        out_specs=(IN_VMEM,) * 3,
        scratch_shapes=[pltpu.VMEM((3, tall, D), bf16), pltpu.VMEM((D, tall), bf16)],
        compiler_params=params(),
        name="back_layer",
    )(dq, dk, dv, cosine, sine, normed, tokens, near, vecs, cot, counts, lens, mixing, middle_grad, out_term, sums, dots)


def adam(param, grad, first, second, decay):
    first_new = beta_one * first + (1.0 - beta_one) * grad
    second_new = beta_two * second + (1.0 - beta_two) * grad * grad
    fix_one = 1.0 - beta_one**adam_step
    fix_two = 1.0 - beta_two**adam_step
    update = first_new / fix_one / (jnp.sqrt(second_new / fix_two) + adam_eps)
    return (-learn_rate * (update + decay * param), first_new)


def adam_kernel(packed, near, up, down, out, *refs):
    given, results = refs[:12], refs[12:]
    for n in range(4):
        param, first, second = given[3 * n : 3 * n + 3]
        grad_out, step_out, first_out = results[3 * n : 3 * n + 3]
        for i in range(param.shape[1] // D):
            lanes = slice(i * D, i * D + D)
            if n == 0 and packed:
                grad = jnp.concatenate(plain_tiles(lambda z: near[z], i, near.shape[0]), 1)
            else:
                grad = near[i] if n == 0 else out[...] if n == 1 else up[i] if n == 2 else down[...]
            grad_out[:, lanes] = grad
            step_out[:, lanes], first_out[:, lanes] = adam(param[:, lanes], grad, first[:, lanes], second[:, lanes], decay_rate)


def adam_all(packed, near, up, down, out, given):
    shapes = []
    for n in range(4):
        shapes += [jax.ShapeDtypeStruct(given[3 * n].shape, f32)] * 3
    return pl.pallas_call(
        functools.partial(adam_kernel, packed),
        out_shape=tuple(shapes),
        in_specs=[IN_VMEM] * 16,
        out_specs=(IN_VMEM,) * 12,
        compiler_params=params(),
        name="adam_all",
    )(near, up, down, out, *given)


def summed(into, index, more, other):
    into[index] = (into[index].astype(f32) + more[other].astype(f32)).astype(bf16)


def fold_kernel(batches, inner, dq, dk, dv, dq_all, dk_all, dv_all, cbuf, xbuf, done, qs, qr, zs, zr, xs, xr, cs, cr, local):
    outer = dq.shape[1]
    across = inner // 2
    here = Place(batches, outer, inner)
    o, a, c = here.o, here.a, here.c
    greet(here.z_peers[1:] + here.x_peers[1:] + [here.twin])
    waits = [carry(dq.at[:, o], dq_all.at[:, o], local.at[0])]
    given = (dk, dv)
    results = (dk_all, dv_all)
    order = [t % outer for t in range(1, outer + 1)]
    xorder = list(range(1, across)) + [0]
    to_twin, over = {}, {}
    for t in order:
        for i in (0, 1):
            for d in xorder:
                z, x = here.zs[t], here.xs[d]
                to_twin[i, t, d] = push(given[i].at[:, z, x * 2 + 1 - c], cbuf.at[i, z, x], cs.at[i, t, d], cr.at[i, t, d], here.twin)
    for t in range(1, outer):
        waits.append(push(dq.at[:, here.zs[t]], dq_all.at[:, o], qs.at[t], qr.at[t], here.z_peers[t]))
    for t in order:
        for i in (0, 1):
            for d in xorder:
                to_twin[i, t, d].wait()
                z, x = here.zs[t], here.xs[d]
                for g in range(dq.shape[0]):
                    summed(cbuf, (i, z, x, g), given[i], (g, z, x * 2 + c))
                if d:
                    over[i, t, d] = push(cbuf.at[i, z, x], xbuf.at[i, z, d], xs.at[i, t, d], xr.at[i, t, d], here.x_peers[d])
    for t in order:
        for i in (0, 1):
            z = here.zs[t]
            total = cbuf[i, z, a].astype(f32)
            for d in range(1, across):
                over[i, t, d].wait()
                total = total + xbuf[i, z, d].astype(f32)
            done[i, z] = total.astype(bf16)
            if t:
                waits.append(push(done.at[i, z], results[i].at[:, o], zs.at[i, t], zr.at[i, t], here.z_peers[t]))
            else:
                waits.append(carry(done.at[i, z], results[i].at[:, o], local.at[1 + i]))
    for copy in waits:
        copy.wait()


def fold_heads(dq, dk, dv, batches, inner, ident):
    groups, outer = dq.shape[:2]
    tail = (groups,) + dq.shape[2:]
    across = inner // 2
    piece = jax.ShapeDtypeStruct(dq.shape, dq.dtype)
    scratch = [pltpu.VMEM((2, outer, across) + tail, bf16)] * 2 + [pltpu.VMEM((2, outer) + tail, bf16)]
    scratch += [DMA((outer,))] * 2 + [DMA((2, outer))] * 2 + [DMA((2, outer, across))] * 4 + [DMA((3,))]
    return pl.pallas_call(
        functools.partial(fold_kernel, batches, inner),
        out_shape=(piece, piece, piece),
        in_specs=[ANYWHERE] + [IN_VMEM] * 2,
        out_specs=(ANYWHERE,) * 3,
        scratch_shapes=scratch,
        compiler_params=remote_params(ident, ROOM),
        name="fold_heads",
    )(dq, dk, dv)


def finish_kernel(batches, outer, inner, *refs):
    refs = list(refs)

    def take(n):
        got = refs[:n]
        del refs[:n]
        return got

    dq, dk, dv, up_terms, down_terms, out_terms, mine, normed, tokens, cot, middle_grad = take(11)
    counts, vecs, sums, dots, cos_t, sin_t, lens, mixing = take(8)
    input_grad, near_out, up_out, down_out, out_out, small_out = take(6)
    cosine, sine, gm, gt, gx, partial, from_left, from_right, weight_grad = take(9)
    rm, rt, ry, rx, rz = take(3), take(3), take(3), take(3), take(3)
    terms_n, nc, na, ny, nx, nz, kept, kept_out, kept_n = take(9)
    small, sc, sx, sy, sz = take(5)
    gls, gcs, gcr, gxs, gxr, hrs, hrr, hls, hlr = take(9)
    rls, rcs, rcr, rys, ryr, rxs, rxr, rzs, rzr = take(9)
    ncs, ncr, nys, nyr, nxs, nxr, nzs, nzr, fs, fr, ss, sr = refs
    across = inner // 2
    here = Place(batches, outer, inner)
    o, a, b, c, j = here.o, here.a, here.batch, here.c, here.j
    tall = tokens.shape[0]
    groups = lens.shape[0]
    rows = tall // groups
    share = down_out.shape[0] // BLOCKS
    table = [sorted((s for s in range(outer) if s != i), key=lambda s: (abs(s - i), s)) + [i] for i in range(outer)]
    give, keep = lane_half(1 - c), lane_half(c)

    def layer(n):
        if n == outer - 1:
            return o
        found = 0
        for i in range(outer):
            found = found + (o == i).astype(jnp.int32) * table[i][outer - 2 - n]
        return found

    for z in range(outer):
        cosine[z] = jnp.concatenate([cos_t[z]] * 4, 0).T
        sine[z] = jnp.concatenate([-sin_t[z], sin_t[z]] * 2, 0).T
    greet(here.z_peers[1:] + here.x_peers[1:] + here.y_peers[1:] + [here.twin])
    given = (dk, dv)
    over = {}
    order = [(g, n) for g in range(groups) for n in range(outer)]

    def give_piece(g, n):
        s = layer(n)
        for i in (0, 1):
            for d in range(across):
                x = here.xs[d]
                over["own", g, n, i, d] = carry(given[i].at[g, s, x * 2 + c], gm.at[g, n, i, d], gls.at[g, n, i, d])
                over["twin", g, n, i, d] = push(
                    given[i].at[g, s, x * 2 + 1 - c], gt.at[g, n, i, d], gcs.at[g, n, i, d], gcr.at[g, n, i, d], here.twin
                )

    def theirs(i, y, x, core):
        if i == 0:
            return up_terms.at[pl.ds(2 * core, 2), y, :, x]
        if i == 1:
            return down_terms.at[y, :, x, core]
        return out_terms.at[y, :, x, :, lane_half(core)]

    corners = [(dy, dx) for dy in list(range(1, batches)) + [0] for dx in list(range(1, across)) + [0]]

    def give_rest(dy, dx):
        y, x = here.ys[dy], here.xs[dx]
        for i in range(3):
            over["rown", i, dy, dx] = carry(theirs(i, y, x, c), rm[i].at[dy, dx], rls.at[i, dy, dx])
            over["rtwin", i, dy, dx] = push(
                theirs(i, y, x, 1 - c), rt[i].at[dy, dx], rcs.at[i, dy, dx], rcr.at[i, dy, dx], here.twin
            )

    for n in range(outer):
        give_piece(0, n)
        if n < len(corners):
            give_rest(*corners[n])
    for corner in corners[outer:]:
        give_rest(*corner)
    for n in range(outer):
        give_piece(1, n)

    def fold_core(g, n):
        for i in (0, 1):
            for d in list(range(1, across)) + [0]:
                over["own", g, n, i, d].wait()
                over["twin", g, n, i, d].wait()
                gm[g, n, i, d] = (gm[g, n, i, d].astype(f32) + gt[g, n, i, d].astype(f32)).astype(bf16)
                if d:
                    over["x", g, n, i, d] = push(
                        gm.at[g, n, i, d], gx.at[g, n, i, d], gxs.at[g, n, i, d], gxr.at[g, n, i, d], here.x_peers[d]
                    )

    small[...] = jnp.zeros(small.shape, f32)
    small[0:16] = sums[...]
    weight_grad[...] = jnp.zeros(weight_grad.shape, f32)
    lane = lax.broadcasted_iota(jnp.int32, (rows, 128), 1)

    def halves(value):
        return value[:rows], jnp.where(lane < HEAD, unfold_single(value[rows:], False), 0.0)

    def piece(g, n):
        s = layer(n)
        totals = [dq[g, s].astype(f32)]
        for i in (0, 1):
            total = gm[g, n, i, 0].astype(f32)
            for d in range(1, across):
                over["x", g, n, i, d].wait()
                total = total + gx[g, n, i, d].astype(f32)
            totals.append(total)
        pairs, singles = [], []
        for i, total in enumerate(totals):
            pair, single = halves(total)
            if i == 1:
                pair, single = turn(pair, cosine[s], -sine[s]), turn(single, cosine[s], -sine[s])
                single = jnp.where(lane < HEAD, single, 0.0)
            pairs.append(pair)
            singles.append(single)
        joined = jnp.concatenate(pairs + singles, 1).astype(bf16)
        small[pl.ds(16 + o, 1)] = small[pl.ds(16 + o, 1)] + jnp.sum(joined.astype(f32), 0, keepdims=True)
        partial[g, n] = mm_nt(joined, mine[...].reshape(D, D)).astype(bf16)
        weight_grad[...] += mm(normed[g, s].T, joined)

    line_sends = []

    def hand(g, n):
        if n == outer - 1:
            return
        s = layer(n)
        for buf, sends, recvs, step, outside, away in (
            (from_left, hrs, hrr, 1, o > 0, o < s),
            (from_right, hls, hlr, -1, o < outer - 1, o > s),
        ):
            to = jnp.clip(o + step, 0, outer - 1)
            copy = pltpu.make_async_remote_copy(
                src_ref=buf.at[g, s],
                dst_ref=buf.at[g, s],
                send_sem=sends.at[g, s],
                recv_sem=recvs.at[g, s],
                device_id=(b, to * inner + j),
                device_id_type=MESH,
            )

            @pl.when(away & outside)
            def _(copy=copy, buf=buf):
                copy.wait_recv()
                buf[g, s] = (buf[g, s].astype(f32) + partial[g, n].astype(f32)).astype(bf16)

            @pl.when(away & jnp.logical_not(outside))
            def _(buf=buf):
                buf[g, s] = partial[g, n]

            @pl.when(away)
            def _(copy=copy):
                copy.start()

            line_sends.append((away, copy))

    slots = lax.axis_size("batch") * lax.axis_size("seq") * tall
    count = counts[0, 0:1, 0:1]
    for y in range(1, batches):
        count = count + counts[y, 0:1, 0:1]
    scale = slots / count.astype(f32)
    row = lax.broadcasted_iota(jnp.int32, (rows, 1), 0) + lax.axis_index("seq") * rows

    def arrive(g):
        back = partial[g, outer - 1].astype(f32)
        for buf, recvs, outside in ((from_left, hrr, o > 0), (from_right, hlr, o < outer - 1)):
            copy = pltpu.make_async_remote_copy(
                src_ref=buf.at[g, o],
                dst_ref=buf.at[g, o],
                send_sem=hrs.at[g, o],
                recv_sem=recvs.at[g, o],
                device_id=here.twin,
                device_id_type=MESH,
            )

            @pl.when(outside)
            def _(copy=copy):
                copy.wait_recv()

            back = back + jnp.where(outside, buf[g, o].astype(f32), 0.0)
        at = slice(g * rows, g * rows + rows)
        hat, inverse = normalize(tokens[at].astype(f32))
        small[0:1] = small[0:1] + jnp.sum(back * hat, 0, keepdims=True)
        small[2:3] = small[2:3] + jnp.sum(back, 0, keepdims=True)
        grad = cot[at].astype(f32) * jnp.where(row < lens[g], scale, 0.0)
        input_grad[at] = mixing[1] * grad + middle_grad[at] + normalize_back(back, hat, inverse, vecs[0:1])

    def each(i, add):
        if i == 0:

            def one(n, _):
                add((lax.div(n, outer), lax.rem(n, outer)))
                return 0

            lax.fori_loop(0, 2 * outer, one, 0)
        else:

            def one(z, _):
                add((z,))
                return 0

            lax.fori_loop(0, outer, one, 0)

    def plus(into, at, more, other):
        into[at] = (into[at].astype(f32) + more[other].astype(f32)).astype(bf16)

    def rest_core(dy, dx):
        for i in range(3):
            over["rown", i, dy, dx].wait()
            over["rtwin", i, dy, dx].wait()
            each(i, lambda at: plus(rm[i], (dy, dx) + at, rt[i], (dy, dx) + at))
        if dy and dx == min(1, across - 1):
            y_push(dy, dx)

    def y_push(dy, dx):
        for i in range(3):
            over["ry", i, dy, dx] = push(
                rm[i].at[dy, dx], ry[i].at[dy - 1, dx], rys.at[i, dy, dx], ryr.at[i, dy, dx], here.y_peers[dy]
            )

    def rest_y(dx):
        for i in range(3):
            for dy in range(1, batches):
                over["ry", i, dy, dx].wait()
        if dx:
            for dy in range(1, batches):
                y_push(dy, (dx + 1) % across)
        for i in range(3):
            for dy in range(1, batches):
                each(i, lambda at: plus(rm[i], (0, dx) + at, ry[i], (dy - 1, dx) + at))
            if dx:
                over["rx", i, dx] = push(rm[i].at[0, dx], rx[i].at[dx - 1], rxs.at[i, dx], rxr.at[i, dx], here.x_peers[dx])

    def line_piece(i, z):
        return rm[i].at[0, 0, :, z] if i == 0 else rm[i].at[0, 0, z]

    def rest_x():
        for i in range(3):
            for d in range(1, across):
                over["rx", i, d].wait()
                each(i, lambda at: plus(rm[i], (0, 0) + at, rx[i], (d - 1,) + at))
            for t in range(1, outer):
                over["rz", i, t] = push(line_piece(i, here.zs[t]), rz[i].at[t], rzs.at[i, t], rzr.at[i, t], here.z_peers[t])

    ends = []

    def rest_last():
        for i in range(3):
            for t in range(1, outer):
                over["rz", i, t].wait()
        for p in (0, 1):
            total = rm[0][0, 0, p, o].astype(f32)
            for t in range(1, outer):
                total = total + rz[0][t, p].astype(f32)
            kept[p] = total
        total, total_out = rm[1][0, 0, o].astype(f32), rm[2][0, 0, o].astype(f32)
        for t in range(1, outer):
            total = total + rz[1][t].astype(f32)
            total_out = total_out + rz[2][t].astype(f32)
        down_out[...] = total
        kept_out[...] = total_out
        theirs_rows = pl.ds(pl.multiple_of(share * (1 - c), 8), share)
        ends.append(push(kept.at[:, theirs_rows], up_out.at[pl.ds(2 * c, 2)], fs.at[0], fr.at[0], here.twin))
        ends.append(push(kept_out.at[theirs_rows], out_out.at[:, keep], fs.at[1], fr.at[1], here.twin))
        for p in (0, 1):
            value = kept[p]
            up_out[2 * c + p] = jnp.where(c == 0, value[:share], value[share:])
        value = kept_out[...]
        out_out[:, keep] = jnp.where(c == 0, value[:share], value[share:])

    events = [functools.partial(rest_core, *corner) for corner in corners]
    events += [functools.partial(rest_y, dx) for dx in list(range(1, across)) + [0]] + [rest_x]

    def event():
        if events:
            events.pop(0)()

    fold_core(*order[0])
    event()
    fold_core(*order[1])
    event()
    for n, at in enumerate(order):
        piece(*at)
        if n + 2 < len(order):
            fold_core(*order[n + 2])
        if n >= 1:
            hand(*order[n - 1])
        if n in (1, 3, 5):
            event()
    hand(*order[-1])

    terms_n[...] = weight_grad[...].reshape(terms_n.shape).astype(bf16)
    near_core = push(terms_n.at[:, :, :, :, give], nc, ncs, ncr, here.twin)
    while events:
        event()
    arrive(0)
    near_core.wait()

    def fold_near(i, _):
        y, z, x = lax.div(i, outer * across), lax.rem(lax.div(i, across), outer), lax.rem(i, across)
        value = terms_n[y, z, x]
        own_half = jnp.where(c == 0, value[:, : D // 2], value[:, D // 2 :])
        na[y, z, x] = (own_half.astype(f32) + nc[y, z, x].astype(f32)).astype(bf16)
        return 0

    lax.fori_loop(0, batches * outer * across, fold_near, 0)
    near_y = [push(na.at[here.ys[d]], ny.at[d - 1], nys.at[d], nyr.at[d], here.y_peers[d]) for d in range(1, batches)]
    for d in range(1, batches):
        near_y[d - 1].wait()

        def add_y(i, _):
            z, x = lax.div(i, across), lax.rem(i, across)
            plus(na, (b, z, x), ny, (d - 1, z, x))
            return 0

        lax.fori_loop(0, outer * across, add_y, 0)
    near_x = [
        push(na.at[b, :, here.xs[d]], nx.at[d - 1], nxs.at[d], nxr.at[d], here.x_peers[d]) for d in range(1, across)
    ]
    arrive(1)
    lane_wide = lax.broadcasted_iota(jnp.int32, (1, D), 1)
    line = jnp.where(lane_wide == 0, jnp.sum(sums[VECTORS : VECTORS + 1], 1, keepdims=True), 0.0)
    for i in range(1, mixing.shape[0]):
        line = line + jnp.where(lane_wide == i, scale * jnp.sum(dots[i : i + 1], 1, keepdims=True), 0.0)
    small[VECTORS : VECTORS + 1] = line
    small_copy = push(small, sc, ss.at[0], sr.at[0], here.twin)
    for d in range(1, across):
        near_x[d - 1].wait()

        def add_x(z, _):
            plus(na, (b, z, a), nx, (d - 1, z))
            return 0

        lax.fori_loop(0, outer, add_x, 0)
    near_z = [push(na.at[b, here.zs[t], a], nz.at[o], nzs.at[t], nzr.at[t], here.z_peers[t]) for t in range(1, outer)]
    nz[o] = na[b, o, a]
    small_copy.wait()
    sc[...] = sc[...] + small[...]
    sx[a] = sc[...]
    copies = [push(sc, sx.at[a], ss.at[d], sr.at[d], here.x_peers[d]) for d in range(1, across)]
    for copy in copies:
        copy.wait()
    total = sx[0]
    for x in range(1, across):
        total = total + sx[x]
    sc[...] = total
    sy[b] = total
    copies = [push(sc, sy.at[b], ss.at[across + d], sr.at[across + d], here.y_peers[d]) for d in range(1, batches)]
    rest_last()
    for copy in near_z:
        copy.wait()
    for z in range(outer):
        kept_n[z] = nz[z].astype(f32)
    theirs_rows = pl.ds(pl.multiple_of(share * (1 - c), 8), share)
    ends.append(push(kept_n.at[:, theirs_rows], near_out.at[:, :, keep], fs.at[2], fr.at[2], here.twin))
    for z in range(outer):
        value = kept_n[z]
        near_out[z, :, keep] = jnp.where(c == 0, value[:share], value[share:])
    for copy in copies:
        copy.wait()
    total = sy[0]
    for y in range(1, batches):
        total = total + sy[y]
    sc[...] = total
    sz[o] = total
    copies = [
        push(sc, sz.at[o], ss.at[across + batches + t], sr.at[across + batches + t], here.z_peers[t]) for t in range(1, outer)
    ]
    for copy in copies:
        copy.wait()
    total = sz[0]
    for z in range(1, outer):
        total = total + sz[z]
    small_out[...] = total[:16]
    for n in range(3):
        small_out[4 + n : 5 + n] = jnp.concatenate(plain_tiles(lambda z: total[16 + z : 17 + z], n, outer), 1)
    for copy in ends:
        copy.wait()
    for away, copy in line_sends:

        @pl.when(away)
        def _(copy=copy):
            copy.wait_send()


def plain_tiles(read, n, outer):
    tiles = []
    for z in range(0, outer, 2):
        even, odd = read(z), read(z + 1)
        pair, single = slice(128 * n, 128 * n + 128), slice(384 + 128 * n, 512 + 128 * n)
        lane = lax.broadcasted_iota(jnp.int32, even[:, single].shape, 1)
        middle = jnp.where(lane < HEAD, even[:, single], pltpu.roll(odd[:, single], HEAD, 1))
        tiles += [even[:, pair], middle, odd[:, pair]]
    return tiles


def finish_layer(
    dq, dk, dv, up_terms, down_terms, out_terms, mine, normed, tokens, cot, middle_grad, counts, vecs, sums, dots, cos_t, sin_t,
    lens, mixing, batches, outer, inner, ident,
):
    across = inner // 2
    tall = tokens.shape[0]
    groups = lens.shape[0]
    rows = tall // groups
    folded = dq.shape[2]
    wide = out_terms.shape[3]
    share = wide // 2
    low = lambda *shape: pltpu.VMEM(shape, bf16)
    full = lambda *shape: pltpu.VMEM(shape, f32)
    tails = ((2, outer, wide, D), (outer, BLOCKS * share, D), (outer, wide, D // 2))
    ends = ((2, wide, D), (BLOCKS * share, D), (wide, D // 2))
    grid = (batches, outer, across)
    scratch = [
        full(outer, rows, 128),
        full(outer, rows, 128),
        low(groups, outer, 2, across, folded, 128),
        low(groups, outer, 2, across, folded, 128),
        low(groups, outer, 2, across, folded, 128),
        low(groups, outer, rows, D),
        low(groups, outer, rows, D),
        low(groups, outer, rows, D),
        full(D, D),
    ]
    scratch += [low(batches, across, *tail) for tail in tails]
    scratch += [low(batches, across, *tail) for tail in tails]
    scratch += [low(batches - 1, across, *tail) for tail in tails]
    scratch += [low(across - 1, *tail) for tail in tails]
    scratch += [low(outer, *end) for end in ends]
    scratch += [
        low(*grid, wide, D),
        low(*grid, wide, D // 2),
        low(*grid, wide, D // 2),
        low(batches - 1, outer, across, wide, D // 2),
        low(across - 1, outer, wide, D // 2),
        low(outer, wide, D // 2),
        full(2, wide, D),
        full(wide, D // 2),
        full(outer, wide, D // 2),
        full(24, D),
        full(24, D),
        full(across, 24, D),
        full(batches, 24, D),
        full(outer, 24, D),
    ]
    scratch += [DMA((groups, outer, 2, across))] * 5 + [DMA((groups, outer))] * 4
    scratch += [DMA((3, batches, across))] * 5 + [DMA((3, across))] * 2 + [DMA((3, outer))] * 2
    scratch += [DMA] * 2 + [DMA((batches,))] * 2 + [DMA((across,))] * 2 + [DMA((outer,))] * 2 + [DMA((3,))] * 2
    scratch += [DMA((across + batches + outer,))] * 2
    return pl.pallas_call(
        functools.partial(finish_kernel, batches, outer, inner),
        out_shape=(
            jax.ShapeDtypeStruct((tall, D), f32),
            jax.ShapeDtypeStruct((outer, share, D), f32),
            jax.ShapeDtypeStruct((BLOCKS, share, D), f32),
            jax.ShapeDtypeStruct((BLOCKS * share, D), f32),
            jax.ShapeDtypeStruct((share, D), f32),
            jax.ShapeDtypeStruct((16, D), f32),
        ),
        in_specs=[IN_VMEM] + [ANYWHERE] * 5 + [IN_VMEM] * 11 + [IN_SMEM] * 2,
        out_specs=(IN_VMEM,) * 6,
        scratch_shapes=scratch,
        compiler_params=remote_params(ident, 60 << 20),
        name="finish_layer",
    )(
        dq, dk, dv, up_terms, down_terms, out_terms, mine, normed, tokens, cot, middle_grad, counts, vecs, sums, dots, cos_t, sin_t,
        lens, mixing,
    )


def body(
    tokens_in,
    earlier_outs,
    out_cotangent,
    seq_lengths,
    qkv_weight,
    out_weight,
    up_weight,
    down_weight,
    qkv_first,
    qkv_second,
    out_first,
    out_second,
    up_first,
    up_second,
    down_first,
    down_second,
    small_params,
    small_first,
    small_second,
):
    groups, rows, _ = tokens_in.shape
    tall = groups * rows
    batches = lax.axis_size("batch")
    seq_count = lax.axis_size("seq")
    seq_rank = lax.axis_index("seq")
    devices = batches * seq_count
    outer = math.gcd(seq_count, D // HEAD)
    inner = seq_count // outer
    share = D // devices
    remote = share % 8 == 0
    everywhere = ("batch", "seq")
    grid = (batches, outer, inner // 2)

    tokens = tokens_in.reshape(tall, D)
    cot = out_cotangent.reshape(tall, D)
    earlier = earlier_outs.reshape(-1, tall, D)
    vecs = jnp.pad(small_params[: VECTORS * D].reshape(VECTORS, D), ((0, 16 - VECTORS), (0, 0)))
    mixing = small_params[VECTORS * D :]

    freq = 10000.0 ** (-jnp.arange(HEAD // 2, dtype=f32) * 2.0 / HEAD)
    query_pos = seq_rank * rows + jnp.arange(rows, dtype=jnp.int32)
    turned = query_pos.astype(f32)[:, None] * freq[None, :]
    cosine = jnp.concatenate([jnp.cos(turned)] * 4, 1)
    sine = jnp.concatenate([-jnp.sin(turned), jnp.sin(turned)] * 2, 1)
    block_pos = (jnp.arange(outer) * inner + seq_rank % inner)[:, None] * rows + jnp.arange(rows)[None, :]
    block_turned = block_pos.astype(f32)[:, None, :] * freq[None, :, None]
    block_cos, block_sin = jnp.cos(block_turned), jnp.sin(block_turned)

    def by_rows(shard):
        return shard.astype(bf16).reshape(share, -1, D).transpose(1, 0, 2)

    def by_blocks(gathered):
        return gathered.transpose(1, 0, 2, 3).reshape(-1, D, D)

    if remote:
        mine, normed, q, k, v, out, up, down, counts, mixture, dots, attended, turned_out, log_total = start_layer(
            qkv_weight, out_weight, up_weight, down_weight, seq_lengths, mixing, tokens, cot, earlier, vecs,
            block_cos, block_sin, batches, outer, inner, 1,
        )
        out, up, down = out.reshape(D, D), up.reshape(BLOCKS, D, D), down.reshape(BLOCKS, D, D)
    else:
        near = by_blocks(lax.all_gather(jnp.concatenate([by_rows(qkv_weight), by_rows(out_weight)], 0), everywhere, axis=0))
        out = near[3]
        up = by_blocks(lax.all_gather(by_rows(up_weight), everywhere, axis=0))
        down = lax.all_gather(down_weight.astype(bf16), everywhere, axis=0).reshape(BLOCKS, D, D)
        counts = jnp.full((1, 8, 128), lax.psum(jnp.sum(seq_lengths), "batch"), jnp.int32)
        wide = tokens.astype(f32)
        normed = (normalize(wide)[0] * vecs[0] + vecs[2]).astype(bf16)
        live = (query_pos[None, :] < seq_lengths[:, None]).astype(f32).reshape(tall, 1)
        terms = [tokens] + [earlier[i] for i in range(earlier.shape[0])]
        mixture = sum(mixing[1 + i] * term.astype(f32) for i, term in enumerate(terms))
        sums = [jnp.sum(cot.astype(f32) * live * term.astype(f32), 0) for term in terms]
        dots = jnp.pad(jnp.stack(sums), ((1, 15 - len(sums)), (0, 0)))
        q, k, v, attended, turned_out, log_total = spread_heads(
            normed, near, vecs, seq_lengths, cosine, sine, batches, outer, inner, 2
        )

    mixed, grad_mine, middle_grad, out_term, up_terms, down_terms, sums = middle_layer(
        attended, out, up, down, tokens, cot, mixture, counts, vecs, seq_lengths, mixing, batches, outer, inner, 3
    )
    dq, dk, dv = attend_back(seq_lengths, q, k, v, grad_mine, turned_out, log_total, block_cos, block_sin, inner)
    if remote:
        pieces = grid + (2 * share, D)
        input_grad, near_grad, up_grad, down_grad, out_grad, small = finish_layer(
            dq, dk, dv, up_terms.reshape((BLOCKS,) + pieces), down_terms.reshape(grid + (2, BLOCKS * share, D)), out_term.reshape(pieces),
            mine, normed, tokens, cot, middle_grad, counts, vecs, sums, dots, block_cos, block_sin, seq_lengths, mixing,
            batches, outer, inner, 4,
        )
    else:

        def scattered(terms):
            return lax.psum_scatter(terms.reshape(-1, devices, share, D), everywhere, scatter_dimension=1).astype(f32)

        dq, dk, dv = fold_heads(dq, dk, dv, batches, inner, 5)
        input_grad, near_terms, small = back_layer(
            dq, dk, dv, cosine, sine, normed, tokens, near, vecs, cot, counts, seq_lengths, mixing, middle_grad, out_term, sums, dots, outer
        )
        near_grad, up_grad = scattered(near_terms), scattered(up_terms)
        out_grad = near_grad[3]
        down_grad = lax.psum_scatter(down_terms.reshape(devices, -1, D), everywhere, scatter_dimension=0).astype(f32)
        small = lax.psum(small, everywhere)
    small_grad = small.reshape(-1)[: small_params.shape[0]]
    small_step, small_first_new = adam(small_params, small_grad, small_first, small_second, 0.0)
    (
        qkv_grad, qkv_step, qkv_first_new, out_grad, out_step, out_first_new,
        up_grad, up_step, up_first_new, down_grad, down_step, down_first_new,
    ) = adam_all(
        remote, near_grad, up_grad, down_grad, out_grad,
        (qkv_weight, qkv_first, qkv_second, out_weight, out_first, out_second,
         up_weight, up_first, up_second, down_weight, down_first, down_second),
    )
    return (
        mixed.reshape(tokens_in.shape),
        input_grad.reshape(tokens_in.shape),
        qkv_grad,
        out_grad,
        up_grad,
        down_grad,
        small_grad,
        qkv_step,
        out_step,
        up_step,
        down_step,
        small_step,
        qkv_first_new,
        out_first_new,
        up_first_new,
        down_first_new,
        small_first_new,
    )


def solution(mesh):
    placed = (
        P("batch", "seq", None),
        P(None, "batch", "seq", None),
        P("batch", "seq", None),
        P("batch"),
        P(("batch", "seq"), None),
        P(("batch", "seq"), None),
        P(("batch", "seq"), None),
        P(("batch", "seq"), None),
        P(("batch", "seq"), None),
        P(("batch", "seq"), None),
        P(("batch", "seq"), None),
        P(("batch", "seq"), None),
        P(("batch", "seq"), None),
        P(("batch", "seq"), None),
        P(("batch", "seq"), None),
        P(("batch", "seq"), None),
        P(),
        P(),
        P(),
    )
    return jax.shard_map(
        body,
        mesh=mesh,
        in_specs=placed,
        out_specs=(
            P("batch", "seq", None),
            P("batch", "seq", None),
            P(("batch", "seq"), None),
            P(("batch", "seq"), None),
            P(("batch", "seq"), None),
            P(("batch", "seq"), None),
            P(),
            P(("batch", "seq"), None),
            P(("batch", "seq"), None),
            P(("batch", "seq"), None),
            P(("batch", "seq"), None),
            P(),
            P(("batch", "seq"), None),
            P(("batch", "seq"), None),
            P(("batch", "seq"), None),
            P(("batch", "seq"), None),
            P(),
        ),
        check_vma=False,
    )
```
